32 devices in a mesh: wide: 8 (over z, core), narrow: 4 (over y, x).
Axes of the slice: x: 2, y: 2, z: 4, core: 2. Of those that a mesh axis runs over, the one named last changes fastest.
Arguments:
- hidden: bfloat16 [16384, 2048], P(('wide', 'narrow')), may hold values from -6 to 6
- mix_weight: bfloat16 [4, 2048, 2048], P(None, None, 'narrow'), may hold values from -0.125 to 0.125
- out_weight: bfloat16 [2048, 2048], P('narrow'), may hold values from -0.125 to 0.125
- ffn_in_weight: bfloat16 [2, 2048, 5632], P(None, None, 'narrow'), may hold values from -0.125 to 0.125
- ffn_out_weight: bfloat16 [5632, 2048], P('narrow'), may hold values from -0.078125 to 0.078125
- seq_lengths: int32 [16], P('wide'), may hold values from 0 to 2048, as said below
- block_seq: int32 [64], P('wide'), may hold values from 0 to 15, as said below
- cotangent: bfloat16 [16384, 2048], P(('wide', 'narrow')), may hold values from -6 to 6
Outputs:
- layer_out: bfloat16 [16384, 2048], P(('wide', 'narrow'))
- input_grad: bfloat16 [16384, 2048], P(('wide', 'narrow'))
- grad_mix: float32 [4, 2048, 2048], P(None, None, 'narrow')
- grad_out: float32 [2048, 2048], P('narrow')
- grad_ffn_in: float32 [2, 2048, 5632], P(None, None, 'narrow')
- grad_ffn_out: float32 [5632, 2048], P('narrow')
The draws below stay inside these ranges and needn't reach their ends.
Inputs may be any that keep to these rules, and one draw needn't show every extreme that they name: `seq_lengths`: slots 2g and 2g + 1 belong to index g of wide; the first holds a sequence of 1024 tokens or more; the second holds 0 or a length of 1024 or more. Index 0 holds one sequence of 2048 tokens. `block_seq`: the 8 blocks of index g of wide name slot 2g, then slot 2g + 1 if that slot's length is not 0; a slot of length L has exactly ceil(L / 256) blocks.
All inputs are finite; a program needn't handle non-finite values.
Results may differ from the reference program's by a relative error of at most 0.023.
Values may be sent and summed in bfloat16 or wider, within the bound.
A program may use at most 320 MiB of HBM per device.

```python
import jax
import jax.numpy as jnp
from jax import lax

D = 2048
HEADS = 16
HS = 128
FF = 5632
BLK = 256
NBLK = 8
TOKENS = 16384
N_WIDE = 8
N_NARROW = 4


def draw_plan(key):
    k_two, k_first, k_pad_one, k_pad_two = jax.random.split(key, 4)
    groups = jnp.arange(N_WIDE, dtype=jnp.int32)
    two_seqs = jax.random.randint(k_two, (N_WIDE,), 0, 2)
    two_seqs = jnp.where(groups == 0, 0, two_seqs)
    first_blocks = jax.random.randint(k_first, (N_WIDE,), 4, NBLK - 3)
    first_blocks = jnp.where(two_seqs == 1, first_blocks, NBLK)
    second_blocks = NBLK - first_blocks
    cap_one = jnp.minimum(BLK - 1, (first_blocks - 4) * BLK)
    cap_two = jnp.maximum(jnp.minimum(BLK - 1, (second_blocks - 4) * BLK), 0)
    pad_one = jax.random.randint(k_pad_one, (N_WIDE,), 0, cap_one + 1)
    pad_one = jnp.where(groups == 0, 0, pad_one)
    pad_two = jax.random.randint(k_pad_two, (N_WIDE,), 0, cap_two + 1)
    len_one = first_blocks * BLK - pad_one
    len_two = jnp.where(two_seqs == 1, second_blocks * BLK - pad_two, 0)
    lengths = jnp.stack([len_one, len_two], axis=1).reshape(-1).astype(jnp.int32)
    block_ids = jnp.arange(NBLK, dtype=jnp.int32)
    owners = 2 * groups[:, None] + (block_ids[None, :] >= first_blocks[:, None]).astype(jnp.int32)
    return (lengths, owners.reshape(-1).astype(jnp.int32))


def draw_seq_lengths(key, part):
    lengths, owners = draw_plan(key)
    return lengths


def draw_block_seq(key, part):
    lengths, owners = draw_plan(key)
    return owners


def shard_levels(key, extent, cuts, least, high):
    factor_of, own = 1.0, jax.random.fold_in(key, 6)
    for axis_at, blocks in cuts:
        draws = jnp.exp(jax.random.uniform(jax.random.fold_in(own, axis_at), (blocks,), jnp.float32, least / len(cuts), high / len(cuts)))
        factor_of = factor_of * jnp.repeat(draws, extent[axis_at] // blocks).reshape([-1 if axis == axis_at else 1 for axis in range(len(extent))])
    return factor_of


def bell_draw(rng, extent, spread, most, shards=(), kind=jnp.bfloat16):
    values = spread * jax.random.normal(rng, extent, jnp.float32)
    if shards:
        values = values * shard_levels(rng, extent, shards, -0.22, 0.18)
    return jnp.clip(values, -most, most).astype(kind)


def setup_inputs(seed: int = 0) -> dict:
    streams_of = jax.random.split(jax.random.key(seed), 9)
    hidden = bell_draw(streams_of[0], (TOKENS, D), 1.0, 6.0, ((0, 32),))
    mix_weight = bell_draw(streams_of[1], (4, D, D), D ** -0.5, 0.125, ((2, 4),))
    out_weight = bell_draw(streams_of[2], (D, D), D ** -0.5, 0.125, ((0, 4),))
    ffn_in_weight = bell_draw(streams_of[3], (2, D, FF), D ** -0.5, 0.125, ((2, 4),))
    ffn_out_weight = bell_draw(streams_of[4], (FF, D), FF ** -0.5, 0.078125, ((0, 4),))
    seq_lengths = draw_seq_lengths(jax.random.fold_in(streams_of[8], 71), 0)
    block_seq = draw_block_seq(jax.random.fold_in(streams_of[8], 71), 0)
    cotangent = bell_draw(streams_of[7], (TOKENS, D), 1.0, 6.0, ((0, 32),))
    return {"hidden": hidden, "mix_weight": mix_weight, "out_weight": out_weight, "ffn_in_weight": ffn_in_weight, "ffn_out_weight": ffn_out_weight, "seq_lengths": seq_lengths, "block_seq": block_seq, "cotangent": cotangent}


epsilon = 1e-06
head_floor = 1.0
highest = lax.Precision.HIGHEST

@jax.custom_vjp
def low(v):
    return lax.optimization_barrier(v.astype(jnp.bfloat16)).astype(jnp.float32)

@jax.custom_vjp
def low_back(v):
    return v

def low_keep(v):
    return (low(v), None)

def low_pass(kept, grad):
    return (grad,)

def back_keep(v):
    return (v, None)

def back_low(kept, grad):
    return (low(grad),)
low.defvjp(low_keep, low_pass)
low_back.defvjp(back_keep, back_low)

def row_norm(values):
    return values * lax.rsqrt(lax.optimization_barrier(jnp.mean(values * values, axis=-1, keepdims=True)) + epsilon)

def head_norm(values):
    return values * lax.rsqrt(lax.optimization_barrier(jnp.mean(values * values, axis=-1, keepdims=True)) + head_floor)

def shard_project(normed, weight):
    width = weight.shape[2] // N_NARROW
    pieces = [jnp.einsum('rd,cde->cre', low_back(normed), weight[:, :, shard * width:(shard + 1) * width], precision=highest) for shard in range(N_NARROW)]
    return jnp.concatenate(pieces, axis=2)

def shard_sum(acts, weight):
    width = weight.shape[0] // N_NARROW
    row_count = acts.shape[0]
    split_acts = acts.reshape(row_count, N_NARROW, width)
    split_weight = weight.reshape(N_NARROW, width, weight.shape[1])
    partial_sums = low(jnp.einsum('rke,ked->krd', split_acts, split_weight, precision=highest))
    return lax.optimization_barrier(jnp.sum(partial_sums, axis=0))

def decay_tables(decay_rates):
    positions = jnp.arange(BLK, dtype=jnp.float32)
    distance = positions[:, None] - positions[None, :]
    causal = distance >= 0
    clipped = jnp.where(causal, distance, 0.0)
    within = jnp.where(causal[None], jnp.exp(-decay_rates[:, None, None] * clipped[None]), 0.0)
    entry_decay = jnp.exp(-(positions[:, None] + 1.0) * decay_rates[None, :])
    exit_decay = jnp.exp(-(BLK - 1.0 - positions[:, None]) * decay_rates[None, :])
    block_decay = jnp.exp(-BLK * decay_rates)
    return (within, entry_decay, exit_decay, block_decay)

def group_masks(lengths, owners):
    seq_slot = (owners - owners[0]).astype(jnp.int32)
    first_count = jnp.sum((seq_slot == 0).astype(jnp.int32)).astype(jnp.int32)
    block_ids = jnp.arange(NBLK, dtype=jnp.int32)
    start_block = jnp.where(seq_slot == 0, jnp.int32(0), first_count).astype(jnp.int32)
    seq_limit = jnp.where(seq_slot == 0, lengths[0], lengths[1]).astype(jnp.int32)
    offsets = ((block_ids - start_block)[:, None] * BLK + jnp.arange(BLK, dtype=jnp.int32)[None, :]).astype(jnp.int32)
    valid_rows = (offsets < seq_limit[:, None]).reshape(-1)
    fresh_block = block_ids == start_block
    return (valid_rows, fresh_block)

def ref_block(tables, kv_state, block_in):
    within, entry_decay, exit_decay, block_decay = tables
    queries, keys_in, values, fresh_block = block_in
    kv_state = jnp.where(fresh_block, 0.0, kv_state)
    scores = low_back(jnp.einsum('ihs,jhs->hij', queries, keys_in, precision=highest))
    weights = low(scores * within)
    inner_part = jnp.einsum('hij,jhs->ihs', weights, values, precision=highest)
    carried = jnp.einsum('ihs,hst->iht', queries * entry_decay[:, :, None], kv_state, precision=highest)
    update = jnp.einsum('ihs,iht->hst', keys_in * exit_decay[:, :, None], values, precision=highest)
    return (block_decay[:, None, None] * kv_state + update, inner_part + carried)

def layer(rows_in, mix_weight, out_weight, ffn_in_weight, ffn_out_weight, valid_rows, fresh_block, tables):
    group_rows = NBLK * BLK
    normed = low(row_norm(rows_in))
    projected = low_back(shard_project(normed, mix_weight))
    queries = low(jax.nn.silu(projected[0])).reshape(NBLK, BLK, HEADS, HS)
    keys_in = low(jax.nn.silu(projected[1])).reshape(NBLK, BLK, HEADS, HS)
    values = low(projected[2]).reshape(NBLK, BLK, HEADS, HS)
    gate_part = projected[3]
    zero_state = jnp.zeros((HEADS, HS, HS), jnp.float32)
    stepper = jax.checkpoint(lambda state_in, block_in: ref_block(tables, state_in, block_in))
    final_state, mixing = lax.scan(stepper, zero_state, (queries, keys_in, values, fresh_block))
    mixing = low_back(mixing.reshape(group_rows, HEADS, HS))
    headed = head_norm(mixing).reshape(group_rows, D)
    gated = low(low_back(headed * gate_part))
    branch = low_back(shard_sum(gated, out_weight))
    middle = rows_in + valid_rows[:, None] * branch
    normed_two = low(row_norm(middle))
    both_parts = low_back(shard_project(normed_two, ffn_in_weight))
    hidden_act = low(both_parts[0] * both_parts[1])
    branch_two = low_back(shard_sum(hidden_act, ffn_out_weight))
    return middle + valid_rows[:, None] * branch_two

def reference(hidden, mix_weight, out_weight, ffn_in_weight, ffn_out_weight, seq_lengths, block_seq, cotangent):
    group_rows = NBLK * BLK
    weights = tuple((weight.astype(jnp.float32) for weight in (mix_weight, out_weight, ffn_in_weight, ffn_out_weight)))
    decay_rates = 2.0 ** (-8.0 * (jnp.arange(HEADS, dtype=jnp.float32) + 1.0) / HEADS)
    tables = decay_tables(decay_rates)
    inputs = hidden.astype(jnp.float32).reshape(N_WIDE, group_rows, D)
    cotangents = cotangent.astype(jnp.float32).reshape(N_WIDE, group_rows, D)
    lengths = seq_lengths.reshape(N_WIDE, 2)
    owners = block_seq.reshape(N_WIDE, NBLK)

    def per_group(totals, group_in):
        rows_in, cot_rows, length_pair, owner_row = group_in
        valid_rows, fresh_block = group_masks(length_pair, owner_row)
        valid_float = valid_rows.astype(jnp.float32)

        def forward(rows_here, mix_here, out_here, ffn_in_here, ffn_out_here):
            return layer(rows_here, mix_here, out_here, ffn_in_here, ffn_out_here, valid_float, fresh_block, tables)
        result, pull_back = jax.vjp(forward, rows_in, *weights)
        grads = pull_back(cot_rows)
        totals = tuple((summed + grad_one for summed, grad_one in zip(totals, grads[1:])))
        return (totals, (result.astype(jnp.bfloat16), grads[0].astype(jnp.bfloat16)))
    zero_grads = tuple((jnp.zeros_like(weight) for weight in weights))
    totals, (results, input_grads) = lax.scan(per_group, zero_grads, (inputs, cotangents, lengths, owners))
    return (results.reshape(TOKENS, D), input_grads.reshape(TOKENS, D), totals[0], totals[1], totals[2], totals[3])
```

```python
import functools

import jax
import jax.numpy as jnp
from jax import lax
from jax.experimental import pallas as pl
from jax.experimental.pallas import tpu as pltpu
from jax.sharding import PartitionSpec as P

HEADS = 16
HS = 128
BLK = 256
NBLK = 8


epsilon = 1e-06
head_floor = 1.0
highest = lax.Precision.HIGHEST


def row_norm(values):
    return values * lax.rsqrt(jnp.mean(values * values, axis=-1, keepdims=True) + epsilon)


def head_norm(values):
    return values * lax.rsqrt(jnp.mean(values * values, axis=-1, keepdims=True) + head_floor)


def silu_slope(values):
    sigmoid_part = jax.nn.sigmoid(values)
    return sigmoid_part * (1.0 + values * (1.0 - sigmoid_part))


def decay_tables(decay_rates):
    positions = jnp.arange(BLK, dtype=jnp.float32)
    distance = positions[:, None] - positions[None, :]
    causal = distance >= 0
    clipped = jnp.where(causal, distance, 0.0)
    within = jnp.where(causal[None], jnp.exp(-decay_rates[:, None, None] * clipped[None]), 0.0)
    entry_decay = jnp.exp(-(positions[:, None] + 1.0) * decay_rates[None, :])
    exit_decay = jnp.exp(-(BLK - 1.0 - positions[:, None]) * decay_rates[None, :])
    block_decay = jnp.exp(-BLK * decay_rates)
    return (within, entry_decay, exit_decay, block_decay)


def group_masks(lengths, owners):
    seq_slot = owners - owners[0]
    first_count = jnp.sum((seq_slot == 0).astype(jnp.int32))
    block_ids = jnp.arange(NBLK, dtype=jnp.int32)
    start_block = jnp.where(seq_slot == 0, jnp.int32(0), first_count)
    seq_limit = jnp.where(seq_slot == 0, lengths[0], lengths[1])
    offsets = (block_ids - start_block)[:, None] * BLK + jnp.arange(BLK, dtype=jnp.int32)[None, :]
    valid_rows = (offsets < seq_limit[:, None]).reshape(-1)
    fresh_block = block_ids == start_block
    return (valid_rows, fresh_block)


def forward_block(tables, kv_state, block_in):
    within, entry_decay, exit_decay, block_decay = tables
    queries, keys_in, values, fresh_block = block_in
    kv_state = jnp.where(fresh_block, 0.0, kv_state)
    scores = jnp.einsum("ihs,jhs->hij", queries, keys_in, preferred_element_type=jnp.float32)
    weights = (scores * within).astype(jnp.bfloat16)
    inner_part = jnp.einsum("hij,jhs->ihs", weights, values, preferred_element_type=jnp.float32)
    carried = jnp.einsum(
        "ihs,hst->iht",
        queries.astype(jnp.float32) * entry_decay[:, :, None],
        kv_state,
        precision=highest,
    )
    update = jnp.einsum(
        "ihs,iht->hst",
        keys_in.astype(jnp.float32) * exit_decay[:, :, None],
        values.astype(jnp.float32),
        precision=highest,
    )
    return (block_decay[:, None, None] * kv_state + update, (inner_part + carried, kv_state))


def backward_block(tables, later_grad, block_in):
    within, entry_decay, exit_decay, block_decay = tables
    queries, keys_in, values, grad_mix, kv_state, fresh_block = block_in
    scores = jnp.einsum("ihs,jhs->hij", queries, keys_in, preferred_element_type=jnp.float32)
    weights = (scores * within).astype(jnp.bfloat16)
    grad_values = jnp.einsum("hij,ihs->jhs", weights, grad_mix, preferred_element_type=jnp.float32)
    grad_weights = jnp.einsum("ihs,jhs->hij", grad_mix, values, preferred_element_type=jnp.float32)
    grad_scores = (grad_weights * within).astype(jnp.bfloat16)
    grad_queries = jnp.einsum(
        "hij,jhs->ihs", grad_scores, keys_in, preferred_element_type=jnp.float32
    )
    grad_keys = jnp.einsum("hij,ihs->jhs", grad_scores, queries, preferred_element_type=jnp.float32)
    grad_float = grad_mix.astype(jnp.float32)
    values_float = values.astype(jnp.float32)
    queries_float = queries.astype(jnp.float32)
    keys_float = keys_in.astype(jnp.float32)
    grad_queries = grad_queries + entry_decay[:, :, None] * jnp.einsum(
        "iht,hst->ihs", grad_float, kv_state, precision=highest
    )
    grad_keys = grad_keys + exit_decay[:, :, None] * jnp.einsum(
        "iht,hst->ihs", values_float, later_grad, precision=highest
    )
    grad_values = grad_values + jnp.einsum(
        "ihs,hst->iht", keys_float * exit_decay[:, :, None], later_grad, precision=highest
    )
    grad_state = jnp.einsum(
        "ihs,iht->hst", queries_float * entry_decay[:, :, None], grad_float, precision=highest
    )
    grad_state = grad_state + block_decay[:, None, None] * later_grad
    grad_state = jnp.where(fresh_block, 0.0, grad_state)
    return (grad_state, (grad_queries, grad_keys, grad_values))


def general_device(
    hidden, mix_weight, out_weight, ffn_in_weight, ffn_out_weight, seq_lengths, block_seq, cotangent
):
    local_rows = hidden.shape[0]
    group_rows = NBLK * BLK
    head_width = mix_weight.shape[2]
    head_count = head_width // HS
    narrow_index = lax.axis_index("narrow")
    valid_all, fresh_block = group_masks(seq_lengths, block_seq)
    valid_rows = lax.dynamic_slice_in_dim(
        valid_all.astype(jnp.float32), narrow_index * local_rows, local_rows
    )[:, None]
    head_ids = narrow_index * head_count + jnp.arange(head_count, dtype=jnp.int32)
    decay_rates = 2.0 ** (-8.0 * (head_ids.astype(jnp.float32) + 1.0) / HEADS)
    tables = decay_tables(decay_rates)

    def split_blocks(flat_rows):
        return flat_rows.reshape(NBLK, BLK, head_count, HS)

    inputs = hidden.astype(jnp.float32)
    normed_low = row_norm(inputs).astype(jnp.bfloat16)
    gathered = lax.all_gather(normed_low, "narrow", axis=0, tiled=True)
    projected = jnp.einsum("rd,cde->cre", gathered, mix_weight, preferred_element_type=jnp.float32)
    queries = jax.nn.silu(projected[0]).astype(jnp.bfloat16)
    keys_in = jax.nn.silu(projected[1]).astype(jnp.bfloat16)
    values = projected[2].astype(jnp.bfloat16)
    gate_part = projected[3]
    zero_state = jnp.zeros((head_count, HS, HS), jnp.float32)
    final_state, (mixing, kept_states) = lax.scan(
        lambda state_in, block_in: forward_block(tables, state_in, block_in),
        zero_state,
        (split_blocks(queries), split_blocks(keys_in), split_blocks(values), fresh_block),
    )
    mixing = mixing.reshape(group_rows, head_count, HS)
    headed = head_norm(mixing).reshape(group_rows, head_width)
    gated_low = (headed * gate_part).astype(jnp.bfloat16)
    branch = lax.psum_scatter(
        jnp.dot(gated_low, out_weight, preferred_element_type=jnp.float32).astype(jnp.bfloat16),
        "narrow",
        scatter_dimension=0,
        tiled=True,
    ).astype(jnp.float32)
    middle = inputs + valid_rows * branch
    normed_two_low = row_norm(middle).astype(jnp.bfloat16)
    gathered_two = lax.all_gather(normed_two_low, "narrow", axis=0, tiled=True)
    both_parts = jnp.einsum(
        "rd,cdf->crf", gathered_two, ffn_in_weight, preferred_element_type=jnp.float32
    )
    hidden_low = (both_parts[0] * both_parts[1]).astype(jnp.bfloat16)
    branch_two = lax.psum_scatter(
        jnp.dot(hidden_low, ffn_out_weight, preferred_element_type=jnp.float32).astype(
            jnp.bfloat16
        ),
        "narrow",
        scatter_dimension=0,
        tiled=True,
    ).astype(jnp.float32)
    layer_out = (middle + valid_rows * branch_two).astype(jnp.bfloat16)
    grad_rows = cotangent.astype(jnp.float32)
    ffn_grad_all = lax.all_gather(
        (valid_rows * grad_rows).astype(jnp.bfloat16), "narrow", axis=0, tiled=True
    )
    grad_ffn_out = jnp.einsum(
        "rf,rd->fd", hidden_low, ffn_grad_all, preferred_element_type=jnp.float32
    )
    grad_hidden = jnp.einsum(
        "rd,fd->rf", ffn_grad_all, ffn_out_weight, preferred_element_type=jnp.float32
    )
    grad_parts = jnp.stack([grad_hidden * both_parts[1], grad_hidden * both_parts[0]]).astype(
        jnp.bfloat16
    )
    grad_ffn_in = jnp.einsum(
        "rd,crf->cdf", gathered_two, grad_parts, preferred_element_type=jnp.float32
    )
    grad_slice = grad_parts
    grad_normed_two = lax.psum_scatter(
        jnp.einsum(
            "crf,cdf->rd", grad_slice, ffn_in_weight, preferred_element_type=jnp.float32
        ).astype(jnp.bfloat16),
        "narrow",
        scatter_dimension=0,
        tiled=True,
    ).astype(jnp.float32)
    norm_value, norm_pull = jax.vjp(row_norm, middle)
    grad_middle = grad_rows + norm_pull(grad_normed_two)[0]
    attn_grad_all = lax.all_gather(
        (valid_rows * grad_middle).astype(jnp.bfloat16), "narrow", axis=0, tiled=True
    )
    grad_out_weight = jnp.einsum(
        "re,rd->ed", gated_low, attn_grad_all, preferred_element_type=jnp.float32
    )
    grad_gated = jnp.einsum(
        "rd,ed->re", attn_grad_all, out_weight, preferred_element_type=jnp.float32
    )
    grad_gated = lax.optimization_barrier(grad_gated.astype(jnp.bfloat16)).astype(jnp.float32)
    grad_gate = grad_gated * headed
    grad_headed = (grad_gated * gate_part).reshape(group_rows, head_count, HS)
    head_value, head_pull = jax.vjp(head_norm, mixing)
    grad_mixing = head_pull(grad_headed)[0].astype(jnp.bfloat16)
    first_grad, (grad_queries, grad_keys, grad_values) = lax.scan(
        lambda later_grad, block_in: backward_block(tables, later_grad, block_in),
        zero_state,
        (
            split_blocks(queries),
            split_blocks(keys_in),
            split_blocks(values),
            split_blocks(grad_mixing),
            kept_states,
            fresh_block,
        ),
        reverse=True,
    )
    grad_projected = jnp.stack(
        [
            grad_queries.reshape(group_rows, head_width) * silu_slope(projected[0]),
            grad_keys.reshape(group_rows, head_width) * silu_slope(projected[1]),
            grad_values.reshape(group_rows, head_width),
            grad_gate,
        ]
    ).astype(jnp.bfloat16)
    grad_mix = jnp.einsum(
        "rd,cre->cde", gathered, grad_projected, preferred_element_type=jnp.float32
    )
    grad_slice = grad_projected
    grad_normed = lax.psum_scatter(
        jnp.einsum(
            "cre,cde->rd", grad_slice, mix_weight, preferred_element_type=jnp.float32
        ).astype(jnp.bfloat16),
        "narrow",
        scatter_dimension=0,
        tiled=True,
    ).astype(jnp.float32)
    first_value, first_pull = jax.vjp(row_norm, inputs)
    input_grad = (grad_middle + first_pull(grad_normed)[0]).astype(jnp.bfloat16)
    grad_mix, grad_out_weight, grad_ffn_in, grad_ffn_out = (
        lax.psum(grad_mix.astype(jnp.bfloat16), "wide").astype(jnp.float32),
        lax.psum(grad_out_weight.astype(jnp.bfloat16), "wide").astype(jnp.float32),
        lax.psum(grad_ffn_in.astype(jnp.bfloat16), "wide").astype(jnp.float32),
        lax.psum(grad_ffn_out.astype(jnp.bfloat16), "wide").astype(jnp.float32),
    )
    return (layer_out, input_grad, grad_mix, grad_out_weight, grad_ffn_in, grad_ffn_out)


HALF = BLK
PIECE = 2 * BLK
LINE = ((0, 1), (3, 2))
MIDDLE = ((1, 2), (2, 1))
BACK = ((1, 0), (2, 3))
VMEM = 60 * 1024 * 1024


def over_x(rows):
    return lax.ppermute(rows, "narrow", [(at, at ^ 1) for at in range(4)])


def over_y(rows):
    return lax.ppermute(rows, "narrow", [(at, at ^ 2) for at in range(4)])


def over_core(rows):
    return lax.ppermute(rows, "wide", [(at, at ^ 1) for at in range(8)])


def over_z(rows, pairs):
    return lax.ppermute(rows, "wide", [(2 * a + c, 2 * b + c) for a, b in pairs for c in range(2)])


def add_low(*terms):
    return sum(term.astype(jnp.float32) for term in terms).astype(jnp.bfloat16)


def gather_pieces(top, low):
    top_x, low_y = over_x(top), over_y(low)
    low_x, top_y = over_x(low), over_y(top)
    low_d, top_d = over_x(low_y), over_y(top_x)
    return ((top, low), (top_x, low_y), (low_x, top_y), (top_d, low_d))


def scatter_pieces(own, first, second, third):
    (top, low), (top_x, low_y), (low_x, top_y), (top_d, low_d) = own, first, second, third
    to_top_x, to_low_y = over_y(top_d), over_x(low_d)
    to_top, to_low = over_y(top_y), over_x(low_x)
    more_top, more_low = over_x(add_low(top_x, to_top_x)), over_y(add_low(low_y, to_low_y))
    total_top = top.astype(jnp.float32) + to_top.astype(jnp.float32) + more_top.astype(jnp.float32)
    total_low = low.astype(jnp.float32) + to_low.astype(jnp.float32) + more_low.astype(jnp.float32)
    return total_top, total_low


def slot_tables(narrow_index, fresh_block):
    block_ids = jnp.arange(NBLK, dtype=jnp.int32)
    partner = (block_ids // 2) ^ narrow_index
    even = jnp.array([0, 2, 5, 6], jnp.int32)[partner]
    odd = jnp.array([1, 4, 3, 7], jnp.int32)[partner]
    return jnp.where(block_ids % 2 == 0, even, odd), fresh_block.astype(jnp.int32)


def wide_sum(grad):
    wide_index = lax.axis_index("wide")
    z, core = wide_index // 2, wide_index % 2
    rows, columns = grad.shape
    quarters = grad.reshape(2, 2, rows // 4, columns)
    mine = lax.dynamic_index_in_dim(quarters, core, 0, keepdims=False)
    other = lax.dynamic_index_in_dim(quarters, 1 - core, 0, keepdims=False)
    both = add_low(mine, over_core(other))
    lined = add_low(both, over_z(both, LINE))
    inner = jnp.where(z == 1, 0, 1)
    kept = lax.dynamic_index_in_dim(lined, inner, 0, keepdims=False)
    sent = lax.dynamic_index_in_dim(lined, 1 - inner, 0, keepdims=False)
    total = add_low(kept, over_z(sent, MIDDLE))
    passed = over_z(total, MIDDLE)
    full = jnp.where(z == 1, jnp.stack([total, passed]), jnp.stack([passed, total]))
    end = (z == 0) | (z == 3)
    result = jnp.where(end, over_z(full, BACK), full)
    partner = over_core(result)
    result = jnp.where(core == 0, jnp.stack([result, partner]), jnp.stack([partner, result]))
    return result.reshape(rows, columns).astype(jnp.float32)


def load_pair(top_ref, low_ref, rows_ref, sems, at):
    return (
        pltpu.make_async_copy(top_ref, rows_ref.at[pl.ds(0, HALF)], sems.at[at]),
        pltpu.make_async_copy(low_ref, rows_ref.at[pl.ds(HALF, HALF)], sems.at[at + 1]),
    )


def across(left, right):
    return lax.dot_general(left, right, (((1,), (1,)), ((), ())), preferred_element_type=jnp.float32)


def down(left, right):
    return lax.dot_general(left, right, (((0,), (0,)), ((), ())), preferred_element_type=jnp.float32)


def straight(left, right):
    return jnp.dot(left, right, preferred_element_type=jnp.float32)


def any_specs(count):
    return [pl.BlockSpec(memory_space=pl.ANY)] * count


def cost(flops, bytes_accessed):
    return pl.CostEstimate(flops=int(flops), bytes_accessed=int(bytes_accessed), transcendentals=0)


def project_piece(pair, weight, kept, piece):
    parts, width, columns = weight.shape
    group_rows = NBLK * BLK

    def body(*refs):
        top_ref, low_ref, weight_ref = refs[:3]
        rows_ref, out_ref, sems = refs[-3:]

        @pl.when(pl.program_id(0) == 0)
        def _():
            copies = load_pair(top_ref, low_ref, rows_ref, sems, 0)
            for copy in copies:
                copy.start()
            for copy in copies:
                copy.wait()

        out_ref[0] = straight(rows_ref[...], weight_ref[0]).astype(jnp.bfloat16)

    return pl.pallas_call(
        body,
        grid=(parts,),
        in_specs=any_specs(2)
        + [pl.BlockSpec((1, width, columns), lambda c: (c, 0, 0))]
        + any_specs(len(kept)),
        out_specs=[
            pl.BlockSpec((PIECE, width), lambda c: (piece, 0)),
            pl.BlockSpec((1, PIECE, columns), lambda c: (c, piece, 0)),
        ],
        out_shape=[
            jax.ShapeDtypeStruct((group_rows, width), jnp.bfloat16),
            jax.ShapeDtypeStruct((parts, group_rows, columns), jnp.bfloat16),
        ],
        scratch_shapes=[pltpu.SemaphoreType.DMA((2,))],
        input_output_aliases={3 + at: at for at in range(len(kept))},
        compiler_params=pltpu.CompilerParams(vmem_limit_bytes=VMEM),
        cost_estimate=cost(2 * PIECE * parts * width * columns, 2 * parts * width * columns + 8e6),
        name="project",
    )(*pair, weight, *kept)


def back_piece(pair, weight, kept, piece):
    columns, width = weight.shape
    group_rows = NBLK * BLK

    def body(*refs):
        top_ref, low_ref, weight_ref = refs[:3]
        rows_ref, out_ref, sems = refs[-3:]
        copies = load_pair(top_ref, low_ref, rows_ref, sems, 0)
        for copy in copies:
            copy.start()
        for copy in copies:
            copy.wait()
        out_ref[...] = across(rows_ref[...], weight_ref[...]).astype(jnp.bfloat16)

    return pl.pallas_call(
        body,
        grid=(1,),
        in_specs=any_specs(2)
        + [pl.BlockSpec((columns, width), lambda c: (0, 0))]
        + any_specs(len(kept)),
        out_specs=[
            pl.BlockSpec((PIECE, width), lambda c: (piece, 0)),
            pl.BlockSpec((PIECE, columns), lambda c: (piece, 0)),
        ],
        out_shape=[
            jax.ShapeDtypeStruct((group_rows, width), jnp.bfloat16),
            jax.ShapeDtypeStruct((group_rows, columns), jnp.bfloat16),
        ],
        scratch_shapes=[pltpu.SemaphoreType.DMA((2,))],
        input_output_aliases={3 + at: at for at in range(len(kept))},
        compiler_params=pltpu.CompilerParams(vmem_limit_bytes=VMEM),
        cost_estimate=cost(2 * PIECE * width * columns, 2 * width * columns + 6e6),
        name="back_project",
    )(*pair, weight, *kept)


def sum_piece(acts, weight, piece, transposed):
    parts, group_rows, columns = acts.shape
    width = weight.shape[1] if transposed else weight.shape[2]

    def body(act_ref, weight_ref, top_ref, low_ref, total):
        part = pl.program_id(0)
        product = (across if transposed else straight)(act_ref[0], weight_ref[0])

        @pl.when(part == 0)
        def _():
            total[...] = product

        @pl.when(part > 0)
        def _():
            total[...] += product

        @pl.when(part == parts - 1)
        def _():
            top_ref[...] = total[:HALF].astype(jnp.bfloat16)
            low_ref[...] = total[HALF:].astype(jnp.bfloat16)

    return pl.pallas_call(
        body,
        grid=(parts,),
        in_specs=[
            pl.BlockSpec((1, PIECE, columns), lambda c: (c, piece, 0)),
            pl.BlockSpec((1,) + weight.shape[1:], lambda c: (c, 0, 0)),
        ],
        out_specs=[pl.BlockSpec((HALF, width), lambda c: (0, 0))] * 2,
        out_shape=[jax.ShapeDtypeStruct((HALF, width), jnp.bfloat16)] * 2,
        scratch_shapes=[pltpu.VMEM((PIECE, width), jnp.float32)],
        compiler_params=pltpu.CompilerParams(vmem_limit_bytes=VMEM),
        cost_estimate=cost(2 * PIECE * parts * width * columns, 2 * parts * width * columns + 4e6),
        name="partial_sum",
    )(acts, weight)


def unit_piece(pair, grad_pair, ffn_in, ffn_out, kept, piece):
    _, width, units = ffn_in.shape
    group_rows = NBLK * BLK
    tile = 256
    steps = pl.cdiv(units, tile)
    last = units - (steps - 1) * tile

    def body(*refs):
        top_ref, low_ref, grad_top_ref, grad_low_ref, in_ref, out_ref = refs[:6]
        rows_ref, grads_ref, act_ref, parts_ref = refs[-11:-7]
        sum_refs = refs[-7:-3]
        total_back, total_two, sems = refs[-3:]
        step = pl.program_id(0)

        @pl.when(step == 0)
        def _():
            copies = load_pair(top_ref, low_ref, rows_ref, sems, 0)
            copies += load_pair(grad_top_ref, grad_low_ref, grads_ref, sems, 2)
            for copy in copies:
                copy.start()
            total_back[...] = jnp.zeros_like(total_back)
            total_two[...] = jnp.zeros_like(total_two)
            for copy in copies:
                copy.wait()

        def work(size):
            rows = rows_ref[...]
            weight_a, weight_b = in_ref[0, :, :size], in_ref[1, :, :size]
            weight_out = out_ref[:size, :]
            part_a = straight(rows, weight_a)
            part_b = straight(rows, weight_b)
            grad_act = across(grads_ref[...], weight_out)
            act = (part_a * part_b).astype(jnp.bfloat16)
            grad_a = (grad_act * part_b).astype(jnp.bfloat16)
            grad_b = (grad_act * part_a).astype(jnp.bfloat16)
            act_ref[:, :size] = act
            parts_ref[0, :, :size] = grad_a
            parts_ref[1, :, :size] = grad_b
            total_two[...] += straight(act, weight_out)
            total_back[...] += across(grad_a, weight_a) + across(grad_b, weight_b)

        if last == tile:
            work(tile)
        else:
            pl.when(step < steps - 1)(lambda: work(tile))
            pl.when(step == steps - 1)(lambda: work(last))

        @pl.when(step == steps - 1)
        def _():
            for total, top_out, low_out in (
                (total_back, sum_refs[0], sum_refs[1]),
                (total_two, sum_refs[2], sum_refs[3]),
            ):
                top_out[...] = total[:HALF].astype(jnp.bfloat16)
                low_out[...] = total[HALF:].astype(jnp.bfloat16)

    low = jnp.bfloat16
    return pl.pallas_call(
        body,
        grid=(steps,),
        in_specs=any_specs(4)
        + [
            pl.BlockSpec((2, width, tile), lambda f: (0, 0, f)),
            pl.BlockSpec((tile, width), lambda f: (f, 0)),
        ]
        + any_specs(len(kept)),
        out_specs=[
            pl.BlockSpec((PIECE, width), lambda f: (piece, 0)),
            pl.BlockSpec((PIECE, width), lambda f: (piece, 0)),
            pl.BlockSpec((PIECE, tile), lambda f: (piece, f)),
            pl.BlockSpec((2, PIECE, tile), lambda f: (0, piece, f)),
        ]
        + [pl.BlockSpec((HALF, width), lambda f: (0, 0))] * 4,
        out_shape=[
            jax.ShapeDtypeStruct((group_rows, width), low),
            jax.ShapeDtypeStruct((group_rows, width), low),
            jax.ShapeDtypeStruct((group_rows, units), low),
            jax.ShapeDtypeStruct((2, group_rows, units), low),
        ]
        + [jax.ShapeDtypeStruct((HALF, width), low)] * 4,
        scratch_shapes=[
            pltpu.VMEM((PIECE, width), jnp.float32),
            pltpu.VMEM((PIECE, width), jnp.float32),
            pltpu.SemaphoreType.DMA((4,)),
        ],
        input_output_aliases={6 + at: at for at in range(len(kept))},
        compiler_params=pltpu.CompilerParams(vmem_limit_bytes=VMEM),
        cost_estimate=cost(12 * PIECE * width * units, 6 * width * units + 12e6),
        name="gated_unit",
    )(*pair, *grad_pair, ffn_in, ffn_out, *kept)


def block_decays(rate):
    row = lax.broadcasted_iota(jnp.int32, (BLK, BLK), 0)
    column = lax.broadcasted_iota(jnp.int32, (BLK, BLK), 1)
    distance = (row - column).astype(jnp.float32)
    within = jnp.where(row >= column, jnp.exp(-rate * jnp.maximum(distance, 0.0)), 0.0)
    place = lax.broadcasted_iota(jnp.int32, (BLK, 1), 0).astype(jnp.float32)
    entry = jnp.exp(-rate * (place + 1.0))
    leave = jnp.exp(-rate * (BLK - 1.0 - place))
    whole = jnp.exp(jnp.full((1, HS), -BLK * rate, jnp.float32))
    return within, entry, leave, whole


def mix_forward(slots, fresh, rates, parts):
    _, group_rows, columns = parts.shape
    heads = columns // HS
    low = jnp.bfloat16

    def body(slot_ref, fresh_ref, rate_ref, parts_ref, gated_ref, mixing_ref, states_ref):
        within, entry, leave, whole = block_decays(rate_ref[pl.program_id(0)])
        state = jnp.zeros((HS, HS), jnp.float32)
        for block in range(NBLK):
            rows = pl.ds(pl.multiple_of(slot_ref[block] * BLK, BLK), BLK)
            queries = jax.nn.silu(parts_ref[0, rows, :].astype(jnp.float32)).astype(low)
            keys = jax.nn.silu(parts_ref[1, rows, :].astype(jnp.float32))
            values = parts_ref[2, rows, :]
            gate = parts_ref[3, rows, :].astype(jnp.float32)
            state = jnp.where(fresh_ref[block] != 0, 0.0, state)
            state_low = state.astype(low)
            states_ref[0, block] = state_low
            weights = (across(queries, keys.astype(low)) * within).astype(low)
            mixing = straight(weights, values) + entry * straight(queries, state_low)
            late_keys = (keys.astype(low).astype(jnp.float32) * leave).astype(low)
            state = whole * state + down(late_keys, values)
            scale = lax.rsqrt(jnp.mean(mixing * mixing, axis=-1, keepdims=True) + head_floor)
            gated_ref[0, rows, :] = (mixing * scale * gate).astype(low)
            mixing_ref[rows, :] = mixing.astype(low)

    return pl.pallas_call(
        body,
        grid_spec=pltpu.PrefetchScalarGridSpec(
            num_scalar_prefetch=3,
            grid=(heads,),
            in_specs=[pl.BlockSpec((4, group_rows, HS), lambda h, *_: (0, 0, h))],
            out_specs=[
                pl.BlockSpec((1, group_rows, HS), lambda h, *_: (0, 0, h)),
                pl.BlockSpec((group_rows, HS), lambda h, *_: (0, h)),
                pl.BlockSpec((1, NBLK, HS, HS), lambda h, *_: (h, 0, 0, 0)),
            ],
        ),
        out_shape=[
            jax.ShapeDtypeStruct((1, group_rows, columns), low),
            jax.ShapeDtypeStruct((group_rows, columns), low),
            jax.ShapeDtypeStruct((heads, NBLK, HS, HS), low),
        ],
        compiler_params=pltpu.CompilerParams(vmem_limit_bytes=VMEM),
        cost_estimate=cost(8e9, 14e6),
        name="mix_forward",
    )(slots, fresh, rates, parts)


def mix_backward(slots, fresh, rates, parts, mixing_all, states, grad_gated):
    _, group_rows, columns = parts.shape
    heads = columns // HS
    low = jnp.bfloat16

    def body(
        slot_ref, fresh_ref, rate_ref, parts_ref, mixing_ref, states_ref, grad_ref, out_ref
    ):
        within, entry, leave, whole = block_decays(rate_ref[pl.program_id(0)])
        later = jnp.zeros((HS, HS), jnp.float32)
        for block in reversed(range(NBLK)):
            rows = pl.ds(pl.multiple_of(slot_ref[block] * BLK, BLK), BLK)
            raw_queries = parts_ref[0, rows, :].astype(jnp.float32)
            raw_keys = parts_ref[1, rows, :].astype(jnp.float32)
            queries_float = jax.nn.silu(raw_queries).astype(low).astype(jnp.float32)
            queries, keys = queries_float.astype(low), jax.nn.silu(raw_keys).astype(low)
            values = parts_ref[2, rows, :]
            gate = parts_ref[3, rows, :].astype(jnp.float32)
            mixing = mixing_ref[rows, :].astype(jnp.float32)
            grad_gated_rows = grad_ref[rows, :].astype(jnp.float32)
            scale = lax.rsqrt(jnp.mean(mixing * mixing, axis=-1, keepdims=True) + head_floor)
            headed = mixing * scale
            out_ref[3, rows, :] = (grad_gated_rows * headed).astype(low)
            grad_headed = grad_gated_rows * gate
            inner = jnp.mean(grad_headed * headed, axis=-1, keepdims=True)
            grad = (scale * (grad_headed - headed * inner)).astype(low)
            weights = (across(queries, keys) * within).astype(low)
            grad_scores = (across(grad, values) * within).astype(low)
            later_low = later.astype(low)
            grad_queries = straight(grad_scores, keys) + entry * across(grad, states_ref[0, block])
            grad_keys = down(grad_scores, queries) + leave * across(values, later_low)
            grad_values = down(weights, grad) + leave * straight(keys, later_low)
            early_queries = (queries_float * entry).astype(low)
            later = jnp.where(fresh_ref[block] != 0, 0.0, whole * later + down(early_queries, grad))
            out_ref[0, rows, :] = (grad_queries * silu_slope(raw_queries)).astype(low)
            out_ref[1, rows, :] = (grad_keys * silu_slope(raw_keys)).astype(low)
            out_ref[2, rows, :] = grad_values.astype(low)

    return pl.pallas_call(
        body,
        grid_spec=pltpu.PrefetchScalarGridSpec(
            num_scalar_prefetch=3,
            grid=(heads,),
            in_specs=[
                pl.BlockSpec((4, group_rows, HS), lambda h, *_: (0, 0, h)),
                pl.BlockSpec((group_rows, HS), lambda h, *_: (0, h)),
                pl.BlockSpec((1, NBLK, HS, HS), lambda h, *_: (h, 0, 0, 0)),
                pl.BlockSpec((group_rows, HS), lambda h, *_: (0, h)),
            ],
            out_specs=pl.BlockSpec((4, group_rows, HS), lambda h, *_: (0, 0, h)),
        ),
        out_shape=jax.ShapeDtypeStruct(parts.shape, low),
        compiler_params=pltpu.CompilerParams(vmem_limit_bytes=VMEM),
        cost_estimate=cost(20e9, 22e6),
        name="mix_backward",
    )(slots, fresh, rates, parts, mixing_all, states, grad_gated)


def norm_back(values, grad):
    scale = lax.rsqrt(jnp.mean(values * values, axis=-1, keepdims=True) + epsilon)
    unit = values * scale
    return scale * (grad - unit * jnp.mean(grad * unit, axis=-1, keepdims=True))


def square_device(
    hidden, mix_weight, out_weight, ffn_in_weight, ffn_out_weight, seq_lengths, block_seq, cotangent
):
    local_rows = hidden.shape[0]
    head_count = mix_weight.shape[2] // HS
    narrow_index = lax.axis_index("narrow")
    valid_all, fresh_block = group_masks(seq_lengths, block_seq)
    live = lax.dynamic_slice_in_dim(
        valid_all.astype(jnp.float32), narrow_index * local_rows, local_rows
    )[:, None]
    head_ids = narrow_index * head_count + jnp.arange(head_count, dtype=jnp.int32)
    rates = 2.0 ** (-8.0 * (head_ids.astype(jnp.float32) + 1.0) / HEADS)
    slots, fresh = slot_tables(narrow_index, fresh_block)
    low = jnp.bfloat16

    def halves(rows):
        return rows[:HALF], rows[HALF:]

    lives = halves(live)
    inputs = [rows.astype(jnp.float32) for rows in halves(hidden)]
    grads_in = [rows.astype(jnp.float32) for rows in halves(cotangent)]

    pieces = gather_pieces(*(row_norm(rows).astype(low) for rows in inputs))
    kept = ()
    for at, pair in enumerate(pieces):
        kept = project_piece(pair, mix_weight, kept, at)
    normed_all, parts = kept
    grad_pieces = gather_pieces(*((m * g).astype(low) for m, g in zip(lives, grads_in)))

    gated, mixing, states = mix_forward(slots, fresh, rates, parts)
    partial = [sum_piece(gated, out_weight[None], at, False) for at in range(4)]
    branch = scatter_pieces(*partial)
    middle = [x + m * b for x, m, b in zip(inputs, lives, branch)]

    pieces = gather_pieces(*(row_norm(rows).astype(low) for rows in middle))
    kept, back_sums, two_sums = (), [], []
    for at, (pair, grad_pair) in enumerate(zip(pieces, grad_pieces)):
        *kept, back_top, back_low, two_top, two_low = unit_piece(
            pair, grad_pair, ffn_in_weight, ffn_out_weight, kept, at
        )
        back_sums.append((back_top, back_low))
        two_sums.append((two_top, two_low))
    normed_two_all, grad_two_all, act, grad_parts = kept
    grad_normed_two = scatter_pieces(*back_sums)
    grad_middle = [g + norm_back(v, n) for g, v, n in zip(grads_in, middle, grad_normed_two)]
    pieces = gather_pieces(*((m * g).astype(low) for m, g in zip(lives, grad_middle)))

    grad_ffn_out = wide_sum(down(act, grad_two_all).astype(low))
    grad_ffn_in = jnp.stack(
        [wide_sum(down(normed_two_all, grad_parts[c]).astype(low)) for c in range(2)]
    )

    kept = ()
    for at, pair in enumerate(pieces):
        kept = back_piece(pair, out_weight, kept, at)
    grad_branch_all, grad_gated = kept
    grad_out = wide_sum(down(gated[0], grad_branch_all).astype(low))
    grad_projected = mix_backward(slots, fresh, rates, parts, mixing, states, grad_gated)
    partial = [sum_piece(grad_projected, mix_weight, at, True) for at in range(4)]
    grad_normed = scatter_pieces(*partial)
    grad_mix = jnp.stack(
        [wide_sum(down(normed_all, grad_projected[c]).astype(low)) for c in range(4)]
    )
    branch_two = scatter_pieces(*two_sums)
    layer_out = jnp.concatenate(
        [(v + m * b).astype(low) for v, m, b in zip(middle, lives, branch_two)]
    )
    input_grad = jnp.concatenate(
        [(g + norm_back(x, n)).astype(low) for g, x, n in zip(grad_middle, inputs, grad_normed)]
    )
    return (layer_out, input_grad, grad_mix, grad_out, grad_ffn_in, grad_ffn_out)


def solution(mesh):
    square = mesh.shape["wide"] == 8 and mesh.shape["narrow"] == 4
    per_device = square_device if square else general_device
    in_specs = (
        P(("wide", "narrow"), None),
        P(None, None, "narrow"),
        P("narrow", None),
        P(None, None, "narrow"),
        P("narrow", None),
        P("wide"),
        P("wide"),
        P(("wide", "narrow"), None),
    )
    out_specs = (
        P(("wide", "narrow"), None),
        P(("wide", "narrow"), None),
        P(None, None, "narrow"),
        P("narrow", None),
        P(None, None, "narrow"),
        P("narrow", None),
    )
    return jax.shard_map(
        per_device, mesh=mesh, in_specs=in_specs, out_specs=out_specs, check_vma=False
    )
```

```python
import functools

import jax
import jax.numpy as jnp
from jax import lax
from jax.experimental import pallas as pl
from jax.experimental.pallas import tpu as pltpu
from jax.sharding import PartitionSpec as P

HEADS = 16
HS = 128
BLK = 256
NBLK = 8


epsilon = 1e-06
head_floor = 1.0
highest = lax.Precision.HIGHEST


def row_norm(values):
    return values * lax.rsqrt(jnp.mean(values * values, axis=-1, keepdims=True) + epsilon)


def head_norm(values):
    return values * lax.rsqrt(jnp.mean(values * values, axis=-1, keepdims=True) + head_floor)


def silu_slope(values):
    sigmoid_part = jax.nn.sigmoid(values)
    return sigmoid_part * (1.0 + values * (1.0 - sigmoid_part))


def decay_tables(decay_rates):
    positions = jnp.arange(BLK, dtype=jnp.float32)
    distance = positions[:, None] - positions[None, :]
    causal = distance >= 0
    clipped = jnp.where(causal, distance, 0.0)
    within = jnp.where(causal[None], jnp.exp(-decay_rates[:, None, None] * clipped[None]), 0.0)
    entry_decay = jnp.exp(-(positions[:, None] + 1.0) * decay_rates[None, :])
    exit_decay = jnp.exp(-(BLK - 1.0 - positions[:, None]) * decay_rates[None, :])
    block_decay = jnp.exp(-BLK * decay_rates)
    return (within, entry_decay, exit_decay, block_decay)


def group_masks(lengths, owners):
    seq_slot = owners - owners[0]
    first_count = jnp.sum((seq_slot == 0).astype(jnp.int32))
    block_ids = jnp.arange(NBLK, dtype=jnp.int32)
    start_block = jnp.where(seq_slot == 0, jnp.int32(0), first_count)
    seq_limit = jnp.where(seq_slot == 0, lengths[0], lengths[1])
    offsets = (block_ids - start_block)[:, None] * BLK + jnp.arange(BLK, dtype=jnp.int32)[None, :]
    valid_rows = (offsets < seq_limit[:, None]).reshape(-1)
    fresh_block = block_ids == start_block
    return (valid_rows, fresh_block)


def forward_block(tables, kv_state, block_in):
    within, entry_decay, exit_decay, block_decay = tables
    queries, keys_in, values, fresh_block = block_in
    kv_state = jnp.where(fresh_block, 0.0, kv_state)
    scores = jnp.einsum("ihs,jhs->hij", queries, keys_in, preferred_element_type=jnp.float32)
    weights = (scores * within).astype(jnp.bfloat16)
    inner_part = jnp.einsum("hij,jhs->ihs", weights, values, preferred_element_type=jnp.float32)
    carried = jnp.einsum(
        "ihs,hst->iht",
        queries.astype(jnp.float32) * entry_decay[:, :, None],
        kv_state,
        precision=highest,
    )
    update = jnp.einsum(
        "ihs,iht->hst",
        keys_in.astype(jnp.float32) * exit_decay[:, :, None],
        values.astype(jnp.float32),
        precision=highest,
    )
    return (block_decay[:, None, None] * kv_state + update, (inner_part + carried, kv_state))


def backward_block(tables, later_grad, block_in):
    within, entry_decay, exit_decay, block_decay = tables
    queries, keys_in, values, grad_mix, kv_state, fresh_block = block_in
    scores = jnp.einsum("ihs,jhs->hij", queries, keys_in, preferred_element_type=jnp.float32)
    weights = (scores * within).astype(jnp.bfloat16)
    grad_values = jnp.einsum("hij,ihs->jhs", weights, grad_mix, preferred_element_type=jnp.float32)
    grad_weights = jnp.einsum("ihs,jhs->hij", grad_mix, values, preferred_element_type=jnp.float32)
    grad_scores = (grad_weights * within).astype(jnp.bfloat16)
    grad_queries = jnp.einsum(
        "hij,jhs->ihs", grad_scores, keys_in, preferred_element_type=jnp.float32
    )
    grad_keys = jnp.einsum("hij,ihs->jhs", grad_scores, queries, preferred_element_type=jnp.float32)
    grad_float = grad_mix.astype(jnp.float32)
    values_float = values.astype(jnp.float32)
    queries_float = queries.astype(jnp.float32)
    keys_float = keys_in.astype(jnp.float32)
    grad_queries = grad_queries + entry_decay[:, :, None] * jnp.einsum(
        "iht,hst->ihs", grad_float, kv_state, precision=highest
    )
    grad_keys = grad_keys + exit_decay[:, :, None] * jnp.einsum(
        "iht,hst->ihs", values_float, later_grad, precision=highest
    )
    grad_values = grad_values + jnp.einsum(
        "ihs,hst->iht", keys_float * exit_decay[:, :, None], later_grad, precision=highest
    )
    grad_state = jnp.einsum(
        "ihs,iht->hst", queries_float * entry_decay[:, :, None], grad_float, precision=highest
    )
    grad_state = grad_state + block_decay[:, None, None] * later_grad
    grad_state = jnp.where(fresh_block, 0.0, grad_state)
    return (grad_state, (grad_queries, grad_keys, grad_values))


def general_device(
    hidden, mix_weight, out_weight, ffn_in_weight, ffn_out_weight, seq_lengths, block_seq, cotangent
):
    local_rows = hidden.shape[0]
    group_rows = NBLK * BLK
    head_width = mix_weight.shape[2]
    head_count = head_width // HS
    narrow_index = lax.axis_index("narrow")
    valid_all, fresh_block = group_masks(seq_lengths, block_seq)
    valid_rows = lax.dynamic_slice_in_dim(
        valid_all.astype(jnp.float32), narrow_index * local_rows, local_rows
    )[:, None]
    head_ids = narrow_index * head_count + jnp.arange(head_count, dtype=jnp.int32)
    decay_rates = 2.0 ** (-8.0 * (head_ids.astype(jnp.float32) + 1.0) / HEADS)
    tables = decay_tables(decay_rates)

    def split_blocks(flat_rows):
        return flat_rows.reshape(NBLK, BLK, head_count, HS)

    inputs = hidden.astype(jnp.float32)
    normed_low = row_norm(inputs).astype(jnp.bfloat16)
    gathered = lax.all_gather(normed_low, "narrow", axis=0, tiled=True)
    projected = jnp.einsum("rd,cde->cre", gathered, mix_weight, preferred_element_type=jnp.float32)
    queries = jax.nn.silu(projected[0]).astype(jnp.bfloat16)
    keys_in = jax.nn.silu(projected[1]).astype(jnp.bfloat16)
    values = projected[2].astype(jnp.bfloat16)
    gate_part = projected[3]
    zero_state = jnp.zeros((head_count, HS, HS), jnp.float32)
    final_state, (mixing, kept_states) = lax.scan(
        lambda state_in, block_in: forward_block(tables, state_in, block_in),
        zero_state,
        (split_blocks(queries), split_blocks(keys_in), split_blocks(values), fresh_block),
    )
    mixing = mixing.reshape(group_rows, head_count, HS)
    headed = head_norm(mixing).reshape(group_rows, head_width)
    gated_low = (headed * gate_part).astype(jnp.bfloat16)
    branch = lax.psum_scatter(
        jnp.dot(gated_low, out_weight, preferred_element_type=jnp.float32).astype(jnp.bfloat16),
        "narrow",
        scatter_dimension=0,
        tiled=True,
    ).astype(jnp.float32)
    middle = inputs + valid_rows * branch
    normed_two_low = row_norm(middle).astype(jnp.bfloat16)
    gathered_two = lax.all_gather(normed_two_low, "narrow", axis=0, tiled=True)
    both_parts = jnp.einsum(
        "rd,cdf->crf", gathered_two, ffn_in_weight, preferred_element_type=jnp.float32
    )
    hidden_low = (both_parts[0] * both_parts[1]).astype(jnp.bfloat16)
    branch_two = lax.psum_scatter(
        jnp.dot(hidden_low, ffn_out_weight, preferred_element_type=jnp.float32).astype(
            jnp.bfloat16
        ),
        "narrow",
        scatter_dimension=0,
        tiled=True,
    ).astype(jnp.float32)
    layer_out = (middle + valid_rows * branch_two).astype(jnp.bfloat16)
    grad_rows = cotangent.astype(jnp.float32)
    ffn_grad_all = lax.all_gather(
        (valid_rows * grad_rows).astype(jnp.bfloat16), "narrow", axis=0, tiled=True
    )
    grad_ffn_out = jnp.einsum(
        "rf,rd->fd", hidden_low, ffn_grad_all, preferred_element_type=jnp.float32
    )
    grad_hidden = jnp.einsum(
        "rd,fd->rf", ffn_grad_all, ffn_out_weight, preferred_element_type=jnp.float32
    )
    grad_parts = jnp.stack([grad_hidden * both_parts[1], grad_hidden * both_parts[0]]).astype(
        jnp.bfloat16
    )
    grad_ffn_in = jnp.einsum(
        "rd,crf->cdf", gathered_two, grad_parts, preferred_element_type=jnp.float32
    )
    grad_slice = grad_parts
    grad_normed_two = lax.psum_scatter(
        jnp.einsum(
            "crf,cdf->rd", grad_slice, ffn_in_weight, preferred_element_type=jnp.float32
        ).astype(jnp.bfloat16),
        "narrow",
        scatter_dimension=0,
        tiled=True,
    ).astype(jnp.float32)
    norm_value, norm_pull = jax.vjp(row_norm, middle)
    grad_middle = grad_rows + norm_pull(grad_normed_two)[0]
    attn_grad_all = lax.all_gather(
        (valid_rows * grad_middle).astype(jnp.bfloat16), "narrow", axis=0, tiled=True
    )
    grad_out_weight = jnp.einsum(
        "re,rd->ed", gated_low, attn_grad_all, preferred_element_type=jnp.float32
    )
    grad_gated = jnp.einsum(
        "rd,ed->re", attn_grad_all, out_weight, preferred_element_type=jnp.float32
    )
    grad_gated = lax.optimization_barrier(grad_gated.astype(jnp.bfloat16)).astype(jnp.float32)
    grad_gate = grad_gated * headed
    grad_headed = (grad_gated * gate_part).reshape(group_rows, head_count, HS)
    head_value, head_pull = jax.vjp(head_norm, mixing)
    grad_mixing = head_pull(grad_headed)[0].astype(jnp.bfloat16)
    first_grad, (grad_queries, grad_keys, grad_values) = lax.scan(
        lambda later_grad, block_in: backward_block(tables, later_grad, block_in),
        zero_state,
        (
            split_blocks(queries),
            split_blocks(keys_in),
            split_blocks(values),
            split_blocks(grad_mixing),
            kept_states,
            fresh_block,
        ),
        reverse=True,
    )
    grad_projected = jnp.stack(
        [
            grad_queries.reshape(group_rows, head_width) * silu_slope(projected[0]),
            grad_keys.reshape(group_rows, head_width) * silu_slope(projected[1]),
            grad_values.reshape(group_rows, head_width),
            grad_gate,
        ]
    ).astype(jnp.bfloat16)
    grad_mix = jnp.einsum(
        "rd,cre->cde", gathered, grad_projected, preferred_element_type=jnp.float32
    )
    grad_slice = grad_projected
    grad_normed = lax.psum_scatter(
        jnp.einsum(
            "cre,cde->rd", grad_slice, mix_weight, preferred_element_type=jnp.float32
        ).astype(jnp.bfloat16),
        "narrow",
        scatter_dimension=0,
        tiled=True,
    ).astype(jnp.float32)
    first_value, first_pull = jax.vjp(row_norm, inputs)
    input_grad = (grad_middle + first_pull(grad_normed)[0]).astype(jnp.bfloat16)
    grad_mix, grad_out_weight, grad_ffn_in, grad_ffn_out = (
        lax.psum(grad_mix.astype(jnp.bfloat16), "wide").astype(jnp.float32),
        lax.psum(grad_out_weight.astype(jnp.bfloat16), "wide").astype(jnp.float32),
        lax.psum(grad_ffn_in.astype(jnp.bfloat16), "wide").astype(jnp.float32),
        lax.psum(grad_ffn_out.astype(jnp.bfloat16), "wide").astype(jnp.float32),
    )
    return (layer_out, input_grad, grad_mix, grad_out_weight, grad_ffn_in, grad_ffn_out)


HALF = BLK
PIECE = 2 * BLK
VMEM = 60 * 1024 * 1024


def over_x(rows):
    return lax.ppermute(rows, "narrow", [(at, at ^ 1) for at in range(4)])


def over_y(rows):
    return lax.ppermute(rows, "narrow", [(at, at ^ 2) for at in range(4)])


def add_low(*terms):
    return sum(term.astype(jnp.float32) for term in terms).astype(jnp.bfloat16)


def gather_pieces(top, low):
    top_x, low_y = over_x(top), over_y(low)
    low_x, top_y = over_x(low), over_y(top)
    low_d, top_d = over_x(low_y), over_y(top_x)
    return ((top, low), (top_x, low_y), (low_x, top_y), (top_d, low_d))


def scatter_pieces(own, first, second, third):
    (top, low), (top_x, low_y), (low_x, top_y), (top_d, low_d) = own, first, second, third
    to_top_y, to_low_x = over_x(top_d), over_y(low_d)
    to_top, to_low = over_x(top_x), over_y(low_y)
    more_top, more_low = over_y(add_low(top_y, to_top_y)), over_x(add_low(low_x, to_low_x))
    return add_rows(top, to_top, more_top), add_rows(low, to_low, more_low)


def add_rows(*terms):
    return sum(term.astype(jnp.float32) for term in terms)


def slot_tables(narrow_index, fresh_block):
    block_ids = jnp.arange(NBLK, dtype=jnp.int32)
    partner = (block_ids // 2) ^ narrow_index
    even = jnp.array([0, 2, 5, 6], jnp.int32)[partner]
    odd = jnp.array([1, 4, 3, 7], jnp.int32)[partner]
    return jnp.where(block_ids % 2 == 0, even, odd), fresh_block.astype(jnp.int32)


def across(left, right):
    return lax.dot_general(left, right, (((1,), (1,)), ((), ())), preferred_element_type=jnp.float32)


def down(left, right):
    return lax.dot_general(left, right, (((0,), (0,)), ((), ())), preferred_element_type=jnp.float32)


def straight(left, right):
    return jnp.dot(left, right, preferred_element_type=jnp.float32)


def any_specs(count):
    return [pl.BlockSpec(memory_space=pl.ANY)] * count


def cost(flops, bytes_accessed):
    return pl.CostEstimate(flops=int(flops), bytes_accessed=int(bytes_accessed), transcendentals=0)


MESH = pl.DeviceIdType.MESH
SLOTS = 13
STAGES = 12
SUB = 128
TILE = 256


def begin(copies):
    for copy in copies:
        copy.start()


def finish(copies):
    for copy in copies:
        copy.wait()


def neighbours():
    wide, narrow = lax.axis_index("wide"), lax.axis_index("narrow")
    z, core = wide // 2, wide % 2
    mate = (wide + 1 - 2 * core, narrow)
    near_x = (wide, narrow + 1 - 2 * (narrow % 2))
    near_y = (wide, (narrow + 2) % 4)
    return wide, narrow, z, core, mate, near_x, near_y


def line_scratch():
    low = jnp.bfloat16
    pair = pltpu.VMEM((SLOTS, 2, SUB, TILE), low)
    return [
        pltpu.VMEM((SLOTS, 4, SUB, TILE), low),
        pair,
        pair,
        pair,
        pltpu.VMEM((SLOTS, SUB, TILE), low),
        pair,
        pair,
        pltpu.SemaphoreType.DMA((14, SLOTS)),
        pltpu.SemaphoreType.DMA((4, SLOTS)),
    ]


def enter(neighbour_places):
    wide, narrow, z, core, mate, near_x, near_y = neighbour_places
    barrier = pltpu.get_barrier_semaphore()

    def greet(place):
        pl.semaphore_signal(barrier, inc=1, device_id=place, device_id_type=MESH)

    for place in (mate, near_x, near_y):
        greet(place)
    middle = (z == 1) | (z == 2)

    @pl.when(middle)
    def _():
        greet((2 * (3 - z) + core, narrow))
        greet((6 * (z - 1) + core, narrow))
        pl.semaphore_wait(barrier, 5)

    @pl.when(jnp.logical_not(middle))
    def _():
        greet((2 * (1 + z // 3) + core, narrow))
        pl.semaphore_wait(barrier, 4)


def line_sum(scratch, places, count, product, targets):
    own, met, both, ended, crossed, full, other, sems, out_sems = scratch
    wide, narrow, z, core, mate, _, _ = places
    region = z // 2
    middle = (z == 1) | (z == 2)
    end = jnp.logical_not(middle)
    inward = (2 * (1 + z // 3) + core, narrow)
    across_line = (2 * (3 - z) + core, narrow)
    outward = (6 * (z - 1) + core, narrow)

    def remote(src, dst, kind, slot, place):
        return pltpu.make_async_remote_copy(
            src_ref=src,
            dst_ref=dst,
            send_sem=sems.at[2 * kind, slot],
            recv_sem=sems.at[2 * kind + 1, slot],
            device_id=place,
            device_id_type=MESH,
        )

    def core_one(s):
        return remote(own.at[s, pl.ds(2 * (1 - core), 2)], met.at[s], 0, s, mate)

    def line_one(s):
        return remote(both.at[s], ended.at[s], 1, s, inward)

    def cross_one(s):
        return remote(both.at[s, 1 - region], crossed.at[s], 2, s, across_line)

    def cross_two(s):
        return remote(full.at[s, region], full.at[s, region], 3, s, across_line)

    def out_one(s):
        return remote(full.at[s, region], full.at[s, region], 4, s, outward)

    def out_two(s):
        return remote(full.at[s, 1 - region], full.at[s, 1 - region], 5, s, outward)

    def core_two(s):
        return remote(full.at[s], other.at[s], 6, s, mate)

    def add(left, right):
        return (left.astype(jnp.float32) + right.astype(jnp.float32)).astype(jnp.bfloat16)

    def deliveries(k, s):
        for t in range(2):
            for which, (src, part) in enumerate(
                ((full.at[s, t], 2 * core + t), (other.at[s, t], 2 * (1 - core) + t))
            ):
                for condition, ref in targets(k, part):
                    yield condition, pltpu.make_async_copy(src, ref, out_sems.at[2 * t + which, s])

    def start(k, s):
        product(k, own.at[s])
        core_one(s).start()

    def cores(k, s):
        core_one(s).wait_recv()
        both[s] = add(own[s, pl.ds(2 * core, 2)], met[s])
        pl.when(end)(lambda: line_one(s).start())

    def ends(k, s):
        @pl.when(middle)
        def _():
            line_one(s).wait_recv()
            both[s] = add(both[s], ended[s])
            cross_one(s).start()

    def centre(k, s):
        @pl.when(middle)
        def _():
            cross_one(s).wait_recv()
            full[s, region] = add(both[s, region], crossed[s])
            cross_two(s).start()
            out_one(s).start()

    def pass_on(k, s):
        @pl.when(middle)
        def _():
            cross_two(s).wait_recv()
            out_two(s).start()

    def back(k, s):
        @pl.when(end)
        def _():
            out_one(s).wait_recv()
            out_two(s).wait_recv()

        core_two(s).start()

    def deliver(k, s):
        core_two(s).wait_recv()
        for condition, copy in deliveries(k, s):
            pl.when(condition)(copy.start)

    def clear(k, s):
        core_one(s).wait_send()
        core_two(s).wait_send()

        @pl.when(end)
        def _():
            line_one(s).wait_send()

        @pl.when(middle)
        def _():
            for copy in (cross_one(s), cross_two(s), out_one(s), out_two(s)):
                copy.wait_send()

        for condition, copy in deliveries(k, s):
            pl.when(condition)(copy.wait)

    stages = (
        (12, clear),
        (10, deliver),
        (9, back),
        (7, pass_on),
        (5, centre),
        (3, ends),
        (1, cores),
        (0, start),
    )

    def step(i, carry):
        for delay, work in stages:
            k = i - delay

            @pl.when((k >= 0) & (k < count))
            def _(work=work, k=k):
                work(k, lax.rem(k + SLOTS, SLOTS))

        return carry

    return step


def square_scratch():
    low = jnp.bfloat16
    block = pltpu.VMEM((2, BLK, HEADS * HS), low)
    return [block, block, pltpu.SemaphoreType.DMA((6, 2)), pltpu.SemaphoreType.DMA((2,))]


def square_sum(scratch, places, parts, landed):
    met, mid, sems, load_sems = scratch
    top_x, low_y, low_x, top_y, top_d, low_d = parts
    near_x, near_y = places[5:]

    def remote(src, dst, kind, place):
        return pltpu.make_async_remote_copy(
            src_ref=src,
            dst_ref=dst,
            send_sem=sems.at[kind, 0],
            recv_sem=sems.at[kind, 1],
            device_id=place,
            device_id_type=MESH,
        )

    first = [remote(top_d, met.at[0], 0, near_x), remote(low_d, met.at[1], 1, near_y)]
    direct = [remote(top_x, landed[0], 2, near_x), remote(low_y, landed[1], 3, near_y)]
    second = [remote(mid.at[0], landed[2], 4, near_y), remote(mid.at[1], landed[3], 5, near_x)]
    loads = [
        pltpu.make_async_copy(top_y, mid.at[0], load_sems.at[0]),
        pltpu.make_async_copy(low_x, mid.at[1], load_sems.at[1]),
    ]

    def open_sum():
        begin(first)
        begin(direct)
        begin(loads)

    def join_sum():
        finish(loads)
        for at in range(2):
            first[at].wait()

            def tile(i, carry, at=at):
                rows = pl.ds(pl.multiple_of(i * 64, 64), 64)
                mid[at, rows, :] = add_low(mid[at, rows, :], met[at, rows, :])
                return carry

            lax.fori_loop(0, BLK // 64, tile, 0)
            second[at].start()

    def close_sum():
        finish(direct)
        finish(second)

    return open_sum, join_sum, close_sum


def unit_grads(act, grad_two_all, normed_two_all, grad_parts, back_sums, middle, cotangent, live):
    rows, units = act.shape
    width = grad_two_all.shape[1]
    local_rows = middle.shape[0]
    low = jnp.bfloat16
    out_blocks, in_blocks = units // SUB, width // SUB
    halves = width // 1024
    out_chunks = out_blocks * halves
    columns = grad_parts.shape[1] // TILE
    in_chunks = (width // PIECE) * columns
    count = out_chunks + in_chunks

    def body(*refs):
        act_in, two_in, normed_in, parts_in = refs[:4]
        partial = refs[4:12]
        middle_in, cot_in, live_ref = refs[12:15]
        out_grad, in_grad, branch_out, middle_out = refs[15:19]
        act_ref, shared, parts_ref, landed, own_ref, cot_ref, mid_ref, grad_ref, branch = refs[19:28]
        load_sems, stage_sems, gather_sems = refs[28:31]
        line = refs[31:40]
        square = refs[40:44]
        places = neighbours()
        near_x, near_y = places[5:]
        enter(places)
        load_act = pltpu.make_async_copy(act_in, act_ref, load_sems.at[0])
        load_two = pltpu.make_async_copy(two_in, shared, load_sems.at[1])
        load_parts = pltpu.make_async_copy(parts_in, parts_ref, load_sems.at[2])
        load_normed = pltpu.make_async_copy(normed_in, shared, load_sems.at[3])
        open_sum, join_sum, close_sum = square_sum(
            square, places, partial[2:], [landed.at[at] for at in range(4)]
        )
        load_two.start()
        load_act.start()
        open_sum()
        load_parts.start()
        load_two.wait()
        load_act.wait()

        def product(k, own):
            @pl.when(k < out_chunks)
            def _():
                rows_at = pl.ds(pl.multiple_of((k // halves) * SUB, SUB), SUB)
                wide_at = pl.ds(pl.multiple_of((k % halves) * 1024, 1024), 1024)
                result = down(act_ref[:, rows_at], shared[:, wide_at]).astype(low)
                for part in range(4):
                    own[part] = result[:, part * TILE : (part + 1) * TILE]

            @pl.when(k == out_chunks)
            def _():
                load_normed.start()
                load_parts.wait()
                load_normed.wait()

            @pl.when(k >= out_chunks)
            def _():
                at = k - out_chunks
                rows_at = pl.ds(pl.multiple_of((at // columns) * PIECE, PIECE), PIECE)
                wide_at = pl.ds(pl.multiple_of((at % columns) * TILE, TILE), TILE)
                result = down(shared[:, rows_at], parts_ref[:, wide_at]).astype(low)
                for part in range(4):
                    own[part] = result[part * SUB : (part + 1) * SUB]

        def targets(k, part):
            wide_at = pl.ds(pl.multiple_of((k % halves) * 1024 + part * TILE, TILE), TILE)
            at = jnp.maximum(k - out_chunks, 0)
            in_at = pl.ds(pl.multiple_of((at % columns) * TILE, TILE), TILE)
            first = jnp.minimum(k, out_chunks - 1) // halves
            return [
                (k < out_chunks, out_grad.at[first, :, wide_at]),
                (k >= out_chunks, in_grad.at[(at // columns) * 4 + part, :, in_at]),
            ]

        step = line_sum(line, places, count, product, targets)

        def block(at):
            return pl.ds(at * BLK, BLK)

        def spread(src, slot, kind, place):
            return pltpu.make_async_remote_copy(
                src_ref=src,
                dst_ref=branch_out.at[block(slot)],
                send_sem=gather_sems.at[kind, 0],
                recv_sem=gather_sems.at[kind, 1],
                device_id=place,
                device_id_type=MESH,
            )

        def stage(half):
            return [
                pltpu.make_async_copy(partial[half], own_ref, stage_sems.at[0]),
                pltpu.make_async_copy(cot_in.at[block(half)], cot_ref, stage_sems.at[1]),
                pltpu.make_async_copy(middle_in.at[block(half)], mid_ref, stage_sems.at[2]),
            ]

        keep = [
            pltpu.make_async_copy(branch.at[at], branch_out.at[block(at)], stage_sems.at[3 + at])
            for at in range(2)
        ]

        def rows_back(half):
            def tile(i, carry):
                at = pl.ds(pl.multiple_of(i * 32, 32), 32)
                grad = own_ref[at, :].astype(jnp.float32)
                grad += landed[half, at, :].astype(jnp.float32)
                grad += landed[2 + half, at, :].astype(jnp.float32)
                result = cot_ref[at, :].astype(jnp.float32) + norm_back(mid_ref[at, :], grad)
                grad_ref[at, :] = result
                live_at = pl.ds(pl.multiple_of(half * BLK + i * 32, 32), 32)
                branch[half, at, :] = (live_ref[live_at, :1] * result).astype(low)
                return carry

            lax.fori_loop(0, BLK // 32, tile, 0)
            copy = pltpu.make_async_copy(grad_ref, middle_out.at[block(half)], stage_sems.at[5])
            copy.start()
            return copy

        sends = [
            spread(branch.at[0], 2, 0, near_x),
            spread(branch.at[1], 3, 1, near_y),
            spread(branch.at[1], 4, 2, near_x),
            spread(branch.at[0], 5, 3, near_y),
        ]
        later = [
            spread(branch_out.at[block(3)], 7, 4, near_x),
            spread(branch_out.at[block(2)], 6, 5, near_y),
        ]

        lax.fori_loop(0, 9, step, 0)
        join_sum()
        begin(stage(0))
        lax.fori_loop(9, 25, step, 0)
        close_sum()
        finish(stage(0))
        written = rows_back(0)
        sends[0].start()
        begin(stage(1))
        finish(stage(1))
        written.wait()
        written = rows_back(1)
        begin([sends[1], sends[2], sends[3]])
        begin(keep)
        lax.fori_loop(25, 33, step, 0)
        sends[0].wait_recv()
        sends[1].wait_recv()
        begin(later)
        lax.fori_loop(33, count + STAGES, step, 0)
        written.wait()
        finish(keep)
        for copy in sends[:2]:
            copy.wait_send()
        finish(sends[2:])
        finish(later)

    return pl.pallas_call(
        body,
        in_specs=any_specs(14) + [pl.BlockSpec(memory_space=pltpu.VMEM)],
        out_specs=any_specs(4),
        out_shape=[
            jax.ShapeDtypeStruct((out_blocks, SUB, width), low),
            jax.ShapeDtypeStruct((in_blocks, SUB, grad_parts.shape[1]), low),
            jax.ShapeDtypeStruct((rows, width), low),
            jax.ShapeDtypeStruct((local_rows, width), jnp.float32),
        ],
        scratch_shapes=[
            pltpu.VMEM(act.shape, low),
            pltpu.VMEM((rows, width), low),
            pltpu.VMEM(grad_parts.shape, low),
            pltpu.VMEM((4, BLK, width), low),
            pltpu.VMEM((BLK, width), low),
            pltpu.VMEM((BLK, width), low),
            pltpu.VMEM((BLK, width), jnp.float32),
            pltpu.VMEM((BLK, width), jnp.float32),
            pltpu.VMEM((2, BLK, width), low),
            pltpu.SemaphoreType.DMA((4,)),
            pltpu.SemaphoreType.DMA((6,)),
            pltpu.SemaphoreType.DMA((6, 2)),
        ]
        + line_scratch()
        + square_scratch(),
        compiler_params=pltpu.CompilerParams(
            vmem_limit_bytes=VMEM, collective_id=1, has_side_effects=True
        ),
        cost_estimate=cost(2 * 3 * rows * width * units, 60e6),
        name="unit_grads",
    )(act, grad_two_all, normed_two_all, grad_parts, *back_sums, middle, cotangent, live)


def mix_grads(gated, grad_branch_all, normed_all, grad_projected, sums, two_sums):
    _, rows, columns = gated.shape
    width = normed_all.shape[1]
    parts = grad_projected.shape[0]
    low = jnp.bfloat16
    out_chunks = width // TILE
    per_row = columns // TILE
    per_part = (width // PIECE) * per_row
    count = out_chunks + parts * per_part

    def body(*refs):
        gated_in, branch_in, normed_in, grads_in = refs[:4]
        partial, two_partial = refs[4:10], refs[10:16]
        out_grad, mix_grad = refs[16:18]
        landed, two_landed = refs[18:22], refs[22:26]
        gated_ref, branch_ref, normed_ref, grads_ref, load_sems = refs[26:31]
        line = refs[31:40]
        square, two_square = refs[40:44], refs[44:48]
        places = neighbours()
        enter(places)
        loads = [
            pltpu.make_async_copy(gated_in.at[0], gated_ref, load_sems.at[0]),
            pltpu.make_async_copy(branch_in, branch_ref, load_sems.at[1]),
            pltpu.make_async_copy(normed_in, normed_ref, load_sems.at[2]),
            pltpu.make_async_copy(grads_in, grads_ref, load_sems.at[3]),
        ]
        begin(loads)
        open_sum, join_sum, close_sum = square_sum(square, places, partial, landed)
        open_two, join_two, close_two = square_sum(two_square, places, two_partial, two_landed)
        open_sum()
        finish(loads[:2])

        def product(k, own):
            @pl.when(k < out_chunks)
            def _():
                wide_at = pl.ds(pl.multiple_of(k * TILE, TILE), TILE)
                result = down(gated_ref[...], branch_ref[:, wide_at]).astype(low)
                for part in range(4):
                    own[part] = result[part * SUB : (part + 1) * SUB]

            @pl.when(k == out_chunks)
            def _():
                finish(loads[2:])

            @pl.when(k >= out_chunks)
            def _():
                at = k - out_chunks
                rows_at = pl.ds(pl.multiple_of(((at // per_row) % 4) * PIECE, PIECE), PIECE)
                wide_at = pl.ds(pl.multiple_of((at % per_row) * TILE, TILE), TILE)
                result = down(normed_ref[:, rows_at], grads_ref[at // per_part, :, wide_at]).astype(low)
                for part in range(4):
                    own[part] = result[part * SUB : (part + 1) * SUB]

        def targets(k, part):
            first_at = pl.ds(pl.multiple_of(jnp.minimum(k, out_chunks - 1) * TILE, TILE), TILE)
            at = jnp.maximum(k - out_chunks, 0)
            wide_at = pl.ds(pl.multiple_of((at % per_row) * TILE, TILE), TILE)
            return [
                (k < out_chunks, out_grad.at[part, :, first_at]),
                (k >= out_chunks, mix_grad.at[(at // per_row) * 4 + part, :, wide_at]),
            ]

        step = line_sum(line, places, count, product, targets)
        lax.fori_loop(0, 9, step, 0)
        join_sum()
        open_two()
        lax.fori_loop(9, 33, step, 0)
        join_two()
        lax.fori_loop(33, count + STAGES, step, 0)
        close_sum()
        close_two()

    return pl.pallas_call(
        body,
        in_specs=any_specs(16),
        out_specs=any_specs(10),
        out_shape=[
            jax.ShapeDtypeStruct((columns // SUB, SUB, width), low),
            jax.ShapeDtypeStruct((parts * width // SUB, SUB, columns), low),
        ]
        + [jax.ShapeDtypeStruct((BLK, width), low)] * 8,
        scratch_shapes=[
            pltpu.VMEM((rows, columns), low),
            pltpu.VMEM((rows, width), low),
            pltpu.VMEM((rows, width), low),
            pltpu.VMEM(grad_projected.shape, low),
            pltpu.SemaphoreType.DMA((4,)),
        ]
        + line_scratch()
        + square_scratch()
        + square_scratch(),
        compiler_params=pltpu.CompilerParams(
            vmem_limit_bytes=VMEM, collective_id=2, has_side_effects=True
        ),
        cost_estimate=cost(2 * 5 * rows * width * columns, 60e6),
        name="mix_grads",
    )(gated, grad_branch_all, normed_all, grad_projected, *sums, *two_sums)


def row_copies(pair, rows, sems, at):
    return [
        pltpu.make_async_copy(src, rows.at[pl.ds(half * HALF, HALF)], sems.at[at + half])
        for half, src in enumerate(pair)
    ]


def project_piece(pair, weight, kept, piece):
    parts, width, columns = weight.shape
    group_rows = NBLK * BLK
    low = jnp.bfloat16
    spot = pl.ds(piece * PIECE, PIECE)
    joined = 2

    def body(*refs):
        weight_in = refs[2]
        rows_out, parts_out, rows, weights, out, row_sems, weight_sems, out_sems = refs[3 + len(kept) :]
        row_loads = row_copies(refs[:2], rows, row_sems, 0)
        weight_loads = [
            pltpu.make_async_copy(
                weight_in.at[c], weights.at[:, pl.ds(c * columns, columns)], weight_sems.at[c]
            )
            for c in range(parts)
        ]
        stores = [
            pltpu.make_async_copy(
                out.at[:, pl.ds(c * columns, columns)], parts_out.at[c, spot, :], out_sems.at[c]
            )
            for c in range(parts)
        ]
        begin(row_loads)
        begin(weight_loads)
        finish(row_loads)
        keep = pltpu.make_async_copy(rows, rows_out.at[spot, :], row_sems.at[2])
        keep.start()
        for c in range(0, parts, joined):
            finish(weight_loads[c : c + joined])
            at = slice(c * columns, (c + joined) * columns)
            out[:, at] = straight(rows[...], weights[:, at]).astype(low)
            begin(stores[c : c + joined])
        finish(stores)
        keep.wait()

    return pl.pallas_call(
        body,
        in_specs=any_specs(3 + len(kept)),
        out_specs=any_specs(2),
        out_shape=[
            jax.ShapeDtypeStruct((group_rows, width), low),
            jax.ShapeDtypeStruct((parts, group_rows, columns), low),
        ],
        scratch_shapes=[
            pltpu.VMEM((PIECE, width), low),
            pltpu.VMEM((width, parts * columns), low),
            pltpu.VMEM((PIECE, parts * columns), low),
            pltpu.SemaphoreType.DMA((3,)),
            pltpu.SemaphoreType.DMA((parts,)),
            pltpu.SemaphoreType.DMA((parts,)),
        ],
        input_output_aliases={3 + at: at for at in range(len(kept))},
        compiler_params=pltpu.CompilerParams(vmem_limit_bytes=VMEM),
        cost_estimate=cost(2 * PIECE * parts * width * columns, 2 * parts * width * columns + 8e6),
        name="project",
    )(*pair, weight, *kept)


def partial_sums(acts, weight, pieces, transposed):
    parts, _, columns = acts.shape
    width = weight.shape[1] if transposed else weight.shape[2]
    deep = parts * columns
    low = jnp.bfloat16
    wide_tile = 1024

    def body(act_in, weight_in, *refs):
        outs = refs[: 2 * len(pieces)]
        acts_ref, weights, out, act_sems, weight_sems, out_sems = refs[2 * len(pieces) :]

        def place(c):
            return pl.ds(c * columns, columns)

        act_loads = [
            [
                pltpu.make_async_copy(
                    act_in.at[c, pl.ds(piece * PIECE, PIECE), :],
                    acts_ref.at[at, :, place(c)],
                    act_sems.at[at, c],
                )
                for c in range(parts)
            ]
            for at, piece in enumerate(pieces)
        ]
        weight_loads = []
        for j in range(width // wide_tile):
            tile = pl.ds(j * wide_tile, wide_tile)
            weight_loads.append(
                [
                    pltpu.make_async_copy(
                        weight_in.at[c, tile, :], weights.at[tile, place(c)], weight_sems.at[j, c]
                    )
                    if transposed
                    else pltpu.make_async_copy(
                        weight_in.at[c, :, tile], weights.at[place(c), tile], weight_sems.at[j, c]
                    )
                    for c in range(parts)
                ]
            )
        begin(act_loads[0])
        for loads in weight_loads:
            begin(loads)
        for loads in act_loads[1:]:
            begin(loads)
        stores = []
        for at in range(len(pieces)):
            finish(act_loads[at])
            for j, loads in enumerate(weight_loads):
                if at == 0:
                    finish(loads)
                tile = slice(j * wide_tile, (j + 1) * wide_tile)
                if transposed:
                    total = across(acts_ref[at], weights[tile, :])
                else:
                    total = straight(acts_ref[at], weights[:, tile])
                out[2 * at, :, tile] = total[:HALF].astype(low)
                out[2 * at + 1, :, tile] = total[HALF:].astype(low)
            now = [
                pltpu.make_async_copy(out.at[at_out], outs[at_out], out_sems.at[at_out])
                for at_out in (2 * at, 2 * at + 1)
            ]
            begin(now)
            stores += now
        finish(stores)

    return pl.pallas_call(
        body,
        in_specs=any_specs(2),
        out_specs=any_specs(2 * len(pieces)),
        out_shape=[jax.ShapeDtypeStruct((HALF, width), low)] * (2 * len(pieces)),
        scratch_shapes=[
            pltpu.VMEM((len(pieces), PIECE, deep), low),
            pltpu.VMEM((width, deep) if transposed else (deep, width), low),
            pltpu.VMEM((2 * len(pieces), HALF, width), low),
            pltpu.SemaphoreType.DMA((len(pieces), parts)),
            pltpu.SemaphoreType.DMA((width // wide_tile, parts)),
            pltpu.SemaphoreType.DMA((2 * len(pieces),)),
        ],
        compiler_params=pltpu.CompilerParams(vmem_limit_bytes=VMEM),
        cost_estimate=cost(
            2 * len(pieces) * PIECE * parts * width * columns, 2 * parts * width * columns + 8e6
        ),
        name="partial_sums",
    )(acts, weight)


def unit_piece(pair, grad_pair, ffn_in, ffn_out, kept, piece):
    _, width, units = ffn_in.shape
    group_rows = NBLK * BLK
    main = units // TILE * TILE
    tail = units - main
    low = jnp.bfloat16
    spot = pl.ds(piece * PIECE, PIECE)
    cuts = ((0, 2 * TILE), (2 * TILE, main - 2 * TILE))
    wide_tile = 1024

    def body(*refs):
        in_ref, out_ref = refs[4:6]
        outs = refs[6 + len(kept) :]
        rows_out, grads_out, act_out, parts_out = outs[:4]
        sum_outs = outs[4:8]
        rows, grads, w_in, w_out, act, parts, sums, row_sems, sems, done_sems, sum_sems = outs[8:]
        loads = row_copies(refs[:2], rows, row_sems, 0)
        grad_loads = row_copies(refs[2:4], grads, row_sems, 2)

        def weight_loads(which, start, size, first, second):
            at = pl.ds(start, size)
            return [
                pltpu.make_async_copy(
                    in_ref.at[0, :, at], w_in.at[:, pl.ds(first, size)], sems.at[which, 0]
                ),
                pltpu.make_async_copy(
                    in_ref.at[1, :, at], w_in.at[:, pl.ds(second, size)], sems.at[which, 1]
                ),
                pltpu.make_async_copy(out_ref.at[at, :], w_out.at[at, :], sems.at[which, 2]),
            ]

        weights = [weight_loads(at, *cut, cut[0], main + cut[0]) for at, cut in enumerate(cuts)]
        weights.append(weight_loads(2, main, tail, 2 * main, 2 * main + tail))
        begin(loads)
        begin(weights[0])
        begin(grad_loads)
        begin(weights[1])
        begin(weights[2])
        finish(loads)
        stores = [
            pltpu.make_async_copy(rows, rows_out.at[spot, :], done_sems.at[0]),
            pltpu.make_async_copy(grads, grads_out.at[spot, :], done_sems.at[1]),
        ]

        def products(at, first, second, part_a, part_b, grad_act):
            act[:, at] = (part_a * part_b).astype(low)
            parts[:, first] = (grad_act * part_b).astype(low)
            parts[:, second] = (grad_act * part_a).astype(low)

        for which, (start, size) in enumerate(cuts):
            finish(weights[which][:1])
            at, second = slice(start, start + size), slice(main + start, main + start + size)
            part_a = straight(rows[...], w_in[:, at])
            finish(weights[which][1:2])
            part_b = straight(rows[...], w_in[:, second])
            finish(weights[which][2:])
            if which == 0:
                finish(grad_loads)
                begin(stores)
            grad_act = across(grads[...], w_out[at, :])
            products(at, at, second, part_a, part_b, grad_act)
        if tail:
            finish(weights[2])
            both = straight(rows[...], w_in[:, 2 * main :])
            grad_act = across(grads[...], w_out[main:, :])
            products(
                slice(main, units),
                slice(2 * main, 2 * main + tail),
                slice(2 * main + tail, 2 * units),
                both[:, :tail],
                both[:, tail:],
                grad_act,
            )
        more = [
            pltpu.make_async_copy(act, act_out.at[spot, :], done_sems.at[2]),
            pltpu.make_async_copy(parts, parts_out.at[spot, :], done_sems.at[3]),
        ]
        begin(more)
        stores += more
        for j in range(width // wide_tile):
            at = slice(j * wide_tile, (j + 1) * wide_tile)
            back = across(parts[...], w_in[at, :])
            sums[0, :, at] = back[:HALF].astype(low)
            sums[1, :, at] = back[HALF:].astype(low)
            two = straight(act[...], w_out[:, at])
            sums[2, :, at] = two[:HALF].astype(low)
            sums[3, :, at] = two[HALF:].astype(low)
            tile = pl.ds(j * wide_tile, wide_tile)
            now = [
                pltpu.make_async_copy(
                    sums.at[at_out, :, tile], sum_outs[at_out].at[:, tile], sum_sems.at[j, at_out]
                )
                for at_out in range(4)
            ]
            begin(now)
            stores += now
        finish(stores)

    return pl.pallas_call(
        body,
        in_specs=any_specs(6 + len(kept)),
        out_specs=any_specs(8),
        out_shape=[
            jax.ShapeDtypeStruct((group_rows, width), low),
            jax.ShapeDtypeStruct((group_rows, width), low),
            jax.ShapeDtypeStruct((group_rows, units), low),
            jax.ShapeDtypeStruct((group_rows, 2 * units), low),
        ]
        + [jax.ShapeDtypeStruct((HALF, width), low)] * 4,
        scratch_shapes=[
            pltpu.VMEM((PIECE, width), low),
            pltpu.VMEM((PIECE, width), low),
            pltpu.VMEM((width, 2 * units), low),
            pltpu.VMEM((units, width), low),
            pltpu.VMEM((PIECE, units), low),
            pltpu.VMEM((PIECE, 2 * units), low),
            pltpu.VMEM((4, HALF, width), low),
            pltpu.SemaphoreType.DMA((4,)),
            pltpu.SemaphoreType.DMA((3, 3)),
            pltpu.SemaphoreType.DMA((4,)),
            pltpu.SemaphoreType.DMA((width // wide_tile, 4)),
        ],
        input_output_aliases={6 + at: at for at in range(len(kept))},
        compiler_params=pltpu.CompilerParams(vmem_limit_bytes=VMEM),
        cost_estimate=cost(12 * PIECE * width * units, 6 * width * units + 12e6),
        name="gated_unit",
    )(*pair, *grad_pair, ffn_in, ffn_out, *kept)


def block_decays(rate):
    row = lax.broadcasted_iota(jnp.int32, (BLK, BLK), 0)
    column = lax.broadcasted_iota(jnp.int32, (BLK, BLK), 1)
    distance = (row - column).astype(jnp.float32)
    within = jnp.where(row >= column, jnp.exp(-rate * jnp.maximum(distance, 0.0)), 0.0)
    place = lax.broadcasted_iota(jnp.int32, (BLK, 1), 0).astype(jnp.float32)
    entry = jnp.exp(-rate * (place + 1.0))
    leave = jnp.exp(-rate * (BLK - 1.0 - place))
    whole = jnp.exp(jnp.full((1, HS), -BLK * rate, jnp.float32))
    return within, entry, leave, whole


def mix_forward(slots, fresh, rates, parts):
    _, group_rows, columns = parts.shape
    heads = columns // HS
    low = jnp.bfloat16

    def body(slot_ref, fresh_ref, rate_ref, parts_ref, gated_ref, mixing_ref, states_ref):
        within, entry, leave, whole = block_decays(rate_ref[pl.program_id(0)])
        state = jnp.zeros((HS, HS), jnp.float32)
        for block in range(NBLK):
            rows = pl.ds(pl.multiple_of(slot_ref[block] * BLK, BLK), BLK)
            queries = jax.nn.silu(parts_ref[0, rows, :].astype(jnp.float32)).astype(low)
            keys = jax.nn.silu(parts_ref[1, rows, :].astype(jnp.float32))
            values = parts_ref[2, rows, :]
            gate = parts_ref[3, rows, :].astype(jnp.float32)
            state = jnp.where(fresh_ref[block] != 0, 0.0, state)
            state_low = state.astype(low)
            states_ref[0, block] = state_low
            weights = (across(queries, keys.astype(low)) * within).astype(low)
            mixing = straight(weights, values) + entry * straight(queries, state_low)
            late_keys = (keys.astype(low).astype(jnp.float32) * leave).astype(low)
            state = whole * state + down(late_keys, values)
            scale = lax.rsqrt(jnp.mean(mixing * mixing, axis=-1, keepdims=True) + head_floor)
            gated_ref[0, rows, :] = (mixing * scale * gate).astype(low)
            mixing_ref[rows, :] = mixing.astype(low)

    return pl.pallas_call(
        body,
        grid_spec=pltpu.PrefetchScalarGridSpec(
            num_scalar_prefetch=3,
            grid=(heads,),
            in_specs=[pl.BlockSpec((4, group_rows, HS), lambda h, *_: (0, 0, h))],
            out_specs=[
                pl.BlockSpec((1, group_rows, HS), lambda h, *_: (0, 0, h)),
                pl.BlockSpec((group_rows, HS), lambda h, *_: (0, h)),
                pl.BlockSpec((1, NBLK, HS, HS), lambda h, *_: (h, 0, 0, 0)),
            ],
        ),
        out_shape=[
            jax.ShapeDtypeStruct((1, group_rows, columns), low),
            jax.ShapeDtypeStruct((group_rows, columns), low),
            jax.ShapeDtypeStruct((heads, NBLK, HS, HS), low),
        ],
        compiler_params=pltpu.CompilerParams(vmem_limit_bytes=VMEM),
        cost_estimate=cost(8e9, 14e6),
        name="mix_forward",
    )(slots, fresh, rates, parts)


def mix_backward(slots, fresh, rates, parts, mixing_all, states, grad_gated):
    _, group_rows, columns = parts.shape
    heads = columns // HS
    low = jnp.bfloat16

    def body(
        slot_ref, fresh_ref, rate_ref, parts_ref, mixing_ref, states_ref, grad_ref, out_ref
    ):
        within, entry, leave, whole = block_decays(rate_ref[pl.program_id(0)])
        later = jnp.zeros((HS, HS), jnp.float32)
        for block in reversed(range(NBLK)):
            rows = pl.ds(pl.multiple_of(slot_ref[block] * BLK, BLK), BLK)
            raw_queries = parts_ref[0, rows, :].astype(jnp.float32)
            raw_keys = parts_ref[1, rows, :].astype(jnp.float32)
            queries_float = jax.nn.silu(raw_queries).astype(low).astype(jnp.float32)
            queries, keys = queries_float.astype(low), jax.nn.silu(raw_keys).astype(low)
            values = parts_ref[2, rows, :]
            gate = parts_ref[3, rows, :].astype(jnp.float32)
            mixing = mixing_ref[rows, :].astype(jnp.float32)
            grad_gated_rows = grad_ref[rows, :].astype(jnp.float32)
            scale = lax.rsqrt(jnp.mean(mixing * mixing, axis=-1, keepdims=True) + head_floor)
            headed = mixing * scale
            out_ref[3, rows, :] = (grad_gated_rows * headed).astype(low)
            grad_headed = grad_gated_rows * gate
            inner = jnp.mean(grad_headed * headed, axis=-1, keepdims=True)
            grad = (scale * (grad_headed - headed * inner)).astype(low)
            weights = (across(queries, keys) * within).astype(low)
            grad_scores = (across(grad, values) * within).astype(low)
            later_low = later.astype(low)
            grad_queries = straight(grad_scores, keys) + entry * across(grad, states_ref[0, block])
            grad_keys = down(grad_scores, queries) + leave * across(values, later_low)
            grad_values = down(weights, grad) + leave * straight(keys, later_low)
            early_queries = (queries_float * entry).astype(low)
            later = jnp.where(fresh_ref[block] != 0, 0.0, whole * later + down(early_queries, grad))
            out_ref[0, rows, :] = (grad_queries * silu_slope(raw_queries)).astype(low)
            out_ref[1, rows, :] = (grad_keys * silu_slope(raw_keys)).astype(low)
            out_ref[2, rows, :] = grad_values.astype(low)

    return pl.pallas_call(
        body,
        grid_spec=pltpu.PrefetchScalarGridSpec(
            num_scalar_prefetch=3,
            grid=(heads,),
            in_specs=[
                pl.BlockSpec((4, group_rows, HS), lambda h, *_: (0, 0, h)),
                pl.BlockSpec((group_rows, HS), lambda h, *_: (0, h)),
                pl.BlockSpec((1, NBLK, HS, HS), lambda h, *_: (h, 0, 0, 0)),
                pl.BlockSpec((group_rows, HS), lambda h, *_: (0, h)),
            ],
            out_specs=pl.BlockSpec((4, group_rows, HS), lambda h, *_: (0, 0, h)),
        ),
        out_shape=jax.ShapeDtypeStruct(parts.shape, low),
        compiler_params=pltpu.CompilerParams(vmem_limit_bytes=VMEM),
        cost_estimate=cost(20e9, 22e6),
        name="mix_backward",
    )(slots, fresh, rates, parts, mixing_all, states, grad_gated)


def norm_back(values, grad):
    scale = lax.rsqrt(jnp.mean(values * values, axis=-1, keepdims=True) + epsilon)
    unit = values * scale
    return scale * (grad - unit * jnp.mean(grad * unit, axis=-1, keepdims=True))


def square_device(
    hidden, mix_weight, out_weight, ffn_in_weight, ffn_out_weight, seq_lengths, block_seq, cotangent
):
    local_rows, width = hidden.shape
    units = ffn_out_weight.shape[0]
    head_count = mix_weight.shape[2] // HS
    narrow_index = lax.axis_index("narrow")
    valid_all, fresh_block = group_masks(seq_lengths, block_seq)
    live = lax.dynamic_slice_in_dim(
        valid_all.astype(jnp.float32), narrow_index * local_rows, local_rows
    )[:, None]
    head_ids = narrow_index * head_count + jnp.arange(head_count, dtype=jnp.int32)
    rates = 2.0 ** (-8.0 * (head_ids.astype(jnp.float32) + 1.0) / HEADS)
    slots, fresh = slot_tables(narrow_index, fresh_block)
    low = jnp.bfloat16

    def halves(rows):
        return rows[:HALF], rows[HALF:]

    lives = halves(live)
    inputs = [rows.astype(jnp.float32) for rows in halves(hidden)]
    grads_in = [rows.astype(jnp.float32) for rows in halves(cotangent)]

    pieces = gather_pieces(*(row_norm(rows).astype(low) for rows in inputs))
    kept = ()
    for at, pair in enumerate(pieces):
        kept = project_piece(pair, mix_weight, kept, at)
    normed_all, parts = kept
    grad_pieces = gather_pieces(*((m * g).astype(low) for m, g in zip(lives, grads_in)))

    gated, mixing, states = mix_forward(slots, fresh, rates, parts)
    far_top, far_low, near_top, near_low = partial_sums(gated, out_weight[None], (3, 1), False)
    side_low, side_top, own_top, own_low = partial_sums(gated, out_weight[None], (2, 0), False)
    branch = scatter_pieces(
        (own_top, own_low), (near_top, near_low), (side_low, side_top), (far_top, far_low)
    )
    middle = [x + m * b for x, m, b in zip(inputs, lives, branch)]

    pieces = gather_pieces(*(row_norm(rows).astype(low) for rows in middle))
    kept, back_sums, two_sums = (), [], []
    for at, (pair, grad_pair) in enumerate(zip(pieces, grad_pieces)):
        *kept, back_top, back_low, two_top, two_low = unit_piece(
            pair, grad_pair, ffn_in_weight, ffn_out_weight, kept, at
        )
        back_sums += [back_top, back_low]
        two_sums += [two_top, two_low]
    normed_two_all, grad_two_all, act, grad_parts = kept

    out_grads, in_grads, grad_branch_all, grad_middle = unit_grads(
        act, grad_two_all, normed_two_all, grad_parts, back_sums, jnp.concatenate(middle), cotangent, live
    )
    main = units // TILE * TILE
    tail = units - main
    in_grads = in_grads.reshape(width, 2 * units)
    grad_ffn_in = jnp.stack(
        [
            jnp.concatenate(
                [
                    in_grads[:, c * main : (c + 1) * main],
                    in_grads[:, 2 * main + c * tail : 2 * main + (c + 1) * tail],
                ],
                axis=1,
            )
            for c in range(2)
        ]
    ).astype(jnp.float32)
    grad_ffn_out = out_grads.reshape(units, width).astype(jnp.float32)

    grad_gated = across(grad_branch_all, out_weight).astype(low)
    grad_projected = mix_backward(slots, fresh, rates, parts, mixing, states, grad_gated)
    sums = partial_sums(grad_projected, mix_weight, (0, 1, 2, 3), True)
    out_grads, mix_grads_low, *terms = mix_grads(
        gated, grad_branch_all, normed_all, grad_projected, sums[2:], two_sums[2:]
    )
    grad_out = out_grads.reshape(out_weight.shape).astype(jnp.float32)
    grad_mix = mix_grads_low.reshape(mix_weight.shape).astype(jnp.float32)
    grad_normed = add_rows(sums[0], terms[0], terms[2]), add_rows(sums[1], terms[1], terms[3])
    branch_two = (
        add_rows(two_sums[0], terms[4], terms[6]),
        add_rows(two_sums[1], terms[5], terms[7]),
    )
    layer_out = jnp.concatenate(
        [(v + m * b).astype(low) for v, m, b in zip(middle, lives, branch_two)]
    )
    input_grad = jnp.concatenate(
        [
            (g + norm_back(x, n)).astype(low)
            for g, x, n in zip(halves(grad_middle), inputs, grad_normed)
        ]
    )
    return (layer_out, input_grad, grad_mix, grad_out, grad_ffn_in, grad_ffn_out)


def solution(mesh):
    square = mesh.shape["wide"] == 8 and mesh.shape["narrow"] == 4
    per_device = square_device if square else general_device
    in_specs = (
        P(("wide", "narrow"), None),
        P(None, None, "narrow"),
        P("narrow", None),
        P(None, None, "narrow"),
        P("narrow", None),
        P("wide"),
        P("wide"),
        P(("wide", "narrow"), None),
    )
    out_specs = (
        P(("wide", "narrow"), None),
        P(("wide", "narrow"), None),
        P(None, None, "narrow"),
        P("narrow", None),
        P(None, None, "narrow"),
        P("narrow", None),
    )
    return jax.shard_map(
        per_device, mesh=mesh, in_specs=in_specs, out_specs=out_specs, check_vma=False
    )
```

```python
import functools

import jax
import jax.numpy as jnp
from jax import lax
from jax.experimental import pallas as pl
from jax.experimental.pallas import tpu as pltpu
from jax.sharding import PartitionSpec as P

HEADS = 16
HS = 128
BLK = 256
NBLK = 8


epsilon = 1e-06
head_floor = 1.0
highest = lax.Precision.HIGHEST


def row_norm(values):
    return values * lax.rsqrt(jnp.mean(values * values, axis=-1, keepdims=True) + epsilon)


def head_norm(values):
    return values * lax.rsqrt(jnp.mean(values * values, axis=-1, keepdims=True) + head_floor)


def silu_slope(values):
    sigmoid_part = jax.nn.sigmoid(values)
    return sigmoid_part * (1.0 + values * (1.0 - sigmoid_part))


def decay_tables(decay_rates):
    positions = jnp.arange(BLK, dtype=jnp.float32)
    distance = positions[:, None] - positions[None, :]
    causal = distance >= 0
    clipped = jnp.where(causal, distance, 0.0)
    within = jnp.where(causal[None], jnp.exp(-decay_rates[:, None, None] * clipped[None]), 0.0)
    entry_decay = jnp.exp(-(positions[:, None] + 1.0) * decay_rates[None, :])
    exit_decay = jnp.exp(-(BLK - 1.0 - positions[:, None]) * decay_rates[None, :])
    block_decay = jnp.exp(-BLK * decay_rates)
    return (within, entry_decay, exit_decay, block_decay)


def group_masks(lengths, owners):
    seq_slot = owners - owners[0]
    first_count = jnp.sum((seq_slot == 0).astype(jnp.int32))
    block_ids = jnp.arange(NBLK, dtype=jnp.int32)
    start_block = jnp.where(seq_slot == 0, jnp.int32(0), first_count)
    seq_limit = jnp.where(seq_slot == 0, lengths[0], lengths[1])
    offsets = (block_ids - start_block)[:, None] * BLK + jnp.arange(BLK, dtype=jnp.int32)[None, :]
    valid_rows = (offsets < seq_limit[:, None]).reshape(-1)
    fresh_block = block_ids == start_block
    return (valid_rows, fresh_block)


def forward_block(tables, kv_state, block_in):
    within, entry_decay, exit_decay, block_decay = tables
    queries, keys_in, values, fresh_block = block_in
    kv_state = jnp.where(fresh_block, 0.0, kv_state)
    scores = jnp.einsum("ihs,jhs->hij", queries, keys_in, preferred_element_type=jnp.float32)
    weights = (scores * within).astype(jnp.bfloat16)
    inner_part = jnp.einsum("hij,jhs->ihs", weights, values, preferred_element_type=jnp.float32)
    carried = jnp.einsum(
        "ihs,hst->iht",
        queries.astype(jnp.float32) * entry_decay[:, :, None],
        kv_state,
        precision=highest,
    )
    update = jnp.einsum(
        "ihs,iht->hst",
        keys_in.astype(jnp.float32) * exit_decay[:, :, None],
        values.astype(jnp.float32),
        precision=highest,
    )
    return (block_decay[:, None, None] * kv_state + update, (inner_part + carried, kv_state))


def backward_block(tables, later_grad, block_in):
    within, entry_decay, exit_decay, block_decay = tables
    queries, keys_in, values, grad_mix, kv_state, fresh_block = block_in
    scores = jnp.einsum("ihs,jhs->hij", queries, keys_in, preferred_element_type=jnp.float32)
    weights = (scores * within).astype(jnp.bfloat16)
    grad_values = jnp.einsum("hij,ihs->jhs", weights, grad_mix, preferred_element_type=jnp.float32)
    grad_weights = jnp.einsum("ihs,jhs->hij", grad_mix, values, preferred_element_type=jnp.float32)
    grad_scores = (grad_weights * within).astype(jnp.bfloat16)
    grad_queries = jnp.einsum(
        "hij,jhs->ihs", grad_scores, keys_in, preferred_element_type=jnp.float32
    )
    grad_keys = jnp.einsum("hij,ihs->jhs", grad_scores, queries, preferred_element_type=jnp.float32)
    grad_float = grad_mix.astype(jnp.float32)
    values_float = values.astype(jnp.float32)
    queries_float = queries.astype(jnp.float32)
    keys_float = keys_in.astype(jnp.float32)
    grad_queries = grad_queries + entry_decay[:, :, None] * jnp.einsum(
        "iht,hst->ihs", grad_float, kv_state, precision=highest
    )
    grad_keys = grad_keys + exit_decay[:, :, None] * jnp.einsum(
        "iht,hst->ihs", values_float, later_grad, precision=highest
    )
    grad_values = grad_values + jnp.einsum(
        "ihs,hst->iht", keys_float * exit_decay[:, :, None], later_grad, precision=highest
    )
    grad_state = jnp.einsum(
        "ihs,iht->hst", queries_float * entry_decay[:, :, None], grad_float, precision=highest
    )
    grad_state = grad_state + block_decay[:, None, None] * later_grad
    grad_state = jnp.where(fresh_block, 0.0, grad_state)
    return (grad_state, (grad_queries, grad_keys, grad_values))


def general_device(
    hidden, mix_weight, out_weight, ffn_in_weight, ffn_out_weight, seq_lengths, block_seq, cotangent
):
    local_rows = hidden.shape[0]
    group_rows = NBLK * BLK
    head_width = mix_weight.shape[2]
    head_count = head_width // HS
    narrow_index = lax.axis_index("narrow")
    valid_all, fresh_block = group_masks(seq_lengths, block_seq)
    valid_rows = lax.dynamic_slice_in_dim(
        valid_all.astype(jnp.float32), narrow_index * local_rows, local_rows
    )[:, None]
    head_ids = narrow_index * head_count + jnp.arange(head_count, dtype=jnp.int32)
    decay_rates = 2.0 ** (-8.0 * (head_ids.astype(jnp.float32) + 1.0) / HEADS)
    tables = decay_tables(decay_rates)

    def split_blocks(flat_rows):
        return flat_rows.reshape(NBLK, BLK, head_count, HS)

    inputs = hidden.astype(jnp.float32)
    normed_low = row_norm(inputs).astype(jnp.bfloat16)
    gathered = lax.all_gather(normed_low, "narrow", axis=0, tiled=True)
    projected = jnp.einsum("rd,cde->cre", gathered, mix_weight, preferred_element_type=jnp.float32)
    queries = jax.nn.silu(projected[0]).astype(jnp.bfloat16)
    keys_in = jax.nn.silu(projected[1]).astype(jnp.bfloat16)
    values = projected[2].astype(jnp.bfloat16)
    gate_part = projected[3]
    zero_state = jnp.zeros((head_count, HS, HS), jnp.float32)
    final_state, (mixing, kept_states) = lax.scan(
        lambda state_in, block_in: forward_block(tables, state_in, block_in),
        zero_state,
        (split_blocks(queries), split_blocks(keys_in), split_blocks(values), fresh_block),
    )
    mixing = mixing.reshape(group_rows, head_count, HS)
    headed = head_norm(mixing).reshape(group_rows, head_width)
    gated_low = (headed * gate_part).astype(jnp.bfloat16)
    branch = lax.psum_scatter(
        jnp.dot(gated_low, out_weight, preferred_element_type=jnp.float32).astype(jnp.bfloat16),
        "narrow",
        scatter_dimension=0,
        tiled=True,
    ).astype(jnp.float32)
    middle = inputs + valid_rows * branch
    normed_two_low = row_norm(middle).astype(jnp.bfloat16)
    gathered_two = lax.all_gather(normed_two_low, "narrow", axis=0, tiled=True)
    both_parts = jnp.einsum(
        "rd,cdf->crf", gathered_two, ffn_in_weight, preferred_element_type=jnp.float32
    )
    hidden_low = (both_parts[0] * both_parts[1]).astype(jnp.bfloat16)
    branch_two = lax.psum_scatter(
        jnp.dot(hidden_low, ffn_out_weight, preferred_element_type=jnp.float32).astype(
            jnp.bfloat16
        ),
        "narrow",
        scatter_dimension=0,
        tiled=True,
    ).astype(jnp.float32)
    layer_out = (middle + valid_rows * branch_two).astype(jnp.bfloat16)
    grad_rows = cotangent.astype(jnp.float32)
    ffn_grad_all = lax.all_gather(
        (valid_rows * grad_rows).astype(jnp.bfloat16), "narrow", axis=0, tiled=True
    )
    grad_ffn_out = jnp.einsum(
        "rf,rd->fd", hidden_low, ffn_grad_all, preferred_element_type=jnp.float32
    )
    grad_hidden = jnp.einsum(
        "rd,fd->rf", ffn_grad_all, ffn_out_weight, preferred_element_type=jnp.float32
    )
    grad_parts = jnp.stack([grad_hidden * both_parts[1], grad_hidden * both_parts[0]]).astype(
        jnp.bfloat16
    )
    grad_ffn_in = jnp.einsum(
        "rd,crf->cdf", gathered_two, grad_parts, preferred_element_type=jnp.float32
    )
    grad_slice = grad_parts
    grad_normed_two = lax.psum_scatter(
        jnp.einsum(
            "crf,cdf->rd", grad_slice, ffn_in_weight, preferred_element_type=jnp.float32
        ).astype(jnp.bfloat16),
        "narrow",
        scatter_dimension=0,
        tiled=True,
    ).astype(jnp.float32)
    norm_value, norm_pull = jax.vjp(row_norm, middle)
    grad_middle = grad_rows + norm_pull(grad_normed_two)[0]
    attn_grad_all = lax.all_gather(
        (valid_rows * grad_middle).astype(jnp.bfloat16), "narrow", axis=0, tiled=True
    )
    grad_out_weight = jnp.einsum(
        "re,rd->ed", gated_low, attn_grad_all, preferred_element_type=jnp.float32
    )
    grad_gated = jnp.einsum(
        "rd,ed->re", attn_grad_all, out_weight, preferred_element_type=jnp.float32
    )
    grad_gated = lax.optimization_barrier(grad_gated.astype(jnp.bfloat16)).astype(jnp.float32)
    grad_gate = grad_gated * headed
    grad_headed = (grad_gated * gate_part).reshape(group_rows, head_count, HS)
    head_value, head_pull = jax.vjp(head_norm, mixing)
    grad_mixing = head_pull(grad_headed)[0].astype(jnp.bfloat16)
    first_grad, (grad_queries, grad_keys, grad_values) = lax.scan(
        lambda later_grad, block_in: backward_block(tables, later_grad, block_in),
        zero_state,
        (
            split_blocks(queries),
            split_blocks(keys_in),
            split_blocks(values),
            split_blocks(grad_mixing),
            kept_states,
            fresh_block,
        ),
        reverse=True,
    )
    grad_projected = jnp.stack(
        [
            grad_queries.reshape(group_rows, head_width) * silu_slope(projected[0]),
            grad_keys.reshape(group_rows, head_width) * silu_slope(projected[1]),
            grad_values.reshape(group_rows, head_width),
            grad_gate,
        ]
    ).astype(jnp.bfloat16)
    grad_mix = jnp.einsum(
        "rd,cre->cde", gathered, grad_projected, preferred_element_type=jnp.float32
    )
    grad_slice = grad_projected
    grad_normed = lax.psum_scatter(
        jnp.einsum(
            "cre,cde->rd", grad_slice, mix_weight, preferred_element_type=jnp.float32
        ).astype(jnp.bfloat16),
        "narrow",
        scatter_dimension=0,
        tiled=True,
    ).astype(jnp.float32)
    first_value, first_pull = jax.vjp(row_norm, inputs)
    input_grad = (grad_middle + first_pull(grad_normed)[0]).astype(jnp.bfloat16)
    grad_mix, grad_out_weight, grad_ffn_in, grad_ffn_out = (
        lax.psum(grad_mix.astype(jnp.bfloat16), "wide").astype(jnp.float32),
        lax.psum(grad_out_weight.astype(jnp.bfloat16), "wide").astype(jnp.float32),
        lax.psum(grad_ffn_in.astype(jnp.bfloat16), "wide").astype(jnp.float32),
        lax.psum(grad_ffn_out.astype(jnp.bfloat16), "wide").astype(jnp.float32),
    )
    return (layer_out, input_grad, grad_mix, grad_out_weight, grad_ffn_in, grad_ffn_out)


HALF = BLK
PIECE = 2 * BLK
VMEM = 60 * 1024 * 1024


def over_x(rows):
    return lax.ppermute(rows, "narrow", [(at, at ^ 1) for at in range(4)])


def over_y(rows):
    return lax.ppermute(rows, "narrow", [(at, at ^ 2) for at in range(4)])


def add_low(*terms):
    return sum(term.astype(jnp.float32) for term in terms).astype(jnp.bfloat16)


def gather_pieces(top, low):
    top_x, low_y = over_x(top), over_y(low)
    low_x, top_y = over_x(low), over_y(top)
    low_d, top_d = over_x(low_y), over_y(top_x)
    return ((top, low), (top_x, low_y), (low_x, top_y), (top_d, low_d))


def scatter_pieces(own, first, second, third):
    (top, low), (top_x, low_y), (low_x, top_y), (top_d, low_d) = own, first, second, third
    to_top_y, to_low_x = over_x(top_d), over_y(low_d)
    to_top, to_low = over_x(top_x), over_y(low_y)
    more_top, more_low = over_y(add_low(top_y, to_top_y)), over_x(add_low(low_x, to_low_x))
    return add_rows(top, to_top, more_top), add_rows(low, to_low, more_low)


def add_rows(*terms):
    return sum(term.astype(jnp.float32) for term in terms)


def slot_tables(narrow_index, fresh_block):
    block_ids = jnp.arange(NBLK, dtype=jnp.int32)
    partner = (block_ids // 2) ^ narrow_index
    even = jnp.array([0, 2, 5, 6], jnp.int32)[partner]
    odd = jnp.array([1, 4, 3, 7], jnp.int32)[partner]
    return jnp.where(block_ids % 2 == 0, even, odd), fresh_block.astype(jnp.int32)


def across(left, right):
    return lax.dot_general(left, right, (((1,), (1,)), ((), ())), preferred_element_type=jnp.float32)


def down(left, right):
    return lax.dot_general(left, right, (((0,), (0,)), ((), ())), preferred_element_type=jnp.float32)


def straight(left, right):
    return jnp.dot(left, right, preferred_element_type=jnp.float32)


def any_specs(count):
    return [pl.BlockSpec(memory_space=pl.ANY)] * count


def cost(flops, bytes_accessed):
    return pl.CostEstimate(flops=int(flops), bytes_accessed=int(bytes_accessed), transcendentals=0)


MESH = pl.DeviceIdType.MESH
SLOTS = 13
STAGES = 12
SUB = 128
TILE = 256


def begin(copies):
    for copy in copies:
        copy.start()


def finish(copies):
    for copy in copies:
        copy.wait()


def neighbours():
    wide, narrow = lax.axis_index("wide"), lax.axis_index("narrow")
    z, core = wide // 2, wide % 2
    mate = (wide + 1 - 2 * core, narrow)
    near_x = (wide, narrow + 1 - 2 * (narrow % 2))
    near_y = (wide, (narrow + 2) % 4)
    return wide, narrow, z, core, mate, near_x, near_y


def line_scratch():
    low = jnp.bfloat16
    pair = pltpu.VMEM((SLOTS, 2, SUB, TILE), low)
    return [
        pltpu.VMEM((SLOTS, 4, SUB, TILE), low),
        pair,
        pair,
        pair,
        pltpu.VMEM((SLOTS, SUB, TILE), low),
        pair,
        pair,
        pltpu.SemaphoreType.DMA((14, SLOTS)),
        pltpu.SemaphoreType.DMA((4, SLOTS)),
    ]


def enter(neighbour_places):
    wide, narrow, z, core, mate, near_x, near_y = neighbour_places
    barrier = pltpu.get_barrier_semaphore()

    def greet(place):
        pl.semaphore_signal(barrier, inc=1, device_id=place, device_id_type=MESH)

    for place in (mate, near_x, near_y):
        greet(place)
    middle = (z == 1) | (z == 2)

    @pl.when(middle)
    def _():
        greet((2 * (3 - z) + core, narrow))
        greet((6 * (z - 1) + core, narrow))
        pl.semaphore_wait(barrier, 5)

    @pl.when(jnp.logical_not(middle))
    def _():
        greet((2 * (1 + z // 3) + core, narrow))
        pl.semaphore_wait(barrier, 4)


def line_sum(scratch, places, count, product, targets):
    own, met, both, ended, crossed, full, other, sems, out_sems = scratch
    wide, narrow, z, core, mate, _, _ = places
    region = z // 2
    middle = (z == 1) | (z == 2)
    end = jnp.logical_not(middle)
    inward = (2 * (1 + z // 3) + core, narrow)
    across_line = (2 * (3 - z) + core, narrow)
    outward = (6 * (z - 1) + core, narrow)

    def remote(src, dst, kind, slot, place):
        return pltpu.make_async_remote_copy(
            src_ref=src,
            dst_ref=dst,
            send_sem=sems.at[2 * kind, slot],
            recv_sem=sems.at[2 * kind + 1, slot],
            device_id=place,
            device_id_type=MESH,
        )

    def core_one(s):
        return remote(own.at[s, pl.ds(2 * (1 - core), 2)], met.at[s], 0, s, mate)

    def line_one(s):
        return remote(both.at[s], ended.at[s], 1, s, inward)

    def cross_one(s):
        return remote(both.at[s, 1 - region], crossed.at[s], 2, s, across_line)

    def cross_two(s):
        return remote(full.at[s, region], full.at[s, region], 3, s, across_line)

    def out_one(s):
        return remote(full.at[s, region], full.at[s, region], 4, s, outward)

    def out_two(s):
        return remote(full.at[s, 1 - region], full.at[s, 1 - region], 5, s, outward)

    def core_two(s):
        return remote(full.at[s], other.at[s], 6, s, mate)

    def add(left, right):
        return (left.astype(jnp.float32) + right.astype(jnp.float32)).astype(jnp.bfloat16)

    def deliveries(k, s):
        for t in range(2):
            for which, (src, part) in enumerate(
                ((full.at[s, t], 2 * core + t), (other.at[s, t], 2 * (1 - core) + t))
            ):
                for condition, ref in targets(k, part):
                    yield condition, pltpu.make_async_copy(src, ref, out_sems.at[2 * t + which, s])

    def start(k, s):
        product(k, own.at[s])
        core_one(s).start()

    def cores(k, s):
        core_one(s).wait_recv()
        both[s] = add(own[s, pl.ds(2 * core, 2)], met[s])
        pl.when(end)(lambda: line_one(s).start())

    def ends(k, s):
        @pl.when(middle)
        def _():
            line_one(s).wait_recv()
            both[s] = add(both[s], ended[s])
            cross_one(s).start()

    def centre(k, s):
        @pl.when(middle)
        def _():
            cross_one(s).wait_recv()
            full[s, region] = add(both[s, region], crossed[s])
            cross_two(s).start()
            out_one(s).start()

    def pass_on(k, s):
        @pl.when(middle)
        def _():
            cross_two(s).wait_recv()
            out_two(s).start()

    def back(k, s):
        @pl.when(end)
        def _():
            out_one(s).wait_recv()
            out_two(s).wait_recv()

        core_two(s).start()

    def deliver(k, s):
        core_two(s).wait_recv()
        for condition, copy in deliveries(k, s):
            pl.when(condition)(copy.start)

    def clear(k, s):
        core_one(s).wait_send()
        core_two(s).wait_send()

        @pl.when(end)
        def _():
            line_one(s).wait_send()

        @pl.when(middle)
        def _():
            for copy in (cross_one(s), cross_two(s), out_one(s), out_two(s)):
                copy.wait_send()

        for condition, copy in deliveries(k, s):
            pl.when(condition)(copy.wait)

    stages = (
        (12, clear),
        (10, deliver),
        (9, back),
        (7, pass_on),
        (5, centre),
        (3, ends),
        (1, cores),
        (0, start),
    )

    def step(i, carry):
        for delay, work in stages:
            k = i - delay

            @pl.when((k >= 0) & (k < count))
            def _(work=work, k=k):
                work(k, lax.rem(k + SLOTS, SLOTS))

        return carry

    return step


def square_scratch():
    low = jnp.bfloat16
    block = pltpu.VMEM((2, BLK, HEADS * HS), low)
    return [block, block, pltpu.SemaphoreType.DMA((6, 2)), pltpu.SemaphoreType.DMA((2,))]


def square_sum(scratch, places, parts, landed):
    met, mid, sems, load_sems = scratch
    top_x, low_y, low_x, top_y, top_d, low_d = parts
    near_x, near_y = places[5:]

    def remote(src, dst, kind, place):
        return pltpu.make_async_remote_copy(
            src_ref=src,
            dst_ref=dst,
            send_sem=sems.at[kind, 0],
            recv_sem=sems.at[kind, 1],
            device_id=place,
            device_id_type=MESH,
        )

    first = [remote(top_d, met.at[0], 0, near_x), remote(low_d, met.at[1], 1, near_y)]
    direct = [remote(top_x, landed[0], 2, near_x), remote(low_y, landed[1], 3, near_y)]
    second = [remote(mid.at[0], landed[2], 4, near_y), remote(mid.at[1], landed[3], 5, near_x)]
    loads = []
    if top_y is not None:
        loads = [
            pltpu.make_async_copy(top_y, mid.at[0], load_sems.at[0]),
            pltpu.make_async_copy(low_x, mid.at[1], load_sems.at[1]),
        ]

    def open_sum():
        begin(first)
        begin(direct)
        begin(loads)

    def join_sum():
        finish(loads)
        for at in range(2):
            first[at].wait()

            def tile(i, carry, at=at):
                rows = pl.ds(pl.multiple_of(i * 64, 64), 64)
                mid[at, rows, :] = add_low(mid[at, rows, :], met[at, rows, :])
                return carry

            lax.fori_loop(0, BLK // 64, tile, 0)
            second[at].start()

    def close_sum():
        finish(direct)
        finish(second)

    return open_sum, join_sum, close_sum, first, direct


def unit_grads(
    act, grad_two_all, normed_two_all, grad_parts, back_sums, middle, cotangent, live, out_weight
):
    rows, units = act.shape
    width = grad_two_all.shape[1]
    local_rows = middle.shape[0]
    low = jnp.bfloat16
    out_blocks, in_blocks = units // SUB, width // SUB
    halves = width // 1024
    out_chunks = out_blocks * halves
    columns = grad_parts.shape[1] // TILE
    in_chunks = (width // PIECE) * columns
    count = out_chunks + in_chunks

    def body(*refs):
        act_in, two_in, normed_in, parts_in = refs[:4]
        partial = refs[4:12]
        middle_in, cot_in, weight_in, live_ref = refs[12:16]
        out_grad, in_grad, branch_out, middle_out, gated_out = refs[16:21]
        act_ref, shared, parts_ref, landed, own_ref, cot_ref, mid_ref, grad_ref, branch = refs[21:30]
        gated_ref, load_sems, stage_sems, gather_sems, back_sems = refs[30:35]
        line = refs[35:44]
        square = refs[44:48]
        places = neighbours()
        near_x, near_y = places[5:]
        enter(places)
        load_act = pltpu.make_async_copy(act_in, act_ref, load_sems.at[0])
        load_two = pltpu.make_async_copy(two_in, shared, load_sems.at[1])
        load_parts = pltpu.make_async_copy(parts_in, parts_ref, load_sems.at[2])
        load_normed = pltpu.make_async_copy(normed_in, shared, load_sems.at[3])
        open_sum, join_sum, close_sum, _, _ = square_sum(
            square, places, partial[2:], [landed.at[at] for at in range(4)]
        )
        load_two.start()
        load_act.start()
        open_sum()
        load_parts.start()
        load_two.wait()
        load_act.wait()

        def product(k, own):
            @pl.when(k < out_chunks)
            def _():
                rows_at = pl.ds(pl.multiple_of((k // halves) * SUB, SUB), SUB)
                wide_at = pl.ds(pl.multiple_of((k % halves) * 1024, 1024), 1024)
                result = down(act_ref[:, rows_at], shared[:, wide_at]).astype(low)
                for part in range(4):
                    own[part] = result[:, part * TILE : (part + 1) * TILE]

            @pl.when(k == out_chunks)
            def _():
                load_normed.start()
                load_parts.wait()
                load_normed.wait()

            @pl.when(k >= out_chunks)
            def _():
                at = k - out_chunks
                rows_at = pl.ds(pl.multiple_of((at // columns) * PIECE, PIECE), PIECE)
                wide_at = pl.ds(pl.multiple_of((at % columns) * TILE, TILE), TILE)
                result = down(shared[:, rows_at], parts_ref[:, wide_at]).astype(low)
                for part in range(4):
                    own[part] = result[part * SUB : (part + 1) * SUB]

        def targets(k, part):
            wide_at = pl.ds(pl.multiple_of((k % halves) * 1024 + part * TILE, TILE), TILE)
            at = jnp.maximum(k - out_chunks, 0)
            in_at = pl.ds(pl.multiple_of((at % columns) * TILE, TILE), TILE)
            first = jnp.minimum(k, out_chunks - 1) // halves
            return [
                (k < out_chunks, out_grad.at[first, :, wide_at]),
                (k >= out_chunks, in_grad.at[(at // columns) * 4 + part, :, in_at]),
            ]

        step = line_sum(line, places, count, product, targets)

        def block(at):
            return pl.ds(at * BLK, BLK)

        def spread(src, slot, kind, place):
            return pltpu.make_async_remote_copy(
                src_ref=src,
                dst_ref=branch_out.at[block(slot)],
                send_sem=gather_sems.at[kind, 0],
                recv_sem=gather_sems.at[kind, 1],
                device_id=place,
                device_id_type=MESH,
            )

        def stage(half):
            return [
                pltpu.make_async_copy(partial[half], own_ref, stage_sems.at[0]),
                pltpu.make_async_copy(cot_in.at[block(half)], cot_ref, stage_sems.at[1]),
                pltpu.make_async_copy(middle_in.at[block(half)], mid_ref, stage_sems.at[2]),
            ]

        keep = [
            pltpu.make_async_copy(branch.at[at], branch_out.at[block(at)], stage_sems.at[3 + at])
            for at in range(2)
        ]

        def rows_back(half):
            def tile(i, carry):
                at = pl.ds(pl.multiple_of(i * 32, 32), 32)
                grad = own_ref[at, :].astype(jnp.float32)
                grad += landed[half, at, :].astype(jnp.float32)
                grad += landed[2 + half, at, :].astype(jnp.float32)
                result = cot_ref[at, :].astype(jnp.float32) + norm_back(mid_ref[at, :], grad)
                grad_ref[at, :] = result
                live_at = pl.ds(pl.multiple_of(half * BLK + i * 32, 32), 32)
                branch[half, at, :] = (live_ref[live_at, :1] * result).astype(low)
                return carry

            lax.fori_loop(0, BLK // 32, tile, 0)
            copy = pltpu.make_async_copy(grad_ref, middle_out.at[block(half)], stage_sems.at[5])
            copy.start()
            return copy

        sends = [
            spread(branch.at[0], 2, 0, near_x),
            spread(branch.at[1], 3, 1, near_y),
            spread(branch.at[1], 4, 2, near_x),
            spread(branch.at[0], 5, 3, near_y),
        ]
        later = [
            spread(branch_out.at[block(3)], 7, 4, near_x),
            spread(branch_out.at[block(2)], 6, 5, near_y),
        ]

        lax.fori_loop(0, 9, step, 0)
        join_sum()
        begin(stage(0))
        lax.fori_loop(9, 25, step, 0)
        close_sum()
        finish(stage(0))
        written = rows_back(0)
        sends[0].start()
        begin(stage(1))
        finish(stage(1))
        written.wait()
        written = rows_back(1)
        begin([sends[1], sends[2], sends[3]])
        begin(keep)
        lax.fori_loop(25, 33, step, 0)
        sends[0].wait_recv()
        sends[1].wait_recv()
        begin(later)
        lax.fori_loop(33, 50, step, 0)
        written.wait()
        finish(keep)
        for copy in sends[:2]:
            copy.wait_send()
        finish(sends[2:])
        finish(later)

        weight_loads = [
            pltpu.make_async_copy(weight_in.at[block(at)], landed.at[at], back_sems.at[at])
            for at in range(weight_in.shape[0] // BLK)
        ]
        stages = (own_ref, cot_ref)

        def row_load(at):
            return pltpu.make_async_copy(
                branch_out.at[block(at)], stages[at % 2], back_sems.at[2 + at % 2]
            )

        def gated_store(at):
            return pltpu.make_async_copy(
                gated_ref.at[at % 2], gated_out.at[block(at)], back_sems.at[4 + at % 2]
            )

        begin(weight_loads)
        row_load(0).start()
        at_step = 50
        for at in range(rows // BLK):
            lax.fori_loop(at_step, at_step + 2, step, 0)
            at_step += 2
            if at == 0:
                finish(weight_loads)
            if at + 1 < rows // BLK:
                row_load(at + 1).start()
            row_load(at).wait()
            if at >= 2:
                gated_store(at - 2).wait()
            for part in range(len(weight_loads)):
                result = across(stages[at % 2][...], landed[part])
                gated_ref[at % 2, :, part * BLK : (part + 1) * BLK] = result.astype(low)
            gated_store(at).start()
        lax.fori_loop(at_step, count + STAGES, step, 0)
        gated_store(rows // BLK - 2).wait()
        gated_store(rows // BLK - 1).wait()

    return pl.pallas_call(
        body,
        in_specs=any_specs(15) + [pl.BlockSpec(memory_space=pltpu.VMEM)],
        out_specs=any_specs(5),
        out_shape=[
            jax.ShapeDtypeStruct((out_blocks, SUB, width), low),
            jax.ShapeDtypeStruct((in_blocks, SUB, grad_parts.shape[1]), low),
            jax.ShapeDtypeStruct((rows, width), low),
            jax.ShapeDtypeStruct((local_rows, width), jnp.float32),
            jax.ShapeDtypeStruct((rows, out_weight.shape[0]), low),
        ],
        scratch_shapes=[
            pltpu.VMEM(act.shape, low),
            pltpu.VMEM((rows, width), low),
            pltpu.VMEM(grad_parts.shape, low),
            pltpu.VMEM((4, BLK, width), low),
            pltpu.VMEM((BLK, width), low),
            pltpu.VMEM((BLK, width), low),
            pltpu.VMEM((BLK, width), jnp.float32),
            pltpu.VMEM((BLK, width), jnp.float32),
            pltpu.VMEM((2, BLK, width), low),
            pltpu.VMEM((2, BLK, out_weight.shape[0]), low),
            pltpu.SemaphoreType.DMA((4,)),
            pltpu.SemaphoreType.DMA((6,)),
            pltpu.SemaphoreType.DMA((6, 2)),
            pltpu.SemaphoreType.DMA((6,)),
        ]
        + line_scratch()
        + square_scratch(),
        compiler_params=pltpu.CompilerParams(
            vmem_limit_bytes=VMEM, collective_id=1, has_side_effects=True
        ),
        cost_estimate=cost(2 * 3 * rows * width * units, 60e6),
        name="unit_grads",
    )(
        act,
        grad_two_all,
        normed_two_all,
        grad_parts,
        *back_sums,
        middle,
        cotangent,
        out_weight,
        live,
    )


def mix_grads(gated, grad_branch_all, normed_all, grad_projected, mix_weight, two_sums):
    _, rows, columns = gated.shape
    width = normed_all.shape[1]
    parts = grad_projected.shape[0]
    low = jnp.bfloat16
    out_chunks = width // TILE
    per_row = columns // TILE
    per_part = (width // PIECE) * per_row
    count = out_chunks + parts * per_part
    wide_tile = 1024

    def body(*refs):
        gated_in, branch_in, normed_in, grads_in, weight_in = refs[:5]
        two_partial = refs[5:11]
        out_grad, mix_grad = refs[11:13]
        own_outs = refs[13:15]
        landed, two_landed = refs[15:19], refs[19:23]
        gated_ref, branch_ref, normed_ref, grads_ref, weight_ref, far, near, own_ref = refs[23:31]
        load_sems, branch_sems, grad_sems, weight_sems, own_sems = refs[31:36]
        line = refs[36:45]
        square, two_square = refs[45:49], refs[49:53]
        mid = square[1]
        places = neighbours()
        enter(places)

        def part_columns(c):
            return pl.ds(c * columns, columns)

        load_gated = pltpu.make_async_copy(gated_in.at[0], gated_ref, load_sems.at[0])
        load_normed = pltpu.make_async_copy(normed_in, normed_ref, load_sems.at[1])

        def load_branch(k):
            at = pl.ds(pl.multiple_of(k * TILE, TILE), TILE)
            slot = k % 2
            return pltpu.make_async_copy(branch_in.at[:, at], branch_ref.at[slot], branch_sems.at[slot])

        grad_loads = [
            pltpu.make_async_copy(grads_in.at[c], grads_ref.at[:, part_columns(c)], grad_sems.at[c])
            for c in range(parts)
        ]
        weight_loads = [
            pltpu.make_async_copy(weight_in.at[c], weight_ref.at[:, part_columns(c)], weight_sems.at[c])
            for c in range(parts)
        ]
        load_gated.start()
        load_branch(0).start()
        begin(grad_loads)
        begin(weight_loads)
        load_normed.start()
        _, join_sum, close_sum, first, direct = square_sum(
            square,
            places,
            (near.at[0], near.at[1], None, None, far.at[0], far.at[1]),
            landed,
        )
        open_two, join_two, close_two, _, _ = square_sum(two_square, places, two_partial, two_landed)
        load_gated.wait()

        def product(k, own):
            @pl.when(k < out_chunks)
            def _():
                load_branch(k).wait()
                pl.when(k + 1 < out_chunks)(lambda: load_branch(k + 1).start())
                result = down(gated_ref[...], branch_ref[k % 2]).astype(low)
                for part in range(4):
                    own[part] = result[part * SUB : (part + 1) * SUB]

            @pl.when(k >= out_chunks)
            def _():
                at = k - out_chunks
                rows_at = pl.ds(pl.multiple_of(((at // per_row) % 4) * PIECE, PIECE), PIECE)
                start = (at // per_part) * columns + (at % per_row) * TILE
                wide_at = pl.ds(pl.multiple_of(start, TILE), TILE)
                result = down(normed_ref[:, rows_at], grads_ref[:, wide_at]).astype(low)
                for part in range(4):
                    own[part] = result[part * SUB : (part + 1) * SUB]

        def targets(k, part):
            first_at = pl.ds(pl.multiple_of(jnp.minimum(k, out_chunks - 1) * TILE, TILE), TILE)
            at = jnp.maximum(k - out_chunks, 0)
            wide_at = pl.ds(pl.multiple_of((at % per_row) * TILE, TILE), TILE)
            return [
                (k < out_chunks, out_grad.at[part, :, first_at]),
                (k >= out_chunks, mix_grad.at[(at // per_row) * 4 + part, :, wide_at]),
            ]

        step = line_sum(line, places, count, product, targets)

        def partial(piece, tile, top, low_part):
            at = slice(tile * wide_tile, (tile + 1) * wide_tile)
            acts = grads_ref[piece * PIECE : (piece + 1) * PIECE, :]
            total = across(acts, weight_ref[at, :])
            top[:, at] = total[:HALF].astype(low)
            low_part[:, at] = total[HALF:].astype(low)

        own_stores = [
            pltpu.make_async_copy(own_ref.at[at], own_outs[at], own_sems.at[at]) for at in range(2)
        ]
        places_of = (
            (3, far.at[0], far.at[1], first),
            (1, near.at[0], near.at[1], direct),
            (2, mid.at[1], mid.at[0], []),
            (0, own_ref.at[0], own_ref.at[1], own_stores),
        )
        lax.fori_loop(0, 2, step, 0)
        finish(grad_loads)
        finish(weight_loads)
        at_step = 2
        for piece, top, low_part, copies in places_of:
            for tile in range(width // wide_tile):
                partial(piece, tile, top, low_part)
                if tile == width // wide_tile - 1:
                    begin(copies)
                lax.fori_loop(at_step, at_step + 1, step, 0)
                at_step += 1
                if at_step == 8:
                    load_normed.wait()
        lax.fori_loop(at_step, 12, step, 0)
        join_sum()
        open_two()
        lax.fori_loop(12, 36, step, 0)
        join_two()
        lax.fori_loop(36, count + STAGES, step, 0)
        close_sum()
        close_two()
        finish(own_stores)

    return pl.pallas_call(
        body,
        in_specs=any_specs(11),
        out_specs=any_specs(12),
        out_shape=[
            jax.ShapeDtypeStruct((columns // SUB, SUB, width), low),
            jax.ShapeDtypeStruct((parts * width // SUB, SUB, columns), low),
        ]
        + [jax.ShapeDtypeStruct((BLK, width), low)] * 10,
        scratch_shapes=[
            pltpu.VMEM((rows, columns), low),
            pltpu.VMEM((2, rows, TILE), low),
            pltpu.VMEM((rows, width), low),
            pltpu.VMEM((rows, parts * columns), low),
            pltpu.VMEM((width, parts * columns), low),
            pltpu.VMEM((2, BLK, width), low),
            pltpu.VMEM((2, BLK, width), low),
            pltpu.VMEM((2, BLK, width), low),
            pltpu.SemaphoreType.DMA((2,)),
            pltpu.SemaphoreType.DMA((2,)),
            pltpu.SemaphoreType.DMA((parts,)),
            pltpu.SemaphoreType.DMA((parts,)),
            pltpu.SemaphoreType.DMA((2,)),
        ]
        + line_scratch()
        + square_scratch()
        + square_scratch(),
        compiler_params=pltpu.CompilerParams(
            vmem_limit_bytes=VMEM, collective_id=2, has_side_effects=True
        ),
        cost_estimate=cost(2 * 9 * rows * width * columns, 60e6),
        name="mix_grads",
    )(gated, grad_branch_all, normed_all, grad_projected, mix_weight, *two_sums)


def row_copies(pair, rows, sems, at):
    return [
        pltpu.make_async_copy(src, rows.at[pl.ds(half * HALF, HALF)], sems.at[at + half])
        for half, src in enumerate(pair)
    ]


def project_piece(pair, weight, kept, piece):
    parts, width, columns = weight.shape
    group_rows = NBLK * BLK
    low = jnp.bfloat16
    spot = pl.ds(piece * PIECE, PIECE)
    joined = 2

    def body(*refs):
        weight_in = refs[2]
        rows_out, parts_out, rows, weights, out, row_sems, weight_sems, out_sems = refs[3 + len(kept) :]
        row_loads = row_copies(refs[:2], rows, row_sems, 0)
        weight_loads = [
            pltpu.make_async_copy(
                weight_in.at[c], weights.at[:, pl.ds(c * columns, columns)], weight_sems.at[c]
            )
            for c in range(parts)
        ]
        stores = [
            pltpu.make_async_copy(
                out.at[:, pl.ds(c * columns, columns)], parts_out.at[c, spot, :], out_sems.at[c]
            )
            for c in range(parts)
        ]
        begin(row_loads)
        begin(weight_loads[:joined])
        finish(row_loads)
        begin(weight_loads[joined:])
        keep = pltpu.make_async_copy(rows, rows_out.at[spot, :], row_sems.at[2])
        keep.start()
        for c in range(0, parts, joined):
            finish(weight_loads[c : c + joined])
            at = slice(c * columns, (c + joined) * columns)
            out[:, at] = straight(rows[...], weights[:, at]).astype(low)
            begin(stores[c : c + joined])
        finish(stores)
        keep.wait()

    return pl.pallas_call(
        body,
        in_specs=any_specs(3 + len(kept)),
        out_specs=any_specs(2),
        out_shape=[
            jax.ShapeDtypeStruct((group_rows, width), low),
            jax.ShapeDtypeStruct((parts, group_rows, columns), low),
        ],
        scratch_shapes=[
            pltpu.VMEM((PIECE, width), low),
            pltpu.VMEM((width, parts * columns), low),
            pltpu.VMEM((PIECE, parts * columns), low),
            pltpu.SemaphoreType.DMA((3,)),
            pltpu.SemaphoreType.DMA((parts,)),
            pltpu.SemaphoreType.DMA((parts,)),
        ],
        input_output_aliases={3 + at: at for at in range(len(kept))},
        compiler_params=pltpu.CompilerParams(vmem_limit_bytes=VMEM),
        cost_estimate=cost(2 * PIECE * parts * width * columns, 2 * parts * width * columns + 8e6),
        name="project",
    )(*pair, weight, *kept)


def partial_sums(acts, weight, pieces, transposed, after=()):
    parts, _, columns = acts.shape
    width = weight.shape[1] if transposed else weight.shape[2]
    deep = parts * columns
    low = jnp.bfloat16
    wide_tile = 1024

    def body(act_in, weight_in, *refs):
        refs = refs[len(after) :]
        outs = refs[: 2 * len(pieces)]
        acts_ref, weights, out, act_sems, weight_sems, out_sems = refs[2 * len(pieces) :]

        def place(c):
            return pl.ds(c * columns, columns)

        act_loads = [
            [
                pltpu.make_async_copy(
                    act_in.at[c, pl.ds(piece * PIECE, PIECE), :],
                    acts_ref.at[at, :, place(c)],
                    act_sems.at[at, c],
                )
                for c in range(parts)
            ]
            for at, piece in enumerate(pieces)
        ]
        weight_loads = []
        for j in range(width // wide_tile):
            tile = pl.ds(j * wide_tile, wide_tile)
            weight_loads.append(
                [
                    pltpu.make_async_copy(
                        weight_in.at[c, tile, :], weights.at[tile, place(c)], weight_sems.at[j, c]
                    )
                    if transposed
                    else pltpu.make_async_copy(
                        weight_in.at[c, :, tile], weights.at[place(c), tile], weight_sems.at[j, c]
                    )
                    for c in range(parts)
                ]
            )
        begin(act_loads[0])
        begin(weight_loads[0])
        stores = []
        for at in range(len(pieces)):
            finish(act_loads[at])
            for j, loads in enumerate(weight_loads):
                if at == 0:
                    finish(loads)
                    if j + 1 < len(weight_loads):
                        begin(weight_loads[j + 1])
                if j == len(weight_loads) - 1 and at + 1 < len(pieces):
                    begin(act_loads[at + 1])
                tile = slice(j * wide_tile, (j + 1) * wide_tile)
                if transposed:
                    total = across(acts_ref[at], weights[tile, :])
                else:
                    total = straight(acts_ref[at], weights[:, tile])
                out[2 * at, :, tile] = total[:HALF].astype(low)
                out[2 * at + 1, :, tile] = total[HALF:].astype(low)
            now = [
                pltpu.make_async_copy(out.at[at_out], outs[at_out], out_sems.at[at_out])
                for at_out in (2 * at, 2 * at + 1)
            ]
            begin(now)
            stores += now
        finish(stores)

    return pl.pallas_call(
        body,
        in_specs=any_specs(2 + len(after)),
        out_specs=any_specs(2 * len(pieces)),
        out_shape=[jax.ShapeDtypeStruct((HALF, width), low)] * (2 * len(pieces)),
        scratch_shapes=[
            pltpu.VMEM((len(pieces), PIECE, deep), low),
            pltpu.VMEM((width, deep) if transposed else (deep, width), low),
            pltpu.VMEM((2 * len(pieces), HALF, width), low),
            pltpu.SemaphoreType.DMA((len(pieces), parts)),
            pltpu.SemaphoreType.DMA((width // wide_tile, parts)),
            pltpu.SemaphoreType.DMA((2 * len(pieces),)),
        ],
        compiler_params=pltpu.CompilerParams(vmem_limit_bytes=VMEM),
        cost_estimate=cost(
            2 * len(pieces) * PIECE * parts * width * columns, 2 * parts * width * columns + 8e6
        ),
        name="partial_sums",
    )(acts, weight, *after)


def unit_piece(pair, grad_pair, ffn_in, ffn_out, kept, piece):
    _, width, units = ffn_in.shape
    group_rows = NBLK * BLK
    main = units // TILE * TILE
    tail = units - main
    low = jnp.bfloat16
    spot = pl.ds(piece * PIECE, PIECE)
    cuts = ((0, 2 * TILE), (2 * TILE, main - 2 * TILE))
    wide_tile = 1024

    def body(*refs):
        in_ref, out_ref = refs[4:6]
        outs = refs[6 + len(kept) :]
        rows_out, grads_out, act_out, parts_out = outs[:4]
        sum_outs = outs[4:8]
        rows, grads, w_in, w_out, act, parts, sums, row_sems, sems, done_sems, sum_sems = outs[8:]
        loads = row_copies(refs[:2], rows, row_sems, 0)
        grad_loads = row_copies(refs[2:4], grads, row_sems, 2)

        def weight_loads(which, start, size, first, second):
            at = pl.ds(start, size)
            return [
                pltpu.make_async_copy(
                    in_ref.at[0, :, at], w_in.at[:, pl.ds(first, size)], sems.at[which, 0]
                ),
                pltpu.make_async_copy(
                    in_ref.at[1, :, at], w_in.at[:, pl.ds(second, size)], sems.at[which, 1]
                ),
                pltpu.make_async_copy(out_ref.at[at, :], w_out.at[at, :], sems.at[which, 2]),
            ]

        weights = [weight_loads(at, *cut, cut[0], main + cut[0]) for at, cut in enumerate(cuts)]
        weights.append(weight_loads(2, main, tail, 2 * main, 2 * main + tail))
        queue = [[copy] for loads_here in weights[:2] for copy in loads_here] + [weights[2]]
        queue[2] = grad_loads + queue[2]
        begin(loads)
        begin(queue[0])
        begin(queue[1])
        finish(loads)
        stores = [
            pltpu.make_async_copy(rows, rows_out.at[spot, :], done_sems.at[0]),
            pltpu.make_async_copy(grads, grads_out.at[spot, :], done_sems.at[1]),
        ]

        def products(at, first, second, part_a, part_b, grad_act):
            act[:, at] = (part_a * part_b).astype(low)
            parts[:, first] = (grad_act * part_b).astype(low)
            parts[:, second] = (grad_act * part_a).astype(low)

        def ready(at):
            if at + 2 < len(queue):
                begin(queue[at + 2])
            finish(queue[at])

        for which, (start, size) in enumerate(cuts):
            at, second = slice(start, start + size), slice(main + start, main + start + size)
            ready(3 * which)
            part_a = straight(rows[...], w_in[:, at])
            ready(3 * which + 1)
            part_b = straight(rows[...], w_in[:, second])
            ready(3 * which + 2)
            if which == 0:
                begin(stores)
            grad_act = across(grads[...], w_out[at, :])
            products(at, at, second, part_a, part_b, grad_act)
        finish(weights[2])
        if tail:
            both = straight(rows[...], w_in[:, 2 * main :])
            grad_act = across(grads[...], w_out[main:, :])
            products(
                slice(main, units),
                slice(2 * main, 2 * main + tail),
                slice(2 * main + tail, 2 * units),
                both[:, :tail],
                both[:, tail:],
                grad_act,
            )
        more = [
            pltpu.make_async_copy(act, act_out.at[spot, :], done_sems.at[2]),
            pltpu.make_async_copy(parts, parts_out.at[spot, :], done_sems.at[3]),
        ]
        begin(more)
        stores += more
        for j in range(width // wide_tile):
            at = slice(j * wide_tile, (j + 1) * wide_tile)
            back = across(parts[...], w_in[at, :])
            sums[0, :, at] = back[:HALF].astype(low)
            sums[1, :, at] = back[HALF:].astype(low)
            two = straight(act[...], w_out[:, at])
            sums[2, :, at] = two[:HALF].astype(low)
            sums[3, :, at] = two[HALF:].astype(low)
            tile = pl.ds(j * wide_tile, wide_tile)
            now = [
                pltpu.make_async_copy(
                    sums.at[at_out, :, tile], sum_outs[at_out].at[:, tile], sum_sems.at[j, at_out]
                )
                for at_out in range(4)
            ]
            begin(now)
            stores += now
        finish(stores)

    return pl.pallas_call(
        body,
        in_specs=any_specs(6 + len(kept)),
        out_specs=any_specs(8),
        out_shape=[
            jax.ShapeDtypeStruct((group_rows, width), low),
            jax.ShapeDtypeStruct((group_rows, width), low),
            jax.ShapeDtypeStruct((group_rows, units), low),
            jax.ShapeDtypeStruct((group_rows, 2 * units), low),
        ]
        + [jax.ShapeDtypeStruct((HALF, width), low)] * 4,
        scratch_shapes=[
            pltpu.VMEM((PIECE, width), low),
            pltpu.VMEM((PIECE, width), low),
            pltpu.VMEM((width, 2 * units), low),
            pltpu.VMEM((units, width), low),
            pltpu.VMEM((PIECE, units), low),
            pltpu.VMEM((PIECE, 2 * units), low),
            pltpu.VMEM((4, HALF, width), low),
            pltpu.SemaphoreType.DMA((4,)),
            pltpu.SemaphoreType.DMA((3, 3)),
            pltpu.SemaphoreType.DMA((4,)),
            pltpu.SemaphoreType.DMA((width // wide_tile, 4)),
        ],
        input_output_aliases={6 + at: at for at in range(len(kept))},
        compiler_params=pltpu.CompilerParams(vmem_limit_bytes=VMEM),
        cost_estimate=cost(12 * PIECE * width * units, 6 * width * units + 12e6),
        name="gated_unit",
    )(*pair, *grad_pair, ffn_in, ffn_out, *kept)


def live_rows(cotangent, live, after):
    width = cotangent.shape[1]

    def body(cot_ref, live_ref, *refs):
        for half, out_ref in enumerate(refs[len(after) :]):
            rows = pl.ds(half * HALF, HALF)
            product = cot_ref[rows, :].astype(jnp.float32) * live_ref[rows, :1]
            out_ref[...] = product.astype(jnp.bfloat16)

    return pl.pallas_call(
        body,
        in_specs=[pl.BlockSpec(memory_space=pltpu.VMEM)] * 2 + any_specs(len(after)),
        out_specs=[pl.BlockSpec(memory_space=pltpu.VMEM)] * 2,
        out_shape=[jax.ShapeDtypeStruct((HALF, width), jnp.bfloat16)] * 2,
        compiler_params=pltpu.CompilerParams(vmem_limit_bytes=VMEM),
        cost_estimate=cost(2e6, 4e6),
        name="live_rows",
    )(cotangent, live, *after)


def finish_rows(mix_low, out_low, hidden, middle, grad_middle, live, normed_terms, two_terms):
    parts, width, columns = mix_low.shape
    local_rows = hidden.shape[0]
    tile = local_rows // parts
    out_tile = out_low.shape[0] // parts
    half_steps = parts // 2
    terms = len(normed_terms) + len(two_terms)

    def body(mix_ref, out_ref, hidden_ref, middle_ref, grad_ref, live_ref, *refs):
        term_refs = refs[:terms]
        mix_out, out_out, layer_ref, input_ref = refs[terms:]
        mix_out[...] = mix_ref[...].astype(jnp.float32)
        out_out[...] = out_ref[...].astype(jnp.float32)

        def rows_of(half):
            normed = add_rows(*(ref[...] for ref in term_refs[3 * half : 3 * half + 3]))
            two = add_rows(*(ref[...] for ref in term_refs[6 + 3 * half : 9 + 3 * half]))
            layer = middle_ref[...] + live_ref[...] * two
            layer_ref[...] = layer.astype(jnp.bfloat16)
            back = norm_back(hidden_ref[...].astype(jnp.float32), normed)
            input_ref[...] = (grad_ref[...] + back).astype(jnp.bfloat16)

        first = pl.program_id(0) < half_steps
        pl.when(first)(lambda: rows_of(0))
        pl.when(jnp.logical_not(first))(lambda: rows_of(1))

    def rows_spec(size):
        return pl.BlockSpec((tile, size), lambda i: (i, 0))

    def half_spec(half):
        if half == 0:
            return pl.BlockSpec((tile, width), lambda i: (jnp.minimum(i, half_steps - 1), 0))
        return pl.BlockSpec((tile, width), lambda i: (jnp.maximum(i - half_steps, 0), 0))

    term_specs = ([half_spec(0)] * 3 + [half_spec(1)] * 3) * 2
    mix_spec = pl.BlockSpec((1, width, columns), lambda i: (i, 0, 0))
    out_spec = pl.BlockSpec((out_tile, out_low.shape[1]), lambda i: (i, 0))
    return pl.pallas_call(
        body,
        grid=(parts,),
        in_specs=[mix_spec, out_spec, rows_spec(width), rows_spec(width), rows_spec(width), rows_spec(1)]
        + term_specs,
        out_specs=[mix_spec, out_spec, rows_spec(width), rows_spec(width)],
        out_shape=[
            jax.ShapeDtypeStruct(mix_low.shape, jnp.float32),
            jax.ShapeDtypeStruct(out_low.shape, jnp.float32),
            jax.ShapeDtypeStruct(hidden.shape, jnp.bfloat16),
            jax.ShapeDtypeStruct(hidden.shape, jnp.bfloat16),
        ],
        compiler_params=pltpu.CompilerParams(vmem_limit_bytes=VMEM),
        cost_estimate=cost(1e8, 60e6),
        name="finish_rows",
    )(mix_low, out_low, hidden, middle, grad_middle, live, *normed_terms, *two_terms)


def block_decays(rate):
    row = lax.broadcasted_iota(jnp.int32, (BLK, BLK), 0)
    column = lax.broadcasted_iota(jnp.int32, (BLK, BLK), 1)
    distance = (row - column).astype(jnp.float32)
    within = jnp.where(row >= column, jnp.exp(-rate * jnp.maximum(distance, 0.0)), 0.0)
    place = lax.broadcasted_iota(jnp.int32, (BLK, 1), 0).astype(jnp.float32)
    entry = jnp.exp(-rate * (place + 1.0))
    leave = jnp.exp(-rate * (BLK - 1.0 - place))
    whole = jnp.exp(jnp.full((1, HS), -BLK * rate, jnp.float32))
    return within, entry, leave, whole


def mix_forward(slots, fresh, rates, parts):
    _, group_rows, columns = parts.shape
    heads = columns // HS
    low = jnp.bfloat16

    def body(slot_ref, fresh_ref, rate_ref, parts_ref, gated_ref, mixing_ref, states_ref):
        within, entry, leave, whole = block_decays(rate_ref[pl.program_id(0)])
        state = jnp.zeros((HS, HS), jnp.float32)
        for block in range(NBLK):
            rows = pl.ds(pl.multiple_of(slot_ref[block] * BLK, BLK), BLK)
            queries = jax.nn.silu(parts_ref[0, rows, :].astype(jnp.float32)).astype(low)
            keys = jax.nn.silu(parts_ref[1, rows, :].astype(jnp.float32))
            values = parts_ref[2, rows, :]
            gate = parts_ref[3, rows, :].astype(jnp.float32)
            state = jnp.where(fresh_ref[block] != 0, 0.0, state)
            state_low = state.astype(low)
            states_ref[0, block] = state_low
            weights = (across(queries, keys.astype(low)) * within).astype(low)
            mixing = straight(weights, values) + entry * straight(queries, state_low)
            late_keys = (keys.astype(low).astype(jnp.float32) * leave).astype(low)
            state = whole * state + down(late_keys, values)
            scale = lax.rsqrt(jnp.mean(mixing * mixing, axis=-1, keepdims=True) + head_floor)
            gated_ref[0, rows, :] = (mixing * scale * gate).astype(low)
            mixing_ref[rows, :] = mixing.astype(low)

    return pl.pallas_call(
        body,
        grid_spec=pltpu.PrefetchScalarGridSpec(
            num_scalar_prefetch=3,
            grid=(heads,),
            in_specs=[pl.BlockSpec((4, group_rows, HS), lambda h, *_: (0, 0, h))],
            out_specs=[
                pl.BlockSpec((1, group_rows, HS), lambda h, *_: (0, 0, h)),
                pl.BlockSpec((group_rows, HS), lambda h, *_: (0, h)),
                pl.BlockSpec((1, NBLK, HS, HS), lambda h, *_: (h, 0, 0, 0)),
            ],
        ),
        out_shape=[
            jax.ShapeDtypeStruct((1, group_rows, columns), low),
            jax.ShapeDtypeStruct((group_rows, columns), low),
            jax.ShapeDtypeStruct((heads, NBLK, HS, HS), low),
        ],
        compiler_params=pltpu.CompilerParams(vmem_limit_bytes=VMEM),
        cost_estimate=cost(8e9, 14e6),
        name="mix_forward",
    )(slots, fresh, rates, parts)


def mix_backward(slots, fresh, rates, parts, mixing_all, states, grad_gated, in_low, out_low):
    _, group_rows, columns = parts.shape
    heads = columns // HS
    low = jnp.bfloat16
    width, both_units = in_low.shape
    units = both_units // 2
    main = units // TILE * TILE
    tail = units - main
    in_rows, out_rows = width // heads, units // heads

    def body(
        slot_ref,
        fresh_ref,
        rate_ref,
        parts_ref,
        mixing_ref,
        states_ref,
        grad_ref,
        in_ref,
        wide_ref,
        out_ref,
        in_out,
        wide_out,
    ):
        wide_out[...] = wide_ref[...].astype(jnp.float32)
        for c in range(2):
            in_out[c, :, :main] = in_ref[:, c * main : (c + 1) * main].astype(jnp.float32)
            rest = slice(2 * main + c * tail, 2 * main + (c + 1) * tail)
            in_out[c, :, main:] = in_ref[:, rest].astype(jnp.float32)
        within, entry, leave, whole = block_decays(rate_ref[pl.program_id(0)])
        later = jnp.zeros((HS, HS), jnp.float32)
        for block in reversed(range(NBLK)):
            rows = pl.ds(pl.multiple_of(slot_ref[block] * BLK, BLK), BLK)
            raw_queries = parts_ref[0, rows, :].astype(jnp.float32)
            raw_keys = parts_ref[1, rows, :].astype(jnp.float32)
            queries_float = jax.nn.silu(raw_queries).astype(low).astype(jnp.float32)
            queries, keys = queries_float.astype(low), jax.nn.silu(raw_keys).astype(low)
            values = parts_ref[2, rows, :]
            gate = parts_ref[3, rows, :].astype(jnp.float32)
            mixing = mixing_ref[rows, :].astype(jnp.float32)
            grad_gated_rows = grad_ref[rows, :].astype(jnp.float32)
            scale = lax.rsqrt(jnp.mean(mixing * mixing, axis=-1, keepdims=True) + head_floor)
            headed = mixing * scale
            out_ref[3, rows, :] = (grad_gated_rows * headed).astype(low)
            grad_headed = grad_gated_rows * gate
            inner = jnp.mean(grad_headed * headed, axis=-1, keepdims=True)
            grad = (scale * (grad_headed - headed * inner)).astype(low)
            weights = (across(queries, keys) * within).astype(low)
            grad_scores = (across(grad, values) * within).astype(low)
            later_low = later.astype(low)
            grad_queries = straight(grad_scores, keys) + entry * across(grad, states_ref[0, block])
            grad_keys = down(grad_scores, queries) + leave * across(values, later_low)
            grad_values = down(weights, grad) + leave * straight(keys, later_low)
            early_queries = (queries_float * entry).astype(low)
            later = jnp.where(fresh_ref[block] != 0, 0.0, whole * later + down(early_queries, grad))
            out_ref[0, rows, :] = (grad_queries * silu_slope(raw_queries)).astype(low)
            out_ref[1, rows, :] = (grad_keys * silu_slope(raw_keys)).astype(low)
            out_ref[2, rows, :] = grad_values.astype(low)

    return pl.pallas_call(
        body,
        grid_spec=pltpu.PrefetchScalarGridSpec(
            num_scalar_prefetch=3,
            grid=(heads,),
            in_specs=[
                pl.BlockSpec((4, group_rows, HS), lambda h, *_: (0, 0, h)),
                pl.BlockSpec((group_rows, HS), lambda h, *_: (0, h)),
                pl.BlockSpec((1, NBLK, HS, HS), lambda h, *_: (h, 0, 0, 0)),
                pl.BlockSpec((group_rows, HS), lambda h, *_: (0, h)),
                pl.BlockSpec((in_rows, both_units), lambda h, *_: (h, 0)),
                pl.BlockSpec((out_rows, width), lambda h, *_: (h, 0)),
            ],
            out_specs=[
                pl.BlockSpec((4, group_rows, HS), lambda h, *_: (0, 0, h)),
                pl.BlockSpec((2, in_rows, units), lambda h, *_: (0, h, 0)),
                pl.BlockSpec((out_rows, width), lambda h, *_: (h, 0)),
            ],
        ),
        out_shape=[
            jax.ShapeDtypeStruct(parts.shape, low),
            jax.ShapeDtypeStruct((2, width, units), jnp.float32),
            jax.ShapeDtypeStruct((units, width), jnp.float32),
        ],
        compiler_params=pltpu.CompilerParams(vmem_limit_bytes=VMEM),
        cost_estimate=cost(20e9, 75e6),
        name="mix_backward",
    )(slots, fresh, rates, parts, mixing_all, states, grad_gated, in_low, out_low)


def norm_back(values, grad):
    scale = lax.rsqrt(jnp.mean(values * values, axis=-1, keepdims=True) + epsilon)
    unit = values * scale
    return scale * (grad - unit * jnp.mean(grad * unit, axis=-1, keepdims=True))


def square_device(
    hidden, mix_weight, out_weight, ffn_in_weight, ffn_out_weight, seq_lengths, block_seq, cotangent
):
    local_rows, width = hidden.shape
    units = ffn_out_weight.shape[0]
    head_count = mix_weight.shape[2] // HS
    narrow_index = lax.axis_index("narrow")
    valid_all, fresh_block = group_masks(seq_lengths, block_seq)
    live = lax.dynamic_slice_in_dim(
        valid_all.astype(jnp.float32), narrow_index * local_rows, local_rows
    )[:, None]
    head_ids = narrow_index * head_count + jnp.arange(head_count, dtype=jnp.int32)
    rates = 2.0 ** (-8.0 * (head_ids.astype(jnp.float32) + 1.0) / HEADS)
    slots, fresh = slot_tables(narrow_index, fresh_block)
    low = jnp.bfloat16

    def halves(rows):
        return rows[:HALF], rows[HALF:]

    lives = halves(live)
    inputs = [rows.astype(jnp.float32) for rows in halves(hidden)]

    pieces = gather_pieces(*(row_norm(rows).astype(low) for rows in inputs))
    kept = ()
    for at, pair in enumerate(pieces):
        kept = project_piece(pair, mix_weight, kept, at)
    normed_all, parts = kept
    grad_pieces = gather_pieces(*live_rows(cotangent, live, pieces[3]))

    gated, mixing, states = mix_forward(slots, fresh, rates, parts)
    far_top, far_low, near_top, near_low = partial_sums(gated, out_weight[None], (3, 1), False)
    side_low, side_top, own_top, own_low = partial_sums(
        gated, out_weight[None], (2, 0), False, after=grad_pieces[1] + grad_pieces[2]
    )
    branch = scatter_pieces(
        (own_top, own_low), (near_top, near_low), (side_low, side_top), (far_top, far_low)
    )
    middle = [x + m * b for x, m, b in zip(inputs, lives, branch)]

    pieces = gather_pieces(*(row_norm(rows).astype(low) for rows in middle))
    kept, back_sums, two_sums = (), [], []
    for at, (pair, grad_pair) in enumerate(zip(pieces, grad_pieces)):
        *kept, back_top, back_low, two_top, two_low = unit_piece(
            pair, grad_pair, ffn_in_weight, ffn_out_weight, kept, at
        )
        back_sums += [back_top, back_low]
        two_sums += [two_top, two_low]
    normed_two_all, grad_two_all, act, grad_parts = kept

    middle = jnp.concatenate(middle)
    out_low, in_low, grad_branch_all, grad_middle, grad_gated = unit_grads(
        act,
        grad_two_all,
        normed_two_all,
        grad_parts,
        back_sums,
        middle,
        cotangent,
        live,
        out_weight,
    )
    grad_projected, grad_ffn_in, grad_ffn_out = mix_backward(
        slots,
        fresh,
        rates,
        parts,
        mixing,
        states,
        grad_gated,
        in_low.reshape(width, 2 * units),
        out_low.reshape(units, width),
    )
    out_low, mix_low, own_top, own_low, *terms = mix_grads(
        gated, grad_branch_all, normed_all, grad_projected, mix_weight, two_sums[2:]
    )
    grad_mix, grad_out, layer_out, input_grad = finish_rows(
        mix_low.reshape(mix_weight.shape),
        out_low.reshape(out_weight.shape),
        hidden,
        middle,
        grad_middle,
        live,
        (own_top, terms[0], terms[2], own_low, terms[1], terms[3]),
        (two_sums[0], terms[4], terms[6], two_sums[1], terms[5], terms[7]),
    )
    return (layer_out, input_grad, grad_mix, grad_out, grad_ffn_in, grad_ffn_out)


def solution(mesh):
    square = mesh.shape["wide"] == 8 and mesh.shape["narrow"] == 4
    per_device = square_device if square else general_device
    in_specs = (
        P(("wide", "narrow"), None),
        P(None, None, "narrow"),
        P("narrow", None),
        P(None, None, "narrow"),
        P("narrow", None),
        P("wide"),
        P("wide"),
        P(("wide", "narrow"), None),
    )
    out_specs = (
        P(("wide", "narrow"), None),
        P(("wide", "narrow"), None),
        P(None, None, "narrow"),
        P("narrow", None),
        P(None, None, "narrow"),
        P("narrow", None),
    )
    return jax.shard_map(
        per_device, mesh=mesh, in_specs=in_specs, out_specs=out_specs, check_vma=False
    )
```

```python
import functools
import math

import jax
import jax.numpy as jnp
from jax import lax
from jax.experimental import pallas as pl
from jax.experimental.pallas import tpu as pltpu
from jax.sharding import PartitionSpec as P

HEADS = 16
HS = 128
BLK = 256
NBLK = 8


epsilon = 1e-06
head_floor = 1.0
highest = lax.Precision.HIGHEST


def row_norm(values):
    return values * lax.rsqrt(jnp.mean(values * values, axis=-1, keepdims=True) + epsilon)


def head_norm(values):
    return values * lax.rsqrt(jnp.mean(values * values, axis=-1, keepdims=True) + head_floor)


def silu_slope(values):
    sigmoid_part = jax.nn.sigmoid(values)
    return sigmoid_part * (1.0 + values * (1.0 - sigmoid_part))


def decay_tables(decay_rates):
    positions = jnp.arange(BLK, dtype=jnp.float32)
    distance = positions[:, None] - positions[None, :]
    causal = distance >= 0
    clipped = jnp.where(causal, distance, 0.0)
    within = jnp.where(causal[None], jnp.exp(-decay_rates[:, None, None] * clipped[None]), 0.0)
    entry_decay = jnp.exp(-(positions[:, None] + 1.0) * decay_rates[None, :])
    exit_decay = jnp.exp(-(BLK - 1.0 - positions[:, None]) * decay_rates[None, :])
    block_decay = jnp.exp(-BLK * decay_rates)
    return (within, entry_decay, exit_decay, block_decay)


def group_masks(lengths, owners):
    seq_slot = owners - owners[0]
    first_count = jnp.sum((seq_slot == 0).astype(jnp.int32))
    block_ids = jnp.arange(NBLK, dtype=jnp.int32)
    start_block = jnp.where(seq_slot == 0, jnp.int32(0), first_count)
    seq_limit = jnp.where(seq_slot == 0, lengths[0], lengths[1])
    offsets = (block_ids - start_block)[:, None] * BLK + jnp.arange(BLK, dtype=jnp.int32)[None, :]
    valid_rows = (offsets < seq_limit[:, None]).reshape(-1)
    fresh_block = block_ids == start_block
    return (valid_rows, fresh_block)


def forward_block(tables, kv_state, block_in):
    within, entry_decay, exit_decay, block_decay = tables
    queries, keys_in, values, fresh_block = block_in
    kv_state = jnp.where(fresh_block, 0.0, kv_state)
    scores = jnp.einsum("ihs,jhs->hij", queries, keys_in, preferred_element_type=jnp.float32)
    weights = (scores * within).astype(jnp.bfloat16)
    inner_part = jnp.einsum("hij,jhs->ihs", weights, values, preferred_element_type=jnp.float32)
    carried = jnp.einsum(
        "ihs,hst->iht",
        queries.astype(jnp.float32) * entry_decay[:, :, None],
        kv_state,
        precision=highest,
    )
    update = jnp.einsum(
        "ihs,iht->hst",
        keys_in.astype(jnp.float32) * exit_decay[:, :, None],
        values.astype(jnp.float32),
        precision=highest,
    )
    return (block_decay[:, None, None] * kv_state + update, (inner_part + carried, kv_state))


def backward_block(tables, later_grad, block_in):
    within, entry_decay, exit_decay, block_decay = tables
    queries, keys_in, values, grad_mix, kv_state, fresh_block = block_in
    scores = jnp.einsum("ihs,jhs->hij", queries, keys_in, preferred_element_type=jnp.float32)
    weights = (scores * within).astype(jnp.bfloat16)
    grad_values = jnp.einsum("hij,ihs->jhs", weights, grad_mix, preferred_element_type=jnp.float32)
    grad_weights = jnp.einsum("ihs,jhs->hij", grad_mix, values, preferred_element_type=jnp.float32)
    grad_scores = (grad_weights * within).astype(jnp.bfloat16)
    grad_queries = jnp.einsum(
        "hij,jhs->ihs", grad_scores, keys_in, preferred_element_type=jnp.float32
    )
    grad_keys = jnp.einsum("hij,ihs->jhs", grad_scores, queries, preferred_element_type=jnp.float32)
    grad_float = grad_mix.astype(jnp.float32)
    values_float = values.astype(jnp.float32)
    queries_float = queries.astype(jnp.float32)
    keys_float = keys_in.astype(jnp.float32)
    grad_queries = grad_queries + entry_decay[:, :, None] * jnp.einsum(
        "iht,hst->ihs", grad_float, kv_state, precision=highest
    )
    grad_keys = grad_keys + exit_decay[:, :, None] * jnp.einsum(
        "iht,hst->ihs", values_float, later_grad, precision=highest
    )
    grad_values = grad_values + jnp.einsum(
        "ihs,hst->iht", keys_float * exit_decay[:, :, None], later_grad, precision=highest
    )
    grad_state = jnp.einsum(
        "ihs,iht->hst", queries_float * entry_decay[:, :, None], grad_float, precision=highest
    )
    grad_state = grad_state + block_decay[:, None, None] * later_grad
    grad_state = jnp.where(fresh_block, 0.0, grad_state)
    return (grad_state, (grad_queries, grad_keys, grad_values))


def general_device(
    hidden, mix_weight, out_weight, ffn_in_weight, ffn_out_weight, seq_lengths, block_seq, cotangent
):
    local_rows = hidden.shape[0]
    group_rows = NBLK * BLK
    head_width = mix_weight.shape[2]
    head_count = head_width // HS
    narrow_index = lax.axis_index("narrow")
    valid_all, fresh_block = group_masks(seq_lengths, block_seq)
    valid_rows = lax.dynamic_slice_in_dim(
        valid_all.astype(jnp.float32), narrow_index * local_rows, local_rows
    )[:, None]
    head_ids = narrow_index * head_count + jnp.arange(head_count, dtype=jnp.int32)
    decay_rates = 2.0 ** (-8.0 * (head_ids.astype(jnp.float32) + 1.0) / HEADS)
    tables = decay_tables(decay_rates)

    def split_blocks(flat_rows):
        return flat_rows.reshape(NBLK, BLK, head_count, HS)

    inputs = hidden.astype(jnp.float32)
    normed_low = row_norm(inputs).astype(jnp.bfloat16)
    gathered = lax.all_gather(normed_low, "narrow", axis=0, tiled=True)
    projected = jnp.einsum("rd,cde->cre", gathered, mix_weight, preferred_element_type=jnp.float32)
    queries = jax.nn.silu(projected[0]).astype(jnp.bfloat16)
    keys_in = jax.nn.silu(projected[1]).astype(jnp.bfloat16)
    values = projected[2].astype(jnp.bfloat16)
    gate_part = projected[3]
    zero_state = jnp.zeros((head_count, HS, HS), jnp.float32)
    final_state, (mixing, kept_states) = lax.scan(
        lambda state_in, block_in: forward_block(tables, state_in, block_in),
        zero_state,
        (split_blocks(queries), split_blocks(keys_in), split_blocks(values), fresh_block),
    )
    mixing = mixing.reshape(group_rows, head_count, HS)
    headed = head_norm(mixing).reshape(group_rows, head_width)
    gated_low = (headed * gate_part).astype(jnp.bfloat16)
    branch = lax.psum_scatter(
        jnp.dot(gated_low, out_weight, preferred_element_type=jnp.float32).astype(jnp.bfloat16),
        "narrow",
        scatter_dimension=0,
        tiled=True,
    ).astype(jnp.float32)
    middle = inputs + valid_rows * branch
    normed_two_low = row_norm(middle).astype(jnp.bfloat16)
    gathered_two = lax.all_gather(normed_two_low, "narrow", axis=0, tiled=True)
    both_parts = jnp.einsum(
        "rd,cdf->crf", gathered_two, ffn_in_weight, preferred_element_type=jnp.float32
    )
    hidden_low = (both_parts[0] * both_parts[1]).astype(jnp.bfloat16)
    branch_two = lax.psum_scatter(
        jnp.dot(hidden_low, ffn_out_weight, preferred_element_type=jnp.float32).astype(
            jnp.bfloat16
        ),
        "narrow",
        scatter_dimension=0,
        tiled=True,
    ).astype(jnp.float32)
    layer_out = (middle + valid_rows * branch_two).astype(jnp.bfloat16)
    grad_rows = cotangent.astype(jnp.float32)
    ffn_grad_all = lax.all_gather(
        (valid_rows * grad_rows).astype(jnp.bfloat16), "narrow", axis=0, tiled=True
    )
    grad_ffn_out = jnp.einsum(
        "rf,rd->fd", hidden_low, ffn_grad_all, preferred_element_type=jnp.float32
    )
    grad_hidden = jnp.einsum(
        "rd,fd->rf", ffn_grad_all, ffn_out_weight, preferred_element_type=jnp.float32
    )
    grad_parts = jnp.stack([grad_hidden * both_parts[1], grad_hidden * both_parts[0]]).astype(
        jnp.bfloat16
    )
    grad_ffn_in = jnp.einsum(
        "rd,crf->cdf", gathered_two, grad_parts, preferred_element_type=jnp.float32
    )
    grad_slice = grad_parts
    grad_normed_two = lax.psum_scatter(
        jnp.einsum(
            "crf,cdf->rd", grad_slice, ffn_in_weight, preferred_element_type=jnp.float32
        ).astype(jnp.bfloat16),
        "narrow",
        scatter_dimension=0,
        tiled=True,
    ).astype(jnp.float32)
    norm_value, norm_pull = jax.vjp(row_norm, middle)
    grad_middle = grad_rows + norm_pull(grad_normed_two)[0]
    attn_grad_all = lax.all_gather(
        (valid_rows * grad_middle).astype(jnp.bfloat16), "narrow", axis=0, tiled=True
    )
    grad_out_weight = jnp.einsum(
        "re,rd->ed", gated_low, attn_grad_all, preferred_element_type=jnp.float32
    )
    grad_gated = jnp.einsum(
        "rd,ed->re", attn_grad_all, out_weight, preferred_element_type=jnp.float32
    )
    grad_gated = lax.optimization_barrier(grad_gated.astype(jnp.bfloat16)).astype(jnp.float32)
    grad_gate = grad_gated * headed
    grad_headed = (grad_gated * gate_part).reshape(group_rows, head_count, HS)
    head_value, head_pull = jax.vjp(head_norm, mixing)
    grad_mixing = head_pull(grad_headed)[0].astype(jnp.bfloat16)
    first_grad, (grad_queries, grad_keys, grad_values) = lax.scan(
        lambda later_grad, block_in: backward_block(tables, later_grad, block_in),
        zero_state,
        (
            split_blocks(queries),
            split_blocks(keys_in),
            split_blocks(values),
            split_blocks(grad_mixing),
            kept_states,
            fresh_block,
        ),
        reverse=True,
    )
    grad_projected = jnp.stack(
        [
            grad_queries.reshape(group_rows, head_width) * silu_slope(projected[0]),
            grad_keys.reshape(group_rows, head_width) * silu_slope(projected[1]),
            grad_values.reshape(group_rows, head_width),
            grad_gate,
        ]
    ).astype(jnp.bfloat16)
    grad_mix = jnp.einsum(
        "rd,cre->cde", gathered, grad_projected, preferred_element_type=jnp.float32
    )
    grad_slice = grad_projected
    grad_normed = lax.psum_scatter(
        jnp.einsum(
            "cre,cde->rd", grad_slice, mix_weight, preferred_element_type=jnp.float32
        ).astype(jnp.bfloat16),
        "narrow",
        scatter_dimension=0,
        tiled=True,
    ).astype(jnp.float32)
    first_value, first_pull = jax.vjp(row_norm, inputs)
    input_grad = (grad_middle + first_pull(grad_normed)[0]).astype(jnp.bfloat16)
    grad_mix, grad_out_weight, grad_ffn_in, grad_ffn_out = (
        lax.psum(grad_mix.astype(jnp.bfloat16), "wide").astype(jnp.float32),
        lax.psum(grad_out_weight.astype(jnp.bfloat16), "wide").astype(jnp.float32),
        lax.psum(grad_ffn_in.astype(jnp.bfloat16), "wide").astype(jnp.float32),
        lax.psum(grad_ffn_out.astype(jnp.bfloat16), "wide").astype(jnp.float32),
    )
    return (layer_out, input_grad, grad_mix, grad_out_weight, grad_ffn_in, grad_ffn_out)


HALF = BLK
PIECE = 2 * BLK
VMEM = 60 * 1024 * 1024


def add_low(*terms):
    return sum(term.astype(jnp.float32) for term in terms).astype(jnp.bfloat16)


def add_rows(*terms):
    return sum(term.astype(jnp.float32) for term in terms)


def slot_tables(narrow_index, fresh_block):
    block_ids = jnp.arange(NBLK, dtype=jnp.int32)
    partner = (block_ids // 2) ^ narrow_index
    even = jnp.array([0, 2, 5, 6], jnp.int32)[partner]
    odd = jnp.array([1, 4, 3, 7], jnp.int32)[partner]
    return jnp.where(block_ids % 2 == 0, even, odd), fresh_block.astype(jnp.int32)


def across(left, right):
    return lax.dot_general(left, right, (((1,), (1,)), ((), ())), preferred_element_type=jnp.float32)


def down(left, right):
    return lax.dot_general(left, right, (((0,), (0,)), ((), ())), preferred_element_type=jnp.float32)


def straight(left, right):
    return jnp.dot(left, right, preferred_element_type=jnp.float32)


def any_specs(count):
    return [pl.BlockSpec(memory_space=pl.ANY)] * count


def cost(flops, bytes_accessed):
    return pl.CostEstimate(flops=int(flops), bytes_accessed=int(bytes_accessed), transcendentals=0)


MESH = pl.DeviceIdType.MESH
SLOTS = 13
STAGES = 12
SUB = 128
TILE = 256


def begin(copies):
    for copy in copies:
        copy.start()


def finish(copies):
    for copy in copies:
        copy.wait()


def neighbours():
    wide, narrow = lax.axis_index("wide"), lax.axis_index("narrow")
    z, core = wide // 2, wide % 2
    mate = (wide + 1 - 2 * core, narrow)
    near_x = (wide, narrow + 1 - 2 * (narrow % 2))
    near_y = (wide, (narrow + 2) % 4)
    return wide, narrow, z, core, mate, near_x, near_y


def line_scratch():
    low = jnp.bfloat16
    pair = pltpu.VMEM((SLOTS, 2, SUB, TILE), low)
    return [
        pltpu.VMEM((SLOTS, 4, SUB, TILE), low),
        pair,
        pair,
        pair,
        pltpu.VMEM((SLOTS, SUB, TILE), low),
        pair,
        pair,
        pltpu.SemaphoreType.DMA((14, SLOTS)),
        pltpu.SemaphoreType.DMA((4, SLOTS)),
    ]


def enter(neighbour_places):
    wide, narrow, z, core, mate, near_x, near_y = neighbour_places
    barrier = pltpu.get_barrier_semaphore()

    def greet(place):
        pl.semaphore_signal(barrier, inc=1, device_id=place, device_id_type=MESH)

    for place in (mate, near_x, near_y):
        greet(place)
    middle = (z == 1) | (z == 2)

    @pl.when(middle)
    def _():
        greet((2 * (3 - z) + core, narrow))
        greet((6 * (z - 1) + core, narrow))
        pl.semaphore_wait(barrier, 5)

    @pl.when(jnp.logical_not(middle))
    def _():
        greet((2 * (1 + z // 3) + core, narrow))
        pl.semaphore_wait(barrier, 4)


def line_sum(scratch, places, count, product, targets):
    own, met, both, ended, crossed, full, other, sems, out_sems = scratch
    wide, narrow, z, core, mate, _, _ = places
    region = z // 2
    middle = (z == 1) | (z == 2)
    end = jnp.logical_not(middle)
    inward = (2 * (1 + z // 3) + core, narrow)
    across_line = (2 * (3 - z) + core, narrow)
    outward = (6 * (z - 1) + core, narrow)

    def remote(src, dst, kind, slot, place):
        return pltpu.make_async_remote_copy(
            src_ref=src,
            dst_ref=dst,
            send_sem=sems.at[2 * kind, slot],
            recv_sem=sems.at[2 * kind + 1, slot],
            device_id=place,
            device_id_type=MESH,
        )

    def core_one(s):
        return remote(own.at[s, pl.ds(2 * (1 - core), 2)], met.at[s], 0, s, mate)

    def line_one(s):
        return remote(both.at[s], ended.at[s], 1, s, inward)

    def cross_one(s):
        return remote(both.at[s, 1 - region], crossed.at[s], 2, s, across_line)

    def cross_two(s):
        return remote(full.at[s, region], full.at[s, region], 3, s, across_line)

    def out_one(s):
        return remote(full.at[s, region], full.at[s, region], 4, s, outward)

    def out_two(s):
        return remote(full.at[s, 1 - region], full.at[s, 1 - region], 5, s, outward)

    def core_two(s):
        return remote(full.at[s], other.at[s], 6, s, mate)

    def add(left, right):
        return (left.astype(jnp.float32) + right.astype(jnp.float32)).astype(jnp.bfloat16)

    def deliveries(k, s):
        for t in range(2):
            for which, (src, part) in enumerate(
                ((full.at[s, t], 2 * core + t), (other.at[s, t], 2 * (1 - core) + t))
            ):
                for condition, ref in targets(k, part):
                    yield condition, pltpu.make_async_copy(src, ref, out_sems.at[2 * t + which, s])

    def start(k, s):
        product(k, own.at[s])
        core_one(s).start()

    def cores(k, s):
        core_one(s).wait_recv()
        both[s] = add(own[s, pl.ds(2 * core, 2)], met[s])
        pl.when(end)(lambda: line_one(s).start())

    def ends(k, s):
        @pl.when(middle)
        def _():
            line_one(s).wait_recv()
            both[s] = add(both[s], ended[s])
            cross_one(s).start()

    def centre(k, s):
        @pl.when(middle)
        def _():
            cross_one(s).wait_recv()
            full[s, region] = add(both[s, region], crossed[s])
            cross_two(s).start()
            out_one(s).start()

    def pass_on(k, s):
        @pl.when(middle)
        def _():
            cross_two(s).wait_recv()
            out_two(s).start()

    def back(k, s):
        @pl.when(end)
        def _():
            out_one(s).wait_recv()
            out_two(s).wait_recv()

        core_two(s).start()

    def deliver(k, s):
        core_two(s).wait_recv()
        for condition, copy in deliveries(k, s):
            pl.when(condition)(copy.start)

    def clear(k, s):
        core_one(s).wait_send()
        core_two(s).wait_send()

        @pl.when(end)
        def _():
            line_one(s).wait_send()

        @pl.when(middle)
        def _():
            for copy in (cross_one(s), cross_two(s), out_one(s), out_two(s)):
                copy.wait_send()

        for condition, copy in deliveries(k, s):
            pl.when(condition)(copy.wait)

    stages = (
        (12, clear),
        (10, deliver),
        (9, back),
        (7, pass_on),
        (5, centre),
        (3, ends),
        (1, cores),
        (0, start),
    )

    def step(i, carry):
        for delay, work in stages:
            k = i - delay

            @pl.when((k >= 0) & (k < count))
            def _(work=work, k=k):
                work(k, lax.rem(k + SLOTS, SLOTS))

        return carry

    return step


def square_scratch():
    low = jnp.bfloat16
    block = pltpu.VMEM((2, BLK, HEADS * HS), low)
    return [block, block, pltpu.SemaphoreType.DMA((6, 2)), pltpu.SemaphoreType.DMA((2,))]


def square_sum(scratch, places, parts, landed):
    met, mid, sems, load_sems = scratch
    top_x, low_y, low_x, top_y, top_d, low_d = parts
    near_x, near_y = places[5:]

    def remote(src, dst, kind, place):
        return pltpu.make_async_remote_copy(
            src_ref=src,
            dst_ref=dst,
            send_sem=sems.at[kind, 0],
            recv_sem=sems.at[kind, 1],
            device_id=place,
            device_id_type=MESH,
        )

    first = [remote(top_d, met.at[0], 0, near_x), remote(low_d, met.at[1], 1, near_y)]
    direct = [remote(top_x, landed[0], 2, near_x), remote(low_y, landed[1], 3, near_y)]
    second = [remote(mid.at[0], landed[2], 4, near_y), remote(mid.at[1], landed[3], 5, near_x)]
    loads = []
    if top_y is not None:
        loads = [
            pltpu.make_async_copy(top_y, mid.at[0], load_sems.at[0]),
            pltpu.make_async_copy(low_x, mid.at[1], load_sems.at[1]),
        ]

    def open_sum():
        begin(first)
        begin(direct)
        begin(loads)

    def join_sum():
        finish(loads)
        for at in range(2):
            first[at].wait()

            def tile(i, carry, at=at):
                rows = pl.ds(pl.multiple_of(i * 64, 64), 64)
                mid[at, rows, :] = add_low(mid[at, rows, :], met[at, rows, :])
                return carry

            lax.fori_loop(0, BLK // 64, tile, 0)
            second[at].start()

    def close_sum():
        finish(direct)
        finish(second)

    return open_sum, join_sum, close_sum, first, direct


def unit_grads(
    act, grad_two_all, normed_two_all, grad_parts, back_sums, middle, cotangent, live, out_weight
):
    rows, units = act.shape
    width = grad_two_all.shape[1]
    local_rows = middle.shape[0]
    low = jnp.bfloat16
    out_blocks, in_blocks = units // SUB, width // SUB
    halves = width // 1024
    out_chunks = out_blocks * halves
    columns = grad_parts.shape[1] // TILE
    in_chunks = (width // PIECE) * columns
    count = out_chunks + in_chunks

    def body(*refs):
        act_in, two_in, normed_in, parts_in = refs[:4]
        partial = [refs[4].at[pl.ds(at * BLK, BLK)] for at in range(8)]
        middle_in, cot_in, weight_in, live_ref = refs[5:9]
        out_grad, in_grad, branch_out, middle_out, gated_out = refs[9:14]
        act_ref, shared, parts_ref, landed, own_ref, cot_ref, mid_ref, grad_ref, branch = refs[14:23]
        gated_ref, load_sems, stage_sems, gather_sems, back_sems = refs[23:28]
        line = refs[28:37]
        square = refs[37:41]
        places = neighbours()
        near_x, near_y = places[5:]
        enter(places)
        load_act = pltpu.make_async_copy(act_in, act_ref, load_sems.at[0])
        load_two = pltpu.make_async_copy(two_in, shared, load_sems.at[1])
        load_parts = pltpu.make_async_copy(parts_in, parts_ref, load_sems.at[2])
        load_normed = pltpu.make_async_copy(normed_in, shared, load_sems.at[3])
        open_sum, join_sum, close_sum, _, _ = square_sum(
            square, places, partial[2:], [landed.at[at] for at in range(4)]
        )
        load_two.start()
        load_act.start()
        open_sum()
        load_parts.start()
        load_two.wait()
        load_act.wait()

        def product(k, own):
            @pl.when(k < out_chunks)
            def _():
                rows_at = pl.ds(pl.multiple_of((k // halves) * SUB, SUB), SUB)
                wide_at = pl.ds(pl.multiple_of((k % halves) * 1024, 1024), 1024)
                result = down(act_ref[:, rows_at], shared[:, wide_at]).astype(low)
                for part in range(4):
                    own[part] = result[:, part * TILE : (part + 1) * TILE]

            @pl.when(k == out_chunks)
            def _():
                load_normed.start()
                load_parts.wait()
                load_normed.wait()

            @pl.when(k >= out_chunks)
            def _():
                at = k - out_chunks
                rows_at = pl.ds(pl.multiple_of((at // columns) * PIECE, PIECE), PIECE)
                wide_at = pl.ds(pl.multiple_of((at % columns) * TILE, TILE), TILE)
                result = down(shared[:, rows_at], parts_ref[:, wide_at]).astype(low)
                for part in range(4):
                    own[part] = result[part * SUB : (part + 1) * SUB]

        def targets(k, part):
            wide_at = pl.ds(pl.multiple_of((k % halves) * 1024 + part * TILE, TILE), TILE)
            at = jnp.maximum(k - out_chunks, 0)
            in_at = pl.ds(pl.multiple_of((at % columns) * TILE, TILE), TILE)
            first = jnp.minimum(k, out_chunks - 1) // halves
            return [
                (k < out_chunks, out_grad.at[first, :, wide_at]),
                (k >= out_chunks, in_grad.at[(at // columns) * 4 + part, :, in_at]),
            ]

        step = line_sum(line, places, count, product, targets)

        def block(at):
            return pl.ds(at * BLK, BLK)

        def spread(src, slot, kind, place):
            return pltpu.make_async_remote_copy(
                src_ref=src,
                dst_ref=branch_out.at[block(slot)],
                send_sem=gather_sems.at[kind, 0],
                recv_sem=gather_sems.at[kind, 1],
                device_id=place,
                device_id_type=MESH,
            )

        def stage(half):
            return [
                pltpu.make_async_copy(partial[half], own_ref, stage_sems.at[0]),
                pltpu.make_async_copy(cot_in.at[block(half)], cot_ref, stage_sems.at[1]),
                pltpu.make_async_copy(middle_in.at[block(half)], mid_ref, stage_sems.at[2]),
            ]

        keep = [
            pltpu.make_async_copy(branch.at[at], branch_out.at[block(at)], stage_sems.at[3 + at])
            for at in range(2)
        ]

        def rows_back(half):
            def tile(i, carry):
                at = pl.ds(pl.multiple_of(i * 32, 32), 32)
                grad = own_ref[at, :].astype(jnp.float32)
                grad += landed[half, at, :].astype(jnp.float32)
                grad += landed[2 + half, at, :].astype(jnp.float32)
                result = cot_ref[at, :].astype(jnp.float32) + norm_back(mid_ref[at, :], grad)
                grad_ref[at, :] = result
                live_at = pl.ds(pl.multiple_of(half * BLK + i * 32, 32), 32)
                branch[half, at, :] = (live_ref[live_at, :1] * result).astype(low)
                return carry

            lax.fori_loop(0, BLK // 32, tile, 0)
            copy = pltpu.make_async_copy(grad_ref, middle_out.at[block(half)], stage_sems.at[5])
            copy.start()
            return copy

        sends = [
            spread(branch.at[0], 2, 0, near_x),
            spread(branch.at[1], 3, 1, near_y),
            spread(branch.at[1], 4, 2, near_x),
            spread(branch.at[0], 5, 3, near_y),
        ]
        later = [
            spread(branch_out.at[block(3)], 7, 4, near_x),
            spread(branch_out.at[block(2)], 6, 5, near_y),
        ]

        lax.fori_loop(0, 9, step, 0)
        join_sum()
        begin(stage(0))
        lax.fori_loop(9, 25, step, 0)
        close_sum()
        finish(stage(0))
        written = rows_back(0)
        sends[0].start()
        begin(stage(1))
        finish(stage(1))
        written.wait()
        written = rows_back(1)
        begin([sends[1], sends[2], sends[3]])
        begin(keep)
        lax.fori_loop(25, 33, step, 0)
        sends[0].wait_recv()
        sends[1].wait_recv()
        begin(later)
        lax.fori_loop(33, 50, step, 0)
        written.wait()
        finish(keep)
        for copy in sends[:2]:
            copy.wait_send()
        finish(sends[2:])
        finish(later)

        weight_loads = [
            pltpu.make_async_copy(weight_in.at[block(at)], landed.at[at], back_sems.at[at])
            for at in range(weight_in.shape[0] // BLK)
        ]
        stages = (own_ref, cot_ref)

        def row_load(at):
            return pltpu.make_async_copy(
                branch_out.at[block(at)], stages[at % 2], back_sems.at[2 + at % 2]
            )

        def gated_store(at):
            return pltpu.make_async_copy(
                gated_ref.at[at % 2], gated_out.at[block(at)], back_sems.at[4 + at % 2]
            )

        begin(weight_loads)
        row_load(0).start()
        at_step = 50
        for at in range(rows // BLK):
            lax.fori_loop(at_step, at_step + 2, step, 0)
            at_step += 2
            if at == 0:
                finish(weight_loads)
            if at + 1 < rows // BLK:
                row_load(at + 1).start()
            row_load(at).wait()
            if at >= 2:
                gated_store(at - 2).wait()
            for part in range(len(weight_loads)):
                result = across(stages[at % 2][...], landed[part])
                gated_ref[at % 2, :, part * BLK : (part + 1) * BLK] = result.astype(low)
            gated_store(at).start()
        lax.fori_loop(at_step, count + STAGES, step, 0)
        gated_store(rows // BLK - 2).wait()
        gated_store(rows // BLK - 1).wait()

    return pl.pallas_call(
        body,
        in_specs=any_specs(8) + [pl.BlockSpec(memory_space=pltpu.VMEM)],
        out_specs=any_specs(5),
        out_shape=[
            jax.ShapeDtypeStruct((out_blocks, SUB, width), low),
            jax.ShapeDtypeStruct((in_blocks, SUB, grad_parts.shape[1]), low),
            jax.ShapeDtypeStruct((rows, width), low),
            jax.ShapeDtypeStruct((local_rows, width), jnp.float32),
            jax.ShapeDtypeStruct((rows, out_weight.shape[0]), low),
        ],
        scratch_shapes=[
            pltpu.VMEM(act.shape, low),
            pltpu.VMEM((rows, width), low),
            pltpu.VMEM(grad_parts.shape, low),
            pltpu.VMEM((4, BLK, width), low),
            pltpu.VMEM((BLK, width), low),
            pltpu.VMEM((BLK, width), low),
            pltpu.VMEM((BLK, width), jnp.float32),
            pltpu.VMEM((BLK, width), jnp.float32),
            pltpu.VMEM((2, BLK, width), low),
            pltpu.VMEM((2, BLK, out_weight.shape[0]), low),
            pltpu.SemaphoreType.DMA((4,)),
            pltpu.SemaphoreType.DMA((6,)),
            pltpu.SemaphoreType.DMA((6, 2)),
            pltpu.SemaphoreType.DMA((6,)),
        ]
        + line_scratch()
        + square_scratch(),
        compiler_params=pltpu.CompilerParams(
            vmem_limit_bytes=VMEM, collective_id=1, has_side_effects=True
        ),
        cost_estimate=cost(2 * 3 * rows * width * units, 60e6),
        name="unit_grads",
    )(
        act,
        grad_two_all,
        normed_two_all,
        grad_parts,
        back_sums,
        middle,
        cotangent,
        out_weight,
        live,
    )


def mix_grads(gated, grad_branch_all, normed_all, grad_projected, mix_weight, two_sums):
    _, rows, columns = gated.shape
    width = normed_all.shape[1]
    parts = grad_projected.shape[0]
    low = jnp.bfloat16
    out_chunks = width // TILE
    per_row = columns // TILE
    per_part = (width // PIECE) * per_row
    count = out_chunks + parts * per_part
    wide_tile = 1024

    def body(*refs):
        gated_in, branch_in, normed_in, grads_in, weight_in = refs[:5]
        two_partial = [refs[5].at[pl.ds(at * BLK, BLK)] for at in range(2, 8)]
        out_grad, mix_grad = refs[6:8]
        own_outs = refs[8:10]
        landed, two_landed = refs[10:14], refs[14:18]
        gated_ref, branch_ref, normed_ref, grads_ref, weight_ref, far, near, own_ref = refs[18:26]
        load_sems, branch_sems, grad_sems, weight_sems, own_sems = refs[26:31]
        line = refs[31:40]
        square, two_square = refs[40:44], refs[44:48]
        mid = square[1]
        places = neighbours()
        enter(places)

        def part_columns(c):
            return pl.ds(c * columns, columns)

        load_gated = pltpu.make_async_copy(gated_in.at[0], gated_ref, load_sems.at[0])
        load_normed = pltpu.make_async_copy(normed_in, normed_ref, load_sems.at[1])

        def load_branch(k):
            at = pl.ds(pl.multiple_of(k * TILE, TILE), TILE)
            slot = k % 2
            return pltpu.make_async_copy(branch_in.at[:, at], branch_ref.at[slot], branch_sems.at[slot])

        grad_loads = [
            pltpu.make_async_copy(grads_in.at[c], grads_ref.at[:, part_columns(c)], grad_sems.at[c])
            for c in range(parts)
        ]
        weight_loads = [
            pltpu.make_async_copy(weight_in.at[c], weight_ref.at[:, part_columns(c)], weight_sems.at[c])
            for c in range(parts)
        ]
        load_gated.start()
        load_branch(0).start()
        begin(grad_loads)
        begin(weight_loads)
        load_normed.start()
        _, join_sum, close_sum, first, direct = square_sum(
            square,
            places,
            (near.at[0], near.at[1], None, None, far.at[0], far.at[1]),
            landed,
        )
        open_two, join_two, close_two, _, _ = square_sum(two_square, places, two_partial, two_landed)
        load_gated.wait()

        def product(k, own):
            @pl.when(k < out_chunks)
            def _():
                load_branch(k).wait()
                pl.when(k + 1 < out_chunks)(lambda: load_branch(k + 1).start())
                result = down(gated_ref[...], branch_ref[k % 2]).astype(low)
                for part in range(4):
                    own[part] = result[part * SUB : (part + 1) * SUB]

            @pl.when(k >= out_chunks)
            def _():
                at = k - out_chunks
                rows_at = pl.ds(pl.multiple_of(((at // per_row) % 4) * PIECE, PIECE), PIECE)
                start = (at // per_part) * columns + (at % per_row) * TILE
                wide_at = pl.ds(pl.multiple_of(start, TILE), TILE)
                result = down(normed_ref[:, rows_at], grads_ref[:, wide_at]).astype(low)
                for part in range(4):
                    own[part] = result[part * SUB : (part + 1) * SUB]

        def targets(k, part):
            first_at = pl.ds(pl.multiple_of(jnp.minimum(k, out_chunks - 1) * TILE, TILE), TILE)
            at = jnp.maximum(k - out_chunks, 0)
            wide_at = pl.ds(pl.multiple_of((at % per_row) * TILE, TILE), TILE)
            return [
                (k < out_chunks, out_grad.at[part, :, first_at]),
                (k >= out_chunks, mix_grad.at[(at // per_row) * 4 + part, :, wide_at]),
            ]

        step = line_sum(line, places, count, product, targets)

        def partial(piece, tile, top, low_part):
            at = slice(tile * wide_tile, (tile + 1) * wide_tile)
            acts = grads_ref[piece * PIECE : (piece + 1) * PIECE, :]
            total = across(acts, weight_ref[at, :])
            top[:, at] = total[:HALF].astype(low)
            low_part[:, at] = total[HALF:].astype(low)

        own_stores = [
            pltpu.make_async_copy(own_ref.at[at], own_outs[at], own_sems.at[at]) for at in range(2)
        ]
        places_of = (
            (3, far.at[0], far.at[1], first),
            (1, near.at[0], near.at[1], direct),
            (2, mid.at[1], mid.at[0], []),
            (0, own_ref.at[0], own_ref.at[1], own_stores),
        )
        lax.fori_loop(0, 2, step, 0)
        finish(grad_loads)
        finish(weight_loads)
        at_step = 2
        for piece, top, low_part, copies in places_of:
            for tile in range(width // wide_tile):
                partial(piece, tile, top, low_part)
                if tile == width // wide_tile - 1:
                    begin(copies)
                lax.fori_loop(at_step, at_step + 1, step, 0)
                at_step += 1
                if at_step == 8:
                    load_normed.wait()
        lax.fori_loop(at_step, 12, step, 0)
        join_sum()
        open_two()
        lax.fori_loop(12, 36, step, 0)
        join_two()
        lax.fori_loop(36, count + STAGES, step, 0)
        close_sum()
        close_two()
        finish(own_stores)

    return pl.pallas_call(
        body,
        in_specs=any_specs(6),
        out_specs=any_specs(12),
        out_shape=[
            jax.ShapeDtypeStruct((columns // SUB, SUB, width), low),
            jax.ShapeDtypeStruct((parts * width // SUB, SUB, columns), low),
        ]
        + [jax.ShapeDtypeStruct((BLK, width), low)] * 10,
        scratch_shapes=[
            pltpu.VMEM((rows, columns), low),
            pltpu.VMEM((2, rows, TILE), low),
            pltpu.VMEM((rows, width), low),
            pltpu.VMEM((rows, parts * columns), low),
            pltpu.VMEM((width, parts * columns), low),
            pltpu.VMEM((2, BLK, width), low),
            pltpu.VMEM((2, BLK, width), low),
            pltpu.VMEM((2, BLK, width), low),
            pltpu.SemaphoreType.DMA((2,)),
            pltpu.SemaphoreType.DMA((2,)),
            pltpu.SemaphoreType.DMA((parts,)),
            pltpu.SemaphoreType.DMA((parts,)),
            pltpu.SemaphoreType.DMA((2,)),
        ]
        + line_scratch()
        + square_scratch()
        + square_scratch(),
        compiler_params=pltpu.CompilerParams(
            vmem_limit_bytes=VMEM, collective_id=2, has_side_effects=True
        ),
        cost_estimate=cost(2 * 9 * rows * width * columns, 60e6),
        name="mix_grads",
    )(gated, grad_branch_all, normed_all, grad_projected, mix_weight, two_sums)


def gated_unit(gated, whole_weight, hidden, live, grads_own, grads_first, ffn_in, ffn_out):
    _, width, units = ffn_in.shape
    local_rows = hidden.shape[0]
    group_rows = NBLK * BLK
    pieces = group_rows // PIECE
    deep = gated.shape[2]
    slices, quarters, slice_rows, _ = whole_weight.shape
    main = units // TILE * TILE
    tail = units - main
    low = jnp.bfloat16
    cuts = ((0, 2 * TILE), (2 * TILE, main - 2 * TILE))
    wide_tile = 1024
    first_half, second_half = pl.ds(0, HALF), pl.ds(HALF, HALF)

    def body(*refs):
        gated_in, weight_in, hidden_in = refs[:3]
        grad_in = refs[3:5]
        in_ref, out_ref, live_ref = refs[5:8]
        middle_out, rows_out, grads_out, act_out, parts_out, back_out, two_out = refs[8:15]
        gated_ref, hidden_ref, middle_ref = refs[15:18]
        rows, grads, sums, w_in, w_out, act, parts = refs[18:25]
        load_sems, slice_sems, weight_sems, done_sems, sum_sems, gated_sems, gather_sems = refs[25:]
        wide, narrow, _, _, _, near_x, near_y = neighbours()
        far = (wide, 3 - narrow)
        barrier = pltpu.get_barrier_semaphore()
        for place in (near_x, near_y, far):
            pl.semaphore_signal(barrier, inc=1, device_id=place, device_id_type=MESH)
        pl.semaphore_wait(barrier, 3)

        here = pl.ds(pl.multiple_of(narrow * deep, deep), deep)

        def send_gated(slot, to, kind, place):
            return pltpu.make_async_remote_copy(
                src_ref=gated_in.at[0, pl.ds(slot * BLK, BLK)],
                dst_ref=gated_ref.at[(first_half, second_half)[to], here],
                send_sem=gated_sems.at[kind, 0],
                recv_sem=gated_sems.at[kind, 1],
                device_id=place,
                device_id_type=MESH,
            )

        gated_sends = [
            send_gated(6, 0, 0, far),
            send_gated(7, 1, 1, far),
            send_gated(2, 0, 2, near_x),
            send_gated(3, 1, 3, near_y),
            send_gated(4, 1, 4, near_x),
            send_gated(5, 0, 5, near_y),
        ]
        keep_gated = pltpu.make_async_copy(
            gated_in.at[0, pl.ds(0, PIECE)], gated_ref.at[:, here], load_sems.at[0]
        )

        def load_slice(at):
            part, quarter = at // quarters, at % quarters
            to = pl.ds(pl.multiple_of(quarter * deep + part * slice_rows, slice_rows), slice_rows)
            return pltpu.make_async_copy(
                weight_in.at[part, quarter], w_in.at[to, pl.ds(0, width)], slice_sems.at[at]
            )

        def start_slice(at, carry):
            load_slice(at).start()
            return carry

        def wait_slice(at, carry):
            load_slice(at).wait()
            return carry

        load_hidden = pltpu.make_async_copy(hidden_in, hidden_ref, load_sems.at[1])
        load_grads = [
            pltpu.make_async_copy(src, grads.at[at], load_sems.at[2 + at])
            for at, src in enumerate(grad_in)
        ]
        weights = []
        for start, size, first, second in tuple((a, b, a, main + a) for a, b in cuts) + (
            (main, tail, 2 * main, 2 * main + tail),
        ):
            at = pl.ds(start, size)
            weights += [
                pltpu.make_async_copy(in_ref.at[0, :, at], w_in.at[:, pl.ds(first, size)], weight_sems.at[len(weights)]),
                pltpu.make_async_copy(in_ref.at[1, :, at], w_in.at[:, pl.ds(second, size)], weight_sems.at[len(weights) + 1]),
                pltpu.make_async_copy(out_ref.at[at, :], w_out.at[at, :], weight_sems.at[len(weights) + 2]),
            ]

        def remote(src, dst, sems, kind, place):
            return pltpu.make_async_remote_copy(
                src_ref=src,
                dst_ref=dst,
                send_sem=sems.at[kind, 0],
                recv_sem=sems.at[kind, 1],
                device_id=place,
                device_id_type=MESH,
            )

        def half(ref, piece, at):
            return ref.at[piece, (first_half, second_half)[at]]

        def gather(ref, kind):
            return (
                [
                    remote(half(ref, 0, 0), half(ref, 1, 0), gather_sems, kind, near_x),
                    remote(half(ref, 0, 1), half(ref, 1, 1), gather_sems, kind + 1, near_y),
                ],
                [
                    remote(half(ref, 0, 1), half(ref, 2, 0), gather_sems, kind + 2, near_x),
                    remote(half(ref, 0, 0), half(ref, 2, 1), gather_sems, kind + 3, near_y),
                ],
                [
                    remote(half(ref, 1, 1), half(ref, 3, 1), gather_sems, kind + 4, near_x),
                    remote(half(ref, 1, 0), half(ref, 3, 0), gather_sems, kind + 5, near_y),
                ],
            )

        row_sends = gather(rows, 0)
        grad_sends = gather(grads, 6)

        begin(gated_sends)
        begin([keep_gated])
        lax.fori_loop(0, slices * quarters, start_slice, 0)
        begin(load_grads)
        begin([load_hidden])
        finish(load_grads)
        begin(grad_sends[1])
        finish([keep_gated, load_hidden])
        lax.fori_loop(0, slices * quarters, wait_slice, 0)
        finish(gated_sends)
        for j in range(width // wide_tile):
            at = slice(j * wide_tile, (j + 1) * wide_tile)
            middle_ref[:, at] = straight(gated_ref[...], w_in[:, at])
        begin(weights)

        def second_norm(i, carry, at):
            here = pl.ds(pl.multiple_of(at * HALF + i * 32, 32), 32)
            middle = hidden_ref[here, :].astype(jnp.float32) + live_ref[here, :1] * middle_ref[here, :]
            middle_ref[here, :] = middle
            rows[0, here, :] = row_norm(middle).astype(low)
            return carry

        for at in range(2):
            lax.fori_loop(0, HALF // 32, functools.partial(second_norm, at=at), 0)
            row_sends[0][at].start()
        begin(row_sends[1])
        begin(grad_sends[2])
        store_middle = pltpu.make_async_copy(middle_ref, middle_out, done_sems.at[0])
        store_middle.start()

        def products(at, first, second, part_a, part_b, grad_act):
            act[:, at] = (part_a * part_b).astype(low)
            parts[:, first] = (grad_act * part_b).astype(low)
            parts[:, second] = (grad_act * part_a).astype(low)

        def sum_stores(piece, j):
            tile = pl.ds(j * wide_tile, wide_tile)
            return [
                pltpu.make_async_copy(
                    sums.at[at, :, tile],
                    (back_out, two_out)[at // 2].at[
                        pl.ds(pl.multiple_of(piece * PIECE + (at % 2) * HALF, HALF), HALF), tile
                    ],
                    sum_sems.at[j, at],
                )
                for at in range(4)
            ]

        def work(piece, carry):
            spot = pl.ds(pl.multiple_of(piece * PIECE, PIECE), PIECE)
            arrived, arrived_grads = rows.at[piece], grads.at[piece]

            @pl.when(piece == 1)
            def _():
                finish(row_sends[0])
                begin(row_sends[2])

            @pl.when(piece == 2)
            def _():
                finish(row_sends[1])
                finish(grad_sends[1])

            @pl.when(piece == 3)
            def _():
                finish(row_sends[2])
                finish(grad_sends[2])

            stores = [
                pltpu.make_async_copy(arrived, rows_out.at[spot, :], done_sems.at[1]),
                pltpu.make_async_copy(arrived_grads, grads_out.at[spot, :], done_sems.at[2]),
            ]
            begin(stores)
            for which, (start, size) in enumerate(cuts):
                at, second = slice(start, start + size), slice(main + start, main + start + size)

                @pl.when(piece == 0)
                def _(which=which):
                    finish(weights[3 * which : 3 * which + 3])

                part_a = straight(arrived[...], w_in[:, at])
                part_b = straight(arrived[...], w_in[:, second])
                grad_act = across(arrived_grads[...], w_out[at, :])
                products(at, at, second, part_a, part_b, grad_act)

            @pl.when(piece == 0)
            def _():
                finish(weights[6:])

            if tail:
                both = straight(arrived[...], w_in[:, 2 * main :])
                grad_act = across(arrived_grads[...], w_out[main:, :])
                products(
                    slice(main, units),
                    slice(2 * main, 2 * main + tail),
                    slice(2 * main + tail, 2 * units),
                    both[:, :tail],
                    both[:, tail:],
                    grad_act,
                )
            stores += [
                pltpu.make_async_copy(act, act_out.at[spot, :], done_sems.at[3]),
                pltpu.make_async_copy(parts, parts_out.at[spot, :], done_sems.at[4]),
            ]
            begin(stores[2:])
            for j in range(width // wide_tile):
                at = slice(j * wide_tile, (j + 1) * wide_tile)

                @pl.when(piece > 0)
                def _(j=j):
                    finish(sum_stores(piece - 1, j))

                back = across(parts[...], w_in[at, :])
                sums[0, :, at] = back[:HALF].astype(low)
                sums[1, :, at] = back[HALF:].astype(low)
                two = straight(act[...], w_out[:, at])
                sums[2, :, at] = two[:HALF].astype(low)
                sums[3, :, at] = two[HALF:].astype(low)
                begin(sum_stores(piece, j))
            finish(stores)
            return carry

        lax.fori_loop(0, pieces, work, 0)
        for j in range(width // wide_tile):
            finish(sum_stores(pieces - 1, j))
        store_middle.wait()

    return pl.pallas_call(
        body,
        in_specs=any_specs(7) + [pl.BlockSpec(memory_space=pltpu.VMEM)],
        out_specs=any_specs(7),
        out_shape=[
            jax.ShapeDtypeStruct((local_rows, width), jnp.float32),
            jax.ShapeDtypeStruct((group_rows, width), low),
            jax.ShapeDtypeStruct((group_rows, width), low),
            jax.ShapeDtypeStruct((group_rows, units), low),
            jax.ShapeDtypeStruct((group_rows, 2 * units), low),
            jax.ShapeDtypeStruct((group_rows, width), low),
            jax.ShapeDtypeStruct((group_rows, width), low),
        ],
        scratch_shapes=[
            pltpu.VMEM((local_rows, quarters * deep), low),
            pltpu.VMEM((local_rows, width), low),
            pltpu.VMEM((local_rows, width), jnp.float32),
            pltpu.VMEM((pieces, PIECE, width), low),
            pltpu.VMEM((pieces, PIECE, width), low),
            pltpu.VMEM((4, HALF, width), low),
            pltpu.VMEM((width, 2 * units), low),
            pltpu.VMEM((units, width), low),
            pltpu.VMEM((PIECE, units), low),
            pltpu.VMEM((PIECE, 2 * units), low),
            pltpu.SemaphoreType.DMA((4,)),
            pltpu.SemaphoreType.DMA((slices * quarters,)),
            pltpu.SemaphoreType.DMA((9,)),
            pltpu.SemaphoreType.DMA((5,)),
            pltpu.SemaphoreType.DMA((width // wide_tile, 4)),
            pltpu.SemaphoreType.DMA((6, 2)),
            pltpu.SemaphoreType.DMA((12, 2)),
        ],
        compiler_params=pltpu.CompilerParams(
            vmem_limit_bytes=VMEM, collective_id=3, has_side_effects=True
        ),
        cost_estimate=cost(12 * group_rows * width * units, 90e6),
        name="gated_unit",
    )(gated, whole_weight, hidden, grads_own, grads_first, ffn_in, ffn_out, live)


def mix_rows(hidden, cotangent, mix_weight, out_weight, live, keep):
    local_rows, width = hidden.shape
    parts, _, columns = mix_weight.shape
    heads = columns // HS
    group_rows = NBLK * BLK
    pieces = group_rows // PIECE
    wide_size = lax.axis_size("wide")
    slice_rows = columns // wide_size
    low = jnp.bfloat16
    joined = 2
    halves_at = (pl.ds(0, HALF), pl.ds(HALF, HALF))

    def body(*refs):
        hidden_in, cot_in, mix_in, out_in, live_ref, keep_ref = refs[:6]
        rows_out, parts_out, gated_out, mixing_out, states_out, grads_out, first_out, whole_out = refs[6:14]
        hidden_ref, cot_ref, rows, weights, parts_ref, gated_ref, mixing_ref, states_ref = refs[14:22]
        load_sems, mix_sems, store_sems, parts_sems, gather_sems, slice_sems, line_sems, core_sems = refs[22:]
        wide, narrow, z, core, mate, near_x, near_y = neighbours()
        far = (wide, 3 - narrow)
        above, below = (wide + 2, narrow), (wide - 2, narrow)
        barrier = pltpu.get_barrier_semaphore()

        def greet(place):
            pl.semaphore_signal(barrier, inc=1, device_id=place, device_id_type=MESH)

        load_hidden = pltpu.make_async_copy(hidden_in, hidden_ref, load_sems.at[0])
        load_cot = pltpu.make_async_copy(cot_in, cot_ref, load_sems.at[1])
        mix_loads = [
            pltpu.make_async_copy(
                mix_in.at[c], weights.at[:, pl.ds(c * columns, columns)], mix_sems.at[c]
            )
            for c in range(parts)
        ]
        load_hidden.start()
        for place in (near_x, near_y, far, mate):
            greet(place)
        pl.when(z < 3)(lambda: greet(above))
        pl.when(z > 0)(lambda: greet(below))
        middle = (z == 1) | (z == 2)
        pl.when(middle)(lambda: pl.semaphore_wait(barrier, 6))
        pl.when(jnp.logical_not(middle))(lambda: pl.semaphore_wait(barrier, 5))

        def remote(src, dst, sems, kind, place):
            return pltpu.make_async_remote_copy(
                src_ref=src,
                dst_ref=dst,
                send_sem=sems.at[kind, 0],
                recv_sem=sems.at[kind, 1],
                device_id=place,
                device_id_type=MESH,
            )

        slice_at = out_in.at[pl.ds(pl.multiple_of(wide * slice_rows, slice_rows), slice_rows)]
        keep_slice = pltpu.make_async_copy(slice_at, whole_out.at[wide, narrow], load_sems.at[2])
        slice_sends = [
            remote(slice_at, whole_out.at[wide, narrow], slice_sems, at, place)
            for at, place in enumerate((far, near_x, near_y))
        ]

        def up(hop):
            return remote(
                whole_out.at[wide - 2 * (hop - 1)], whole_out.at[wide - 2 * (hop - 1)], line_sems, hop - 1, above
            )

        def down_line(hop):
            return remote(
                whole_out.at[wide + 2 * (hop - 1)], whole_out.at[wide + 2 * (hop - 1)], line_sems, 2 + hop, below
            )

        def to_mate(hop, sign):
            at = wide + sign * 2 * hop
            return remote(whole_out.at[at], whole_out.at[at], core_sems, 3 + sign * hop, mate)

        def send_hop(hop):
            pl.when((z < 3) & (z >= hop - 1))(lambda: up(hop).start())
            pl.when((z > 0) & (z + hop - 1 <= 3))(lambda: down_line(hop).start())

        def take_hop(hop):
            @pl.when(z >= hop)
            def _():
                up(hop).wait_recv()
                to_mate(hop, -1).start()

            @pl.when(z + hop <= 3)
            def _():
                down_line(hop).wait_recv()
                to_mate(hop, 1).start()

        def end_hop(hop):
            pl.when((z < 3) & (z >= hop - 1))(lambda: up(hop).wait_send())
            pl.when((z > 0) & (z + hop - 1 <= 3))(lambda: down_line(hop).wait_send())
            pl.when(z >= hop)(lambda: to_mate(hop, -1).wait())
            pl.when(z + hop <= 3)(lambda: to_mate(hop, 1).wait())

        begin(slice_sends)
        keep_slice.start()

        def half(piece, at):
            return rows.at[piece, halves_at[at]]

        row_sends = (
            [remote(half(0, 0), half(1, 0), gather_sems, 0, near_x), remote(half(0, 1), half(1, 1), gather_sems, 1, near_y)],
            [remote(half(0, 1), half(2, 0), gather_sems, 2, near_x), remote(half(0, 0), half(2, 1), gather_sems, 3, near_y)],
            [remote(half(1, 1), half(3, 1), gather_sems, 4, near_x), remote(half(1, 0), half(3, 0), gather_sems, 5, near_y)],
        )
        grad_sends = [
            remote(cot_ref.at[halves_at[0]], first_out.at[halves_at[0]], gather_sems, 6, near_x),
            remote(cot_ref.at[halves_at[1]], first_out.at[halves_at[1]], gather_sems, 7, near_y),
        ]
        load_hidden.wait()
        begin(mix_loads)
        load_cot.start()

        def first_norm(i, carry):
            at = pl.ds(pl.multiple_of(i * 32, 32), 32)
            rows[0, at, :] = row_norm(hidden_ref[at, :].astype(jnp.float32)).astype(low)
            return carry

        for at in range(2):
            lax.fori_loop(at * HALF // 32, (at + 1) * HALF // 32, first_norm, 0)
            row_sends[0][at].start()
        begin(row_sends[1])

        def row_store(piece):
            at = pl.ds(piece * PIECE, PIECE)
            return pltpu.make_async_copy(rows.at[piece], rows_out.at[at, :], store_sems.at[piece])

        def part_stores(piece):
            at = pl.ds(piece * PIECE, PIECE)
            return [
                pltpu.make_async_copy(
                    parts_ref.at[at, pl.ds(c * columns, columns)], parts_out.at[c, at, :], parts_sems.at[piece, c]
                )
                for c in range(parts)
            ]

        def project(piece):
            row_store(piece).start()
            for c in range(0, parts, joined):
                if piece == 0:
                    finish(mix_loads[c : c + joined])
                at = slice(c * columns, (c + joined) * columns)
                result = straight(rows[piece], weights[:, at]).astype(low)
                parts_ref[piece * PIECE : (piece + 1) * PIECE, at] = result
            begin(part_stores(piece))

        project(0)
        load_cot.wait()

        def live_cot(i, carry):
            at = pl.ds(pl.multiple_of(i * 32, 32), 32)
            cot_ref[at, :] = (live_ref[at, :1] * cot_ref[at, :].astype(jnp.float32)).astype(low)
            return carry

        keep_slice.wait()
        finish(slice_sends)
        to_mate(0, 1).start()
        send_hop(1)
        lax.fori_loop(0, local_rows // 32, live_cot, 0)
        store_grads = pltpu.make_async_copy(cot_ref, grads_out, load_sems.at[3])
        store_grads.start()
        finish(row_sends[0])
        begin(row_sends[2])
        begin(grad_sends)
        project(1)
        take_hop(1)
        send_hop(2)
        finish(row_sends[1])
        project(2)
        take_hop(2)
        send_hop(3)
        finish(row_sends[2])
        project(3)

        def slot_of(block):
            off_x = (block // 2 % 2 + narrow % 2) % 2
            off_y = (block // 4 + narrow // 2) % 2
            if block % 2:
                return 1 + 3 * off_x + 2 * off_y + off_x * off_y
            return 2 * off_x + 5 * off_y - off_x * off_y

        def attend(head, carry):
            head_id = (heads * narrow + head).astype(jnp.float32)
            rate = jnp.exp(jnp.full((1, 1), -0.5 * math.log(2.0), jnp.float32) * (head_id + 1.0))
            within, entry, leave, whole = block_decays(rate)
            state = jnp.zeros((HS, HS), jnp.float32)

            def part(c, rows_at):
                at = pl.ds(pl.multiple_of(c * columns + head * HS, HS), HS)
                return parts_ref[rows_at, at]

            for block in range(NBLK):
                rows_at = pl.ds(pl.multiple_of(slot_of(block) * BLK, BLK), BLK)
                queries = jax.nn.silu(part(0, rows_at).astype(jnp.float32)).astype(low)
                keys = jax.nn.silu(part(1, rows_at).astype(jnp.float32)).astype(low)
                values = part(2, rows_at)
                gate = part(3, rows_at).astype(jnp.float32)
                state = keep_ref[block : block + 1, :] * state
                state_low = state.astype(low)
                states_ref[head, block] = state_low
                scores = (across(queries, keys) * within).astype(low)
                mixing = straight(scores, values) + entry * straight(queries, state_low)
                late_keys = (keys.astype(jnp.float32) * leave).astype(low)
                state = whole * state + down(late_keys, values)
                scale = lax.rsqrt(jnp.mean(mixing * mixing, axis=-1, keepdims=True) + head_floor)
                at = pl.ds(pl.multiple_of(head * HS, HS), HS)
                gated_ref[rows_at, at] = (mixing * scale * gate).astype(low)
                mixing_ref[rows_at, at] = mixing.astype(low)
            return carry

        lax.fori_loop(0, heads // 2, attend, 0)
        take_hop(3)
        lax.fori_loop(heads // 2, heads, attend, 0)
        stores = [
            pltpu.make_async_copy(gated_ref, gated_out.at[0], load_sems.at[4]),
            pltpu.make_async_copy(mixing_ref, mixing_out, load_sems.at[5]),
            pltpu.make_async_copy(states_ref, states_out, load_sems.at[6]),
        ]
        begin(stores)
        to_mate(0, 1).wait()
        for hop in range(1, 4):
            end_hop(hop)
        finish(grad_sends)
        store_grads.wait()
        for piece in range(pieces):
            row_store(piece).wait()
            finish(part_stores(piece))
        finish(stores)

    low_shape = functools.partial(jax.ShapeDtypeStruct, dtype=low)
    return pl.pallas_call(
        body,
        in_specs=any_specs(4) + [pl.BlockSpec(memory_space=pltpu.VMEM)] * 2,
        out_specs=any_specs(8),
        out_shape=[
            low_shape((group_rows, width)),
            low_shape((parts, group_rows, columns)),
            low_shape((1, group_rows, columns)),
            low_shape((group_rows, columns)),
            low_shape((heads, NBLK, HS, HS)),
            low_shape((local_rows, width)),
            low_shape((local_rows, width)),
            low_shape((wide_size, pieces, slice_rows, width)),
        ],
        scratch_shapes=[
            pltpu.VMEM((local_rows, width), low),
            pltpu.VMEM((local_rows, width), low),
            pltpu.VMEM((pieces, PIECE, width), low),
            pltpu.VMEM((width, parts * columns), low),
            pltpu.VMEM((group_rows, parts * columns), low),
            pltpu.VMEM((group_rows, columns), low),
            pltpu.VMEM((group_rows, columns), low),
            pltpu.VMEM((heads, NBLK, HS, HS), low),
            pltpu.SemaphoreType.DMA((7,)),
            pltpu.SemaphoreType.DMA((parts,)),
            pltpu.SemaphoreType.DMA((pieces,)),
            pltpu.SemaphoreType.DMA((pieces, parts)),
            pltpu.SemaphoreType.DMA((8, 2)),
            pltpu.SemaphoreType.DMA((3, 2)),
            pltpu.SemaphoreType.DMA((6, 2)),
            pltpu.SemaphoreType.DMA((7, 2)),
        ],
        compiler_params=pltpu.CompilerParams(
            vmem_limit_bytes=VMEM, collective_id=4, has_side_effects=True
        ),
        cost_estimate=cost(2 * group_rows * parts * width * columns, 50e6),
        name="mix_rows",
    )(hidden, cotangent, mix_weight, out_weight, live, keep)


def finish_rows(mix_low, out_low, hidden, middle, grad_middle, live, normed_terms, two_sums, two_terms):
    parts, width, columns = mix_low.shape
    local_rows = hidden.shape[0]
    tile = local_rows // parts
    out_tile = out_low.shape[0] // parts
    half_steps = parts // 2
    terms = len(normed_terms) + len(two_terms)

    def body(mix_ref, out_ref, hidden_ref, middle_ref, grad_ref, live_ref, own_ref, *refs):
        term_refs = refs[:terms]
        mix_out, out_out, layer_ref, input_ref = refs[terms:]
        mix_out[...] = mix_ref[...].astype(jnp.float32)
        out_out[...] = out_ref[...].astype(jnp.float32)

        def rows_of(half):
            normed = add_rows(*(ref[...] for ref in term_refs[3 * half : 3 * half + 3]))
            two = add_rows(*(ref[...] for ref in term_refs[6 + 2 * half : 8 + 2 * half]), own_ref[...])
            layer = middle_ref[...] + live_ref[...] * two
            layer_ref[...] = layer.astype(jnp.bfloat16)
            back = norm_back(hidden_ref[...].astype(jnp.float32), normed)
            input_ref[...] = (grad_ref[...] + back).astype(jnp.bfloat16)

        first = pl.program_id(0) < half_steps
        pl.when(first)(lambda: rows_of(0))
        pl.when(jnp.logical_not(first))(lambda: rows_of(1))

    def rows_spec(size):
        return pl.BlockSpec((tile, size), lambda i: (i, 0))

    def half_spec(half):
        if half == 0:
            return pl.BlockSpec((tile, width), lambda i: (jnp.minimum(i, half_steps - 1), 0))
        return pl.BlockSpec((tile, width), lambda i: (jnp.maximum(i - half_steps, 0), 0))

    term_specs = [half_spec(0)] * 3 + [half_spec(1)] * 3 + [half_spec(0)] * 2 + [half_spec(1)] * 2
    mix_spec = pl.BlockSpec((1, width, columns), lambda i: (i, 0, 0))
    out_spec = pl.BlockSpec((out_tile, out_low.shape[1]), lambda i: (i, 0))
    return pl.pallas_call(
        body,
        grid=(parts,),
        in_specs=[mix_spec, out_spec]
        + [rows_spec(width)] * 3
        + [rows_spec(1), rows_spec(width)]
        + term_specs,
        out_specs=[mix_spec, out_spec, rows_spec(width), rows_spec(width)],
        out_shape=[
            jax.ShapeDtypeStruct(mix_low.shape, jnp.float32),
            jax.ShapeDtypeStruct(out_low.shape, jnp.float32),
            jax.ShapeDtypeStruct(hidden.shape, jnp.bfloat16),
            jax.ShapeDtypeStruct(hidden.shape, jnp.bfloat16),
        ],
        compiler_params=pltpu.CompilerParams(vmem_limit_bytes=VMEM),
        cost_estimate=cost(1e8, 60e6),
        name="finish_rows",
    )(mix_low, out_low, hidden, middle, grad_middle, live, two_sums, *normed_terms, *two_terms)


def block_decays(rate):
    row = lax.broadcasted_iota(jnp.int32, (BLK, BLK), 0)
    column = lax.broadcasted_iota(jnp.int32, (BLK, BLK), 1)
    distance = (row - column).astype(jnp.float32)
    within = jnp.where(row >= column, jnp.exp(-rate * jnp.maximum(distance, 0.0)), 0.0)
    place = lax.broadcasted_iota(jnp.int32, (BLK, 1), 0).astype(jnp.float32)
    entry = jnp.exp(-rate * (place + 1.0))
    leave = jnp.exp(-rate * (BLK - 1.0 - place))
    whole = jnp.exp(-BLK * rate * jnp.ones((1, HS), jnp.float32))
    return within, entry, leave, whole


def mix_backward(slots, fresh, rates, parts, mixing_all, states, grad_gated, in_low, out_low):
    _, group_rows, columns = parts.shape
    heads = columns // HS
    low = jnp.bfloat16
    width, both_units = in_low.shape
    units = both_units // 2
    main = units // TILE * TILE
    tail = units - main
    in_rows, out_rows = width // heads, units // heads

    def body(
        slot_ref,
        fresh_ref,
        rate_ref,
        parts_ref,
        mixing_ref,
        states_ref,
        grad_ref,
        in_ref,
        wide_ref,
        out_ref,
        in_out,
        wide_out,
    ):
        wide_out[...] = wide_ref[...].astype(jnp.float32)
        for c in range(2):
            in_out[c, :, :main] = in_ref[:, c * main : (c + 1) * main].astype(jnp.float32)
            rest = slice(2 * main + c * tail, 2 * main + (c + 1) * tail)
            in_out[c, :, main:] = in_ref[:, rest].astype(jnp.float32)
        within, entry, leave, whole = block_decays(rate_ref[pl.program_id(0)])
        later = jnp.zeros((HS, HS), jnp.float32)
        for block in reversed(range(NBLK)):
            rows = pl.ds(pl.multiple_of(slot_ref[block] * BLK, BLK), BLK)
            raw_queries = parts_ref[0, rows, :].astype(jnp.float32)
            raw_keys = parts_ref[1, rows, :].astype(jnp.float32)
            queries_float = jax.nn.silu(raw_queries).astype(low).astype(jnp.float32)
            queries, keys = queries_float.astype(low), jax.nn.silu(raw_keys).astype(low)
            values = parts_ref[2, rows, :]
            gate = parts_ref[3, rows, :].astype(jnp.float32)
            mixing = mixing_ref[rows, :].astype(jnp.float32)
            grad_gated_rows = grad_ref[rows, :].astype(jnp.float32)
            scale = lax.rsqrt(jnp.mean(mixing * mixing, axis=-1, keepdims=True) + head_floor)
            headed = mixing * scale
            out_ref[3, rows, :] = (grad_gated_rows * headed).astype(low)
            grad_headed = grad_gated_rows * gate
            inner = jnp.mean(grad_headed * headed, axis=-1, keepdims=True)
            grad = (scale * (grad_headed - headed * inner)).astype(low)
            weights = (across(queries, keys) * within).astype(low)
            grad_scores = (across(grad, values) * within).astype(low)
            later_low = later.astype(low)
            grad_queries = straight(grad_scores, keys) + entry * across(grad, states_ref[0, block])
            grad_keys = down(grad_scores, queries) + leave * across(values, later_low)
            grad_values = down(weights, grad) + leave * straight(keys, later_low)
            early_queries = (queries_float * entry).astype(low)
            later = jnp.where(fresh_ref[block] != 0, 0.0, whole * later + down(early_queries, grad))
            out_ref[0, rows, :] = (grad_queries * silu_slope(raw_queries)).astype(low)
            out_ref[1, rows, :] = (grad_keys * silu_slope(raw_keys)).astype(low)
            out_ref[2, rows, :] = grad_values.astype(low)

    return pl.pallas_call(
        body,
        grid_spec=pltpu.PrefetchScalarGridSpec(
            num_scalar_prefetch=3,
            grid=(heads,),
            in_specs=[
                pl.BlockSpec((4, group_rows, HS), lambda h, *_: (0, 0, h)),
                pl.BlockSpec((group_rows, HS), lambda h, *_: (0, h)),
                pl.BlockSpec((1, NBLK, HS, HS), lambda h, *_: (h, 0, 0, 0)),
                pl.BlockSpec((group_rows, HS), lambda h, *_: (0, h)),
                pl.BlockSpec((in_rows, both_units), lambda h, *_: (h, 0)),
                pl.BlockSpec((out_rows, width), lambda h, *_: (h, 0)),
            ],
            out_specs=[
                pl.BlockSpec((4, group_rows, HS), lambda h, *_: (0, 0, h)),
                pl.BlockSpec((2, in_rows, units), lambda h, *_: (0, h, 0)),
                pl.BlockSpec((out_rows, width), lambda h, *_: (h, 0)),
            ],
        ),
        out_shape=[
            jax.ShapeDtypeStruct(parts.shape, low),
            jax.ShapeDtypeStruct((2, width, units), jnp.float32),
            jax.ShapeDtypeStruct((units, width), jnp.float32),
        ],
        compiler_params=pltpu.CompilerParams(vmem_limit_bytes=VMEM),
        cost_estimate=cost(20e9, 75e6),
        name="mix_backward",
    )(slots, fresh, rates, parts, mixing_all, states, grad_gated, in_low, out_low)


def norm_back(values, grad):
    scale = lax.rsqrt(jnp.mean(values * values, axis=-1, keepdims=True) + epsilon)
    unit = values * scale
    return scale * (grad - unit * jnp.mean(grad * unit, axis=-1, keepdims=True))


def square_device(
    hidden, mix_weight, out_weight, ffn_in_weight, ffn_out_weight, seq_lengths, block_seq, cotangent
):
    local_rows, width = hidden.shape
    units = ffn_out_weight.shape[0]
    head_count = mix_weight.shape[2] // HS
    narrow_index = lax.axis_index("narrow")
    valid_all, fresh_block = group_masks(seq_lengths, block_seq)
    live = lax.dynamic_slice_in_dim(
        valid_all.astype(jnp.float32), narrow_index * local_rows, local_rows
    )[:, None]
    head_ids = narrow_index * head_count + jnp.arange(head_count, dtype=jnp.int32)
    rates = 2.0 ** (-8.0 * (head_ids.astype(jnp.float32) + 1.0) / HEADS)
    slots, fresh = slot_tables(narrow_index, fresh_block)
    low = jnp.bfloat16

    keep = jnp.broadcast_to(jnp.where(fresh_block, 0.0, 1.0)[:, None], (NBLK, HS))
    normed_all, parts, gated, mixing, states, grads_own, grads_first, whole_weight = mix_rows(
        hidden, cotangent, mix_weight, out_weight, live, keep
    )
    middle, normed_two_all, grad_two_all, act, grad_parts, back_sums, two_sums = gated_unit(
        gated,
        whole_weight,
        hidden,
        live,
        grads_own,
        grads_first,
        ffn_in_weight,
        ffn_out_weight,
    )
    out_low, in_low, grad_branch_all, grad_middle, grad_gated = unit_grads(
        act,
        grad_two_all,
        normed_two_all,
        grad_parts,
        back_sums,
        middle,
        cotangent,
        live,
        out_weight,
    )
    grad_projected, grad_ffn_in, grad_ffn_out = mix_backward(
        slots,
        fresh,
        rates,
        parts,
        mixing,
        states,
        grad_gated,
        in_low.reshape(width, 2 * units),
        out_low.reshape(units, width),
    )
    out_low, mix_low, own_top, own_low, *terms = mix_grads(
        gated, grad_branch_all, normed_all, grad_projected, mix_weight, two_sums
    )
    grad_mix, grad_out, layer_out, input_grad = finish_rows(
        mix_low.reshape(mix_weight.shape),
        out_low.reshape(out_weight.shape),
        hidden,
        middle,
        grad_middle,
        live,
        (own_top, terms[0], terms[2], own_low, terms[1], terms[3]),
        two_sums,
        (terms[4], terms[6], terms[5], terms[7]),
    )
    return (layer_out, input_grad, grad_mix, grad_out, grad_ffn_in, grad_ffn_out)


def solution(mesh):
    square = mesh.shape["wide"] == 8 and mesh.shape["narrow"] == 4
    per_device = square_device if square else general_device
    in_specs = (
        P(("wide", "narrow"), None),
        P(None, None, "narrow"),
        P("narrow", None),
        P(None, None, "narrow"),
        P("narrow", None),
        P("wide"),
        P("wide"),
        P(("wide", "narrow"), None),
    )
    out_specs = (
        P(("wide", "narrow"), None),
        P(("wide", "narrow"), None),
        P(None, None, "narrow"),
        P("narrow", None),
        P(None, None, "narrow"),
        P("narrow", None),
    )
    return jax.shard_map(
        per_device, mesh=mesh, in_specs=in_specs, out_specs=out_specs, check_vma=False
    )
```

```python
import functools
import math

import jax
import jax.numpy as jnp
from jax import lax
from jax.experimental import pallas as pl
from jax.experimental.pallas import tpu as pltpu
from jax.sharding import PartitionSpec as P

HEADS = 16
HS = 128
BLK = 256
NBLK = 8


epsilon = 1e-06
head_floor = 1.0
highest = lax.Precision.HIGHEST


def row_norm(values):
    return values * lax.rsqrt(jnp.mean(values * values, axis=-1, keepdims=True) + epsilon)


def head_norm(values):
    return values * lax.rsqrt(jnp.mean(values * values, axis=-1, keepdims=True) + head_floor)


def silu_slope(values):
    sigmoid_part = jax.nn.sigmoid(values)
    return sigmoid_part * (1.0 + values * (1.0 - sigmoid_part))


def decay_tables(decay_rates):
    positions = jnp.arange(BLK, dtype=jnp.float32)
    distance = positions[:, None] - positions[None, :]
    causal = distance >= 0
    clipped = jnp.where(causal, distance, 0.0)
    within = jnp.where(causal[None], jnp.exp(-decay_rates[:, None, None] * clipped[None]), 0.0)
    entry_decay = jnp.exp(-(positions[:, None] + 1.0) * decay_rates[None, :])
    exit_decay = jnp.exp(-(BLK - 1.0 - positions[:, None]) * decay_rates[None, :])
    block_decay = jnp.exp(-BLK * decay_rates)
    return (within, entry_decay, exit_decay, block_decay)


def group_masks(lengths, owners):
    seq_slot = owners - owners[0]
    first_count = jnp.sum((seq_slot == 0).astype(jnp.int32))
    block_ids = jnp.arange(NBLK, dtype=jnp.int32)
    start_block = jnp.where(seq_slot == 0, jnp.int32(0), first_count)
    seq_limit = jnp.where(seq_slot == 0, lengths[0], lengths[1])
    offsets = (block_ids - start_block)[:, None] * BLK + jnp.arange(BLK, dtype=jnp.int32)[None, :]
    valid_rows = (offsets < seq_limit[:, None]).reshape(-1)
    fresh_block = block_ids == start_block
    return (valid_rows, fresh_block)


def forward_block(tables, kv_state, block_in):
    within, entry_decay, exit_decay, block_decay = tables
    queries, keys_in, values, fresh_block = block_in
    kv_state = jnp.where(fresh_block, 0.0, kv_state)
    scores = jnp.einsum("ihs,jhs->hij", queries, keys_in, preferred_element_type=jnp.float32)
    weights = (scores * within).astype(jnp.bfloat16)
    inner_part = jnp.einsum("hij,jhs->ihs", weights, values, preferred_element_type=jnp.float32)
    carried = jnp.einsum(
        "ihs,hst->iht",
        queries.astype(jnp.float32) * entry_decay[:, :, None],
        kv_state,
        precision=highest,
    )
    update = jnp.einsum(
        "ihs,iht->hst",
        keys_in.astype(jnp.float32) * exit_decay[:, :, None],
        values.astype(jnp.float32),
        precision=highest,
    )
    return (block_decay[:, None, None] * kv_state + update, (inner_part + carried, kv_state))


def backward_block(tables, later_grad, block_in):
    within, entry_decay, exit_decay, block_decay = tables
    queries, keys_in, values, grad_mix, kv_state, fresh_block = block_in
    scores = jnp.einsum("ihs,jhs->hij", queries, keys_in, preferred_element_type=jnp.float32)
    weights = (scores * within).astype(jnp.bfloat16)
    grad_values = jnp.einsum("hij,ihs->jhs", weights, grad_mix, preferred_element_type=jnp.float32)
    grad_weights = jnp.einsum("ihs,jhs->hij", grad_mix, values, preferred_element_type=jnp.float32)
    grad_scores = (grad_weights * within).astype(jnp.bfloat16)
    grad_queries = jnp.einsum(
        "hij,jhs->ihs", grad_scores, keys_in, preferred_element_type=jnp.float32
    )
    grad_keys = jnp.einsum("hij,ihs->jhs", grad_scores, queries, preferred_element_type=jnp.float32)
    grad_float = grad_mix.astype(jnp.float32)
    values_float = values.astype(jnp.float32)
    queries_float = queries.astype(jnp.float32)
    keys_float = keys_in.astype(jnp.float32)
    grad_queries = grad_queries + entry_decay[:, :, None] * jnp.einsum(
        "iht,hst->ihs", grad_float, kv_state, precision=highest
    )
    grad_keys = grad_keys + exit_decay[:, :, None] * jnp.einsum(
        "iht,hst->ihs", values_float, later_grad, precision=highest
    )
    grad_values = grad_values + jnp.einsum(
        "ihs,hst->iht", keys_float * exit_decay[:, :, None], later_grad, precision=highest
    )
    grad_state = jnp.einsum(
        "ihs,iht->hst", queries_float * entry_decay[:, :, None], grad_float, precision=highest
    )
    grad_state = grad_state + block_decay[:, None, None] * later_grad
    grad_state = jnp.where(fresh_block, 0.0, grad_state)
    return (grad_state, (grad_queries, grad_keys, grad_values))


def general_device(
    hidden, mix_weight, out_weight, ffn_in_weight, ffn_out_weight, seq_lengths, block_seq, cotangent
):
    local_rows = hidden.shape[0]
    group_rows = NBLK * BLK
    head_width = mix_weight.shape[2]
    head_count = head_width // HS
    narrow_index = lax.axis_index("narrow")
    valid_all, fresh_block = group_masks(seq_lengths, block_seq)
    valid_rows = lax.dynamic_slice_in_dim(
        valid_all.astype(jnp.float32), narrow_index * local_rows, local_rows
    )[:, None]
    head_ids = narrow_index * head_count + jnp.arange(head_count, dtype=jnp.int32)
    decay_rates = 2.0 ** (-8.0 * (head_ids.astype(jnp.float32) + 1.0) / HEADS)
    tables = decay_tables(decay_rates)

    def split_blocks(flat_rows):
        return flat_rows.reshape(NBLK, BLK, head_count, HS)

    inputs = hidden.astype(jnp.float32)
    normed_low = row_norm(inputs).astype(jnp.bfloat16)
    gathered = lax.all_gather(normed_low, "narrow", axis=0, tiled=True)
    projected = jnp.einsum("rd,cde->cre", gathered, mix_weight, preferred_element_type=jnp.float32)
    queries = jax.nn.silu(projected[0]).astype(jnp.bfloat16)
    keys_in = jax.nn.silu(projected[1]).astype(jnp.bfloat16)
    values = projected[2].astype(jnp.bfloat16)
    gate_part = projected[3]
    zero_state = jnp.zeros((head_count, HS, HS), jnp.float32)
    final_state, (mixing, kept_states) = lax.scan(
        lambda state_in, block_in: forward_block(tables, state_in, block_in),
        zero_state,
        (split_blocks(queries), split_blocks(keys_in), split_blocks(values), fresh_block),
    )
    mixing = mixing.reshape(group_rows, head_count, HS)
    headed = head_norm(mixing).reshape(group_rows, head_width)
    gated_low = (headed * gate_part).astype(jnp.bfloat16)
    branch = lax.psum_scatter(
        jnp.dot(gated_low, out_weight, preferred_element_type=jnp.float32).astype(jnp.bfloat16),
        "narrow",
        scatter_dimension=0,
        tiled=True,
    ).astype(jnp.float32)
    middle = inputs + valid_rows * branch
    normed_two_low = row_norm(middle).astype(jnp.bfloat16)
    gathered_two = lax.all_gather(normed_two_low, "narrow", axis=0, tiled=True)
    both_parts = jnp.einsum(
        "rd,cdf->crf", gathered_two, ffn_in_weight, preferred_element_type=jnp.float32
    )
    hidden_low = (both_parts[0] * both_parts[1]).astype(jnp.bfloat16)
    branch_two = lax.psum_scatter(
        jnp.dot(hidden_low, ffn_out_weight, preferred_element_type=jnp.float32).astype(
            jnp.bfloat16
        ),
        "narrow",
        scatter_dimension=0,
        tiled=True,
    ).astype(jnp.float32)
    layer_out = (middle + valid_rows * branch_two).astype(jnp.bfloat16)
    grad_rows = cotangent.astype(jnp.float32)
    ffn_grad_all = lax.all_gather(
        (valid_rows * grad_rows).astype(jnp.bfloat16), "narrow", axis=0, tiled=True
    )
    grad_ffn_out = jnp.einsum(
        "rf,rd->fd", hidden_low, ffn_grad_all, preferred_element_type=jnp.float32
    )
    grad_hidden = jnp.einsum(
        "rd,fd->rf", ffn_grad_all, ffn_out_weight, preferred_element_type=jnp.float32
    )
    grad_parts = jnp.stack([grad_hidden * both_parts[1], grad_hidden * both_parts[0]]).astype(
        jnp.bfloat16
    )
    grad_ffn_in = jnp.einsum(
        "rd,crf->cdf", gathered_two, grad_parts, preferred_element_type=jnp.float32
    )
    grad_slice = grad_parts
    grad_normed_two = lax.psum_scatter(
        jnp.einsum(
            "crf,cdf->rd", grad_slice, ffn_in_weight, preferred_element_type=jnp.float32
        ).astype(jnp.bfloat16),
        "narrow",
        scatter_dimension=0,
        tiled=True,
    ).astype(jnp.float32)
    norm_value, norm_pull = jax.vjp(row_norm, middle)
    grad_middle = grad_rows + norm_pull(grad_normed_two)[0]
    attn_grad_all = lax.all_gather(
        (valid_rows * grad_middle).astype(jnp.bfloat16), "narrow", axis=0, tiled=True
    )
    grad_out_weight = jnp.einsum(
        "re,rd->ed", gated_low, attn_grad_all, preferred_element_type=jnp.float32
    )
    grad_gated = jnp.einsum(
        "rd,ed->re", attn_grad_all, out_weight, preferred_element_type=jnp.float32
    )
    grad_gated = lax.optimization_barrier(grad_gated.astype(jnp.bfloat16)).astype(jnp.float32)
    grad_gate = grad_gated * headed
    grad_headed = (grad_gated * gate_part).reshape(group_rows, head_count, HS)
    head_value, head_pull = jax.vjp(head_norm, mixing)
    grad_mixing = head_pull(grad_headed)[0].astype(jnp.bfloat16)
    first_grad, (grad_queries, grad_keys, grad_values) = lax.scan(
        lambda later_grad, block_in: backward_block(tables, later_grad, block_in),
        zero_state,
        (
            split_blocks(queries),
            split_blocks(keys_in),
            split_blocks(values),
            split_blocks(grad_mixing),
            kept_states,
            fresh_block,
        ),
        reverse=True,
    )
    grad_projected = jnp.stack(
        [
            grad_queries.reshape(group_rows, head_width) * silu_slope(projected[0]),
            grad_keys.reshape(group_rows, head_width) * silu_slope(projected[1]),
            grad_values.reshape(group_rows, head_width),
            grad_gate,
        ]
    ).astype(jnp.bfloat16)
    grad_mix = jnp.einsum(
        "rd,cre->cde", gathered, grad_projected, preferred_element_type=jnp.float32
    )
    grad_slice = grad_projected
    grad_normed = lax.psum_scatter(
        jnp.einsum(
            "cre,cde->rd", grad_slice, mix_weight, preferred_element_type=jnp.float32
        ).astype(jnp.bfloat16),
        "narrow",
        scatter_dimension=0,
        tiled=True,
    ).astype(jnp.float32)
    first_value, first_pull = jax.vjp(row_norm, inputs)
    input_grad = (grad_middle + first_pull(grad_normed)[0]).astype(jnp.bfloat16)
    grad_mix, grad_out_weight, grad_ffn_in, grad_ffn_out = (
        lax.psum(grad_mix.astype(jnp.bfloat16), "wide").astype(jnp.float32),
        lax.psum(grad_out_weight.astype(jnp.bfloat16), "wide").astype(jnp.float32),
        lax.psum(grad_ffn_in.astype(jnp.bfloat16), "wide").astype(jnp.float32),
        lax.psum(grad_ffn_out.astype(jnp.bfloat16), "wide").astype(jnp.float32),
    )
    return (layer_out, input_grad, grad_mix, grad_out_weight, grad_ffn_in, grad_ffn_out)


HALF = BLK
PIECE = 2 * BLK
VMEM = 60 * 1024 * 1024


def add_low(*terms):
    return sum(term.astype(jnp.float32) for term in terms).astype(jnp.bfloat16)


def add_rows(*terms):
    return sum(term.astype(jnp.float32) for term in terms)


def across(left, right):
    return lax.dot_general(left, right, (((1,), (1,)), ((), ())), preferred_element_type=jnp.float32)


def down(left, right):
    return lax.dot_general(left, right, (((0,), (0,)), ((), ())), preferred_element_type=jnp.float32)


def straight(left, right):
    return jnp.dot(left, right, preferred_element_type=jnp.float32)


def any_specs(count):
    return [pl.BlockSpec(memory_space=pl.ANY)] * count


def cost(flops, bytes_accessed):
    return pl.CostEstimate(flops=int(flops), bytes_accessed=int(bytes_accessed), transcendentals=0)


MESH = pl.DeviceIdType.MESH
SLOTS = 13
STAGES = 12
SUB = 128
TILE = 256


def begin(copies):
    for copy in copies:
        copy.start()


def finish(copies):
    for copy in copies:
        copy.wait()


def neighbours():
    wide, narrow = lax.axis_index("wide"), lax.axis_index("narrow")
    z, core = wide // 2, wide % 2
    mate = (wide + 1 - 2 * core, narrow)
    near_x = (wide, narrow + 1 - 2 * (narrow % 2))
    near_y = (wide, (narrow + 2) % 4)
    return wide, narrow, z, core, mate, near_x, near_y


def slot_of(block, narrow):
    off_x = (block // 2 % 2 + narrow % 2) % 2
    off_y = (block // 4 + narrow // 2) % 2
    if block % 2:
        return 1 + 3 * off_x + 2 * off_y + off_x * off_y
    return 2 * off_x + 5 * off_y - off_x * off_y


def head_rate(head):
    return jnp.exp(jnp.full((1, 1), -8.0 / HEADS * math.log(2.0), jnp.float32) * (head.astype(jnp.float32) + 1.0))


def line_scratch():
    low = jnp.bfloat16
    pair = pltpu.VMEM((SLOTS, 2, SUB, TILE), low)
    return [
        pltpu.VMEM((SLOTS, 4, SUB, TILE), low),
        pair,
        pair,
        pair,
        pltpu.VMEM((SLOTS, SUB, TILE), low),
        pair,
        pair,
        pltpu.SemaphoreType.DMA((14, SLOTS)),
        pltpu.SemaphoreType.DMA((4, SLOTS)),
    ]


def enter(neighbour_places):
    wide, narrow, z, core, mate, near_x, near_y = neighbour_places
    barrier = pltpu.get_barrier_semaphore()

    def greet(place):
        pl.semaphore_signal(barrier, inc=1, device_id=place, device_id_type=MESH)

    for place in (mate, near_x, near_y):
        greet(place)
    middle = (z == 1) | (z == 2)

    @pl.when(middle)
    def _():
        greet((2 * (3 - z) + core, narrow))
        greet((6 * (z - 1) + core, narrow))
        pl.semaphore_wait(barrier, 5)

    @pl.when(jnp.logical_not(middle))
    def _():
        greet((2 * (1 + z // 3) + core, narrow))
        pl.semaphore_wait(barrier, 4)


def line_sum(scratch, places, count, product, targets):
    own, met, both, ended, crossed, full, other, sems, out_sems = scratch
    wide, narrow, z, core, mate, _, _ = places
    region = z // 2
    middle = (z == 1) | (z == 2)
    end = jnp.logical_not(middle)
    inward = (2 * (1 + z // 3) + core, narrow)
    across_line = (2 * (3 - z) + core, narrow)
    outward = (6 * (z - 1) + core, narrow)

    def remote(src, dst, kind, slot, place):
        return pltpu.make_async_remote_copy(
            src_ref=src,
            dst_ref=dst,
            send_sem=sems.at[2 * kind, slot],
            recv_sem=sems.at[2 * kind + 1, slot],
            device_id=place,
            device_id_type=MESH,
        )

    def core_one(s):
        return remote(own.at[s, pl.ds(2 * (1 - core), 2)], met.at[s], 0, s, mate)

    def line_one(s):
        return remote(both.at[s], ended.at[s], 1, s, inward)

    def cross_one(s):
        return remote(both.at[s, 1 - region], crossed.at[s], 2, s, across_line)

    def cross_two(s):
        return remote(full.at[s, region], full.at[s, region], 3, s, across_line)

    def out_one(s):
        return remote(full.at[s, region], full.at[s, region], 4, s, outward)

    def out_two(s):
        return remote(full.at[s, 1 - region], full.at[s, 1 - region], 5, s, outward)

    def core_two(s):
        return remote(full.at[s], other.at[s], 6, s, mate)

    def add(left, right):
        return (left.astype(jnp.float32) + right.astype(jnp.float32)).astype(jnp.bfloat16)

    def deliveries(k, s):
        for t in range(2):
            for which, (src, part) in enumerate(
                ((full.at[s, t], 2 * core + t), (other.at[s, t], 2 * (1 - core) + t))
            ):
                for condition, ref in targets(k, part):
                    yield condition, pltpu.make_async_copy(src, ref, out_sems.at[2 * t + which, s])

    def start(k, s):
        product(k, own.at[s])
        core_one(s).start()

    def cores(k, s):
        core_one(s).wait_recv()
        both[s] = add(own[s, pl.ds(2 * core, 2)], met[s])
        pl.when(end)(lambda: line_one(s).start())

    def ends(k, s):
        @pl.when(middle)
        def _():
            line_one(s).wait_recv()
            both[s] = add(both[s], ended[s])
            cross_one(s).start()

    def centre(k, s):
        @pl.when(middle)
        def _():
            cross_one(s).wait_recv()
            full[s, region] = add(both[s, region], crossed[s])
            cross_two(s).start()
            out_one(s).start()

    def pass_on(k, s):
        @pl.when(middle)
        def _():
            cross_two(s).wait_recv()
            out_two(s).start()

    def back(k, s):
        @pl.when(end)
        def _():
            out_one(s).wait_recv()
            out_two(s).wait_recv()

        core_two(s).start()

    def deliver(k, s):
        core_two(s).wait_recv()
        for condition, copy in deliveries(k, s):
            pl.when(condition)(copy.start)

    def clear(k, s):
        core_one(s).wait_send()
        core_two(s).wait_send()

        @pl.when(end)
        def _():
            line_one(s).wait_send()

        @pl.when(middle)
        def _():
            for copy in (cross_one(s), cross_two(s), out_one(s), out_two(s)):
                copy.wait_send()

        for t in range(2):
            for which, src in enumerate((full, other)):
                ref = targets(k, 0)[0][1]
                pltpu.make_async_copy(src.at[s, t], ref, out_sems.at[2 * t + which, s]).wait()

    stages = (
        (12, clear),
        (10, deliver),
        (9, back),
        (7, pass_on),
        (5, centre),
        (3, ends),
        (1, cores),
        (0, start),
    )

    def step(i, carry):
        for delay, work in stages:
            k = i - delay

            @pl.when((k >= 0) & (k < count))
            def _(work=work, k=k):
                work(k, lax.rem(k + SLOTS, SLOTS))

        return carry

    return step


def square_scratch(uses):
    block = pltpu.VMEM((2, BLK, HEADS * HS), jnp.bfloat16)
    return [block, block, pltpu.SemaphoreType.DMA((uses, 6, 2)), pltpu.SemaphoreType.DMA((uses, 2))]


def square_sum(scratch, places, parts, landed, use):
    met, mid, sems, load_sems = scratch
    top_x, low_y, low_x, top_y, top_d, low_d = parts
    near_x, near_y = places[5:]

    def remote(src, dst, kind, place):
        return pltpu.make_async_remote_copy(
            src_ref=src,
            dst_ref=dst,
            send_sem=sems.at[use, kind, 0],
            recv_sem=sems.at[use, kind, 1],
            device_id=place,
            device_id_type=MESH,
        )

    first = [remote(top_d, met.at[0], 0, near_x), remote(low_d, met.at[1], 1, near_y)]
    direct = [remote(top_x, landed[0], 2, near_x), remote(low_y, landed[1], 3, near_y)]
    second = [remote(mid.at[0], landed[2], 4, near_y), remote(mid.at[1], landed[3], 5, near_x)]
    loads = []
    if top_y is not None:
        loads = [
            pltpu.make_async_copy(top_y, mid.at[0], load_sems.at[use, 0]),
            pltpu.make_async_copy(low_x, mid.at[1], load_sems.at[use, 1]),
        ]

    def open_sum():
        begin(first)
        begin(direct)
        begin(loads)

    def join_sum():
        finish(loads)
        for at in range(2):
            first[at].wait()

            def tile(i, carry, at=at):
                rows = pl.ds(pl.multiple_of(i * 64, 64), 64)
                mid[at, rows, :] = add_low(mid[at, rows, :], met[at, rows, :])
                return carry

            lax.fori_loop(0, BLK // 64, tile, 0)
        begin(second)

    def close_sum():
        finish(direct)
        finish(second)

    return open_sum, join_sum, close_sum


def weight_grads(
    act,
    grad_two_all,
    normed_two_all,
    grad_parts,
    back_sums,
    two_sums,
    middle,
    cotangent,
    out_weight,
    mix_weight,
    parts_all,
    mixing_all,
    states_all,
    gated,
    normed_all,
    live,
    keep,
):
    rows, units = act.shape
    width = grad_two_all.shape[1]
    local_rows = middle.shape[0]
    parts, _, columns = parts_all.shape
    heads = columns // HS
    low = jnp.bfloat16
    in_columns = grad_parts.shape[1] // TILE
    in_rows = width // PIECE
    out_blocks = units // SUB
    halves = width // 1024
    first_out = in_rows * in_columns
    first_branch = first_out + halves * out_blocks
    first_mix = first_branch + width // TILE
    per_row = columns // TILE
    per_part = in_rows * per_row
    count = first_mix + parts * per_part

    def body(*refs):
        act_in, two_in, normed_two_in, parts_in, back_in, two_sums_in = refs[:6]
        middle_in, cot_in, weight_in, mix_in = refs[6:10]
        all_in, mixing_in, states_in, gated_in, normed_in, live_ref, keep_ref = refs[10:17]
        in_grad, out_grad, branch_grad, mix_grad, branch_out, middle_out = refs[17:23]
        own_outs, last_landed, two_landed = refs[23:25], refs[25:29], refs[29:33]
        shared, wide_ref, act_ref, landed, stage_ref, mid_ref, grad_ref, branch = refs[33:41]
        near, gated_grad, states_ref = refs[41:44]
        normed_sems, parts_sems, load_sems, stage_sems, gather_sems, back_sems, head_sems, mix_sems = refs[44:52]
        tile_sems, own_sems = refs[52:54]
        line, square = refs[54:63], refs[63:67]
        mid = square[1]
        places = neighbours()
        narrow, near_x, near_y = places[1], places[5], places[6]
        enter(places)

        def block(at):
            return pl.ds(at * BLK, BLK)

        def cols(at, size):
            return pl.ds(pl.multiple_of(at, 128), size)

        def load_normed_two(at):
            here = cols(at * PIECE, PIECE)
            return pltpu.make_async_copy(normed_two_in.at[:, here], shared.at[:, here], normed_sems.at[at])

        def load_parts(at):
            here = cols(at * TILE, TILE)
            return pltpu.make_async_copy(parts_in.at[:, here], wide_ref.at[:, here], parts_sems.at[at])

        def load_half(src, half, sem):
            here = pl.ds(half * 1024, 1024)
            return pltpu.make_async_copy(src.at[:, here], shared.at[:, here], load_sems.at[sem])

        load_act = pltpu.make_async_copy(act_in, act_ref, load_sems.at[0])
        load_two = [load_half(two_in, half, 1 + half) for half in range(halves)]
        load_normed = [load_half(normed_in, half, 3 + half) for half in range(halves)]
        load_gated = pltpu.make_async_copy(gated_in.at[0], act_ref.at[:, pl.ds(0, columns)], load_sems.at[5])

        def load_branch(at):
            slot = at % 2
            return pltpu.make_async_copy(
                branch_out.at[:, cols(at * TILE, TILE)],
                act_ref.at[:, cols(columns + slot * TILE, TILE)],
                tile_sems.at[slot],
            )

        def product(k, own):
            def split_rows(result):
                for part in range(4):
                    own[part] = result[part * SUB : (part + 1) * SUB]

            @pl.when(k < first_out)
            def _():
                row, column = k // in_columns, k % in_columns

                @pl.when(column == 0)
                def _():
                    load_normed_two(row).wait()

                @pl.when(row == 0)
                def _():
                    load_parts(column).wait()

                here, there = cols(row * PIECE, PIECE), cols(column * TILE, TILE)
                split_rows(down(shared[:, here], wide_ref[:, there]).astype(low))

                @pl.when(k == first_out - in_columns)
                def _():
                    load_two[0].start()

            @pl.when(k == first_out)
            def _():
                begin(load_two[1:])
                load_act.wait()
                load_two[0].wait()

            @pl.when(k == first_out + out_blocks)
            def _():
                finish(load_two[1:])
                load_normed[0].start()

            @pl.when((k >= first_out) & (k < first_branch))
            def _():
                at = k - first_out
                here = cols((at % out_blocks) * SUB, SUB)
                there = cols((at // out_blocks) * 1024, 1024)
                result = down(act_ref[:, here], shared[:, there]).astype(low)
                for part in range(4):
                    own[part] = result[:, part * TILE : (part + 1) * TILE]

            @pl.when(k == first_branch)
            def _():
                load_branch(0).start()
                load_gated.start()
                begin(load_normed[1:])
                load_gated.wait()

            @pl.when((k >= first_branch) & (k < first_mix))
            def _():
                at = k - first_branch
                load_branch(at).wait()
                pl.when(k + 1 < first_mix)(lambda: load_branch(at + 1).start())
                there = cols(columns + (at % 2) * TILE, TILE)
                split_rows(down(act_ref[:, :columns], act_ref[:, there]).astype(low))

            @pl.when(k == first_mix)
            def _():
                finish(load_normed)

            @pl.when(k >= first_mix)
            def _():
                at = k - first_mix
                here = cols(((at // per_row) % in_rows) * PIECE, PIECE)
                there = cols((at // per_part) * columns + (at % per_row) * TILE, TILE)
                split_rows(down(shared[:, here], wide_ref[:, there]).astype(low))

        def targets(k, part):
            one = jnp.minimum(k, first_out - 1)
            two = jnp.clip(k - first_out, 0, first_branch - first_out - 1)
            three = jnp.clip(k - first_branch, 0, first_mix - first_branch - 1)
            four = jnp.maximum(k - first_mix, 0)
            return [
                (
                    k < first_out,
                    in_grad.at[(one // in_columns) * 4 + part, :, cols((one % in_columns) * TILE, TILE)],
                ),
                (
                    (k >= first_out) & (k < first_branch),
                    out_grad.at[two % out_blocks, :, cols((two // out_blocks) * 1024 + part * TILE, TILE)],
                ),
                (
                    (k >= first_branch) & (k < first_mix),
                    branch_grad.at[part, :, cols(three * TILE, TILE)],
                ),
                (
                    k >= first_mix,
                    mix_grad.at[(four // per_row) * 4 + part, :, cols((four % per_row) * TILE, TILE)],
                ),
            ]

        step = line_sum(line, places, count, product, targets)
        now = [0]

        def run(steps):
            lax.fori_loop(now[0], now[0] + steps, step, 0)
            now[0] += steps

        open_sum, join_sum, close_sum = square_sum(
            square,
            places,
            [back_in.at[block(at)] for at in range(2, 8)],
            [landed.at[at] for at in range(4)],
            0,
        )
        load_normed_two(0).start()
        load_parts(0).start()
        open_sum()
        for at in range(1, in_columns):
            load_parts(at).start()
        for at in range(1, in_rows):
            load_normed_two(at).start()
        load_act.start()

        def spread(src, slot, kind, place):
            return pltpu.make_async_remote_copy(
                src_ref=src,
                dst_ref=branch_out.at[block(slot)],
                send_sem=gather_sems.at[kind, 0],
                recv_sem=gather_sems.at[kind, 1],
                device_id=place,
                device_id_type=MESH,
            )

        def stage(half):
            return [
                pltpu.make_async_copy(back_in.at[block(half)], stage_ref.at[0], stage_sems.at[0]),
                pltpu.make_async_copy(cot_in.at[block(half)], stage_ref.at[1], stage_sems.at[1]),
                pltpu.make_async_copy(middle_in.at[block(half)], mid_ref, stage_sems.at[2]),
            ]

        keep_branch = [
            pltpu.make_async_copy(branch.at[at], branch_out.at[block(at)], stage_sems.at[3 + at])
            for at in range(2)
        ]

        def rows_back(half):
            def tile(i, carry):
                at = pl.ds(pl.multiple_of(i * 32, 32), 32)
                grad = add_rows(stage_ref[0, at, :], landed[half, at, :], landed[2 + half, at, :])
                result = stage_ref[1, at, :].astype(jnp.float32) + norm_back(mid_ref[at, :], grad)
                grad_ref[at, :] = result
                live_at = pl.ds(pl.multiple_of(half * BLK + i * 32, 32), 32)
                branch[half, at, :] = (live_ref[live_at, :1] * result).astype(low)
                return carry

            lax.fori_loop(0, BLK // 32, tile, 0)
            copy = pltpu.make_async_copy(grad_ref, middle_out.at[block(half)], stage_sems.at[5])
            copy.start()
            return copy

        sends = [
            spread(branch.at[0], 2, 0, near_x),
            spread(branch.at[1], 3, 1, near_y),
            spread(branch.at[1], 4, 2, near_x),
            spread(branch.at[0], 5, 3, near_y),
        ]
        later = [
            spread(branch_out.at[block(3)], 7, 4, near_x),
            spread(branch_out.at[block(2)], 6, 5, near_y),
        ]
        run(9)
        join_sum()
        begin(stage(0))
        run(16)
        close_sum()
        finish(stage(0))
        written = rows_back(0)
        sends[0].start()
        begin(stage(1))
        finish(stage(1))
        written.wait()
        written = rows_back(1)
        begin(sends[1:])
        begin(keep_branch)
        run(8)
        sends[0].wait_recv()
        sends[1].wait_recv()
        begin(later)
        run(17)
        written.wait()
        finish(keep_branch)
        for copy in sends[:2]:
            copy.wait_send()
        finish(sends[2:])
        finish(later)

        open_two, join_two, close_two = square_sum(
            square, places, [two_sums_in.at[block(at)] for at in range(2, 8)], two_landed, 1
        )
        open_two()

        def head_loads(head):
            here = cols(head * HS, HS)
            loads = [
                pltpu.make_async_copy(
                    all_in.at[c, :, here],
                    wide_ref.at[:, pl.ds(parts * columns + c * HS, HS)],
                    head_sems.at[c],
                )
                for c in range(parts)
            ]
            loads.append(
                pltpu.make_async_copy(
                    mixing_in.at[:, here],
                    wide_ref.at[:, pl.ds(parts * columns + parts * HS, HS)],
                    head_sems.at[parts],
                )
            )
            loads.append(pltpu.make_async_copy(states_in.at[head], states_ref, head_sems.at[parts + 1]))
            return loads

        weight_loads = [
            pltpu.make_async_copy(weight_in.at[block(at)], landed.at[at], back_sems.at[at])
            for at in range(columns // BLK)
        ]

        def row_load(at):
            here = pl.ds(pl.multiple_of(at * BLK, BLK), BLK)
            return pltpu.make_async_copy(branch_out.at[here], stage_ref.at[at % 2], back_sems.at[2 + at % 2])

        begin(weight_loads)
        row_load(0).start()
        begin(head_loads(0))
        finish(weight_loads)
        back_from = now[0]

        def back_block(at, carry):
            step(back_from + at, 0)
            row_load(at).wait()
            pl.when(at + 1 < rows // BLK)(lambda: row_load(at + 1).start())
            here = pl.ds(pl.multiple_of(at * BLK, BLK), BLK)
            for part in range(len(weight_loads)):
                result = across(stage_ref[at % 2], landed[part])
                gated_grad[here, part * BLK : (part + 1) * BLK] = result.astype(low)
            return carry

        lax.fori_loop(0, rows // BLK, back_block, 0)
        now[0] += rows // BLK
        join_two()

        def load_mix(at):
            here = pl.ds(pl.multiple_of(at * BLK, BLK), BLK)
            slot = at % 4
            return [
                pltpu.make_async_copy(
                    mix_in.at[c, here, :], landed.at[slot, :, pl.ds(c * columns, columns)], mix_sems.at[slot, c]
                )
                for c in range(parts)
            ]

        for at in range(4):
            begin(load_mix(at))
        attend_from = now[0]

        def attend(head, carry):
            rate = head_rate(heads * narrow + head)
            within, entry, leave, whole = block_decays(rate)
            finish(head_loads(head))
            later_grad = jnp.zeros((HS, HS), jnp.float32)
            base = parts * columns
            for at in range(NBLK):
                block_at = NBLK - 1 - at
                here = pl.ds(pl.multiple_of(slot_of(block_at, narrow) * BLK, BLK), BLK)

                def load(c, here=here):
                    return wide_ref[here, base + c * HS : base + (c + 1) * HS]

                def store(c, value, here=here):
                    wide_ref[here, cols(c * columns + head * HS, HS)] = value.astype(low)

                raw_queries = load(0).astype(jnp.float32)
                raw_keys = load(1).astype(jnp.float32)
                queries, keys = jax.nn.silu(raw_queries).astype(low), jax.nn.silu(raw_keys).astype(low)
                values = load(2)
                gate = load(3).astype(jnp.float32)
                mixing = load(4).astype(jnp.float32)
                grad_rows = gated_grad[here, cols(head * HS, HS)].astype(jnp.float32)
                scale = lax.rsqrt(jnp.mean(mixing * mixing, axis=-1, keepdims=True) + head_floor)
                headed = mixing * scale
                store(3, grad_rows * headed)
                grad_headed = grad_rows * gate
                inner = jnp.mean(grad_headed * headed, axis=-1, keepdims=True)
                grad = (scale * (grad_headed - headed * inner)).astype(low)
                scores = (across(queries, keys) * within).astype(low)
                grad_scores = (across(grad, values) * within).astype(low)
                later_low = later_grad.astype(low)
                grad_queries = straight(grad_scores, keys) + entry * across(grad, states_ref[block_at])
                grad_keys = down(grad_scores, queries) + leave * across(values, later_low)
                grad_values = down(scores, grad) + leave * straight(keys, later_low)
                early_queries = (queries.astype(jnp.float32) * entry).astype(low)
                later_grad = keep_ref[block_at : block_at + 1, :1] * (
                    whole * later_grad + down(early_queries, grad)
                )
                store(0, grad_queries * silu_slope(raw_queries))
                store(1, grad_keys * silu_slope(raw_keys))
                store(2, grad_values)
                if at % 2:
                    step(attend_from + head * (NBLK // 2) + at // 2, 0)
            pl.when(head + 1 < heads)(lambda: begin(head_loads(head + 1)))
            return carry

        lax.fori_loop(0, heads, attend, 0)
        now[0] += heads * (NBLK // 2)

        sum_from = now[0]
        outs = ((3, branch, False), (1, near, False), (2, mid, True), (0, stage_ref, False))

        def sum_tile(at, carry):
            finish(load_mix(at))
            here = cols(at * BLK, BLK)
            for piece, out, swapped in outs:
                acts = wide_ref[piece * PIECE : (piece + 1) * PIECE, : parts * columns]
                total = across(acts, landed[at % 4]).astype(low)
                out[int(swapped), :, here] = total[:HALF]
                out[1 - int(swapped), :, here] = total[HALF:]
            pl.when(at + 4 < width // BLK)(lambda: begin(load_mix(at + 4)))
            step(sum_from + at, 0)
            return carry

        close_two()
        lax.fori_loop(0, width // BLK, sum_tile, 0)
        now[0] += width // BLK
        open_last, join_last, close_last = square_sum(
            square,
            places,
            (near.at[0], near.at[1], None, None, branch.at[0], branch.at[1]),
            last_landed,
            2,
        )
        own_stores = [
            pltpu.make_async_copy(stage_ref.at[at], own_outs[at], own_sems.at[at]) for at in range(2)
        ]
        open_last()
        begin(own_stores)
        run(9)
        join_last()
        run(count + STAGES - now[0])
        close_last()
        finish(own_stores)

    def low_shape(*shape):
        return jax.ShapeDtypeStruct(shape, low)

    sem = pltpu.SemaphoreType.DMA
    return pl.pallas_call(
        body,
        in_specs=any_specs(15) + [pl.BlockSpec(memory_space=pltpu.VMEM)] * 2,
        out_specs=any_specs(16),
        out_shape=[
            low_shape(width // SUB, SUB, grad_parts.shape[1]),
            low_shape(out_blocks, SUB, width),
            low_shape(columns // SUB, SUB, width),
            low_shape(parts * width // SUB, SUB, columns),
            low_shape(rows, width),
            jax.ShapeDtypeStruct((local_rows, width), jnp.float32),
        ]
        + [low_shape(BLK, width)] * 10,
        scratch_shapes=[
            pltpu.VMEM((rows, width), low),
            pltpu.VMEM(grad_parts.shape, low),
            pltpu.VMEM(act.shape, low),
            pltpu.VMEM((4, BLK, width), low),
            pltpu.VMEM((2, BLK, width), low),
            pltpu.VMEM((BLK, width), jnp.float32),
            pltpu.VMEM((BLK, width), jnp.float32),
            pltpu.VMEM((2, BLK, width), low),
            pltpu.VMEM((2, BLK, width), low),
            pltpu.VMEM((rows, columns), low),
            pltpu.VMEM((NBLK, HS, HS), low),
            sem((in_rows,)),
            sem((in_columns,)),
            sem((6,)),
            sem((6,)),
            sem((6, 2)),
            sem((4,)),
            sem((parts + 2,)),
            sem((4, parts)),
            sem((2,)),
            sem((2,)),
        ]
        + line_scratch()
        + square_scratch(3),
        compiler_params=pltpu.CompilerParams(
            vmem_limit_bytes=VMEM, collective_id=1, has_side_effects=True
        ),
        cost_estimate=cost(2 * rows * width * (3 * units + 9 * columns), 120e6),
        name="weight_grads",
    )(
        act,
        grad_two_all,
        normed_two_all,
        grad_parts,
        back_sums,
        two_sums,
        middle,
        cotangent,
        out_weight,
        mix_weight,
        parts_all,
        mixing_all,
        states_all,
        gated,
        normed_all,
        live,
        keep,
    )


def gated_unit(gated, whole_weight, hidden, live, grads_own, grads_first, ffn_in, ffn_out):
    _, width, units = ffn_in.shape
    local_rows = hidden.shape[0]
    group_rows = NBLK * BLK
    pieces = group_rows // PIECE
    deep = gated.shape[2]
    slices, quarters, slice_rows, _ = whole_weight.shape
    main = units // TILE * TILE
    tail = units - main
    low = jnp.bfloat16
    cuts = ((0, 2 * TILE), (2 * TILE, main - 2 * TILE))
    wide_tile = 1024
    first_half, second_half = pl.ds(0, HALF), pl.ds(HALF, HALF)

    def body(*refs):
        gated_in, weight_in, hidden_in = refs[:3]
        grad_in = refs[3:5]
        in_ref, out_ref, live_ref = refs[5:8]
        middle_out, rows_out, grads_out, act_out, parts_out, back_out, two_out = refs[8:15]
        gated_ref, hidden_ref, middle_ref = refs[15:18]
        rows, grads, sums, w_in, w_out, act, parts = refs[18:25]
        load_sems, slice_sems, weight_sems, done_sems, sum_sems, gated_sems, gather_sems = refs[25:]
        wide, narrow, _, _, _, near_x, near_y = neighbours()
        far = (wide, 3 - narrow)
        barrier = pltpu.get_barrier_semaphore()
        for place in (near_x, near_y, far):
            pl.semaphore_signal(barrier, inc=1, device_id=place, device_id_type=MESH)
        pl.semaphore_wait(barrier, 3)

        here = pl.ds(pl.multiple_of(narrow * deep, deep), deep)

        def send_gated(slot, to, kind, place):
            return pltpu.make_async_remote_copy(
                src_ref=gated_in.at[0, pl.ds(slot * BLK, BLK)],
                dst_ref=gated_ref.at[(first_half, second_half)[to], here],
                send_sem=gated_sems.at[kind, 0],
                recv_sem=gated_sems.at[kind, 1],
                device_id=place,
                device_id_type=MESH,
            )

        gated_sends = [
            send_gated(6, 0, 0, far),
            send_gated(7, 1, 1, far),
            send_gated(2, 0, 2, near_x),
            send_gated(3, 1, 3, near_y),
            send_gated(4, 1, 4, near_x),
            send_gated(5, 0, 5, near_y),
        ]
        keep_gated = pltpu.make_async_copy(
            gated_in.at[0, pl.ds(0, PIECE)], gated_ref.at[:, here], load_sems.at[0]
        )

        def load_slice(at):
            part, quarter = at // quarters, at % quarters
            to = pl.ds(pl.multiple_of(quarter * deep + part * slice_rows, slice_rows), slice_rows)
            return pltpu.make_async_copy(
                weight_in.at[part, quarter], w_in.at[to, pl.ds(0, width)], slice_sems.at[at]
            )

        def start_slice(at, carry):
            load_slice(at).start()
            return carry

        def wait_slice(at, carry):
            load_slice(at).wait()
            return carry

        load_hidden = pltpu.make_async_copy(hidden_in, hidden_ref, load_sems.at[1])
        load_grads = [
            pltpu.make_async_copy(src, grads.at[at], load_sems.at[2 + at])
            for at, src in enumerate(grad_in)
        ]
        weights = []
        for start, size, first, second in tuple((a, b, a, main + a) for a, b in cuts) + (
            (main, tail, 2 * main, 2 * main + tail),
        ):
            at = pl.ds(start, size)
            weights += [
                pltpu.make_async_copy(in_ref.at[0, :, at], w_in.at[:, pl.ds(first, size)], weight_sems.at[len(weights)]),
                pltpu.make_async_copy(in_ref.at[1, :, at], w_in.at[:, pl.ds(second, size)], weight_sems.at[len(weights) + 1]),
                pltpu.make_async_copy(out_ref.at[at, :], w_out.at[at, :], weight_sems.at[len(weights) + 2]),
            ]

        def remote(src, dst, sems, kind, place):
            return pltpu.make_async_remote_copy(
                src_ref=src,
                dst_ref=dst,
                send_sem=sems.at[kind, 0],
                recv_sem=sems.at[kind, 1],
                device_id=place,
                device_id_type=MESH,
            )

        def half(ref, piece, at):
            return ref.at[piece, (first_half, second_half)[at]]

        def gather(ref, kind):
            return (
                [
                    remote(half(ref, 0, 0), half(ref, 1, 0), gather_sems, kind, near_x),
                    remote(half(ref, 0, 1), half(ref, 1, 1), gather_sems, kind + 1, near_y),
                ],
                [
                    remote(half(ref, 0, 1), half(ref, 2, 0), gather_sems, kind + 2, near_x),
                    remote(half(ref, 0, 0), half(ref, 2, 1), gather_sems, kind + 3, near_y),
                ],
                [
                    remote(half(ref, 1, 1), half(ref, 3, 1), gather_sems, kind + 4, near_x),
                    remote(half(ref, 1, 0), half(ref, 3, 0), gather_sems, kind + 5, near_y),
                ],
            )

        row_sends = gather(rows, 0)
        grad_sends = gather(grads, 6)

        begin(gated_sends)
        begin([keep_gated])
        lax.fori_loop(0, slices * quarters, start_slice, 0)
        begin(load_grads)
        begin([load_hidden])
        finish(load_grads)
        begin(grad_sends[1])
        finish([keep_gated, load_hidden])
        lax.fori_loop(0, slices * quarters, wait_slice, 0)
        finish(gated_sends)
        for j in range(width // wide_tile):
            at = slice(j * wide_tile, (j + 1) * wide_tile)
            middle_ref[:, at] = straight(gated_ref[...], w_in[:, at])
        begin(weights)

        def second_norm(i, carry, at):
            here = pl.ds(pl.multiple_of(at * HALF + i * 32, 32), 32)
            middle = hidden_ref[here, :].astype(jnp.float32) + live_ref[here, :1] * middle_ref[here, :]
            middle_ref[here, :] = middle
            rows[0, here, :] = row_norm(middle).astype(low)
            return carry

        for at in range(2):
            lax.fori_loop(0, HALF // 32, functools.partial(second_norm, at=at), 0)
            row_sends[0][at].start()
        begin(row_sends[1])
        begin(grad_sends[2])
        store_middle = pltpu.make_async_copy(middle_ref, middle_out, done_sems.at[0])
        store_middle.start()

        def products(at, first, second, part_a, part_b, grad_act):
            act[:, at] = (part_a * part_b).astype(low)
            parts[:, first] = (grad_act * part_b).astype(low)
            parts[:, second] = (grad_act * part_a).astype(low)

        def sum_stores(piece, j):
            tile = pl.ds(j * wide_tile, wide_tile)
            return [
                pltpu.make_async_copy(
                    sums.at[at, :, tile],
                    (back_out, two_out)[at // 2].at[
                        pl.ds(pl.multiple_of(piece * PIECE + (at % 2) * HALF, HALF), HALF), tile
                    ],
                    sum_sems.at[j, at],
                )
                for at in range(4)
            ]

        def work(piece, carry):
            spot = pl.ds(pl.multiple_of(piece * PIECE, PIECE), PIECE)
            arrived, arrived_grads = rows.at[piece], grads.at[piece]

            @pl.when(piece == 1)
            def _():
                finish(row_sends[0])
                begin(row_sends[2])

            @pl.when(piece == 2)
            def _():
                finish(row_sends[1])
                finish(grad_sends[1])

            @pl.when(piece == 3)
            def _():
                finish(row_sends[2])
                finish(grad_sends[2])

            stores = [
                pltpu.make_async_copy(arrived, rows_out.at[spot, :], done_sems.at[1]),
                pltpu.make_async_copy(arrived_grads, grads_out.at[spot, :], done_sems.at[2]),
            ]
            begin(stores)
            for which, (start, size) in enumerate(cuts):
                at, second = slice(start, start + size), slice(main + start, main + start + size)

                @pl.when(piece == 0)
                def _(which=which):
                    finish(weights[3 * which : 3 * which + 3])

                part_a = straight(arrived[...], w_in[:, at])
                part_b = straight(arrived[...], w_in[:, second])
                grad_act = across(arrived_grads[...], w_out[at, :])
                products(at, at, second, part_a, part_b, grad_act)

            @pl.when(piece == 0)
            def _():
                finish(weights[6:])

            if tail:
                both = straight(arrived[...], w_in[:, 2 * main :])
                grad_act = across(arrived_grads[...], w_out[main:, :])
                products(
                    slice(main, units),
                    slice(2 * main, 2 * main + tail),
                    slice(2 * main + tail, 2 * units),
                    both[:, :tail],
                    both[:, tail:],
                    grad_act,
                )
            stores += [
                pltpu.make_async_copy(act, act_out.at[spot, :], done_sems.at[3]),
                pltpu.make_async_copy(parts, parts_out.at[spot, :], done_sems.at[4]),
            ]
            begin(stores[2:])
            for j in range(width // wide_tile):
                at = slice(j * wide_tile, (j + 1) * wide_tile)

                @pl.when(piece > 0)
                def _(j=j):
                    finish(sum_stores(piece - 1, j))

                back = across(parts[...], w_in[at, :])
                sums[0, :, at] = back[:HALF].astype(low)
                sums[1, :, at] = back[HALF:].astype(low)
                two = straight(act[...], w_out[:, at])
                sums[2, :, at] = two[:HALF].astype(low)
                sums[3, :, at] = two[HALF:].astype(low)
                begin(sum_stores(piece, j))
            finish(stores)
            return carry

        lax.fori_loop(0, pieces, work, 0)
        for j in range(width // wide_tile):
            finish(sum_stores(pieces - 1, j))
        store_middle.wait()

    return pl.pallas_call(
        body,
        in_specs=any_specs(7) + [pl.BlockSpec(memory_space=pltpu.VMEM)],
        out_specs=any_specs(7),
        out_shape=[
            jax.ShapeDtypeStruct((local_rows, width), jnp.float32),
            jax.ShapeDtypeStruct((group_rows, width), low),
            jax.ShapeDtypeStruct((group_rows, width), low),
            jax.ShapeDtypeStruct((group_rows, units), low),
            jax.ShapeDtypeStruct((group_rows, 2 * units), low),
            jax.ShapeDtypeStruct((group_rows, width), low),
            jax.ShapeDtypeStruct((group_rows, width), low),
        ],
        scratch_shapes=[
            pltpu.VMEM((local_rows, quarters * deep), low),
            pltpu.VMEM((local_rows, width), low),
            pltpu.VMEM((local_rows, width), jnp.float32),
            pltpu.VMEM((pieces, PIECE, width), low),
            pltpu.VMEM((pieces, PIECE, width), low),
            pltpu.VMEM((4, HALF, width), low),
            pltpu.VMEM((width, 2 * units), low),
            pltpu.VMEM((units, width), low),
            pltpu.VMEM((PIECE, units), low),
            pltpu.VMEM((PIECE, 2 * units), low),
            pltpu.SemaphoreType.DMA((4,)),
            pltpu.SemaphoreType.DMA((slices * quarters,)),
            pltpu.SemaphoreType.DMA((9,)),
            pltpu.SemaphoreType.DMA((5,)),
            pltpu.SemaphoreType.DMA((width // wide_tile, 4)),
            pltpu.SemaphoreType.DMA((6, 2)),
            pltpu.SemaphoreType.DMA((12, 2)),
        ],
        compiler_params=pltpu.CompilerParams(
            vmem_limit_bytes=VMEM, collective_id=3, has_side_effects=True
        ),
        cost_estimate=cost(12 * group_rows * width * units, 90e6),
        name="gated_unit",
    )(gated, whole_weight, hidden, grads_own, grads_first, ffn_in, ffn_out, live)


def mix_rows(hidden, cotangent, mix_weight, out_weight, live, keep):
    local_rows, width = hidden.shape
    parts, _, columns = mix_weight.shape
    heads = columns // HS
    group_rows = NBLK * BLK
    pieces = group_rows // PIECE
    wide_size = lax.axis_size("wide")
    slice_rows = columns // wide_size
    low = jnp.bfloat16
    joined = 2
    halves_at = (pl.ds(0, HALF), pl.ds(HALF, HALF))

    def body(*refs):
        hidden_in, cot_in, mix_in, out_in, live_ref, keep_ref = refs[:6]
        rows_out, parts_out, gated_out, mixing_out, states_out, grads_out, first_out, whole_out = refs[6:14]
        hidden_ref, cot_ref, rows, weights, parts_ref, gated_ref, mixing_ref, states_ref = refs[14:22]
        load_sems, mix_sems, store_sems, parts_sems, gather_sems, slice_sems, line_sems, core_sems = refs[22:]
        wide, narrow, z, core, mate, near_x, near_y = neighbours()
        far = (wide, 3 - narrow)
        above, below = (wide + 2, narrow), (wide - 2, narrow)
        barrier = pltpu.get_barrier_semaphore()

        def greet(place):
            pl.semaphore_signal(barrier, inc=1, device_id=place, device_id_type=MESH)

        load_hidden = pltpu.make_async_copy(hidden_in, hidden_ref, load_sems.at[0])
        load_cot = pltpu.make_async_copy(cot_in, cot_ref, load_sems.at[1])
        mix_loads = [
            pltpu.make_async_copy(
                mix_in.at[c], weights.at[:, pl.ds(c * columns, columns)], mix_sems.at[c]
            )
            for c in range(parts)
        ]
        load_hidden.start()
        for place in (near_x, near_y, far, mate):
            greet(place)
        pl.when(z < 3)(lambda: greet(above))
        pl.when(z > 0)(lambda: greet(below))
        middle = (z == 1) | (z == 2)
        pl.when(middle)(lambda: pl.semaphore_wait(barrier, 6))
        pl.when(jnp.logical_not(middle))(lambda: pl.semaphore_wait(barrier, 5))

        def remote(src, dst, sems, kind, place):
            return pltpu.make_async_remote_copy(
                src_ref=src,
                dst_ref=dst,
                send_sem=sems.at[kind, 0],
                recv_sem=sems.at[kind, 1],
                device_id=place,
                device_id_type=MESH,
            )

        slice_at = out_in.at[pl.ds(pl.multiple_of(wide * slice_rows, slice_rows), slice_rows)]
        keep_slice = pltpu.make_async_copy(slice_at, whole_out.at[wide, narrow], load_sems.at[2])
        slice_sends = [
            remote(slice_at, whole_out.at[wide, narrow], slice_sems, at, place)
            for at, place in enumerate((far, near_x, near_y))
        ]

        def up(hop):
            return remote(
                whole_out.at[wide - 2 * (hop - 1)], whole_out.at[wide - 2 * (hop - 1)], line_sems, hop - 1, above
            )

        def down_line(hop):
            return remote(
                whole_out.at[wide + 2 * (hop - 1)], whole_out.at[wide + 2 * (hop - 1)], line_sems, 2 + hop, below
            )

        def to_mate(hop, sign):
            at = wide + sign * 2 * hop
            return remote(whole_out.at[at], whole_out.at[at], core_sems, 3 + sign * hop, mate)

        def send_hop(hop):
            pl.when((z < 3) & (z >= hop - 1))(lambda: up(hop).start())
            pl.when((z > 0) & (z + hop - 1 <= 3))(lambda: down_line(hop).start())

        def take_hop(hop):
            @pl.when(z >= hop)
            def _():
                up(hop).wait_recv()
                to_mate(hop, -1).start()

            @pl.when(z + hop <= 3)
            def _():
                down_line(hop).wait_recv()
                to_mate(hop, 1).start()

        def end_hop(hop):
            pl.when((z < 3) & (z >= hop - 1))(lambda: up(hop).wait_send())
            pl.when((z > 0) & (z + hop - 1 <= 3))(lambda: down_line(hop).wait_send())
            pl.when(z >= hop)(lambda: to_mate(hop, -1).wait())
            pl.when(z + hop <= 3)(lambda: to_mate(hop, 1).wait())

        begin(slice_sends)
        keep_slice.start()

        def half(piece, at):
            return rows.at[piece, halves_at[at]]

        row_sends = (
            [remote(half(0, 0), half(1, 0), gather_sems, 0, near_x), remote(half(0, 1), half(1, 1), gather_sems, 1, near_y)],
            [remote(half(0, 1), half(2, 0), gather_sems, 2, near_x), remote(half(0, 0), half(2, 1), gather_sems, 3, near_y)],
            [remote(half(1, 1), half(3, 1), gather_sems, 4, near_x), remote(half(1, 0), half(3, 0), gather_sems, 5, near_y)],
        )
        grad_sends = [
            remote(cot_ref.at[halves_at[0]], first_out.at[halves_at[0]], gather_sems, 6, near_x),
            remote(cot_ref.at[halves_at[1]], first_out.at[halves_at[1]], gather_sems, 7, near_y),
        ]
        load_hidden.wait()
        begin(mix_loads)
        load_cot.start()

        def first_norm(i, carry):
            at = pl.ds(pl.multiple_of(i * 32, 32), 32)
            rows[0, at, :] = row_norm(hidden_ref[at, :].astype(jnp.float32)).astype(low)
            return carry

        for at in range(2):
            lax.fori_loop(at * HALF // 32, (at + 1) * HALF // 32, first_norm, 0)
            row_sends[0][at].start()
        begin(row_sends[1])

        def row_store(piece):
            at = pl.ds(piece * PIECE, PIECE)
            return pltpu.make_async_copy(rows.at[piece], rows_out.at[at, :], store_sems.at[piece])

        def part_stores(piece):
            at = pl.ds(piece * PIECE, PIECE)
            return [
                pltpu.make_async_copy(
                    parts_ref.at[at, pl.ds(c * columns, columns)], parts_out.at[c, at, :], parts_sems.at[piece, c]
                )
                for c in range(parts)
            ]

        def project(piece):
            row_store(piece).start()
            for c in range(0, parts, joined):
                if piece == 0:
                    finish(mix_loads[c : c + joined])
                at = slice(c * columns, (c + joined) * columns)
                result = straight(rows[piece], weights[:, at]).astype(low)
                parts_ref[piece * PIECE : (piece + 1) * PIECE, at] = result
            begin(part_stores(piece))

        project(0)
        load_cot.wait()

        def live_cot(i, carry):
            at = pl.ds(pl.multiple_of(i * 32, 32), 32)
            cot_ref[at, :] = (live_ref[at, :1] * cot_ref[at, :].astype(jnp.float32)).astype(low)
            return carry

        keep_slice.wait()
        finish(slice_sends)
        to_mate(0, 1).start()
        send_hop(1)
        lax.fori_loop(0, local_rows // 32, live_cot, 0)
        store_grads = pltpu.make_async_copy(cot_ref, grads_out, load_sems.at[3])
        store_grads.start()
        finish(row_sends[0])
        begin(row_sends[2])
        begin(grad_sends)
        project(1)
        take_hop(1)
        send_hop(2)
        finish(row_sends[1])
        project(2)
        take_hop(2)
        send_hop(3)
        finish(row_sends[2])
        project(3)

        def attend(head, carry):
            within, entry, leave, whole = block_decays(head_rate(heads * narrow + head))
            state = jnp.zeros((HS, HS), jnp.float32)

            def part(c, rows_at):
                at = pl.ds(pl.multiple_of(c * columns + head * HS, HS), HS)
                return parts_ref[rows_at, at]

            for block in range(NBLK):
                rows_at = pl.ds(pl.multiple_of(slot_of(block, narrow) * BLK, BLK), BLK)
                queries = jax.nn.silu(part(0, rows_at).astype(jnp.float32)).astype(low)
                keys = jax.nn.silu(part(1, rows_at).astype(jnp.float32)).astype(low)
                values = part(2, rows_at)
                gate = part(3, rows_at).astype(jnp.float32)
                state = keep_ref[block : block + 1, :] * state
                state_low = state.astype(low)
                states_ref[head, block] = state_low
                scores = (across(queries, keys) * within).astype(low)
                mixing = straight(scores, values) + entry * straight(queries, state_low)
                late_keys = (keys.astype(jnp.float32) * leave).astype(low)
                state = whole * state + down(late_keys, values)
                scale = lax.rsqrt(jnp.mean(mixing * mixing, axis=-1, keepdims=True) + head_floor)
                at = pl.ds(pl.multiple_of(head * HS, HS), HS)
                gated_ref[rows_at, at] = (mixing * scale * gate).astype(low)
                mixing_ref[rows_at, at] = mixing.astype(low)
            return carry

        lax.fori_loop(0, heads // 2, attend, 0)
        take_hop(3)
        lax.fori_loop(heads // 2, heads, attend, 0)
        stores = [
            pltpu.make_async_copy(gated_ref, gated_out.at[0], load_sems.at[4]),
            pltpu.make_async_copy(mixing_ref, mixing_out, load_sems.at[5]),
            pltpu.make_async_copy(states_ref, states_out, load_sems.at[6]),
        ]
        begin(stores)
        to_mate(0, 1).wait()
        for hop in range(1, 4):
            end_hop(hop)
        finish(grad_sends)
        store_grads.wait()
        for piece in range(pieces):
            row_store(piece).wait()
            finish(part_stores(piece))
        finish(stores)

    low_shape = functools.partial(jax.ShapeDtypeStruct, dtype=low)
    return pl.pallas_call(
        body,
        in_specs=any_specs(4) + [pl.BlockSpec(memory_space=pltpu.VMEM)] * 2,
        out_specs=any_specs(8),
        out_shape=[
            low_shape((group_rows, width)),
            low_shape((parts, group_rows, columns)),
            low_shape((1, group_rows, columns)),
            low_shape((group_rows, columns)),
            low_shape((heads, NBLK, HS, HS)),
            low_shape((local_rows, width)),
            low_shape((local_rows, width)),
            low_shape((wide_size, pieces, slice_rows, width)),
        ],
        scratch_shapes=[
            pltpu.VMEM((local_rows, width), low),
            pltpu.VMEM((local_rows, width), low),
            pltpu.VMEM((pieces, PIECE, width), low),
            pltpu.VMEM((width, parts * columns), low),
            pltpu.VMEM((group_rows, parts * columns), low),
            pltpu.VMEM((group_rows, columns), low),
            pltpu.VMEM((group_rows, columns), low),
            pltpu.VMEM((heads, NBLK, HS, HS), low),
            pltpu.SemaphoreType.DMA((7,)),
            pltpu.SemaphoreType.DMA((parts,)),
            pltpu.SemaphoreType.DMA((pieces,)),
            pltpu.SemaphoreType.DMA((pieces, parts)),
            pltpu.SemaphoreType.DMA((8, 2)),
            pltpu.SemaphoreType.DMA((3, 2)),
            pltpu.SemaphoreType.DMA((6, 2)),
            pltpu.SemaphoreType.DMA((7, 2)),
        ],
        compiler_params=pltpu.CompilerParams(
            vmem_limit_bytes=VMEM, collective_id=4, has_side_effects=True
        ),
        cost_estimate=cost(2 * group_rows * parts * width * columns, 50e6),
        name="mix_rows",
    )(hidden, cotangent, mix_weight, out_weight, live, keep)


def finish_rows(
    mix_low, out_low, in_low, wide_low, hidden, middle, grad_middle, live, normed_terms, two_sums, two_terms
):
    parts, width, columns = mix_low.shape
    local_rows = hidden.shape[0]
    units = wide_low.shape[0]
    main = units // TILE * TILE
    tail = units - main
    steps = 2 * parts
    tile, out_tile = local_rows // steps, out_low.shape[0] // steps
    in_tile, unit_tile, mix_tile = width // steps, units // steps, width // 2
    half_steps = steps // 2
    terms = len(normed_terms) + len(two_terms)

    def body(
        mix_ref, out_ref, in_ref, wide_ref, hidden_ref, middle_ref, grad_ref, live_ref, own_ref, *refs
    ):
        term_refs = refs[:terms]
        mix_out, out_out, in_out, wide_out, layer_ref, input_ref = refs[terms:]
        mix_out[...] = mix_ref[...].astype(jnp.float32)
        out_out[...] = out_ref[...].astype(jnp.float32)
        wide_out[...] = wide_ref[...].astype(jnp.float32)
        for c in range(2):
            in_out[c, :, :main] = in_ref[:, c * main : (c + 1) * main].astype(jnp.float32)
            rest = slice(2 * main + c * tail, 2 * main + (c + 1) * tail)
            in_out[c, :, main:] = in_ref[:, rest].astype(jnp.float32)

        def rows_of(half):
            normed = add_rows(*(ref[...] for ref in term_refs[3 * half : 3 * half + 3]))
            two = add_rows(*(ref[...] for ref in term_refs[6 + 2 * half : 8 + 2 * half]), own_ref[...])
            layer = middle_ref[...] + live_ref[:, :1] * two
            layer_ref[...] = layer.astype(jnp.bfloat16)
            back = norm_back(hidden_ref[...].astype(jnp.float32), normed)
            input_ref[...] = (grad_ref[...] + back).astype(jnp.bfloat16)

        first = pl.program_id(0) < half_steps
        pl.when(first)(lambda: rows_of(0))
        pl.when(jnp.logical_not(first))(lambda: rows_of(1))

    def rows_spec(size, height=tile):
        return pl.BlockSpec((height, size), lambda i: (i, 0))

    def half_spec(half):
        if half == 0:
            return pl.BlockSpec((tile, width), lambda i: (jnp.minimum(i, half_steps - 1), 0))
        return pl.BlockSpec((tile, width), lambda i: (jnp.maximum(i - half_steps, 0), 0))

    term_specs = [half_spec(0)] * 3 + [half_spec(1)] * 3 + [half_spec(0)] * 2 + [half_spec(1)] * 2
    mix_spec = pl.BlockSpec((1, mix_tile, columns), lambda i: (i // 2, i % 2, 0))
    out_spec = rows_spec(width, out_tile)
    wide_spec = rows_spec(width, unit_tile)
    wide_float = jnp.float32
    return pl.pallas_call(
        body,
        grid=(steps,),
        in_specs=[mix_spec, out_spec, rows_spec(2 * units, in_tile), wide_spec]
        + [rows_spec(width)] * 3
        + [rows_spec(live.shape[1]), rows_spec(width)]
        + term_specs,
        out_specs=[
            mix_spec,
            out_spec,
            pl.BlockSpec((2, in_tile, units), lambda i: (0, i, 0)),
            wide_spec,
            rows_spec(width),
            rows_spec(width),
        ],
        out_shape=[
            jax.ShapeDtypeStruct(mix_low.shape, wide_float),
            jax.ShapeDtypeStruct(out_low.shape, wide_float),
            jax.ShapeDtypeStruct((2, width, units), wide_float),
            jax.ShapeDtypeStruct(wide_low.shape, wide_float),
            jax.ShapeDtypeStruct(hidden.shape, jnp.bfloat16),
            jax.ShapeDtypeStruct(hidden.shape, jnp.bfloat16),
        ],
        compiler_params=pltpu.CompilerParams(vmem_limit_bytes=VMEM),
        cost_estimate=cost(1e8, 110e6),
        name="finish_rows",
    )(
        mix_low,
        out_low,
        in_low,
        wide_low,
        hidden,
        middle,
        grad_middle,
        live,
        two_sums,
        *normed_terms,
        *two_terms,
    )


def block_decays(rate):
    row = lax.broadcasted_iota(jnp.int32, (BLK, BLK), 0)
    column = lax.broadcasted_iota(jnp.int32, (BLK, BLK), 1)
    distance = (row - column).astype(jnp.float32)
    within = jnp.where(row >= column, jnp.exp(-rate * jnp.maximum(distance, 0.0)), 0.0)
    place = lax.broadcasted_iota(jnp.int32, (BLK, 1), 0).astype(jnp.float32)
    entry = jnp.exp(-rate * (place + 1.0))
    leave = jnp.exp(-rate * (BLK - 1.0 - place))
    whole = jnp.exp(-BLK * rate * jnp.ones((1, HS), jnp.float32))
    return within, entry, leave, whole


def norm_back(values, grad):
    scale = lax.rsqrt(jnp.mean(values * values, axis=-1, keepdims=True) + epsilon)
    unit = values * scale
    return scale * (grad - unit * jnp.mean(grad * unit, axis=-1, keepdims=True))


def square_device(
    hidden, mix_weight, out_weight, ffn_in_weight, ffn_out_weight, seq_lengths, block_seq, cotangent
):
    local_rows, width = hidden.shape
    units = ffn_out_weight.shape[0]
    narrow_index = lax.axis_index("narrow")
    valid_all, fresh_block = group_masks(seq_lengths, block_seq)
    live = lax.dynamic_slice_in_dim(
        valid_all.astype(jnp.float32), narrow_index * local_rows, local_rows
    )[:, None]

    keep = jnp.broadcast_to(jnp.where(fresh_block, 0.0, 1.0)[:, None], (NBLK, HS))
    normed_all, parts, gated, mixing, states, grads_own, grads_first, whole_weight = mix_rows(
        hidden, cotangent, mix_weight, out_weight, live, keep
    )
    middle, normed_two_all, grad_two_all, act, grad_parts, back_sums, two_sums = gated_unit(
        gated,
        whole_weight,
        hidden,
        live,
        grads_own,
        grads_first,
        ffn_in_weight,
        ffn_out_weight,
    )
    in_low, wide_low, out_low, mix_low, _, grad_middle, own_top, own_low, *terms = weight_grads(
        act,
        grad_two_all,
        normed_two_all,
        grad_parts,
        back_sums,
        two_sums,
        middle,
        cotangent,
        out_weight,
        mix_weight,
        parts,
        mixing,
        states,
        gated,
        normed_all,
        live,
        keep,
    )
    grad_mix, grad_out, grad_ffn_in, grad_ffn_out, layer_out, input_grad = finish_rows(
        mix_low.reshape(mix_weight.shape),
        out_low.reshape(out_weight.shape),
        in_low.reshape(width, 2 * units),
        wide_low.reshape(units, width),
        hidden,
        middle,
        grad_middle,
        live,
        (own_top, terms[0], terms[2], own_low, terms[1], terms[3]),
        two_sums,
        (terms[4], terms[6], terms[5], terms[7]),
    )
    return (layer_out, input_grad, grad_mix, grad_out, grad_ffn_in, grad_ffn_out)


def solution(mesh):
    square = mesh.shape["wide"] == 8 and mesh.shape["narrow"] == 4
    per_device = square_device if square else general_device
    in_specs = (
        P(("wide", "narrow"), None),
        P(None, None, "narrow"),
        P("narrow", None),
        P(None, None, "narrow"),
        P("narrow", None),
        P("wide"),
        P("wide"),
        P(("wide", "narrow"), None),
    )
    out_specs = (
        P(("wide", "narrow"), None),
        P(("wide", "narrow"), None),
        P(None, None, "narrow"),
        P("narrow", None),
        P(None, None, "narrow"),
        P("narrow", None),
    )
    return jax.shard_map(
        per_device, mesh=mesh, in_specs=in_specs, out_specs=out_specs, check_vma=False
    )
```

```python
import functools
import math

import jax
import jax.numpy as jnp
from jax import lax
from jax.experimental import pallas as pl
from jax.experimental.pallas import tpu as pltpu
from jax.sharding import PartitionSpec as P

HEADS = 16
HS = 128
BLK = 256
NBLK = 8


epsilon = 1e-06
head_floor = 1.0
highest = lax.Precision.HIGHEST


def row_norm(values):
    return values * lax.rsqrt(jnp.mean(values * values, axis=-1, keepdims=True) + epsilon)


def head_norm(values):
    return values * lax.rsqrt(jnp.mean(values * values, axis=-1, keepdims=True) + head_floor)


def silu_slope(values):
    sigmoid_part = jax.nn.sigmoid(values)
    return sigmoid_part * (1.0 + values * (1.0 - sigmoid_part))


def decay_tables(decay_rates):
    positions = jnp.arange(BLK, dtype=jnp.float32)
    distance = positions[:, None] - positions[None, :]
    causal = distance >= 0
    clipped = jnp.where(causal, distance, 0.0)
    within = jnp.where(causal[None], jnp.exp(-decay_rates[:, None, None] * clipped[None]), 0.0)
    entry_decay = jnp.exp(-(positions[:, None] + 1.0) * decay_rates[None, :])
    exit_decay = jnp.exp(-(BLK - 1.0 - positions[:, None]) * decay_rates[None, :])
    block_decay = jnp.exp(-BLK * decay_rates)
    return (within, entry_decay, exit_decay, block_decay)


def group_masks(lengths, owners):
    seq_slot = owners - owners[0]
    first_count = jnp.sum((seq_slot == 0).astype(jnp.int32))
    block_ids = jnp.arange(NBLK, dtype=jnp.int32)
    start_block = jnp.where(seq_slot == 0, jnp.int32(0), first_count)
    seq_limit = jnp.where(seq_slot == 0, lengths[0], lengths[1])
    offsets = (block_ids - start_block)[:, None] * BLK + jnp.arange(BLK, dtype=jnp.int32)[None, :]
    valid_rows = (offsets < seq_limit[:, None]).reshape(-1)
    fresh_block = block_ids == start_block
    return (valid_rows, fresh_block)


def forward_block(tables, kv_state, block_in):
    within, entry_decay, exit_decay, block_decay = tables
    queries, keys_in, values, fresh_block = block_in
    kv_state = jnp.where(fresh_block, 0.0, kv_state)
    scores = jnp.einsum("ihs,jhs->hij", queries, keys_in, preferred_element_type=jnp.float32)
    weights = (scores * within).astype(jnp.bfloat16)
    inner_part = jnp.einsum("hij,jhs->ihs", weights, values, preferred_element_type=jnp.float32)
    carried = jnp.einsum(
        "ihs,hst->iht",
        queries.astype(jnp.float32) * entry_decay[:, :, None],
        kv_state,
        precision=highest,
    )
    update = jnp.einsum(
        "ihs,iht->hst",
        keys_in.astype(jnp.float32) * exit_decay[:, :, None],
        values.astype(jnp.float32),
        precision=highest,
    )
    return (block_decay[:, None, None] * kv_state + update, (inner_part + carried, kv_state))


def backward_block(tables, later_grad, block_in):
    within, entry_decay, exit_decay, block_decay = tables
    queries, keys_in, values, grad_mix, kv_state, fresh_block = block_in
    scores = jnp.einsum("ihs,jhs->hij", queries, keys_in, preferred_element_type=jnp.float32)
    weights = (scores * within).astype(jnp.bfloat16)
    grad_values = jnp.einsum("hij,ihs->jhs", weights, grad_mix, preferred_element_type=jnp.float32)
    grad_weights = jnp.einsum("ihs,jhs->hij", grad_mix, values, preferred_element_type=jnp.float32)
    grad_scores = (grad_weights * within).astype(jnp.bfloat16)
    grad_queries = jnp.einsum(
        "hij,jhs->ihs", grad_scores, keys_in, preferred_element_type=jnp.float32
    )
    grad_keys = jnp.einsum("hij,ihs->jhs", grad_scores, queries, preferred_element_type=jnp.float32)
    grad_float = grad_mix.astype(jnp.float32)
    values_float = values.astype(jnp.float32)
    queries_float = queries.astype(jnp.float32)
    keys_float = keys_in.astype(jnp.float32)
    grad_queries = grad_queries + entry_decay[:, :, None] * jnp.einsum(
        "iht,hst->ihs", grad_float, kv_state, precision=highest
    )
    grad_keys = grad_keys + exit_decay[:, :, None] * jnp.einsum(
        "iht,hst->ihs", values_float, later_grad, precision=highest
    )
    grad_values = grad_values + jnp.einsum(
        "ihs,hst->iht", keys_float * exit_decay[:, :, None], later_grad, precision=highest
    )
    grad_state = jnp.einsum(
        "ihs,iht->hst", queries_float * entry_decay[:, :, None], grad_float, precision=highest
    )
    grad_state = grad_state + block_decay[:, None, None] * later_grad
    grad_state = jnp.where(fresh_block, 0.0, grad_state)
    return (grad_state, (grad_queries, grad_keys, grad_values))


def general_device(
    hidden, mix_weight, out_weight, ffn_in_weight, ffn_out_weight, seq_lengths, block_seq, cotangent
):
    local_rows = hidden.shape[0]
    group_rows = NBLK * BLK
    head_width = mix_weight.shape[2]
    head_count = head_width // HS
    narrow_index = lax.axis_index("narrow")
    valid_all, fresh_block = group_masks(seq_lengths, block_seq)
    valid_rows = lax.dynamic_slice_in_dim(
        valid_all.astype(jnp.float32), narrow_index * local_rows, local_rows
    )[:, None]
    head_ids = narrow_index * head_count + jnp.arange(head_count, dtype=jnp.int32)
    decay_rates = 2.0 ** (-8.0 * (head_ids.astype(jnp.float32) + 1.0) / HEADS)
    tables = decay_tables(decay_rates)

    def split_blocks(flat_rows):
        return flat_rows.reshape(NBLK, BLK, head_count, HS)

    inputs = hidden.astype(jnp.float32)
    normed_low = row_norm(inputs).astype(jnp.bfloat16)
    gathered = lax.all_gather(normed_low, "narrow", axis=0, tiled=True)
    projected = jnp.einsum("rd,cde->cre", gathered, mix_weight, preferred_element_type=jnp.float32)
    queries = jax.nn.silu(projected[0]).astype(jnp.bfloat16)
    keys_in = jax.nn.silu(projected[1]).astype(jnp.bfloat16)
    values = projected[2].astype(jnp.bfloat16)
    gate_part = projected[3]
    zero_state = jnp.zeros((head_count, HS, HS), jnp.float32)
    final_state, (mixing, kept_states) = lax.scan(
        lambda state_in, block_in: forward_block(tables, state_in, block_in),
        zero_state,
        (split_blocks(queries), split_blocks(keys_in), split_blocks(values), fresh_block),
    )
    mixing = mixing.reshape(group_rows, head_count, HS)
    headed = head_norm(mixing).reshape(group_rows, head_width)
    gated_low = (headed * gate_part).astype(jnp.bfloat16)
    branch = lax.psum_scatter(
        jnp.dot(gated_low, out_weight, preferred_element_type=jnp.float32).astype(jnp.bfloat16),
        "narrow",
        scatter_dimension=0,
        tiled=True,
    ).astype(jnp.float32)
    middle = inputs + valid_rows * branch
    normed_two_low = row_norm(middle).astype(jnp.bfloat16)
    gathered_two = lax.all_gather(normed_two_low, "narrow", axis=0, tiled=True)
    both_parts = jnp.einsum(
        "rd,cdf->crf", gathered_two, ffn_in_weight, preferred_element_type=jnp.float32
    )
    hidden_low = (both_parts[0] * both_parts[1]).astype(jnp.bfloat16)
    branch_two = lax.psum_scatter(
        jnp.dot(hidden_low, ffn_out_weight, preferred_element_type=jnp.float32).astype(
            jnp.bfloat16
        ),
        "narrow",
        scatter_dimension=0,
        tiled=True,
    ).astype(jnp.float32)
    layer_out = (middle + valid_rows * branch_two).astype(jnp.bfloat16)
    grad_rows = cotangent.astype(jnp.float32)
    ffn_grad_all = lax.all_gather(
        (valid_rows * grad_rows).astype(jnp.bfloat16), "narrow", axis=0, tiled=True
    )
    grad_ffn_out = jnp.einsum(
        "rf,rd->fd", hidden_low, ffn_grad_all, preferred_element_type=jnp.float32
    )
    grad_hidden = jnp.einsum(
        "rd,fd->rf", ffn_grad_all, ffn_out_weight, preferred_element_type=jnp.float32
    )
    grad_parts = jnp.stack([grad_hidden * both_parts[1], grad_hidden * both_parts[0]]).astype(
        jnp.bfloat16
    )
    grad_ffn_in = jnp.einsum(
        "rd,crf->cdf", gathered_two, grad_parts, preferred_element_type=jnp.float32
    )
    grad_slice = grad_parts
    grad_normed_two = lax.psum_scatter(
        jnp.einsum(
            "crf,cdf->rd", grad_slice, ffn_in_weight, preferred_element_type=jnp.float32
        ).astype(jnp.bfloat16),
        "narrow",
        scatter_dimension=0,
        tiled=True,
    ).astype(jnp.float32)
    norm_value, norm_pull = jax.vjp(row_norm, middle)
    grad_middle = grad_rows + norm_pull(grad_normed_two)[0]
    attn_grad_all = lax.all_gather(
        (valid_rows * grad_middle).astype(jnp.bfloat16), "narrow", axis=0, tiled=True
    )
    grad_out_weight = jnp.einsum(
        "re,rd->ed", gated_low, attn_grad_all, preferred_element_type=jnp.float32
    )
    grad_gated = jnp.einsum(
        "rd,ed->re", attn_grad_all, out_weight, preferred_element_type=jnp.float32
    )
    grad_gated = lax.optimization_barrier(grad_gated.astype(jnp.bfloat16)).astype(jnp.float32)
    grad_gate = grad_gated * headed
    grad_headed = (grad_gated * gate_part).reshape(group_rows, head_count, HS)
    head_value, head_pull = jax.vjp(head_norm, mixing)
    grad_mixing = head_pull(grad_headed)[0].astype(jnp.bfloat16)
    first_grad, (grad_queries, grad_keys, grad_values) = lax.scan(
        lambda later_grad, block_in: backward_block(tables, later_grad, block_in),
        zero_state,
        (
            split_blocks(queries),
            split_blocks(keys_in),
            split_blocks(values),
            split_blocks(grad_mixing),
            kept_states,
            fresh_block,
        ),
        reverse=True,
    )
    grad_projected = jnp.stack(
        [
            grad_queries.reshape(group_rows, head_width) * silu_slope(projected[0]),
            grad_keys.reshape(group_rows, head_width) * silu_slope(projected[1]),
            grad_values.reshape(group_rows, head_width),
            grad_gate,
        ]
    ).astype(jnp.bfloat16)
    grad_mix = jnp.einsum(
        "rd,cre->cde", gathered, grad_projected, preferred_element_type=jnp.float32
    )
    grad_slice = grad_projected
    grad_normed = lax.psum_scatter(
        jnp.einsum(
            "cre,cde->rd", grad_slice, mix_weight, preferred_element_type=jnp.float32
        ).astype(jnp.bfloat16),
        "narrow",
        scatter_dimension=0,
        tiled=True,
    ).astype(jnp.float32)
    first_value, first_pull = jax.vjp(row_norm, inputs)
    input_grad = (grad_middle + first_pull(grad_normed)[0]).astype(jnp.bfloat16)
    grad_mix, grad_out_weight, grad_ffn_in, grad_ffn_out = (
        lax.psum(grad_mix.astype(jnp.bfloat16), "wide").astype(jnp.float32),
        lax.psum(grad_out_weight.astype(jnp.bfloat16), "wide").astype(jnp.float32),
        lax.psum(grad_ffn_in.astype(jnp.bfloat16), "wide").astype(jnp.float32),
        lax.psum(grad_ffn_out.astype(jnp.bfloat16), "wide").astype(jnp.float32),
    )
    return (layer_out, input_grad, grad_mix, grad_out_weight, grad_ffn_in, grad_ffn_out)


HALF = BLK
PIECE = 2 * BLK
VMEM = 60 * 1024 * 1024


def add_low(*terms):
    return sum(term.astype(jnp.float32) for term in terms).astype(jnp.bfloat16)


def add_rows(*terms):
    return sum(term.astype(jnp.float32) for term in terms)


def across(left, right):
    return lax.dot_general(left, right, (((1,), (1,)), ((), ())), preferred_element_type=jnp.float32)


def down(left, right):
    return lax.dot_general(left, right, (((0,), (0,)), ((), ())), preferred_element_type=jnp.float32)


def straight(left, right):
    return jnp.dot(left, right, preferred_element_type=jnp.float32)


def any_specs(count):
    return [pl.BlockSpec(memory_space=pl.ANY)] * count


def cost(flops, bytes_accessed):
    return pl.CostEstimate(flops=int(flops), bytes_accessed=int(bytes_accessed), transcendentals=0)


MESH = pl.DeviceIdType.MESH
SLOTS = 12
STAGES = 11
SUB = 128
TILE = 256


def begin(copies):
    for copy in copies:
        copy.start()


def finish(copies):
    for copy in copies:
        copy.wait()


def neighbours():
    wide, narrow = lax.axis_index("wide"), lax.axis_index("narrow")
    z, core = wide // 2, wide % 2
    mate = (wide + 1 - 2 * core, narrow)
    near_x = (wide, narrow + 1 - 2 * (narrow % 2))
    near_y = (wide, (narrow + 2) % 4)
    return wide, narrow, z, core, mate, near_x, near_y


def slot_of(block, narrow):
    off_x = (block // 2 % 2 + narrow % 2) % 2
    off_y = (block // 4 + narrow // 2) % 2
    if block % 2:
        return 1 + 3 * off_x + 2 * off_y + off_x * off_y
    return 2 * off_x + 5 * off_y - off_x * off_y


def head_rate(head):
    return jnp.exp(jnp.full((1, 1), -8.0 / HEADS * math.log(2.0), jnp.float32) * (head.astype(jnp.float32) + 1.0))


def line_scratch():
    low = jnp.bfloat16
    pair = pltpu.VMEM((SLOTS, 2, SUB, TILE), low)
    return [
        pltpu.VMEM((SLOTS, 4, SUB, TILE), low),
        pair,
        pair,
        pair,
        pltpu.VMEM((SLOTS, SUB, TILE), low),
        pair,
        pair,
        pltpu.SemaphoreType.DMA((14, SLOTS)),
        pltpu.SemaphoreType.DMA((4, SLOTS)),
    ]


def enter(neighbour_places):
    wide, narrow, z, core, mate, near_x, near_y = neighbour_places
    barrier = pltpu.get_barrier_semaphore()

    def greet(place):
        pl.semaphore_signal(barrier, inc=1, device_id=place, device_id_type=MESH)

    for place in (mate, near_x, near_y):
        greet(place)
    middle = (z == 1) | (z == 2)

    @pl.when(middle)
    def _():
        greet((2 * (3 - z) + core, narrow))
        greet((6 * (z - 1) + core, narrow))
        pl.semaphore_wait(barrier, 5)

    @pl.when(jnp.logical_not(middle))
    def _():
        greet((2 * (1 + z // 3) + core, narrow))
        pl.semaphore_wait(barrier, 4)


def line_sum(scratch, places, count, product, targets):
    own, met, both, ended, crossed, full, other, sems, out_sems = scratch
    wide, narrow, z, core, mate, _, _ = places
    region = z // 2
    middle = (z == 1) | (z == 2)
    end = jnp.logical_not(middle)
    inward = (2 * (1 + z // 3) + core, narrow)
    across_line = (2 * (3 - z) + core, narrow)
    outward = (6 * (z - 1) + core, narrow)

    def remote(src, dst, kind, slot, place):
        return pltpu.make_async_remote_copy(
            src_ref=src,
            dst_ref=dst,
            send_sem=sems.at[2 * kind, slot],
            recv_sem=sems.at[2 * kind + 1, slot],
            device_id=place,
            device_id_type=MESH,
        )

    def core_one(s):
        return remote(own.at[s, pl.ds(2 * (1 - core), 2)], met.at[s], 0, s, mate)

    def line_one(s):
        return remote(both.at[s], ended.at[s], 1, s, inward)

    def cross_one(s):
        return remote(both.at[s, 1 - region], crossed.at[s], 2, s, across_line)

    def cross_two(s):
        return remote(full.at[s, region], full.at[s, region], 3, s, across_line)

    def out_one(s):
        return remote(full.at[s, region], full.at[s, region], 4, s, outward)

    def out_two(s):
        return remote(full.at[s, 1 - region], full.at[s, 1 - region], 5, s, outward)

    def core_two(s):
        return remote(full.at[s], other.at[s], 6, s, mate)

    def add(left, right):
        return (left.astype(jnp.float32) + right.astype(jnp.float32)).astype(jnp.bfloat16)

    def deliveries(k, s):
        for t in range(2):
            for which, (src, part) in enumerate(
                ((full.at[s, t], 2 * core + t), (other.at[s, t], 2 * (1 - core) + t))
            ):
                for condition, ref in targets(k, part):
                    yield condition, pltpu.make_async_copy(src, ref, out_sems.at[2 * t + which, s])

    def start(k, s):
        product(k, own.at[s])
        core_one(s).start()

    def cores(k, s):
        core_one(s).wait_recv()
        both[s] = add(own[s, pl.ds(2 * core, 2)], met[s])
        pl.when(end)(lambda: line_one(s).start())

    def ends(k, s):
        @pl.when(middle)
        def _():
            line_one(s).wait_recv()
            both[s] = add(both[s], ended[s])
            cross_one(s).start()

    def centre(k, s):
        @pl.when(middle)
        def _():
            cross_one(s).wait_recv()
            full[s, region] = add(both[s, region], crossed[s])
            cross_two(s).start()
            out_one(s).start()

    def pass_on(k, s):
        @pl.when(middle)
        def _():
            cross_two(s).wait_recv()
            out_two(s).start()

    def back(k, s):
        @pl.when(end)
        def _():
            out_one(s).wait_recv()
            out_two(s).wait_recv()

        core_two(s).start()

    def deliver(k, s):
        core_two(s).wait_recv()
        for condition, copy in deliveries(k, s):
            pl.when(condition)(copy.start)

    def clear(k, s):
        core_one(s).wait_send()
        core_two(s).wait_send()

        @pl.when(end)
        def _():
            line_one(s).wait_send()

        @pl.when(middle)
        def _():
            for copy in (cross_one(s), cross_two(s), out_one(s), out_two(s)):
                copy.wait_send()

        for t in range(2):
            for which, src in enumerate((full, other)):
                ref = targets(k, 0)[0][1]
                pltpu.make_async_copy(src.at[s, t], ref, out_sems.at[2 * t + which, s]).wait()

    stages = (
        (11, clear),
        (10, deliver),
        (9, back),
        (7, pass_on),
        (5, centre),
        (3, ends),
        (1, cores),
        (0, start),
    )

    def step(i, carry):
        for delay, work in stages:
            k = i - delay

            @pl.when((k >= 0) & (k < count))
            def _(work=work, k=k):
                work(k, lax.rem(k + SLOTS, SLOTS))

        return carry

    return step


def square_scratch(uses):
    block = pltpu.VMEM((2, BLK, HEADS * HS), jnp.bfloat16)
    return [block, block, pltpu.SemaphoreType.DMA((uses, 6, 2)), pltpu.SemaphoreType.DMA((uses, 2))]


def square_sum(scratch, places, parts, landed, use):
    met, mid, sems, load_sems = scratch
    top_x, low_y, low_x, top_y, top_d, low_d = parts
    near_x, near_y = places[5:]

    def remote(src, dst, kind, place):
        return pltpu.make_async_remote_copy(
            src_ref=src,
            dst_ref=dst,
            send_sem=sems.at[use, kind, 0],
            recv_sem=sems.at[use, kind, 1],
            device_id=place,
            device_id_type=MESH,
        )

    first = [remote(top_d, met.at[0], 0, near_x), remote(low_d, met.at[1], 1, near_y)]
    direct = [remote(top_x, landed[0], 2, near_x), remote(low_y, landed[1], 3, near_y)]
    second = [remote(mid.at[0], landed[2], 4, near_y), remote(mid.at[1], landed[3], 5, near_x)]
    loads = []
    if top_y is not None:
        loads = [
            pltpu.make_async_copy(top_y, mid.at[0], load_sems.at[use, 0]),
            pltpu.make_async_copy(low_x, mid.at[1], load_sems.at[use, 1]),
        ]

    def open_sum():
        begin(first)
        begin(direct)
        begin(loads)

    def join_sum():
        finish(loads)
        for at in range(2):
            first[at].wait()

            def tile(i, carry, at=at):
                rows = pl.ds(pl.multiple_of(i * 64, 64), 64)
                mid[at, rows, :] = add_low(mid[at, rows, :], met[at, rows, :])
                return carry

            lax.fori_loop(0, BLK // 64, tile, 0)
        begin(second)

    def close_sum():
        finish(direct)
        finish(second)

    return open_sum, join_sum, close_sum


def weight_grads(
    act,
    grad_two_all,
    normed_two_all,
    grad_parts,
    back_sums,
    two_sums,
    middle,
    cotangent,
    out_weight,
    mix_weight,
    parts_all,
    mixing_all,
    states_all,
    gated,
    normed_all,
    live,
    keep,
):
    rows, units = act.shape
    width = grad_two_all.shape[1]
    local_rows = middle.shape[0]
    parts, _, columns = parts_all.shape
    heads = columns // HS
    low = jnp.bfloat16
    in_columns = grad_parts.shape[1] // TILE
    in_rows = width // PIECE
    out_blocks = units // SUB
    halves = width // 1024
    first_out = in_rows * in_columns
    first_branch = first_out + halves * out_blocks
    first_mix = first_branch + width // TILE
    per_row = columns // TILE
    per_part = in_rows * per_row
    count = first_mix + parts * per_part

    def body(*refs):
        act_in, two_in, normed_two_in, parts_in, back_in, two_sums_in = refs[:6]
        middle_in, cot_in, weight_in, mix_in = refs[6:10]
        all_in, mixing_in, states_in, gated_in, normed_in, live_ref, keep_ref = refs[10:17]
        in_grad, out_grad, branch_grad, mix_grad, branch_out, middle_out = refs[17:23]
        own_outs, last_landed, two_landed = refs[23:25], refs[25:29], refs[29:33]
        shared, wide_ref, act_ref, landed, stage_ref, mid_ref, grad_ref, branch = refs[33:41]
        near, gated_grad, states_ref = refs[41:44]
        normed_sems, parts_sems, load_sems, stage_sems, gather_sems, back_sems, head_sems, mix_sems = refs[44:52]
        tile_sems, own_sems = refs[52:54]
        line, square = refs[54:63], refs[63:67]
        mid = square[1]
        places = neighbours()
        narrow, near_x, near_y = places[1], places[5], places[6]
        enter(places)

        def block(at):
            return pl.ds(at * BLK, BLK)

        def cols(at, size):
            return pl.ds(pl.multiple_of(at, 128), size)

        def load_normed_two(at):
            here = cols(at * PIECE, PIECE)
            return pltpu.make_async_copy(normed_two_in.at[:, here], shared.at[:, here], normed_sems.at[at])

        def load_parts(at):
            here = cols(at * TILE, TILE)
            return pltpu.make_async_copy(parts_in.at[:, here], wide_ref.at[:, here], parts_sems.at[at])

        def load_half(src, half, sem):
            here = pl.ds(half * 1024, 1024)
            return pltpu.make_async_copy(src.at[:, here], shared.at[:, here], load_sems.at[sem])

        load_act = pltpu.make_async_copy(act_in, act_ref, load_sems.at[0])
        load_two = [load_half(two_in, half, 1 + half) for half in range(halves)]
        load_normed = [load_half(normed_in, half, 3 + half) for half in range(halves)]
        load_gated = pltpu.make_async_copy(gated_in.at[0], act_ref.at[:, pl.ds(0, columns)], load_sems.at[5])

        def load_branch(at):
            slot = at % 2
            return pltpu.make_async_copy(
                branch_out.at[:, cols(at * TILE, TILE)],
                act_ref.at[:, cols(columns + slot * TILE, TILE)],
                tile_sems.at[slot],
            )

        def product(k, own):
            def split_rows(result):
                for part in range(4):
                    own[part] = result[part * SUB : (part + 1) * SUB]

            @pl.when(k < first_out)
            def _():
                row, column = k // in_columns, k % in_columns

                @pl.when(column == 0)
                def _():
                    load_normed_two(row).wait()

                @pl.when(row == 0)
                def _():
                    load_parts(column).wait()

                here, there = cols(row * PIECE, PIECE), cols(column * TILE, TILE)
                split_rows(down(shared[:, here], wide_ref[:, there]).astype(low))

                @pl.when(k == first_out - in_columns)
                def _():
                    load_two[0].start()

            @pl.when(k == first_out)
            def _():
                begin(load_two[1:])
                load_act.wait()
                load_two[0].wait()

            @pl.when(k == first_out + out_blocks)
            def _():
                finish(load_two[1:])
                load_normed[0].start()

            @pl.when((k >= first_out) & (k < first_branch))
            def _():
                at = k - first_out
                here = cols((at % out_blocks) * SUB, SUB)
                there = cols((at // out_blocks) * 1024, 1024)
                result = down(act_ref[:, here], shared[:, there]).astype(low)
                for part in range(4):
                    own[part] = result[:, part * TILE : (part + 1) * TILE]

            @pl.when(k == first_branch)
            def _():
                load_branch(0).start()
                load_gated.start()
                begin(load_normed[1:])
                load_gated.wait()

            @pl.when((k >= first_branch) & (k < first_mix))
            def _():
                at = k - first_branch
                load_branch(at).wait()
                pl.when(k + 1 < first_mix)(lambda: load_branch(at + 1).start())
                there = cols(columns + (at % 2) * TILE, TILE)
                split_rows(down(act_ref[:, :columns], act_ref[:, there]).astype(low))

            @pl.when(k == first_mix)
            def _():
                finish(load_normed)

            @pl.when(k >= first_mix)
            def _():
                at = k - first_mix
                here = cols(((at // per_row) % in_rows) * PIECE, PIECE)
                there = cols((at // per_part) * columns + (at % per_row) * TILE, TILE)
                split_rows(down(shared[:, here], wide_ref[:, there]).astype(low))

        def targets(k, part):
            one = jnp.minimum(k, first_out - 1)
            two = jnp.clip(k - first_out, 0, first_branch - first_out - 1)
            three = jnp.clip(k - first_branch, 0, first_mix - first_branch - 1)
            four = jnp.maximum(k - first_mix, 0)
            return [
                (
                    k < first_out,
                    in_grad.at[(one // in_columns) * 4 + part, :, cols((one % in_columns) * TILE, TILE)],
                ),
                (
                    (k >= first_out) & (k < first_branch),
                    out_grad.at[two % out_blocks, :, cols((two // out_blocks) * 1024 + part * TILE, TILE)],
                ),
                (
                    (k >= first_branch) & (k < first_mix),
                    branch_grad.at[part, :, cols(three * TILE, TILE)],
                ),
                (
                    k >= first_mix,
                    mix_grad.at[(four // per_row) * 4 + part, :, cols((four % per_row) * TILE, TILE)],
                ),
            ]

        step = line_sum(line, places, count, product, targets)
        now = [0]

        def run(steps):
            lax.fori_loop(now[0], now[0] + steps, step, 0)
            now[0] += steps

        open_sum, join_sum, close_sum = square_sum(
            square,
            places,
            [back_in.at[block(at)] for at in range(2, 8)],
            [landed.at[at] for at in range(4)],
            0,
        )
        load_normed_two(0).start()
        load_parts(0).start()
        open_sum()
        for at in range(1, in_columns):
            load_parts(at).start()
        for at in range(1, in_rows):
            load_normed_two(at).start()
        load_act.start()

        def spread(src, slot, kind, place):
            return pltpu.make_async_remote_copy(
                src_ref=src,
                dst_ref=branch_out.at[block(slot)],
                send_sem=gather_sems.at[kind, 0],
                recv_sem=gather_sems.at[kind, 1],
                device_id=place,
                device_id_type=MESH,
            )

        def stage(half):
            return [
                pltpu.make_async_copy(back_in.at[block(half)], stage_ref.at[0], stage_sems.at[0]),
                pltpu.make_async_copy(cot_in.at[block(half)], stage_ref.at[1], stage_sems.at[1]),
                pltpu.make_async_copy(middle_in.at[block(half)], mid_ref, stage_sems.at[2]),
            ]

        keep_branch = [
            pltpu.make_async_copy(branch.at[at], branch_out.at[block(at)], stage_sems.at[3 + at])
            for at in range(2)
        ]

        def rows_back(half):
            def tile(i, carry):
                at = pl.ds(pl.multiple_of(i * 32, 32), 32)
                grad = add_rows(stage_ref[0, at, :], landed[half, at, :], landed[2 + half, at, :])
                result = stage_ref[1, at, :].astype(jnp.float32) + norm_back(mid_ref[at, :], grad)
                grad_ref[at, :] = result
                live_at = pl.ds(pl.multiple_of(half * BLK + i * 32, 32), 32)
                branch[half, at, :] = (live_ref[live_at, :1] * result).astype(low)
                return carry

            lax.fori_loop(0, BLK // 32, tile, 0)
            copy = pltpu.make_async_copy(grad_ref, middle_out.at[block(half)], stage_sems.at[5])
            copy.start()
            return copy

        sends = [
            spread(branch.at[0], 2, 0, near_x),
            spread(branch.at[1], 3, 1, near_y),
            spread(branch.at[1], 4, 2, near_x),
            spread(branch.at[0], 5, 3, near_y),
        ]
        later = [
            spread(branch_out.at[block(3)], 7, 4, near_x),
            spread(branch_out.at[block(2)], 6, 5, near_y),
        ]
        run(9)
        join_sum()
        begin(stage(0))
        run(16)
        close_sum()
        finish(stage(0))
        written = rows_back(0)
        sends[0].start()
        begin(stage(1))
        finish(stage(1))
        written.wait()
        written = rows_back(1)
        begin(sends[1:])
        begin(keep_branch)
        run(8)
        sends[0].wait_recv()
        sends[1].wait_recv()
        begin(later)
        run(17)
        written.wait()
        finish(keep_branch)
        for copy in sends[:2]:
            copy.wait_send()
        finish(sends[2:])
        finish(later)

        open_two, join_two, close_two = square_sum(
            square, places, [two_sums_in.at[block(at)] for at in range(2, 8)], two_landed, 1
        )
        open_two()

        def head_loads(head):
            here = cols(head * HS, HS)
            loads = [
                pltpu.make_async_copy(
                    all_in.at[c, :, here],
                    wide_ref.at[:, pl.ds(parts * columns + c * HS, HS)],
                    head_sems.at[c],
                )
                for c in range(parts)
            ]
            loads.append(
                pltpu.make_async_copy(
                    mixing_in.at[:, here],
                    wide_ref.at[:, pl.ds(parts * columns + parts * HS, HS)],
                    head_sems.at[parts],
                )
            )
            loads.append(pltpu.make_async_copy(states_in.at[head], states_ref, head_sems.at[parts + 1]))
            return loads

        weight_loads = [
            pltpu.make_async_copy(weight_in.at[block(at)], landed.at[at], back_sems.at[at])
            for at in range(columns // BLK)
        ]

        def row_load(at):
            here = pl.ds(pl.multiple_of(at * BLK, BLK), BLK)
            return pltpu.make_async_copy(branch_out.at[here], stage_ref.at[at % 2], back_sems.at[2 + at % 2])

        begin(weight_loads)
        row_load(0).start()
        begin(head_loads(0))
        finish(weight_loads)
        back_from = now[0]

        def back_block(at, carry):
            step(back_from + at, 0)
            row_load(at).wait()
            pl.when(at + 1 < rows // BLK)(lambda: row_load(at + 1).start())
            here = pl.ds(pl.multiple_of(at * BLK, BLK), BLK)
            for part in range(len(weight_loads)):
                result = across(stage_ref[at % 2], landed[part])
                gated_grad[here, part * BLK : (part + 1) * BLK] = result.astype(low)
            return carry

        lax.fori_loop(0, rows // BLK, back_block, 0)
        now[0] += rows // BLK
        join_two()

        def load_mix(at):
            here = pl.ds(pl.multiple_of(at * BLK, BLK), BLK)
            slot = at % 4
            return [
                pltpu.make_async_copy(
                    mix_in.at[c, here, :], landed.at[slot, :, pl.ds(c * columns, columns)], mix_sems.at[slot, c]
                )
                for c in range(parts)
            ]

        for at in range(4):
            begin(load_mix(at))
        attend_from = now[0]

        def attend(head, carry):
            rate = head_rate(heads * narrow + head)
            within, entry, leave, whole = block_decays(rate)
            finish(head_loads(head))
            later_grad = jnp.zeros((HS, HS), jnp.float32)
            base = parts * columns
            for at in range(NBLK):
                block_at = NBLK - 1 - at
                here = pl.ds(pl.multiple_of(slot_of(block_at, narrow) * BLK, BLK), BLK)

                def load(c, here=here):
                    return wide_ref[here, base + c * HS : base + (c + 1) * HS]

                def store(c, value, here=here):
                    wide_ref[here, cols(c * columns + head * HS, HS)] = value.astype(low)

                raw_queries = load(0).astype(jnp.float32)
                raw_keys = load(1).astype(jnp.float32)
                queries, keys = jax.nn.silu(raw_queries).astype(low), jax.nn.silu(raw_keys).astype(low)
                values = load(2)
                gate = load(3).astype(jnp.float32)
                mixing = load(4).astype(jnp.float32)
                grad_rows = gated_grad[here, cols(head * HS, HS)].astype(jnp.float32)
                scale = lax.rsqrt(jnp.mean(mixing * mixing, axis=-1, keepdims=True) + head_floor)
                headed = mixing * scale
                store(3, grad_rows * headed)
                grad_headed = grad_rows * gate
                inner = jnp.mean(grad_headed * headed, axis=-1, keepdims=True)
                grad = (scale * (grad_headed - headed * inner)).astype(low)
                scores = (across(queries, keys) * within).astype(low)
                grad_scores = (across(grad, values) * within).astype(low)
                later_low = later_grad.astype(low)
                grad_queries = straight(grad_scores, keys) + entry * across(grad, states_ref[block_at])
                grad_keys = down(grad_scores, queries) + leave * across(values, later_low)
                grad_values = down(scores, grad) + leave * straight(keys, later_low)
                early_queries = (queries.astype(jnp.float32) * entry).astype(low)
                later_grad = keep_ref[block_at : block_at + 1, :1] * (
                    whole * later_grad + down(early_queries, grad)
                )
                store(0, grad_queries * silu_slope(raw_queries))
                store(1, grad_keys * silu_slope(raw_keys))
                store(2, grad_values)
                if at % 2:
                    step(attend_from + head * (NBLK // 2) + at // 2, 0)
            pl.when(head + 1 < heads)(lambda: begin(head_loads(head + 1)))
            return carry

        lax.fori_loop(0, heads, attend, 0)
        now[0] += heads * (NBLK // 2)

        sum_from = now[0]
        outs = ((3, branch, False), (1, near, False), (2, mid, True), (0, stage_ref, False))

        def sum_tile(at, carry):
            finish(load_mix(at))
            here = cols(at * BLK, BLK)
            for piece, out, swapped in outs:
                acts = wide_ref[piece * PIECE : (piece + 1) * PIECE, : parts * columns]
                total = across(acts, landed[at % 4]).astype(low)
                out[int(swapped), :, here] = total[:HALF]
                out[1 - int(swapped), :, here] = total[HALF:]
            pl.when(at + 4 < width // BLK)(lambda: begin(load_mix(at + 4)))
            step(sum_from + at, 0)
            return carry

        close_two()
        lax.fori_loop(0, width // BLK, sum_tile, 0)
        now[0] += width // BLK
        open_last, join_last, close_last = square_sum(
            square,
            places,
            (near.at[0], near.at[1], None, None, branch.at[0], branch.at[1]),
            last_landed,
            2,
        )
        own_stores = [
            pltpu.make_async_copy(stage_ref.at[at], own_outs[at], own_sems.at[at]) for at in range(2)
        ]
        open_last()
        begin(own_stores)
        run(9)
        join_last()
        run(count + STAGES - now[0])
        close_last()
        finish(own_stores)

    def low_shape(*shape):
        return jax.ShapeDtypeStruct(shape, low)

    sem = pltpu.SemaphoreType.DMA
    return pl.pallas_call(
        body,
        in_specs=any_specs(15) + [pl.BlockSpec(memory_space=pltpu.VMEM)] * 2,
        out_specs=any_specs(16),
        out_shape=[
            low_shape(width // SUB, SUB, grad_parts.shape[1]),
            low_shape(out_blocks, SUB, width),
            low_shape(columns // SUB, SUB, width),
            low_shape(parts * width // SUB, SUB, columns),
            low_shape(rows, width),
            jax.ShapeDtypeStruct((local_rows, width), jnp.float32),
        ]
        + [low_shape(BLK, width)] * 10,
        scratch_shapes=[
            pltpu.VMEM((rows, width), low),
            pltpu.VMEM(grad_parts.shape, low),
            pltpu.VMEM(act.shape, low),
            pltpu.VMEM((4, BLK, width), low),
            pltpu.VMEM((2, BLK, width), low),
            pltpu.VMEM((BLK, width), jnp.float32),
            pltpu.VMEM((BLK, width), jnp.float32),
            pltpu.VMEM((2, BLK, width), low),
            pltpu.VMEM((2, BLK, width), low),
            pltpu.VMEM((rows, columns), low),
            pltpu.VMEM((NBLK, HS, HS), low),
            sem((in_rows,)),
            sem((in_columns,)),
            sem((6,)),
            sem((6,)),
            sem((6, 2)),
            sem((4,)),
            sem((parts + 2,)),
            sem((4, parts)),
            sem((2,)),
            sem((2,)),
        ]
        + line_scratch()
        + square_scratch(3),
        compiler_params=pltpu.CompilerParams(
            vmem_limit_bytes=VMEM, collective_id=1, has_side_effects=True
        ),
        cost_estimate=cost(2 * rows * width * (3 * units + 9 * columns), 120e6),
        name="weight_grads",
    )(
        act,
        grad_two_all,
        normed_two_all,
        grad_parts,
        back_sums,
        two_sums,
        middle,
        cotangent,
        out_weight,
        mix_weight,
        parts_all,
        mixing_all,
        states_all,
        gated,
        normed_all,
        live,
        keep,
    )


def gated_unit(gated, whole_weight, hidden, live, grads_own, grads_first, ffn_in, ffn_out):
    _, width, units = ffn_in.shape
    local_rows = hidden.shape[0]
    group_rows = NBLK * BLK
    pieces = group_rows // PIECE
    deep = gated.shape[2]
    slices, quarters, slice_rows, _ = whole_weight.shape
    main = units // TILE * TILE
    tail = units - main
    low = jnp.bfloat16
    cuts = ((0, 2 * TILE), (2 * TILE, main - 2 * TILE))
    wide_tile = 1024
    first_half, second_half = pl.ds(0, HALF), pl.ds(HALF, HALF)

    def body(*refs):
        gated_in, weight_in, hidden_in = refs[:3]
        grad_in = refs[3:5]
        in_ref, out_ref, live_ref = refs[5:8]
        middle_out, rows_out, grads_out, act_out, parts_out, back_out, two_out = refs[8:15]
        gated_ref, hidden_ref, middle_ref = refs[15:18]
        rows, grads, sums, w_in, w_out, act, parts = refs[18:25]
        load_sems, slice_sems, weight_sems, done_sems, sum_sems, last_sems, gated_sems, gather_sems = refs[25:]
        wide, narrow, _, _, _, near_x, near_y = neighbours()
        far = (wide, 3 - narrow)
        barrier = pltpu.get_barrier_semaphore()
        for place in (near_x, near_y, far):
            pl.semaphore_signal(barrier, inc=1, device_id=place, device_id_type=MESH)
        pl.semaphore_wait(barrier, 3)

        here = pl.ds(pl.multiple_of(narrow * deep, deep), deep)

        def send_gated(slot, to, kind, place):
            return pltpu.make_async_remote_copy(
                src_ref=gated_in.at[0, pl.ds(slot * BLK, BLK)],
                dst_ref=gated_ref.at[(first_half, second_half)[to], here],
                send_sem=gated_sems.at[kind, 0],
                recv_sem=gated_sems.at[kind, 1],
                device_id=place,
                device_id_type=MESH,
            )

        gated_sends = [
            send_gated(6, 0, 0, far),
            send_gated(7, 1, 1, far),
            send_gated(2, 0, 2, near_x),
            send_gated(3, 1, 3, near_y),
            send_gated(4, 1, 4, near_x),
            send_gated(5, 0, 5, near_y),
        ]
        keep_gated = pltpu.make_async_copy(
            gated_in.at[0, pl.ds(0, PIECE)], gated_ref.at[:, here], load_sems.at[0]
        )

        def load_slice(at):
            part, quarter = at // quarters, at % quarters
            to = pl.ds(pl.multiple_of(quarter * deep + part * slice_rows, slice_rows), slice_rows)
            return pltpu.make_async_copy(
                weight_in.at[part, quarter], w_in.at[to, pl.ds(0, width)], slice_sems.at[at]
            )

        def start_slice(at, carry):
            load_slice(at).start()
            return carry

        def wait_slice(at, carry):
            load_slice(at).wait()
            return carry

        load_hidden = pltpu.make_async_copy(hidden_in, hidden_ref, load_sems.at[1])
        load_grads = [
            pltpu.make_async_copy(src, grads.at[at], load_sems.at[2 + at])
            for at, src in enumerate(grad_in)
        ]
        weights = []
        for start, size, first, second in tuple((a, b, a, main + a) for a, b in cuts) + (
            (main, tail, 2 * main, 2 * main + tail),
        ):
            at = pl.ds(start, size)
            weights += [
                pltpu.make_async_copy(in_ref.at[0, :, at], w_in.at[:, pl.ds(first, size)], weight_sems.at[len(weights)]),
                pltpu.make_async_copy(in_ref.at[1, :, at], w_in.at[:, pl.ds(second, size)], weight_sems.at[len(weights) + 1]),
                pltpu.make_async_copy(out_ref.at[at, :], w_out.at[at, :], weight_sems.at[len(weights) + 2]),
            ]

        def remote(src, dst, sems, kind, place):
            return pltpu.make_async_remote_copy(
                src_ref=src,
                dst_ref=dst,
                send_sem=sems.at[kind, 0],
                recv_sem=sems.at[kind, 1],
                device_id=place,
                device_id_type=MESH,
            )

        def half(ref, piece, at):
            return ref.at[piece, (first_half, second_half)[at]]

        def quarter(ref, piece, at):
            return ref.at[piece, pl.ds(at * SUB, SUB)]

        def gather(ref, kind):
            return (
                [
                    remote(half(ref, 0, 0), half(ref, 1, 0), gather_sems, kind, near_x),
                    remote(half(ref, 0, 1), half(ref, 1, 1), gather_sems, kind + 1, near_y),
                ],
                [
                    remote(half(ref, 0, 1), half(ref, 2, 0), gather_sems, kind + 2, near_x),
                    remote(half(ref, 0, 0), half(ref, 2, 1), gather_sems, kind + 3, near_y),
                ],
                [
                    remote(quarter(ref, 1, 2), quarter(ref, 3, 1), gather_sems, kind + 4, near_x),
                    remote(quarter(ref, 1, 0), quarter(ref, 3, 0), gather_sems, kind + 5, near_y),
                ],
                [
                    remote(quarter(ref, 1, 3), quarter(ref, 3, 3), gather_sems, kind + 6, near_x),
                    remote(quarter(ref, 1, 1), quarter(ref, 3, 2), gather_sems, kind + 7, near_y),
                ],
            )

        row_sends = gather(rows, 0)
        grad_sends = gather(grads, 8)

        begin(gated_sends)
        begin([keep_gated])
        lax.fori_loop(0, slices * quarters, start_slice, 0)
        begin(load_grads)
        begin([load_hidden])
        finish(load_grads)
        begin(grad_sends[1])
        finish([keep_gated, load_hidden])
        lax.fori_loop(0, slices * quarters, wait_slice, 0)
        finish(gated_sends)
        for j in range(width // wide_tile):
            at = slice(j * wide_tile, (j + 1) * wide_tile)
            middle_ref[:, at] = straight(gated_ref[...], w_in[:, at])
        begin(weights)

        def second_norm(i, carry, at):
            here = pl.ds(pl.multiple_of(at * HALF + i * 32, 32), 32)
            middle = hidden_ref[here, :].astype(jnp.float32) + live_ref[here, :1] * middle_ref[here, :]
            middle_ref[here, :] = middle
            rows[0, here, :] = row_norm(middle).astype(low)
            return carry

        for at in range(2):
            lax.fori_loop(0, HALF // 32, functools.partial(second_norm, at=at), 0)
            row_sends[0][at].start()
        begin(row_sends[1])
        store_middle = pltpu.make_async_copy(middle_ref, middle_out, done_sems.at[0])
        store_middle.start()

        def products(size, at, first, second, part_a, part_b, grad_act):
            act[:size, at] = (part_a * part_b).astype(low)
            parts[:size, first] = (grad_act * part_b).astype(low)
            parts[:size, second] = (grad_act * part_a).astype(low)

        def unit(arrived, arrived_grads, size, weights_wait):
            for which, (start, count) in enumerate(cuts):
                at, second = slice(start, start + count), slice(main + start, main + start + count)
                weights_wait(3 * which, 3 * which + 3)
                part_a = straight(arrived[...], w_in[:, at])
                part_b = straight(arrived[...], w_in[:, second])
                grad_act = across(arrived_grads[...], w_out[at, :])
                products(size, at, at, second, part_a, part_b, grad_act)
            weights_wait(6, 9)
            if tail:
                both = straight(arrived[...], w_in[:, 2 * main :])
                grad_act = across(arrived_grads[...], w_out[main:, :])
                products(
                    size,
                    slice(main, units),
                    slice(2 * main, 2 * main + tail),
                    slice(2 * main + tail, 2 * units),
                    both[:, :tail],
                    both[:, tail:],
                    grad_act,
                )

        def row_stores(arrived, arrived_grads, at):
            return [
                pltpu.make_async_copy(arrived, rows_out.at[at, :], done_sems.at[1]),
                pltpu.make_async_copy(arrived_grads, grads_out.at[at, :], done_sems.at[2]),
            ]

        def unit_stores(size, at):
            here = pl.ds(0, size)
            return [
                pltpu.make_async_copy(act.at[here], act_out.at[at, :], done_sems.at[3]),
                pltpu.make_async_copy(parts.at[here], parts_out.at[at, :], done_sems.at[4]),
            ]

        def sum_stores(piece, j):
            tile = pl.ds(j * wide_tile, wide_tile)
            return [
                pltpu.make_async_copy(
                    sums.at[at, :, tile],
                    (back_out, two_out)[at // 2].at[
                        pl.ds(pl.multiple_of(piece * PIECE + (at % 2) * HALF, HALF), HALF), tile
                    ],
                    sum_sems.at[j, at],
                )
                for at in range(4)
            ]

        def work(piece, carry):
            at = pl.ds(pl.multiple_of(piece * PIECE, PIECE), PIECE)
            arrived, arrived_grads = rows.at[piece], grads.at[piece]

            @pl.when(piece == 1)
            def _():
                finish(row_sends[0])
                for step in (2, 3):
                    begin(row_sends[step])
                    begin(grad_sends[step])

            @pl.when(piece == 2)
            def _():
                finish(row_sends[1])
                finish(grad_sends[1])

            stores = row_stores(arrived, arrived_grads, at)
            begin(stores)

            def weights_wait(start, stop):
                pl.when(piece == 0)(lambda: finish(weights[start:stop]))

            unit(arrived, arrived_grads, PIECE, weights_wait)
            more = unit_stores(PIECE, at)
            begin(more)
            for j in range(width // wide_tile):
                tile = slice(j * wide_tile, (j + 1) * wide_tile)

                @pl.when(piece > 0)
                def _(j=j):
                    finish(sum_stores(piece - 1, j))

                back = across(parts[...], w_in[tile, :])
                sums[0, :, tile] = back[:HALF].astype(low)
                sums[1, :, tile] = back[HALF:].astype(low)
                two = straight(act[...], w_out[:, tile])
                sums[2, :, tile] = two[:HALF].astype(low)
                sums[3, :, tile] = two[HALF:].astype(low)
                begin(sum_stores(piece, j))
            finish(stores)
            finish(more)
            return carry

        lax.fori_loop(0, pieces - 1, work, 0)
        for j in range(width // wide_tile):
            finish(sum_stores(pieces - 2, j))

        def last_stores(which):
            return [
                pltpu.make_async_copy(
                    sums.at[2 * total + which, pl.ds(part * SUB, SUB)],
                    (back_out, two_out)[total].at[
                        pl.ds(pl.multiple_of((pieces - 1) * PIECE + part * HALF + which * SUB, SUB), SUB)
                    ],
                    last_sems.at[which, 2 * total + part],
                )
                for total in range(2)
                for part in range(2)
            ]

        def last_work(which, carry):
            @pl.when(which == 0)
            def _():
                finish(row_sends[2])
                finish(grad_sends[2])

            @pl.when(which == 1)
            def _():
                finish(row_sends[3])
                finish(grad_sends[3])

            here = pl.ds(pl.multiple_of(which * HALF, HALF), HALF)
            at = pl.ds(pl.multiple_of((pieces - 1) * PIECE + which * HALF, HALF), HALF)
            arrived, arrived_grads = rows.at[pieces - 1, here], grads.at[pieces - 1, here]
            stores = row_stores(arrived, arrived_grads, at)
            begin(stores)
            unit(arrived, arrived_grads, HALF, lambda start, stop: None)
            more = unit_stores(HALF, at)
            begin(more)
            for j in range(width // wide_tile):
                tile = slice(j * wide_tile, (j + 1) * wide_tile)
                sums[which, :, tile] = across(parts[:HALF], w_in[tile, :]).astype(low)
                sums[2 + which, :, tile] = straight(act[:HALF], w_out[:, tile]).astype(low)
            begin(last_stores(which))
            finish(stores)
            finish(more)
            return carry

        lax.fori_loop(0, 2, last_work, 0)
        for which in range(2):
            finish(last_stores(which))
        store_middle.wait()

    return pl.pallas_call(
        body,
        in_specs=any_specs(7) + [pl.BlockSpec(memory_space=pltpu.VMEM)],
        out_specs=any_specs(7),
        out_shape=[
            jax.ShapeDtypeStruct((local_rows, width), jnp.float32),
            jax.ShapeDtypeStruct((group_rows, width), low),
            jax.ShapeDtypeStruct((group_rows, width), low),
            jax.ShapeDtypeStruct((group_rows, units), low),
            jax.ShapeDtypeStruct((group_rows, 2 * units), low),
            jax.ShapeDtypeStruct((group_rows, width), low),
            jax.ShapeDtypeStruct((group_rows, width), low),
        ],
        scratch_shapes=[
            pltpu.VMEM((local_rows, quarters * deep), low),
            pltpu.VMEM((local_rows, width), low),
            pltpu.VMEM((local_rows, width), jnp.float32),
            pltpu.VMEM((pieces, PIECE, width), low),
            pltpu.VMEM((pieces, PIECE, width), low),
            pltpu.VMEM((4, HALF, width), low),
            pltpu.VMEM((width, 2 * units), low),
            pltpu.VMEM((units, width), low),
            pltpu.VMEM((PIECE, units), low),
            pltpu.VMEM((PIECE, 2 * units), low),
            pltpu.SemaphoreType.DMA((4,)),
            pltpu.SemaphoreType.DMA((slices * quarters,)),
            pltpu.SemaphoreType.DMA((9,)),
            pltpu.SemaphoreType.DMA((5,)),
            pltpu.SemaphoreType.DMA((width // wide_tile, 4)),
            pltpu.SemaphoreType.DMA((2, 4)),
            pltpu.SemaphoreType.DMA((6, 2)),
            pltpu.SemaphoreType.DMA((16, 2)),
        ],
        compiler_params=pltpu.CompilerParams(
            vmem_limit_bytes=VMEM, collective_id=3, has_side_effects=True
        ),
        cost_estimate=cost(12 * group_rows * width * units, 90e6),
        name="gated_unit",
    )(gated, whole_weight, hidden, grads_own, grads_first, ffn_in, ffn_out, live)


def mix_rows(hidden, cotangent, mix_weight, out_weight, seq_lengths, block_seq):
    local_rows, width = hidden.shape
    parts, _, columns = mix_weight.shape
    heads = columns // HS
    group_rows = NBLK * BLK
    pieces = group_rows // PIECE
    wide_size = lax.axis_size("wide")
    slice_rows = columns // wide_size
    low = jnp.bfloat16
    joined = 2
    halves_at = (pl.ds(0, HALF), pl.ds(HALF, HALF))

    def body(*refs):
        hidden_in, cot_in, mix_in, out_in, length_ref, owner_ref = refs[:6]
        rows_out, parts_out, gated_out, mixing_out, states_out, grads_out, first_out, whole_out = refs[6:14]
        live_ref, keep_ref = refs[14:16]
        hidden_ref, cot_ref, rows, weights, parts_ref, gated_ref, mixing_ref, states_ref = refs[16:24]
        load_sems, mix_sems, store_sems, parts_sems, gather_sems, slice_sems, line_sems, core_sems = refs[24:]
        wide, narrow, z, core, mate, near_x, near_y = neighbours()
        far = (wide, 3 - narrow)
        above, below = (wide + 2, narrow), (wide - 2, narrow)
        barrier = pltpu.get_barrier_semaphore()

        def greet(place):
            pl.semaphore_signal(barrier, inc=1, device_id=place, device_id_type=MESH)

        load_hidden = pltpu.make_async_copy(hidden_in, hidden_ref, load_sems.at[0])
        load_cot = pltpu.make_async_copy(cot_in, cot_ref, load_sems.at[1])
        mix_loads = [
            pltpu.make_async_copy(
                mix_in.at[c], weights.at[:, pl.ds(c * columns, columns)], mix_sems.at[c]
            )
            for c in range(parts)
        ]
        load_hidden.start()
        for place in (near_x, near_y, far, mate):
            greet(place)
        pl.when(z < 3)(lambda: greet(above))
        pl.when(z > 0)(lambda: greet(below))
        middle = (z == 1) | (z == 2)
        pl.when(middle)(lambda: pl.semaphore_wait(barrier, 6))
        pl.when(jnp.logical_not(middle))(lambda: pl.semaphore_wait(barrier, 5))

        def remote(src, dst, sems, kind, place):
            return pltpu.make_async_remote_copy(
                src_ref=src,
                dst_ref=dst,
                send_sem=sems.at[kind, 0],
                recv_sem=sems.at[kind, 1],
                device_id=place,
                device_id_type=MESH,
            )

        slice_at = out_in.at[pl.ds(pl.multiple_of(wide * slice_rows, slice_rows), slice_rows)]
        keep_slice = pltpu.make_async_copy(slice_at, whole_out.at[wide, narrow], load_sems.at[2])
        slice_sends = [
            remote(slice_at, whole_out.at[wide, narrow], slice_sems, at, place)
            for at, place in enumerate((far, near_x, near_y))
        ]

        def up(hop):
            return remote(
                whole_out.at[wide - 2 * (hop - 1)], whole_out.at[wide - 2 * (hop - 1)], line_sems, hop - 1, above
            )

        def down_line(hop):
            return remote(
                whole_out.at[wide + 2 * (hop - 1)], whole_out.at[wide + 2 * (hop - 1)], line_sems, 2 + hop, below
            )

        def to_mate(hop, sign):
            at = wide + sign * 2 * hop
            return remote(whole_out.at[at], whole_out.at[at], core_sems, 3 + sign * hop, mate)

        def send_hop(hop):
            pl.when((z < 3) & (z >= hop - 1))(lambda: up(hop).start())
            pl.when((z > 0) & (z + hop - 1 <= 3))(lambda: down_line(hop).start())

        def take_hop(hop):
            @pl.when(z >= hop)
            def _():
                up(hop).wait_recv()
                to_mate(hop, -1).start()

            @pl.when(z + hop <= 3)
            def _():
                down_line(hop).wait_recv()
                to_mate(hop, 1).start()

        def end_hop(hop):
            pl.when((z < 3) & (z >= hop - 1))(lambda: up(hop).wait_send())
            pl.when((z > 0) & (z + hop - 1 <= 3))(lambda: down_line(hop).wait_send())
            pl.when(z >= hop)(lambda: to_mate(hop, -1).wait())
            pl.when(z + hop <= 3)(lambda: to_mate(hop, 1).wait())

        begin(slice_sends)
        keep_slice.start()

        def half(piece, at):
            return rows.at[piece, halves_at[at]]

        row_sends = (
            [remote(half(0, 0), half(1, 0), gather_sems, 0, near_x), remote(half(0, 1), half(1, 1), gather_sems, 1, near_y)],
            [remote(half(0, 1), half(2, 0), gather_sems, 2, near_x), remote(half(0, 0), half(2, 1), gather_sems, 3, near_y)],
            [remote(half(1, 1), half(3, 1), gather_sems, 4, near_x), remote(half(1, 0), half(3, 0), gather_sems, 5, near_y)],
        )
        grad_sends = [
            remote(cot_ref.at[halves_at[0]], first_out.at[halves_at[0]], gather_sems, 6, near_x),
            remote(cot_ref.at[halves_at[1]], first_out.at[halves_at[1]], gather_sems, 7, near_y),
        ]
        load_hidden.wait()
        begin(mix_loads)
        load_cot.start()

        def first_norm(i, carry):
            at = pl.ds(pl.multiple_of(i * 32, 32), 32)
            rows[0, at, :] = row_norm(hidden_ref[at, :].astype(jnp.float32)).astype(low)
            return carry

        for at in range(2):
            lax.fori_loop(at * HALF // 32, (at + 1) * HALF // 32, first_norm, 0)
            row_sends[0][at].start()
        begin(row_sends[1])

        def row_store(piece):
            at = pl.ds(piece * PIECE, PIECE)
            return pltpu.make_async_copy(rows.at[piece], rows_out.at[at, :], store_sems.at[piece])

        def part_stores(piece):
            at = pl.ds(piece * PIECE, PIECE)
            return [
                pltpu.make_async_copy(
                    parts_ref.at[at, pl.ds(c * columns, columns)], parts_out.at[c, at, :], parts_sems.at[piece, c]
                )
                for c in range(parts)
            ]

        def project(piece):
            row_store(piece).start()
            for c in range(0, parts, joined):
                if piece == 0:
                    finish(mix_loads[c : c + joined])
                at = slice(c * columns, (c + joined) * columns)
                result = straight(rows[piece], weights[:, at]).astype(low)
                parts_ref[piece * PIECE : (piece + 1) * PIECE, at] = result
            begin(part_stores(piece))

        def same_slot(block):
            return owner_ref[block] == owner_ref[0]

        first_count = sum(jnp.where(same_slot(block), 1, 0) for block in range(NBLK))

        def start_of(block):
            return jnp.where(same_slot(block), 0, first_count)

        for block in range(NBLK):
            entering = jnp.where(start_of(block) == block, 0.0, 1.0)
            keep_ref[block : block + 1, :] = jnp.full((1, HS), entering, jnp.float32)
        for at in range(local_rows // BLK):
            block = narrow * (local_rows // BLK) + at
            limit = jnp.where(same_slot(block), length_ref[0], length_ref[1])
            place = lax.broadcasted_iota(jnp.int32, (BLK, HS), 0) + (block - start_of(block)) * BLK
            live_ref[at * BLK : (at + 1) * BLK, :] = jnp.where(place < limit, 1.0, 0.0)
        project(0)
        load_cot.wait()

        def live_cot(i, carry):
            at = pl.ds(pl.multiple_of(i * 32, 32), 32)
            cot_ref[at, :] = (live_ref[at, :1] * cot_ref[at, :].astype(jnp.float32)).astype(low)
            return carry

        keep_slice.wait()
        finish(slice_sends)
        to_mate(0, 1).start()
        send_hop(1)
        lax.fori_loop(0, local_rows // 32, live_cot, 0)
        store_grads = pltpu.make_async_copy(cot_ref, grads_out, load_sems.at[3])
        store_grads.start()
        finish(row_sends[0])
        begin(row_sends[2])
        begin(grad_sends)
        project(1)
        take_hop(1)
        send_hop(2)
        finish(row_sends[1])
        project(2)
        take_hop(2)
        send_hop(3)
        finish(row_sends[2])
        project(3)

        def attend(head, carry):
            within, entry, leave, whole = block_decays(head_rate(heads * narrow + head))
            state = jnp.zeros((HS, HS), jnp.float32)

            def part(c, rows_at):
                at = pl.ds(pl.multiple_of(c * columns + head * HS, HS), HS)
                return parts_ref[rows_at, at]

            for block in range(NBLK):
                rows_at = pl.ds(pl.multiple_of(slot_of(block, narrow) * BLK, BLK), BLK)
                queries = jax.nn.silu(part(0, rows_at).astype(jnp.float32)).astype(low)
                keys = jax.nn.silu(part(1, rows_at).astype(jnp.float32)).astype(low)
                values = part(2, rows_at)
                gate = part(3, rows_at).astype(jnp.float32)
                state = keep_ref[block : block + 1, :] * state
                state_low = state.astype(low)
                states_ref[head, block] = state_low
                scores = (across(queries, keys) * within).astype(low)
                mixing = straight(scores, values) + entry * straight(queries, state_low)
                late_keys = (keys.astype(jnp.float32) * leave).astype(low)
                state = whole * state + down(late_keys, values)
                scale = lax.rsqrt(jnp.mean(mixing * mixing, axis=-1, keepdims=True) + head_floor)
                at = pl.ds(pl.multiple_of(head * HS, HS), HS)
                gated_ref[rows_at, at] = (mixing * scale * gate).astype(low)
                mixing_ref[rows_at, at] = mixing.astype(low)
            return carry

        lax.fori_loop(0, heads // 2, attend, 0)
        take_hop(3)
        lax.fori_loop(heads // 2, heads, attend, 0)
        stores = [
            pltpu.make_async_copy(gated_ref, gated_out.at[0], load_sems.at[4]),
            pltpu.make_async_copy(mixing_ref, mixing_out, load_sems.at[5]),
            pltpu.make_async_copy(states_ref, states_out, load_sems.at[6]),
        ]
        begin(stores)
        to_mate(0, 1).wait()
        for hop in range(1, 4):
            end_hop(hop)
        finish(grad_sends)
        store_grads.wait()
        for piece in range(pieces):
            row_store(piece).wait()
            finish(part_stores(piece))
        finish(stores)

    low_shape = functools.partial(jax.ShapeDtypeStruct, dtype=low)
    return pl.pallas_call(
        body,
        in_specs=any_specs(4) + [pl.BlockSpec(memory_space=pltpu.SMEM)] * 2,
        out_specs=any_specs(8) + [pl.BlockSpec(memory_space=pltpu.VMEM)] * 2,
        out_shape=[
            low_shape((group_rows, width)),
            low_shape((parts, group_rows, columns)),
            low_shape((1, group_rows, columns)),
            low_shape((group_rows, columns)),
            low_shape((heads, NBLK, HS, HS)),
            low_shape((local_rows, width)),
            low_shape((local_rows, width)),
            low_shape((wide_size, pieces, slice_rows, width)),
            jax.ShapeDtypeStruct((local_rows, HS), jnp.float32),
            jax.ShapeDtypeStruct((NBLK, HS), jnp.float32),
        ],
        scratch_shapes=[
            pltpu.VMEM((local_rows, width), low),
            pltpu.VMEM((local_rows, width), low),
            pltpu.VMEM((pieces, PIECE, width), low),
            pltpu.VMEM((width, parts * columns), low),
            pltpu.VMEM((group_rows, parts * columns), low),
            pltpu.VMEM((group_rows, columns), low),
            pltpu.VMEM((group_rows, columns), low),
            pltpu.VMEM((heads, NBLK, HS, HS), low),
            pltpu.SemaphoreType.DMA((7,)),
            pltpu.SemaphoreType.DMA((parts,)),
            pltpu.SemaphoreType.DMA((pieces,)),
            pltpu.SemaphoreType.DMA((pieces, parts)),
            pltpu.SemaphoreType.DMA((8, 2)),
            pltpu.SemaphoreType.DMA((3, 2)),
            pltpu.SemaphoreType.DMA((6, 2)),
            pltpu.SemaphoreType.DMA((7, 2)),
        ],
        compiler_params=pltpu.CompilerParams(
            vmem_limit_bytes=VMEM, collective_id=4, has_side_effects=True
        ),
        cost_estimate=cost(2 * group_rows * parts * width * columns, 50e6),
        name="mix_rows",
    )(hidden, cotangent, mix_weight, out_weight, seq_lengths, block_seq)


def finish_rows(
    mix_low, out_low, in_low, wide_low, hidden, middle, grad_middle, live, normed_terms, two_sums, two_terms
):
    parts, width, columns = mix_low.shape
    local_rows = hidden.shape[0]
    units = wide_low.shape[0]
    main = units // TILE * TILE
    tail = units - main
    steps = 2 * parts
    tile, out_tile = local_rows // steps, out_low.shape[0] // steps
    in_tile, unit_tile, mix_tile = width // steps, units // steps, width // 2
    half_steps = steps // 2
    terms = len(normed_terms) + len(two_terms)

    def body(
        mix_ref, out_ref, in_ref, wide_ref, hidden_ref, middle_ref, grad_ref, live_ref, own_ref, *refs
    ):
        term_refs = refs[:terms]
        mix_out, out_out, in_out, wide_out, layer_ref, input_ref = refs[terms:]
        mix_out[...] = mix_ref[...].astype(jnp.float32)
        out_out[...] = out_ref[...].astype(jnp.float32)
        wide_out[...] = wide_ref[...].astype(jnp.float32)
        for c in range(2):
            in_out[c, :, :main] = in_ref[:, c * main : (c + 1) * main].astype(jnp.float32)
            rest = slice(2 * main + c * tail, 2 * main + (c + 1) * tail)
            in_out[c, :, main:] = in_ref[:, rest].astype(jnp.float32)

        def rows_of(half):
            normed = add_rows(*(ref[...] for ref in term_refs[3 * half : 3 * half + 3]))
            two = add_rows(*(ref[...] for ref in term_refs[6 + 2 * half : 8 + 2 * half]), own_ref[...])
            layer = middle_ref[...] + live_ref[:, :1] * two
            layer_ref[...] = layer.astype(jnp.bfloat16)
            back = norm_back(hidden_ref[...].astype(jnp.float32), normed)
            input_ref[...] = (grad_ref[...] + back).astype(jnp.bfloat16)

        first = pl.program_id(0) < half_steps
        pl.when(first)(lambda: rows_of(0))
        pl.when(jnp.logical_not(first))(lambda: rows_of(1))

    def rows_spec(size, height=tile):
        return pl.BlockSpec((height, size), lambda i: (i, 0))

    def half_spec(half):
        if half == 0:
            return pl.BlockSpec((tile, width), lambda i: (jnp.minimum(i, half_steps - 1), 0))
        return pl.BlockSpec((tile, width), lambda i: (jnp.maximum(i - half_steps, 0), 0))

    term_specs = [half_spec(0)] * 3 + [half_spec(1)] * 3 + [half_spec(0)] * 2 + [half_spec(1)] * 2
    mix_spec = pl.BlockSpec((1, mix_tile, columns), lambda i: (i // 2, i % 2, 0))
    out_spec = rows_spec(width, out_tile)
    wide_spec = rows_spec(width, unit_tile)
    wide_float = jnp.float32
    return pl.pallas_call(
        body,
        grid=(steps,),
        in_specs=[mix_spec, out_spec, rows_spec(2 * units, in_tile), wide_spec]
        + [rows_spec(width)] * 3
        + [rows_spec(live.shape[1]), rows_spec(width)]
        + term_specs,
        out_specs=[
            mix_spec,
            out_spec,
            pl.BlockSpec((2, in_tile, units), lambda i: (0, i, 0)),
            wide_spec,
            rows_spec(width),
            rows_spec(width),
        ],
        out_shape=[
            jax.ShapeDtypeStruct(mix_low.shape, wide_float),
            jax.ShapeDtypeStruct(out_low.shape, wide_float),
            jax.ShapeDtypeStruct((2, width, units), wide_float),
            jax.ShapeDtypeStruct(wide_low.shape, wide_float),
            jax.ShapeDtypeStruct(hidden.shape, jnp.bfloat16),
            jax.ShapeDtypeStruct(hidden.shape, jnp.bfloat16),
        ],
        compiler_params=pltpu.CompilerParams(vmem_limit_bytes=VMEM),
        cost_estimate=cost(1e8, 110e6),
        name="finish_rows",
    )(
        mix_low,
        out_low,
        in_low,
        wide_low,
        hidden,
        middle,
        grad_middle,
        live,
        two_sums,
        *normed_terms,
        *two_terms,
    )


def block_decays(rate):
    row = lax.broadcasted_iota(jnp.int32, (BLK, BLK), 0)
    column = lax.broadcasted_iota(jnp.int32, (BLK, BLK), 1)
    distance = (row - column).astype(jnp.float32)
    within = jnp.where(row >= column, jnp.exp(-rate * jnp.maximum(distance, 0.0)), 0.0)
    place = lax.broadcasted_iota(jnp.int32, (BLK, 1), 0).astype(jnp.float32)
    entry = jnp.exp(-rate * (place + 1.0))
    leave = jnp.exp(-rate * (BLK - 1.0 - place))
    whole = jnp.exp(-BLK * rate * jnp.ones((1, HS), jnp.float32))
    return within, entry, leave, whole


def norm_back(values, grad):
    scale = lax.rsqrt(jnp.mean(values * values, axis=-1, keepdims=True) + epsilon)
    unit = values * scale
    return scale * (grad - unit * jnp.mean(grad * unit, axis=-1, keepdims=True))


def square_device(
    hidden, mix_weight, out_weight, ffn_in_weight, ffn_out_weight, seq_lengths, block_seq, cotangent
):
    width = hidden.shape[1]
    units = ffn_out_weight.shape[0]
    normed_all, parts, gated, mixing, states, grads_own, grads_first, whole_weight, live, keep = mix_rows(
        hidden, cotangent, mix_weight, out_weight, seq_lengths, block_seq
    )
    middle, normed_two_all, grad_two_all, act, grad_parts, back_sums, two_sums = gated_unit(
        gated,
        whole_weight,
        hidden,
        live,
        grads_own,
        grads_first,
        ffn_in_weight,
        ffn_out_weight,
    )
    in_low, wide_low, out_low, mix_low, _, grad_middle, own_top, own_low, *terms = weight_grads(
        act,
        grad_two_all,
        normed_two_all,
        grad_parts,
        back_sums,
        two_sums,
        middle,
        cotangent,
        out_weight,
        mix_weight,
        parts,
        mixing,
        states,
        gated,
        normed_all,
        live,
        keep,
    )
    grad_mix, grad_out, grad_ffn_in, grad_ffn_out, layer_out, input_grad = finish_rows(
        mix_low.reshape(mix_weight.shape),
        out_low.reshape(out_weight.shape),
        in_low.reshape(width, 2 * units),
        wide_low.reshape(units, width),
        hidden,
        middle,
        grad_middle,
        live,
        (own_top, terms[0], terms[2], own_low, terms[1], terms[3]),
        two_sums,
        (terms[4], terms[6], terms[5], terms[7]),
    )
    return (layer_out, input_grad, grad_mix, grad_out, grad_ffn_in, grad_ffn_out)


def solution(mesh):
    square = mesh.shape["wide"] == 8 and mesh.shape["narrow"] == 4
    per_device = square_device if square else general_device
    in_specs = (
        P(("wide", "narrow"), None),
        P(None, None, "narrow"),
        P("narrow", None),
        P(None, None, "narrow"),
        P("narrow", None),
        P("wide"),
        P("wide"),
        P(("wide", "narrow"), None),
    )
    out_specs = (
        P(("wide", "narrow"), None),
        P(("wide", "narrow"), None),
        P(None, None, "narrow"),
        P("narrow", None),
        P(None, None, "narrow"),
        P("narrow", None),
    )
    return jax.shard_map(
        per_device, mesh=mesh, in_specs=in_specs, out_specs=out_specs, check_vma=False
    )
```

```python
import functools
import math

import jax
import jax.numpy as jnp
from jax import lax
from jax.experimental import pallas as pl
from jax.experimental.pallas import tpu as pltpu
from jax.sharding import PartitionSpec as P

HEADS = 16
HS = 128
BLK = 256
NBLK = 8


epsilon = 1e-06
head_floor = 1.0
highest = lax.Precision.HIGHEST


def row_norm(values):
    return values * lax.rsqrt(jnp.mean(values * values, axis=-1, keepdims=True) + epsilon)


def head_norm(values):
    return values * lax.rsqrt(jnp.mean(values * values, axis=-1, keepdims=True) + head_floor)


def silu_slope(values):
    sigmoid_part = jax.nn.sigmoid(values)
    return sigmoid_part * (1.0 + values * (1.0 - sigmoid_part))


def decay_tables(decay_rates):
    positions = jnp.arange(BLK, dtype=jnp.float32)
    distance = positions[:, None] - positions[None, :]
    causal = distance >= 0
    clipped = jnp.where(causal, distance, 0.0)
    within = jnp.where(causal[None], jnp.exp(-decay_rates[:, None, None] * clipped[None]), 0.0)
    entry_decay = jnp.exp(-(positions[:, None] + 1.0) * decay_rates[None, :])
    exit_decay = jnp.exp(-(BLK - 1.0 - positions[:, None]) * decay_rates[None, :])
    block_decay = jnp.exp(-BLK * decay_rates)
    return (within, entry_decay, exit_decay, block_decay)


def group_masks(lengths, owners):
    seq_slot = owners - owners[0]
    first_count = jnp.sum((seq_slot == 0).astype(jnp.int32))
    block_ids = jnp.arange(NBLK, dtype=jnp.int32)
    start_block = jnp.where(seq_slot == 0, jnp.int32(0), first_count)
    seq_limit = jnp.where(seq_slot == 0, lengths[0], lengths[1])
    offsets = (block_ids - start_block)[:, None] * BLK + jnp.arange(BLK, dtype=jnp.int32)[None, :]
    valid_rows = (offsets < seq_limit[:, None]).reshape(-1)
    fresh_block = block_ids == start_block
    return (valid_rows, fresh_block)


def forward_block(tables, kv_state, block_in):
    within, entry_decay, exit_decay, block_decay = tables
    queries, keys_in, values, fresh_block = block_in
    kv_state = jnp.where(fresh_block, 0.0, kv_state)
    scores = jnp.einsum("ihs,jhs->hij", queries, keys_in, preferred_element_type=jnp.float32)
    weights = (scores * within).astype(jnp.bfloat16)
    inner_part = jnp.einsum("hij,jhs->ihs", weights, values, preferred_element_type=jnp.float32)
    carried = jnp.einsum(
        "ihs,hst->iht",
        queries.astype(jnp.float32) * entry_decay[:, :, None],
        kv_state,
        precision=highest,
    )
    update = jnp.einsum(
        "ihs,iht->hst",
        keys_in.astype(jnp.float32) * exit_decay[:, :, None],
        values.astype(jnp.float32),
        precision=highest,
    )
    return (block_decay[:, None, None] * kv_state + update, (inner_part + carried, kv_state))


def backward_block(tables, later_grad, block_in):
    within, entry_decay, exit_decay, block_decay = tables
    queries, keys_in, values, grad_mix, kv_state, fresh_block = block_in
    scores = jnp.einsum("ihs,jhs->hij", queries, keys_in, preferred_element_type=jnp.float32)
    weights = (scores * within).astype(jnp.bfloat16)
    grad_values = jnp.einsum("hij,ihs->jhs", weights, grad_mix, preferred_element_type=jnp.float32)
    grad_weights = jnp.einsum("ihs,jhs->hij", grad_mix, values, preferred_element_type=jnp.float32)
    grad_scores = (grad_weights * within).astype(jnp.bfloat16)
    grad_queries = jnp.einsum(
        "hij,jhs->ihs", grad_scores, keys_in, preferred_element_type=jnp.float32
    )
    grad_keys = jnp.einsum("hij,ihs->jhs", grad_scores, queries, preferred_element_type=jnp.float32)
    grad_float = grad_mix.astype(jnp.float32)
    values_float = values.astype(jnp.float32)
    queries_float = queries.astype(jnp.float32)
    keys_float = keys_in.astype(jnp.float32)
    grad_queries = grad_queries + entry_decay[:, :, None] * jnp.einsum(
        "iht,hst->ihs", grad_float, kv_state, precision=highest
    )
    grad_keys = grad_keys + exit_decay[:, :, None] * jnp.einsum(
        "iht,hst->ihs", values_float, later_grad, precision=highest
    )
    grad_values = grad_values + jnp.einsum(
        "ihs,hst->iht", keys_float * exit_decay[:, :, None], later_grad, precision=highest
    )
    grad_state = jnp.einsum(
        "ihs,iht->hst", queries_float * entry_decay[:, :, None], grad_float, precision=highest
    )
    grad_state = grad_state + block_decay[:, None, None] * later_grad
    grad_state = jnp.where(fresh_block, 0.0, grad_state)
    return (grad_state, (grad_queries, grad_keys, grad_values))


def general_device(
    hidden, mix_weight, out_weight, ffn_in_weight, ffn_out_weight, seq_lengths, block_seq, cotangent
):
    local_rows = hidden.shape[0]
    group_rows = NBLK * BLK
    head_width = mix_weight.shape[2]
    head_count = head_width // HS
    narrow_index = lax.axis_index("narrow")
    valid_all, fresh_block = group_masks(seq_lengths, block_seq)
    valid_rows = lax.dynamic_slice_in_dim(
        valid_all.astype(jnp.float32), narrow_index * local_rows, local_rows
    )[:, None]
    head_ids = narrow_index * head_count + jnp.arange(head_count, dtype=jnp.int32)
    decay_rates = 2.0 ** (-8.0 * (head_ids.astype(jnp.float32) + 1.0) / HEADS)
    tables = decay_tables(decay_rates)

    def split_blocks(flat_rows):
        return flat_rows.reshape(NBLK, BLK, head_count, HS)

    inputs = hidden.astype(jnp.float32)
    normed_low = row_norm(inputs).astype(jnp.bfloat16)
    gathered = lax.all_gather(normed_low, "narrow", axis=0, tiled=True)
    projected = jnp.einsum("rd,cde->cre", gathered, mix_weight, preferred_element_type=jnp.float32)
    queries = jax.nn.silu(projected[0]).astype(jnp.bfloat16)
    keys_in = jax.nn.silu(projected[1]).astype(jnp.bfloat16)
    values = projected[2].astype(jnp.bfloat16)
    gate_part = projected[3]
    zero_state = jnp.zeros((head_count, HS, HS), jnp.float32)
    final_state, (mixing, kept_states) = lax.scan(
        lambda state_in, block_in: forward_block(tables, state_in, block_in),
        zero_state,
        (split_blocks(queries), split_blocks(keys_in), split_blocks(values), fresh_block),
    )
    mixing = mixing.reshape(group_rows, head_count, HS)
    headed = head_norm(mixing).reshape(group_rows, head_width)
    gated_low = (headed * gate_part).astype(jnp.bfloat16)
    branch = lax.psum_scatter(
        jnp.dot(gated_low, out_weight, preferred_element_type=jnp.float32).astype(jnp.bfloat16),
        "narrow",
        scatter_dimension=0,
        tiled=True,
    ).astype(jnp.float32)
    middle = inputs + valid_rows * branch
    normed_two_low = row_norm(middle).astype(jnp.bfloat16)
    gathered_two = lax.all_gather(normed_two_low, "narrow", axis=0, tiled=True)
    both_parts = jnp.einsum(
        "rd,cdf->crf", gathered_two, ffn_in_weight, preferred_element_type=jnp.float32
    )
    hidden_low = (both_parts[0] * both_parts[1]).astype(jnp.bfloat16)
    branch_two = lax.psum_scatter(
        jnp.dot(hidden_low, ffn_out_weight, preferred_element_type=jnp.float32).astype(
            jnp.bfloat16
        ),
        "narrow",
        scatter_dimension=0,
        tiled=True,
    ).astype(jnp.float32)
    layer_out = (middle + valid_rows * branch_two).astype(jnp.bfloat16)
    grad_rows = cotangent.astype(jnp.float32)
    ffn_grad_all = lax.all_gather(
        (valid_rows * grad_rows).astype(jnp.bfloat16), "narrow", axis=0, tiled=True
    )
    grad_ffn_out = jnp.einsum(
        "rf,rd->fd", hidden_low, ffn_grad_all, preferred_element_type=jnp.float32
    )
    grad_hidden = jnp.einsum(
        "rd,fd->rf", ffn_grad_all, ffn_out_weight, preferred_element_type=jnp.float32
    )
    grad_parts = jnp.stack([grad_hidden * both_parts[1], grad_hidden * both_parts[0]]).astype(
        jnp.bfloat16
    )
    grad_ffn_in = jnp.einsum(
        "rd,crf->cdf", gathered_two, grad_parts, preferred_element_type=jnp.float32
    )
    grad_slice = grad_parts
    grad_normed_two = lax.psum_scatter(
        jnp.einsum(
            "crf,cdf->rd", grad_slice, ffn_in_weight, preferred_element_type=jnp.float32
        ).astype(jnp.bfloat16),
        "narrow",
        scatter_dimension=0,
        tiled=True,
    ).astype(jnp.float32)
    norm_value, norm_pull = jax.vjp(row_norm, middle)
    grad_middle = grad_rows + norm_pull(grad_normed_two)[0]
    attn_grad_all = lax.all_gather(
        (valid_rows * grad_middle).astype(jnp.bfloat16), "narrow", axis=0, tiled=True
    )
    grad_out_weight = jnp.einsum(
        "re,rd->ed", gated_low, attn_grad_all, preferred_element_type=jnp.float32
    )
    grad_gated = jnp.einsum(
        "rd,ed->re", attn_grad_all, out_weight, preferred_element_type=jnp.float32
    )
    grad_gated = lax.optimization_barrier(grad_gated.astype(jnp.bfloat16)).astype(jnp.float32)
    grad_gate = grad_gated * headed
    grad_headed = (grad_gated * gate_part).reshape(group_rows, head_count, HS)
    head_value, head_pull = jax.vjp(head_norm, mixing)
    grad_mixing = head_pull(grad_headed)[0].astype(jnp.bfloat16)
    first_grad, (grad_queries, grad_keys, grad_values) = lax.scan(
        lambda later_grad, block_in: backward_block(tables, later_grad, block_in),
        zero_state,
        (
            split_blocks(queries),
            split_blocks(keys_in),
            split_blocks(values),
            split_blocks(grad_mixing),
            kept_states,
            fresh_block,
        ),
        reverse=True,
    )
    grad_projected = jnp.stack(
        [
            grad_queries.reshape(group_rows, head_width) * silu_slope(projected[0]),
            grad_keys.reshape(group_rows, head_width) * silu_slope(projected[1]),
            grad_values.reshape(group_rows, head_width),
            grad_gate,
        ]
    ).astype(jnp.bfloat16)
    grad_mix = jnp.einsum(
        "rd,cre->cde", gathered, grad_projected, preferred_element_type=jnp.float32
    )
    grad_slice = grad_projected
    grad_normed = lax.psum_scatter(
        jnp.einsum(
            "cre,cde->rd", grad_slice, mix_weight, preferred_element_type=jnp.float32
        ).astype(jnp.bfloat16),
        "narrow",
        scatter_dimension=0,
        tiled=True,
    ).astype(jnp.float32)
    first_value, first_pull = jax.vjp(row_norm, inputs)
    input_grad = (grad_middle + first_pull(grad_normed)[0]).astype(jnp.bfloat16)
    grad_mix, grad_out_weight, grad_ffn_in, grad_ffn_out = (
        lax.psum(grad_mix.astype(jnp.bfloat16), "wide").astype(jnp.float32),
        lax.psum(grad_out_weight.astype(jnp.bfloat16), "wide").astype(jnp.float32),
        lax.psum(grad_ffn_in.astype(jnp.bfloat16), "wide").astype(jnp.float32),
        lax.psum(grad_ffn_out.astype(jnp.bfloat16), "wide").astype(jnp.float32),
    )
    return (layer_out, input_grad, grad_mix, grad_out_weight, grad_ffn_in, grad_ffn_out)


HALF = BLK
PIECE = 2 * BLK
VMEM = 60 * 1024 * 1024


def add_low(*terms):
    return sum(term.astype(jnp.float32) for term in terms).astype(jnp.bfloat16)


def add_rows(*terms):
    return sum(term.astype(jnp.float32) for term in terms)


def across(left, right):
    return lax.dot_general(left, right, (((1,), (1,)), ((), ())), preferred_element_type=jnp.float32)


def down(left, right):
    return lax.dot_general(left, right, (((0,), (0,)), ((), ())), preferred_element_type=jnp.float32)


def straight(left, right):
    return jnp.dot(left, right, preferred_element_type=jnp.float32)


def any_specs(count):
    return [pl.BlockSpec(memory_space=pl.ANY)] * count


def cost(flops, bytes_accessed):
    return pl.CostEstimate(flops=int(flops), bytes_accessed=int(bytes_accessed), transcendentals=0)


MESH = pl.DeviceIdType.MESH
SLOTS = 12
STAGES = 11
SUB = 128
TILE = 256


def begin(copies):
    for copy in copies:
        copy.start()


def finish(copies):
    for copy in copies:
        copy.wait()


def neighbours():
    wide, narrow = lax.axis_index("wide"), lax.axis_index("narrow")
    z, core = wide // 2, wide % 2
    mate = (wide + 1 - 2 * core, narrow)
    near_x = (wide, narrow + 1 - 2 * (narrow % 2))
    near_y = (wide, (narrow + 2) % 4)
    return wide, narrow, z, core, mate, near_x, near_y


def slot_of(block, narrow):
    off_x = (block // 2 % 2 + narrow % 2) % 2
    off_y = (block // 4 + narrow // 2) % 2
    if block % 2:
        return 1 + 3 * off_x + 2 * off_y + off_x * off_y
    return 2 * off_x + 5 * off_y - off_x * off_y


def head_rate(head):
    return jnp.exp(jnp.full((1, 1), -8.0 / HEADS * math.log(2.0), jnp.float32) * (head.astype(jnp.float32) + 1.0))


def line_scratch():
    low = jnp.bfloat16
    pair = pltpu.VMEM((SLOTS, 2, SUB, TILE), low)
    return [
        pltpu.VMEM((SLOTS, 4, SUB, TILE), low),
        pair,
        pair,
        pair,
        pltpu.VMEM((SLOTS, SUB, TILE), low),
        pair,
        pair,
        pltpu.SemaphoreType.DMA((14, SLOTS)),
        pltpu.SemaphoreType.DMA((4, SLOTS)),
    ]


def enter(neighbour_places):
    wide, narrow, z, core, mate, near_x, near_y = neighbour_places
    barrier = pltpu.get_barrier_semaphore()

    def greet(place):
        pl.semaphore_signal(barrier, inc=1, device_id=place, device_id_type=MESH)

    for place in (mate, near_x, near_y):
        greet(place)
    middle = (z == 1) | (z == 2)

    @pl.when(middle)
    def _():
        greet((2 * (3 - z) + core, narrow))
        greet((6 * (z - 1) + core, narrow))
        pl.semaphore_wait(barrier, 5)

    @pl.when(jnp.logical_not(middle))
    def _():
        greet((2 * (1 + z // 3) + core, narrow))
        pl.semaphore_wait(barrier, 4)


def line_sum(scratch, places, count, product, targets):
    own, met, both, ended, crossed, full, other, sems, out_sems = scratch
    wide, narrow, z, core, mate, _, _ = places
    region = z // 2
    middle = (z == 1) | (z == 2)
    end = jnp.logical_not(middle)
    inward = (2 * (1 + z // 3) + core, narrow)
    across_line = (2 * (3 - z) + core, narrow)
    outward = (6 * (z - 1) + core, narrow)

    def remote(src, dst, kind, slot, place):
        return pltpu.make_async_remote_copy(
            src_ref=src,
            dst_ref=dst,
            send_sem=sems.at[2 * kind, slot],
            recv_sem=sems.at[2 * kind + 1, slot],
            device_id=place,
            device_id_type=MESH,
        )

    def core_one(s):
        return remote(own.at[s, pl.ds(2 * (1 - core), 2)], met.at[s], 0, s, mate)

    def line_one(s):
        return remote(both.at[s], ended.at[s], 1, s, inward)

    def cross_one(s):
        return remote(both.at[s, 1 - region], crossed.at[s], 2, s, across_line)

    def cross_two(s):
        return remote(full.at[s, region], full.at[s, region], 3, s, across_line)

    def out_one(s):
        return remote(full.at[s, region], full.at[s, region], 4, s, outward)

    def out_two(s):
        return remote(full.at[s, 1 - region], full.at[s, 1 - region], 5, s, outward)

    def core_two(s):
        return remote(full.at[s], other.at[s], 6, s, mate)

    def add(left, right):
        return (left.astype(jnp.float32) + right.astype(jnp.float32)).astype(jnp.bfloat16)

    def deliveries(k, s):
        for t in range(2):
            for which, (src, part) in enumerate(
                ((full.at[s, t], 2 * core + t), (other.at[s, t], 2 * (1 - core) + t))
            ):
                for condition, ref in targets(k, part):
                    yield condition, pltpu.make_async_copy(src, ref, out_sems.at[2 * t + which, s])

    def start(k, s):
        product(k, own.at[s])
        core_one(s).start()

    def cores(k, s):
        core_one(s).wait_recv()
        both[s] = add(own[s, pl.ds(2 * core, 2)], met[s])
        pl.when(end)(lambda: line_one(s).start())

    def ends(k, s):
        @pl.when(middle)
        def _():
            line_one(s).wait_recv()
            both[s] = add(both[s], ended[s])
            cross_one(s).start()

    def centre(k, s):
        @pl.when(middle)
        def _():
            cross_one(s).wait_recv()
            full[s, region] = add(both[s, region], crossed[s])
            cross_two(s).start()
            out_one(s).start()

    def pass_on(k, s):
        @pl.when(middle)
        def _():
            cross_two(s).wait_recv()
            out_two(s).start()

    def back(k, s):
        @pl.when(end)
        def _():
            out_one(s).wait_recv()
            out_two(s).wait_recv()

        core_two(s).start()

    def deliver(k, s):
        core_two(s).wait_recv()
        for condition, copy in deliveries(k, s):
            pl.when(condition)(copy.start)

    def clear(k, s):
        core_one(s).wait_send()
        core_two(s).wait_send()

        @pl.when(end)
        def _():
            line_one(s).wait_send()

        @pl.when(middle)
        def _():
            for copy in (cross_one(s), cross_two(s), out_one(s), out_two(s)):
                copy.wait_send()

        for t in range(2):
            for which, src in enumerate((full, other)):
                ref = targets(k, 0)[0][1]
                pltpu.make_async_copy(src.at[s, t], ref, out_sems.at[2 * t + which, s]).wait()

    stages = (
        (11, clear),
        (10, deliver),
        (9, back),
        (7, pass_on),
        (5, centre),
        (3, ends),
        (1, cores),
        (0, start),
    )

    def step(i, carry):
        for delay, work in stages:
            k = i - delay

            @pl.when((k >= 0) & (k < count))
            def _(work=work, k=k):
                work(k, lax.rem(k + SLOTS, SLOTS))

        return carry

    return step


def square_scratch(uses):
    block = pltpu.VMEM((2, BLK, HEADS * HS), jnp.bfloat16)
    return [block, block, pltpu.SemaphoreType.DMA((uses, 6, 2)), pltpu.SemaphoreType.DMA((uses, 2))]


def square_sum(scratch, places, parts, landed, use, side=None):
    met, mid, sems, load_sems = scratch
    top_x, low_y, low_x, top_y, top_d, low_d = parts
    near_x, near_y = places[5:]

    def remote(src, dst, kind, place):
        return pltpu.make_async_remote_copy(
            src_ref=src,
            dst_ref=dst,
            send_sem=sems.at[use, kind, 0],
            recv_sem=sems.at[use, kind, 1],
            device_id=place,
            device_id_type=MESH,
        )

    first = [remote(top_d, met.at[0], 0, near_x), remote(low_d, met.at[1], 1, near_y)]
    direct = [remote(top_x, landed[0], 2, near_x), remote(low_y, landed[1], 3, near_y)]
    second = [remote(mid.at[0], landed[2], 4, near_y), remote(mid.at[1], landed[3], 5, near_x)]
    loads = []
    if top_y is not None:
        loads = [
            pltpu.make_async_copy(top_y, mid.at[0], load_sems.at[use, 0]),
            pltpu.make_async_copy(low_x, mid.at[1], load_sems.at[use, 1]),
        ]

    def open_sum():
        begin(first)
        begin(direct)
        begin(loads)

    def join_sum():
        finish(loads)
        for at in range(2):
            first[at].wait()

            def tile(i, carry, at=at):
                rows = pl.ds(pl.multiple_of(i * 64, 64), 64)
                mine = mid[at, rows, :] if side is None else side[at][rows, :]
                mid[at, rows, :] = add_low(mine, met[at, rows, :])
                return carry

            lax.fori_loop(0, BLK // 64, tile, 0)
        begin(second)

    def close_sum():
        finish(direct)
        finish(second)

    return open_sum, join_sum, close_sum


def weight_grads(
    act,
    grad_two_all,
    normed_two_all,
    grad_parts,
    back_sums,
    two_sums,
    middle,
    cotangent,
    out_weight,
    mix_weight,
    parts_all,
    mixing_all,
    states_all,
    gated,
    normed_all,
    hidden,
    live,
    keep,
):
    rows, units = act.shape
    width = grad_two_all.shape[1]
    local_rows = middle.shape[0]
    parts, _, columns = parts_all.shape
    heads = columns // HS
    low = jnp.bfloat16
    in_columns = grad_parts.shape[1] // TILE
    in_rows = width // PIECE
    out_blocks = units // SUB
    halves = width // 1024
    first_out = in_rows * in_columns
    first_branch = first_out + halves * out_blocks
    first_mix = first_branch + width // TILE
    per_row = columns // TILE
    per_part = in_rows * per_row
    count = first_mix + parts * per_part

    def body(*refs):
        act_in, two_in, normed_two_in, parts_in, back_in, two_sums_in = refs[:6]
        middle_in, cot_in, weight_in, mix_in = refs[6:10]
        all_in, mixing_in, states_in, gated_in, normed_in, hidden_in, live_ref, keep_ref = refs[10:18]
        in_grad, out_grad, branch_grad, mix_grad, branch_out, middle_out, layer_out, input_out = refs[18:26]
        last_landed, two_landed = refs[26:30], refs[30:34]
        shared, wide_ref, act_ref, landed, stage_ref, mid_ref, grad_ref, branch = refs[34:42]
        near, gated_grad, states_ref = refs[42:45]
        normed_sems, parts_sems, load_sems, stage_sems, gather_sems, back_sems, head_sems, mix_sems = refs[45:53]
        tile_sems, last_sems = refs[53:55]
        line, square = refs[55:64], refs[64:68]
        places = neighbours()
        narrow, near_x, near_y = places[1], places[5], places[6]

        def block(at):
            return pl.ds(at * BLK, BLK)

        def cols(at, size):
            return pl.ds(pl.multiple_of(at, 128), size)

        def load_normed_two(at):
            here = cols(at * PIECE, PIECE)
            return pltpu.make_async_copy(normed_two_in.at[:, here], shared.at[:, here], normed_sems.at[at])

        def load_parts(at):
            here = cols(at * TILE, TILE)
            return pltpu.make_async_copy(parts_in.at[:, here], wide_ref.at[:, here], parts_sems.at[at])

        def load_half(src, half, sem):
            here = pl.ds(half * 1024, 1024)
            return pltpu.make_async_copy(src.at[:, here], shared.at[:, here], load_sems.at[sem])

        load_act = pltpu.make_async_copy(act_in, act_ref, load_sems.at[0])
        load_two = [load_half(two_in, half, 1 + half) for half in range(halves)]
        load_normed = [load_half(normed_in, half, 3 + half) for half in range(halves)]
        load_gated = pltpu.make_async_copy(gated_in.at[0], act_ref.at[:, pl.ds(0, columns)], load_sems.at[5])

        def load_branch(at):
            slot = at % 2
            return pltpu.make_async_copy(
                branch_out.at[:, cols(at * TILE, TILE)],
                act_ref.at[:, cols(columns + slot * TILE, TILE)],
                tile_sems.at[slot],
            )

        def product(k, own):
            def split_rows(result):
                for part in range(4):
                    own[part] = result[part * SUB : (part + 1) * SUB]

            @pl.when(k < first_out)
            def _():
                row, column = k // in_columns, k % in_columns

                @pl.when(column == 0)
                def _():
                    load_normed_two(row).wait()

                @pl.when(row == 0)
                def _():
                    load_parts(column).wait()

                here, there = cols(row * PIECE, PIECE), cols(column * TILE, TILE)
                split_rows(down(shared[:, here], wide_ref[:, there]).astype(low))

                @pl.when(k == first_out - in_columns)
                def _():
                    load_two[0].start()

            @pl.when(k == first_out)
            def _():
                begin(load_two[1:])
                load_act.wait()
                load_two[0].wait()

            @pl.when(k == first_out + out_blocks)
            def _():
                finish(load_two[1:])
                load_normed[0].start()

            @pl.when((k >= first_out) & (k < first_branch))
            def _():
                at = k - first_out
                here = cols((at % out_blocks) * SUB, SUB)
                there = cols((at // out_blocks) * 1024, 1024)
                result = down(act_ref[:, here], shared[:, there]).astype(low)
                for part in range(4):
                    own[part] = result[:, part * TILE : (part + 1) * TILE]

            pl.when(k == first_branch - out_blocks + columns // SUB)(lambda: load_gated.start())
            pl.when(k == first_branch - out_blocks + (columns + TILE) // SUB)(lambda: load_branch(0).start())

            @pl.when(k == first_branch)
            def _():
                begin(load_normed[1:])
                load_gated.wait()

            @pl.when((k >= first_branch) & (k < first_mix))
            def _():
                at = k - first_branch
                load_branch(at).wait()
                pl.when(k + 1 < first_mix)(lambda: load_branch(at + 1).start())
                there = cols(columns + (at % 2) * TILE, TILE)
                split_rows(down(act_ref[:, :columns], act_ref[:, there]).astype(low))

            @pl.when(k == first_mix)
            def _():
                finish(load_normed)

            @pl.when(k >= first_mix)
            def _():
                at = k - first_mix
                here = cols(((at // per_row) % in_rows) * PIECE, PIECE)
                there = cols((at // per_part) * columns + (at % per_row) * TILE, TILE)
                split_rows(down(shared[:, here], wide_ref[:, there]).astype(low))

        def targets(k, part):
            one = jnp.minimum(k, first_out - 1)
            two = jnp.clip(k - first_out, 0, first_branch - first_out - 1)
            three = jnp.clip(k - first_branch, 0, first_mix - first_branch - 1)
            four = jnp.maximum(k - first_mix, 0)
            return [
                (
                    k < first_out,
                    in_grad.at[(one // in_columns) * 4 + part, :, cols((one % in_columns) * TILE, TILE)],
                ),
                (
                    (k >= first_out) & (k < first_branch),
                    out_grad.at[two % out_blocks, :, cols((two // out_blocks) * 1024 + part * TILE, TILE)],
                ),
                (
                    (k >= first_branch) & (k < first_mix),
                    branch_grad.at[part, :, cols(three * TILE, TILE)],
                ),
                (
                    k >= first_mix,
                    mix_grad.at[(four // per_row) * 4 + part, :, cols((four % per_row) * TILE, TILE)],
                ),
            ]

        step = line_sum(line, places, count, product, targets)
        now = [0]

        def run(steps):
            lax.fori_loop(now[0], now[0] + steps, step, 0)
            now[0] += steps

        open_sum, join_sum, close_sum = square_sum(
            square,
            places,
            [back_in.at[block(at)] for at in range(2, 8)],
            [landed.at[at] for at in range(4)],
            0,
        )
        load_normed_two(0).start()
        load_parts(0).start()
        enter(places)
        open_sum()
        for at in range(1, in_columns):
            load_parts(at).start()
        for at in range(1, in_rows):
            load_normed_two(at).start()
        load_act.start()

        def spread(src, slot, kind, place):
            return pltpu.make_async_remote_copy(
                src_ref=src,
                dst_ref=branch_out.at[block(slot)],
                send_sem=gather_sems.at[kind, 0],
                recv_sem=gather_sems.at[kind, 1],
                device_id=place,
                device_id_type=MESH,
            )

        def stage(half):
            return [
                pltpu.make_async_copy(back_in.at[block(half)], stage_ref.at[0], stage_sems.at[0]),
                pltpu.make_async_copy(cot_in.at[block(half)], stage_ref.at[1], stage_sems.at[1]),
                pltpu.make_async_copy(middle_in.at[block(half)], mid_ref, stage_sems.at[2]),
            ]

        keep_branch = [
            pltpu.make_async_copy(branch.at[at], branch_out.at[block(at)], stage_sems.at[3 + at])
            for at in range(2)
        ]

        def rows_back(half):
            def tile(i, carry):
                at = pl.ds(pl.multiple_of(i * 32, 32), 32)
                grad = add_rows(stage_ref[0, at, :], landed[half, at, :], landed[2 + half, at, :])
                result = stage_ref[1, at, :].astype(jnp.float32) + norm_back(mid_ref[at, :], grad)
                grad_ref[at, :] = result
                live_at = pl.ds(pl.multiple_of(half * BLK + i * 32, 32), 32)
                branch[half, at, :] = (live_ref[live_at, :1] * result).astype(low)
                return carry

            lax.fori_loop(0, BLK // 32, tile, 0)
            copy = pltpu.make_async_copy(grad_ref, middle_out.at[block(half)], stage_sems.at[5])
            copy.start()
            return copy

        sends = [
            spread(branch.at[0], 2, 0, near_x),
            spread(branch.at[1], 3, 1, near_y),
            spread(branch.at[1], 4, 2, near_x),
            spread(branch.at[0], 5, 3, near_y),
        ]
        later = [
            spread(branch_out.at[block(3)], 7, 4, near_x),
            spread(branch_out.at[block(2)], 6, 5, near_y),
        ]
        weight_loads = [
            pltpu.make_async_copy(weight_in.at[block(at)], landed.at[at], back_sems.at[at])
            for at in range(columns // BLK)
        ]

        def row_loads(slot):
            return [
                pltpu.make_async_copy(branch_out.at[block(slot + at)], stage_ref.at[at], back_sems.at[2 + at])
                for at in range(2)
            ]

        def back_rows(slot, rows_ref):
            for at in range(2):
                for part in range(len(weight_loads)):
                    result = across(rows_ref[at], landed[part]).astype(low)
                    gated_grad[(slot + at) * BLK : (slot + at + 1) * BLK, part * BLK : (part + 1) * BLK] = result

        def head_loads(head):
            here = cols(head * HS, HS)
            loads = [
                pltpu.make_async_copy(
                    all_in.at[c, :, here],
                    wide_ref.at[:, pl.ds(parts * columns + c * HS, HS)],
                    head_sems.at[c],
                )
                for c in range(parts)
            ]
            loads.append(
                pltpu.make_async_copy(
                    mixing_in.at[:, here],
                    wide_ref.at[:, pl.ds(parts * columns + parts * HS, HS)],
                    head_sems.at[parts],
                )
            )
            loads.append(pltpu.make_async_copy(states_in.at[head], states_ref, head_sems.at[parts + 1]))
            return loads

        open_two, join_two, close_two = square_sum(
            square, places, [two_sums_in.at[block(at)] for at in range(2, 8)], two_landed, 1
        )
        run(9)
        join_sum()
        begin(stage(0))
        run(16)
        close_sum()
        finish(stage(0))
        written = rows_back(0)
        sends[0].start()
        begin(stage(1))
        run(1)
        finish(stage(1))
        written.wait()
        written = rows_back(1)
        begin(sends[1:])
        begin(keep_branch)
        begin(weight_loads)
        run(2)
        finish(weight_loads)
        back_rows(0, branch)
        run(6)
        for copy in sends[:2]:
            copy.wait_recv()
        begin(later)
        begin(row_loads(2))
        run(1)
        finish(row_loads(2))
        back_rows(2, stage_ref)
        run(7)
        for copy in sends[2:]:
            copy.wait_recv()
        begin(row_loads(4))
        run(1)
        finish(row_loads(4))
        back_rows(4, stage_ref)
        run(8)
        begin(head_loads(0))
        for copy in later:
            copy.wait_recv()
        begin(row_loads(6))
        run(1)
        finish(row_loads(6))
        back_rows(6, stage_ref)
        written.wait()
        finish(keep_branch)
        for copy in sends + later:
            copy.wait_send()
        open_two()

        def load_mix(at):
            here = pl.ds(pl.multiple_of(at * BLK, BLK), BLK)
            slot = at % 4
            return [
                pltpu.make_async_copy(
                    mix_in.at[c, here, :], landed.at[slot, :, pl.ds(c * columns, columns)], mix_sems.at[slot, c]
                )
                for c in range(parts)
            ]

        for at in range(4):
            begin(load_mix(at))
        attend_from = now[0]
        breaks = (2, 5, NBLK - 1)

        def attend(head, carry):
            rate = head_rate(heads * narrow + head)
            within, entry, leave, whole = block_decays(rate)
            finish(head_loads(head))
            pl.when(head == heads - 1)(join_two)
            later_grad = jnp.zeros((HS, HS), jnp.float32)
            base = parts * columns
            for at in range(NBLK):
                block_at = NBLK - 1 - at
                here = pl.ds(pl.multiple_of(slot_of(block_at, narrow) * BLK, BLK), BLK)

                def load(c, here=here):
                    return wide_ref[here, base + c * HS : base + (c + 1) * HS]

                def store(c, value, here=here):
                    wide_ref[here, cols(c * columns + head * HS, HS)] = value.astype(low)

                raw_queries = load(0).astype(jnp.float32)
                raw_keys = load(1).astype(jnp.float32)
                queries, keys = jax.nn.silu(raw_queries).astype(low), jax.nn.silu(raw_keys).astype(low)
                values = load(2)
                gate = load(3).astype(jnp.float32)
                mixing = load(4).astype(jnp.float32)
                grad_rows = gated_grad[here, cols(head * HS, HS)].astype(jnp.float32)
                scale = lax.rsqrt(jnp.mean(mixing * mixing, axis=-1, keepdims=True) + head_floor)
                headed = mixing * scale
                store(3, grad_rows * headed)
                grad_headed = grad_rows * gate
                inner = jnp.mean(grad_headed * headed, axis=-1, keepdims=True)
                grad = (scale * (grad_headed - headed * inner)).astype(low)
                scores = (across(queries, keys) * within).astype(low)
                grad_scores = (across(grad, values) * within).astype(low)
                later_low = later_grad.astype(low)
                grad_queries = straight(grad_scores, keys) + entry * across(grad, states_ref[block_at])
                grad_keys = down(grad_scores, queries) + leave * across(values, later_low)
                grad_values = down(scores, grad) + leave * straight(keys, later_low)
                early_queries = (queries.astype(jnp.float32) * entry).astype(low)
                later_grad = keep_ref[block_at : block_at + 1, :1] * (
                    whole * later_grad + down(early_queries, grad)
                )
                store(0, grad_queries * silu_slope(raw_queries))
                store(1, grad_keys * silu_slope(raw_keys))
                store(2, grad_values)
                if at == NBLK - 1:
                    pl.when(head + 1 < heads)(lambda: begin(head_loads(head + 1)))
                if at in breaks:
                    step(attend_from + head * len(breaks) + breaks.index(at), 0)
            return carry

        lax.fori_loop(0, heads, attend, 0)
        now[0] += heads * len(breaks)

        sum_from = now[0]
        side = (mid_ref, grad_ref)

        def put(pair):
            def store(at, here, value):
                pair[at, :, here] = value

            return store

        def put_side(at, here, value):
            side[1 - at][:, here] = value.astype(jnp.float32)

        outs = ((3, put(branch)), (1, put(near)), (2, put_side), (0, put(stage_ref)))

        def sum_tile(at, carry):
            finish(load_mix(at))
            here = cols(at * BLK, BLK)
            for which, (piece, store) in enumerate(outs):
                acts = wide_ref[piece * PIECE : (piece + 1) * PIECE, : parts * columns]
                total = across(acts, landed[at % 4]).astype(low)
                store(0, here, total[:HALF])
                store(1, here, total[HALF:])
                if which == 3:
                    pl.when(at + 4 < width // BLK)(lambda: begin(load_mix(at + 4)))
                if which % 2:
                    step(sum_from + 2 * at + which // 2, 0)
            return carry

        lax.fori_loop(0, width // BLK, sum_tile, 0)
        now[0] += 2 * (width // BLK)
        open_last, join_last, close_last = square_sum(
            square,
            places,
            (near.at[0], near.at[1], None, None, branch.at[0], branch.at[1]),
            last_landed,
            2,
            side,
        )
        close_two()
        open_last()
        run(9)
        join_last()

        def block_loads(half, terms, floats):
            loads = [
                pltpu.make_async_copy(src, landed.at[at], last_sems.at[at]) for at, src in enumerate(terms)
            ]
            loads.append(pltpu.make_async_copy(floats.at[block(half)], mid_ref, last_sems.at[3]))
            return loads

        def block_store(half, out):
            return pltpu.make_async_copy(landed.at[3], out.at[block(half)], last_sems.at[4])

        def layer_loads(half):
            terms = (two_sums_in.at[block(half)], two_landed[half], two_landed[2 + half])
            return block_loads(half, terms, middle_in)

        def input_loads(half):
            terms = (last_landed[half], last_landed[2 + half], hidden_in.at[block(half)])
            return block_loads(half, terms, middle_out)

        def layer_tile(i, carry, half):
            at = pl.ds(pl.multiple_of(i * 32, 32), 32)
            live_at = pl.ds(pl.multiple_of(half * BLK + i * 32, 32), 32)
            branch_two = add_rows(landed[0, at, :], landed[1, at, :], landed[2, at, :])
            landed[3, at, :] = (mid_ref[at, :] + live_ref[live_at, :1] * branch_two).astype(low)
            return carry

        def input_tile(i, carry, half):
            at = pl.ds(pl.multiple_of(i * 32, 32), 32)
            grad_normed = add_rows(stage_ref[half, at, :], landed[0, at, :], landed[1, at, :])
            back = norm_back(landed[2, at, :].astype(jnp.float32), grad_normed)
            landed[3, at, :] = (mid_ref[at, :] + back).astype(low)
            return carry

        def rows_out(loads, tile, out):
            tiles = BLK // 32 // 4
            for half in range(2):
                begin(loads(half))
                run(1)
                finish(loads(half))
                if half:
                    block_store(0, out).wait()
                base = now[0]

                def part(at, carry, half=half, base=base):
                    for one in range(tiles):
                        tile(tiles * at + one, 0, half)
                    step(base + at, 0)
                    return carry

                lax.fori_loop(0, 4, part, 0)
                now[0] += 4
                block_store(half, out).start()

        rows_out(layer_loads, layer_tile, layer_out)
        run(first_mix + 31 - now[0])
        block_store(1, layer_out).wait()
        close_last()
        rows_out(input_loads, input_tile, input_out)
        run(count + STAGES - now[0])
        block_store(1, input_out).wait()

    def low_shape(*shape):
        return jax.ShapeDtypeStruct(shape, low)

    sem = pltpu.SemaphoreType.DMA
    return pl.pallas_call(
        body,
        in_specs=any_specs(16) + [pl.BlockSpec(memory_space=pltpu.VMEM)] * 2,
        out_specs=any_specs(16),
        out_shape=[
            low_shape(width // SUB, SUB, grad_parts.shape[1]),
            low_shape(out_blocks, SUB, width),
            low_shape(columns // SUB, SUB, width),
            low_shape(parts * width // SUB, SUB, columns),
            low_shape(rows, width),
            jax.ShapeDtypeStruct((local_rows, width), jnp.float32),
            low_shape(local_rows, width),
            low_shape(local_rows, width),
        ]
        + [low_shape(BLK, width)] * 8,
        scratch_shapes=[
            pltpu.VMEM((rows, width), low),
            pltpu.VMEM(grad_parts.shape, low),
            pltpu.VMEM(act.shape, low),
            pltpu.VMEM((4, BLK, width), low),
            pltpu.VMEM((2, BLK, width), low),
            pltpu.VMEM((BLK, width), jnp.float32),
            pltpu.VMEM((BLK, width), jnp.float32),
            pltpu.VMEM((2, BLK, width), low),
            pltpu.VMEM((2, BLK, width), low),
            pltpu.VMEM((rows, columns), low),
            pltpu.VMEM((NBLK, HS, HS), low),
            sem((in_rows,)),
            sem((in_columns,)),
            sem((6,)),
            sem((6,)),
            sem((6, 2)),
            sem((4,)),
            sem((parts + 2,)),
            sem((4, parts)),
            sem((2,)),
            sem((5,)),
        ]
        + line_scratch()
        + square_scratch(3),
        compiler_params=pltpu.CompilerParams(
            vmem_limit_bytes=VMEM, collective_id=1, has_side_effects=True
        ),
        cost_estimate=cost(2 * rows * width * (3 * units + 9 * columns), 120e6),
        name="weight_grads",
    )(
        act,
        grad_two_all,
        normed_two_all,
        grad_parts,
        back_sums,
        two_sums,
        middle,
        cotangent,
        out_weight,
        mix_weight,
        parts_all,
        mixing_all,
        states_all,
        gated,
        normed_all,
        hidden,
        live,
        keep,
    )


def gated_unit(gated, whole_weight, hidden, live, grads_own, grads_first, ffn_in, ffn_out):
    _, width, units = ffn_in.shape
    local_rows = hidden.shape[0]
    group_rows = NBLK * BLK
    pieces = group_rows // PIECE
    deep = gated.shape[2]
    slices, quarters, slice_rows, _ = whole_weight.shape
    main = units // TILE * TILE
    tail = units - main
    low = jnp.bfloat16
    cuts = ((0, 2 * TILE), (2 * TILE, main - 2 * TILE))
    wide_tile = 1024
    first_half, second_half = pl.ds(0, HALF), pl.ds(HALF, HALF)

    def body(*refs):
        gated_in, weight_in, hidden_in = refs[:3]
        grad_in = refs[3:5]
        in_ref, out_ref, live_ref = refs[5:8]
        middle_out, rows_out, grads_out, act_out, parts_out, back_out, two_out = refs[8:15]
        gated_ref, hidden_ref, middle_ref = refs[15:18]
        rows, grads, sums, w_in, w_out, act, parts = refs[18:25]
        load_sems, slice_sems, weight_sems, done_sems, sum_sems, last_sems, gated_sems, gather_sems = refs[25:]
        wide, narrow, _, _, _, near_x, near_y = neighbours()
        far = (wide, 3 - narrow)
        here = pl.ds(pl.multiple_of(narrow * deep, deep), deep)

        def send_gated(slot, to, kind, place):
            return pltpu.make_async_remote_copy(
                src_ref=gated_in.at[0, pl.ds(slot * BLK, BLK)],
                dst_ref=gated_ref.at[(first_half, second_half)[to], here],
                send_sem=gated_sems.at[kind, 0],
                recv_sem=gated_sems.at[kind, 1],
                device_id=place,
                device_id_type=MESH,
            )

        gated_sends = [
            send_gated(6, 0, 0, far),
            send_gated(7, 1, 1, far),
            send_gated(2, 0, 2, near_x),
            send_gated(3, 1, 3, near_y),
            send_gated(4, 1, 4, near_x),
            send_gated(5, 0, 5, near_y),
        ]
        keep_gated = pltpu.make_async_copy(
            gated_in.at[0, pl.ds(0, PIECE)], gated_ref.at[:, here], load_sems.at[0]
        )

        def load_slice(at):
            part, quarter = at // quarters, at % quarters
            to = pl.ds(pl.multiple_of(quarter * deep + part * slice_rows, slice_rows), slice_rows)
            return pltpu.make_async_copy(
                weight_in.at[part, quarter], w_in.at[to, pl.ds(0, width)], slice_sems.at[at]
            )

        def start_slice(at, carry):
            load_slice(at).start()
            return carry

        def wait_slice(at, carry):
            load_slice(at).wait()
            return carry

        load_hidden = pltpu.make_async_copy(hidden_in, hidden_ref, load_sems.at[1])
        load_grads = [
            pltpu.make_async_copy(src, grads.at[at], load_sems.at[2 + at])
            for at, src in enumerate(grad_in)
        ]
        weights = []
        for start, size, first, second in tuple((a, b, a, main + a) for a, b in cuts) + (
            (main, tail, 2 * main, 2 * main + tail),
        ):
            at = pl.ds(start, size)
            weights += [
                pltpu.make_async_copy(in_ref.at[0, :, at], w_in.at[:, pl.ds(first, size)], weight_sems.at[len(weights)]),
                pltpu.make_async_copy(in_ref.at[1, :, at], w_in.at[:, pl.ds(second, size)], weight_sems.at[len(weights) + 1]),
                pltpu.make_async_copy(out_ref.at[at, :], w_out.at[at, :], weight_sems.at[len(weights) + 2]),
            ]

        def remote(src, dst, sems, kind, place):
            return pltpu.make_async_remote_copy(
                src_ref=src,
                dst_ref=dst,
                send_sem=sems.at[kind, 0],
                recv_sem=sems.at[kind, 1],
                device_id=place,
                device_id_type=MESH,
            )

        def half(ref, piece, at):
            return ref.at[piece, (first_half, second_half)[at]]

        def quarter(ref, piece, at):
            return ref.at[piece, pl.ds(at * SUB, SUB)]

        def gather(ref, kind):
            return (
                [
                    remote(half(ref, 0, 0), half(ref, 1, 0), gather_sems, kind, near_x),
                    remote(half(ref, 0, 1), half(ref, 1, 1), gather_sems, kind + 1, near_y),
                ],
                [
                    remote(half(ref, 0, 1), half(ref, 2, 0), gather_sems, kind + 2, near_x),
                    remote(half(ref, 0, 0), half(ref, 2, 1), gather_sems, kind + 3, near_y),
                ],
                [
                    remote(quarter(ref, 1, 2), quarter(ref, 3, 1), gather_sems, kind + 4, near_x),
                    remote(quarter(ref, 1, 0), quarter(ref, 3, 0), gather_sems, kind + 5, near_y),
                ],
                [
                    remote(quarter(ref, 1, 3), quarter(ref, 3, 3), gather_sems, kind + 6, near_x),
                    remote(quarter(ref, 1, 1), quarter(ref, 3, 2), gather_sems, kind + 7, near_y),
                ],
            )

        row_sends = gather(rows, 0)
        grad_sends = gather(grads, 8)

        begin(load_grads)
        begin([keep_gated, load_hidden])
        barrier = pltpu.get_barrier_semaphore()
        for place in (near_x, near_y, far):
            pl.semaphore_signal(barrier, inc=1, device_id=place, device_id_type=MESH)
        pl.semaphore_wait(barrier, 3)
        begin(gated_sends)
        lax.fori_loop(0, slices * quarters, start_slice, 0)
        finish(load_grads)
        begin(grad_sends[1])
        finish([keep_gated, load_hidden])
        lax.fori_loop(0, slices * quarters, wait_slice, 0)
        finish(gated_sends)
        for j in range(width // wide_tile):
            at = slice(j * wide_tile, (j + 1) * wide_tile)
            middle_ref[:, at] = straight(gated_ref[...], w_in[:, at])
        begin(weights)

        def second_norm(i, carry, at):
            here = pl.ds(pl.multiple_of(at * HALF + i * 32, 32), 32)
            middle = hidden_ref[here, :].astype(jnp.float32) + live_ref[here, :1] * middle_ref[here, :]
            middle_ref[here, :] = middle
            rows[0, here, :] = row_norm(middle).astype(low)
            return carry

        for at in range(2):
            lax.fori_loop(0, HALF // 32, functools.partial(second_norm, at=at), 0)
            row_sends[0][at].start()
        begin(row_sends[1])
        store_middle = pltpu.make_async_copy(middle_ref, middle_out, done_sems.at[0])
        store_middle.start()

        def products(size, at, first, second, part_a, part_b, grad_act):
            act[:size, at] = (part_a * part_b).astype(low)
            parts[:size, first] = (grad_act * part_b).astype(low)
            parts[:size, second] = (grad_act * part_a).astype(low)

        def unit(arrived, arrived_grads, size, weights_wait):
            for which, (start, count) in enumerate(cuts):
                at, second = slice(start, start + count), slice(main + start, main + start + count)
                weights_wait(3 * which, 3 * which + 3)
                part_a = straight(arrived[...], w_in[:, at])
                part_b = straight(arrived[...], w_in[:, second])
                grad_act = across(arrived_grads[...], w_out[at, :])
                products(size, at, at, second, part_a, part_b, grad_act)
            weights_wait(6, 9)
            if tail:
                both = straight(arrived[...], w_in[:, 2 * main :])
                grad_act = across(arrived_grads[...], w_out[main:, :])
                products(
                    size,
                    slice(main, units),
                    slice(2 * main, 2 * main + tail),
                    slice(2 * main + tail, 2 * units),
                    both[:, :tail],
                    both[:, tail:],
                    grad_act,
                )

        def row_stores(arrived, arrived_grads, at):
            return [
                pltpu.make_async_copy(arrived, rows_out.at[at, :], done_sems.at[1]),
                pltpu.make_async_copy(arrived_grads, grads_out.at[at, :], done_sems.at[2]),
            ]

        def unit_stores(size, at):
            here = pl.ds(0, size)
            return [
                pltpu.make_async_copy(act.at[here], act_out.at[at, :], done_sems.at[3]),
                pltpu.make_async_copy(parts.at[here], parts_out.at[at, :], done_sems.at[4]),
            ]

        def sum_stores(piece, j):
            tile = pl.ds(j * wide_tile, wide_tile)
            return [
                pltpu.make_async_copy(
                    sums.at[at, :, tile],
                    (back_out, two_out)[at // 2].at[
                        pl.ds(pl.multiple_of(piece * PIECE + (at % 2) * HALF, HALF), HALF), tile
                    ],
                    sum_sems.at[j, at],
                )
                for at in range(4)
            ]

        def work(piece, carry):
            at = pl.ds(pl.multiple_of(piece * PIECE, PIECE), PIECE)
            arrived, arrived_grads = rows.at[piece], grads.at[piece]

            @pl.when(piece == 1)
            def _():
                finish(row_sends[0])
                for step in (2, 3):
                    begin(row_sends[step])
                    begin(grad_sends[step])

            @pl.when(piece == 2)
            def _():
                finish(row_sends[1])
                finish(grad_sends[1])

            stores = row_stores(arrived, arrived_grads, at)
            begin(stores)

            def weights_wait(start, stop):
                pl.when(piece == 0)(lambda: finish(weights[start:stop]))

            unit(arrived, arrived_grads, PIECE, weights_wait)
            more = unit_stores(PIECE, at)
            begin(more)
            for j in range(width // wide_tile):
                tile = slice(j * wide_tile, (j + 1) * wide_tile)

                @pl.when(piece > 0)
                def _(j=j):
                    finish(sum_stores(piece - 1, j))

                back = across(parts[...], w_in[tile, :])
                sums[0, :, tile] = back[:HALF].astype(low)
                sums[1, :, tile] = back[HALF:].astype(low)
                two = straight(act[...], w_out[:, tile])
                sums[2, :, tile] = two[:HALF].astype(low)
                sums[3, :, tile] = two[HALF:].astype(low)
                begin(sum_stores(piece, j))
            finish(stores)
            finish(more)
            return carry

        lax.fori_loop(0, pieces - 1, work, 0)
        for j in range(width // wide_tile):
            finish(sum_stores(pieces - 2, j))

        def last_stores(which):
            return [
                pltpu.make_async_copy(
                    sums.at[2 * total + which, pl.ds(part * SUB, SUB)],
                    (back_out, two_out)[total].at[
                        pl.ds(pl.multiple_of((pieces - 1) * PIECE + part * HALF + which * SUB, SUB), SUB)
                    ],
                    last_sems.at[which, 2 * total + part],
                )
                for total in range(2)
                for part in range(2)
            ]

        def last_work(which, carry):
            @pl.when(which == 0)
            def _():
                finish(row_sends[2])
                finish(grad_sends[2])

            @pl.when(which == 1)
            def _():
                finish(row_sends[3])
                finish(grad_sends[3])

            here = pl.ds(pl.multiple_of(which * HALF, HALF), HALF)
            at = pl.ds(pl.multiple_of((pieces - 1) * PIECE + which * HALF, HALF), HALF)
            arrived, arrived_grads = rows.at[pieces - 1, here], grads.at[pieces - 1, here]
            stores = row_stores(arrived, arrived_grads, at)
            begin(stores)
            unit(arrived, arrived_grads, HALF, lambda start, stop: None)
            more = unit_stores(HALF, at)
            begin(more)
            for j in range(width // wide_tile):
                tile = slice(j * wide_tile, (j + 1) * wide_tile)
                sums[which, :, tile] = across(parts[:HALF], w_in[tile, :]).astype(low)
                sums[2 + which, :, tile] = straight(act[:HALF], w_out[:, tile]).astype(low)
            begin(last_stores(which))
            finish(stores)
            finish(more)
            return carry

        lax.fori_loop(0, 2, last_work, 0)
        for which in range(2):
            finish(last_stores(which))
        store_middle.wait()

    return pl.pallas_call(
        body,
        in_specs=any_specs(7) + [pl.BlockSpec(memory_space=pltpu.VMEM)],
        out_specs=any_specs(7),
        out_shape=[
            jax.ShapeDtypeStruct((local_rows, width), jnp.float32),
            jax.ShapeDtypeStruct((group_rows, width), low),
            jax.ShapeDtypeStruct((group_rows, width), low),
            jax.ShapeDtypeStruct((group_rows, units), low),
            jax.ShapeDtypeStruct((group_rows, 2 * units), low),
            jax.ShapeDtypeStruct((group_rows, width), low),
            jax.ShapeDtypeStruct((group_rows, width), low),
        ],
        scratch_shapes=[
            pltpu.VMEM((local_rows, quarters * deep), low),
            pltpu.VMEM((local_rows, width), low),
            pltpu.VMEM((local_rows, width), jnp.float32),
            pltpu.VMEM((pieces, PIECE, width), low),
            pltpu.VMEM((pieces, PIECE, width), low),
            pltpu.VMEM((4, HALF, width), low),
            pltpu.VMEM((width, 2 * units), low),
            pltpu.VMEM((units, width), low),
            pltpu.VMEM((PIECE, units), low),
            pltpu.VMEM((PIECE, 2 * units), low),
            pltpu.SemaphoreType.DMA((4,)),
            pltpu.SemaphoreType.DMA((slices * quarters,)),
            pltpu.SemaphoreType.DMA((9,)),
            pltpu.SemaphoreType.DMA((5,)),
            pltpu.SemaphoreType.DMA((width // wide_tile, 4)),
            pltpu.SemaphoreType.DMA((2, 4)),
            pltpu.SemaphoreType.DMA((6, 2)),
            pltpu.SemaphoreType.DMA((16, 2)),
        ],
        compiler_params=pltpu.CompilerParams(
            vmem_limit_bytes=VMEM, collective_id=3, has_side_effects=True
        ),
        cost_estimate=cost(12 * group_rows * width * units, 90e6),
        name="gated_unit",
    )(gated, whole_weight, hidden, grads_own, grads_first, ffn_in, ffn_out, live)


def mix_rows(hidden, cotangent, mix_weight, out_weight, seq_lengths, block_seq):
    local_rows, width = hidden.shape
    parts, _, columns = mix_weight.shape
    heads = columns // HS
    group_rows = NBLK * BLK
    pieces = group_rows // PIECE
    wide_size = lax.axis_size("wide")
    slice_rows = columns // wide_size
    low = jnp.bfloat16
    joined = 2
    halves_at = (pl.ds(0, HALF), pl.ds(HALF, HALF))

    def body(*refs):
        hidden_in, cot_in, mix_in, out_in, length_ref, owner_ref = refs[:6]
        rows_out, parts_out, gated_out, mixing_out, states_out, grads_out, first_out, whole_out = refs[6:14]
        live_ref, keep_ref = refs[14:16]
        hidden_ref, cot_ref, rows, weights, parts_ref, gated_ref, mixing_ref, states_ref = refs[16:24]
        load_sems, mix_sems, store_sems, parts_sems, gather_sems, slice_sems, line_sems, core_sems = refs[24:]
        wide, narrow, z, core, mate, near_x, near_y = neighbours()
        far = (wide, 3 - narrow)
        above, below = (wide + 2, narrow), (wide - 2, narrow)
        barrier = pltpu.get_barrier_semaphore()

        def greet(place):
            pl.semaphore_signal(barrier, inc=1, device_id=place, device_id_type=MESH)

        load_hidden = pltpu.make_async_copy(hidden_in, hidden_ref, load_sems.at[0])
        load_cot = pltpu.make_async_copy(cot_in, cot_ref, load_sems.at[1])
        mix_loads = [
            pltpu.make_async_copy(
                mix_in.at[c], weights.at[:, pl.ds(c * columns, columns)], mix_sems.at[c]
            )
            for c in range(parts)
        ]
        load_hidden.start()
        for place in (near_x, near_y, far, mate):
            greet(place)
        pl.when(z < 3)(lambda: greet(above))
        pl.when(z > 0)(lambda: greet(below))
        middle = (z == 1) | (z == 2)
        pl.when(middle)(lambda: pl.semaphore_wait(barrier, 6))
        pl.when(jnp.logical_not(middle))(lambda: pl.semaphore_wait(barrier, 5))

        def remote(src, dst, sems, kind, place):
            return pltpu.make_async_remote_copy(
                src_ref=src,
                dst_ref=dst,
                send_sem=sems.at[kind, 0],
                recv_sem=sems.at[kind, 1],
                device_id=place,
                device_id_type=MESH,
            )

        slice_at = out_in.at[pl.ds(pl.multiple_of(wide * slice_rows, slice_rows), slice_rows)]
        keep_slice = pltpu.make_async_copy(slice_at, whole_out.at[wide, narrow], load_sems.at[2])
        slice_sends = [
            remote(slice_at, whole_out.at[wide, narrow], slice_sems, at, place)
            for at, place in enumerate((far, near_x, near_y))
        ]

        def up(hop):
            return remote(
                whole_out.at[wide - 2 * (hop - 1)], whole_out.at[wide - 2 * (hop - 1)], line_sems, hop - 1, above
            )

        def down_line(hop):
            return remote(
                whole_out.at[wide + 2 * (hop - 1)], whole_out.at[wide + 2 * (hop - 1)], line_sems, 2 + hop, below
            )

        def to_mate(hop, sign):
            at = wide + sign * 2 * hop
            return remote(whole_out.at[at], whole_out.at[at], core_sems, 3 + sign * hop, mate)

        def send_hop(hop):
            pl.when((z < 3) & (z >= hop - 1))(lambda: up(hop).start())
            pl.when((z > 0) & (z + hop - 1 <= 3))(lambda: down_line(hop).start())

        def take_hop(hop):
            @pl.when(z >= hop)
            def _():
                up(hop).wait_recv()
                to_mate(hop, -1).start()

            @pl.when(z + hop <= 3)
            def _():
                down_line(hop).wait_recv()
                to_mate(hop, 1).start()

        def end_hop(hop):
            pl.when((z < 3) & (z >= hop - 1))(lambda: up(hop).wait_send())
            pl.when((z > 0) & (z + hop - 1 <= 3))(lambda: down_line(hop).wait_send())
            pl.when(z >= hop)(lambda: to_mate(hop, -1).wait())
            pl.when(z + hop <= 3)(lambda: to_mate(hop, 1).wait())

        begin(slice_sends)
        keep_slice.start()

        def half(piece, at):
            return rows.at[piece, halves_at[at]]

        row_sends = (
            [remote(half(0, 0), half(1, 0), gather_sems, 0, near_x), remote(half(0, 1), half(1, 1), gather_sems, 1, near_y)],
            [remote(half(0, 1), half(2, 0), gather_sems, 2, near_x), remote(half(0, 0), half(2, 1), gather_sems, 3, near_y)],
            [remote(half(1, 1), half(3, 1), gather_sems, 4, near_x), remote(half(1, 0), half(3, 0), gather_sems, 5, near_y)],
        )
        grad_sends = [
            remote(cot_ref.at[halves_at[0]], first_out.at[halves_at[0]], gather_sems, 6, near_x),
            remote(cot_ref.at[halves_at[1]], first_out.at[halves_at[1]], gather_sems, 7, near_y),
        ]
        load_hidden.wait()
        begin(mix_loads)
        load_cot.start()

        def first_norm(i, carry):
            at = pl.ds(pl.multiple_of(i * 32, 32), 32)
            rows[0, at, :] = row_norm(hidden_ref[at, :].astype(jnp.float32)).astype(low)
            return carry

        for at in range(2):
            lax.fori_loop(at * HALF // 32, (at + 1) * HALF // 32, first_norm, 0)
            row_sends[0][at].start()
        begin(row_sends[1])

        def row_store(piece):
            at = pl.ds(piece * PIECE, PIECE)
            return pltpu.make_async_copy(rows.at[piece], rows_out.at[at, :], store_sems.at[piece])

        def part_stores(piece):
            at = pl.ds(piece * PIECE, PIECE)
            return [
                pltpu.make_async_copy(
                    parts_ref.at[at, pl.ds(c * columns, columns)], parts_out.at[c, at, :], parts_sems.at[piece, c]
                )
                for c in range(parts)
            ]

        def project(piece):
            row_store(piece).start()
            for c in range(0, parts, joined):
                if piece == 0:
                    finish(mix_loads[c : c + joined])
                at = slice(c * columns, (c + joined) * columns)
                result = straight(rows[piece], weights[:, at]).astype(low)
                parts_ref[piece * PIECE : (piece + 1) * PIECE, at] = result
            begin(part_stores(piece))

        def same_slot(block):
            return owner_ref[block] == owner_ref[0]

        first_count = sum(jnp.where(same_slot(block), 1, 0) for block in range(NBLK))

        def start_of(block):
            return jnp.where(same_slot(block), 0, first_count)

        for block in range(NBLK):
            entering = jnp.where(start_of(block) == block, 0.0, 1.0)
            keep_ref[block : block + 1, :] = jnp.full((1, HS), entering, jnp.float32)
        for at in range(local_rows // BLK):
            block = narrow * (local_rows // BLK) + at
            limit = jnp.where(same_slot(block), length_ref[0], length_ref[1])
            place = lax.broadcasted_iota(jnp.int32, (BLK, HS), 0) + (block - start_of(block)) * BLK
            live_ref[at * BLK : (at + 1) * BLK, :] = jnp.where(place < limit, 1.0, 0.0)
        project(0)
        load_cot.wait()

        def live_cot(i, carry):
            at = pl.ds(pl.multiple_of(i * 32, 32), 32)
            cot_ref[at, :] = (live_ref[at, :1] * cot_ref[at, :].astype(jnp.float32)).astype(low)
            return carry

        keep_slice.wait()
        finish(slice_sends)
        to_mate(0, 1).start()
        send_hop(1)
        lax.fori_loop(0, local_rows // 32, live_cot, 0)
        store_grads = pltpu.make_async_copy(cot_ref, grads_out, load_sems.at[3])
        store_grads.start()
        finish(row_sends[0])
        begin(row_sends[2])
        begin(grad_sends)
        project(1)
        take_hop(1)
        send_hop(2)
        finish(row_sends[1])
        project(2)
        take_hop(2)
        send_hop(3)
        finish(row_sends[2])
        project(3)

        def attend(head, carry):
            within, entry, leave, whole = block_decays(head_rate(heads * narrow + head))
            state = jnp.zeros((HS, HS), jnp.float32)

            def part(c, rows_at):
                at = pl.ds(pl.multiple_of(c * columns + head * HS, HS), HS)
                return parts_ref[rows_at, at]

            for block in range(NBLK):
                rows_at = pl.ds(pl.multiple_of(slot_of(block, narrow) * BLK, BLK), BLK)
                queries = jax.nn.silu(part(0, rows_at).astype(jnp.float32)).astype(low)
                keys = jax.nn.silu(part(1, rows_at).astype(jnp.float32)).astype(low)
                values = part(2, rows_at)
                gate = part(3, rows_at).astype(jnp.float32)
                state = keep_ref[block : block + 1, :] * state
                state_low = state.astype(low)
                states_ref[head, block] = state_low
                scores = (across(queries, keys) * within).astype(low)
                mixing = straight(scores, values) + entry * straight(queries, state_low)
                late_keys = (keys.astype(jnp.float32) * leave).astype(low)
                state = whole * state + down(late_keys, values)
                scale = lax.rsqrt(jnp.mean(mixing * mixing, axis=-1, keepdims=True) + head_floor)
                at = pl.ds(pl.multiple_of(head * HS, HS), HS)
                gated_ref[rows_at, at] = (mixing * scale * gate).astype(low)
                mixing_ref[rows_at, at] = mixing.astype(low)
            return carry

        lax.fori_loop(0, heads // 2, attend, 0)
        take_hop(3)
        lax.fori_loop(heads // 2, heads, attend, 0)
        stores = [
            pltpu.make_async_copy(gated_ref, gated_out.at[0], load_sems.at[4]),
            pltpu.make_async_copy(mixing_ref, mixing_out, load_sems.at[5]),
            pltpu.make_async_copy(states_ref, states_out, load_sems.at[6]),
        ]
        begin(stores)
        to_mate(0, 1).wait()
        for hop in range(1, 4):
            end_hop(hop)
        finish(grad_sends)
        store_grads.wait()
        for piece in range(pieces):
            row_store(piece).wait()
            finish(part_stores(piece))
        finish(stores)

    low_shape = functools.partial(jax.ShapeDtypeStruct, dtype=low)
    return pl.pallas_call(
        body,
        in_specs=any_specs(4) + [pl.BlockSpec(memory_space=pltpu.SMEM)] * 2,
        out_specs=any_specs(8) + [pl.BlockSpec(memory_space=pltpu.VMEM)] * 2,
        out_shape=[
            low_shape((group_rows, width)),
            low_shape((parts, group_rows, columns)),
            low_shape((1, group_rows, columns)),
            low_shape((group_rows, columns)),
            low_shape((heads, NBLK, HS, HS)),
            low_shape((local_rows, width)),
            low_shape((local_rows, width)),
            low_shape((wide_size, pieces, slice_rows, width)),
            jax.ShapeDtypeStruct((local_rows, HS), jnp.float32),
            jax.ShapeDtypeStruct((NBLK, HS), jnp.float32),
        ],
        scratch_shapes=[
            pltpu.VMEM((local_rows, width), low),
            pltpu.VMEM((local_rows, width), low),
            pltpu.VMEM((pieces, PIECE, width), low),
            pltpu.VMEM((width, parts * columns), low),
            pltpu.VMEM((group_rows, parts * columns), low),
            pltpu.VMEM((group_rows, columns), low),
            pltpu.VMEM((group_rows, columns), low),
            pltpu.VMEM((heads, NBLK, HS, HS), low),
            pltpu.SemaphoreType.DMA((7,)),
            pltpu.SemaphoreType.DMA((parts,)),
            pltpu.SemaphoreType.DMA((pieces,)),
            pltpu.SemaphoreType.DMA((pieces, parts)),
            pltpu.SemaphoreType.DMA((8, 2)),
            pltpu.SemaphoreType.DMA((3, 2)),
            pltpu.SemaphoreType.DMA((6, 2)),
            pltpu.SemaphoreType.DMA((7, 2)),
        ],
        compiler_params=pltpu.CompilerParams(
            vmem_limit_bytes=VMEM, collective_id=4, has_side_effects=True
        ),
        cost_estimate=cost(2 * group_rows * parts * width * columns, 50e6),
        name="mix_rows",
    )(hidden, cotangent, mix_weight, out_weight, seq_lengths, block_seq)


def widen(mix_low, out_low, in_low, wide_low, rows):
    parts, width, columns = mix_low.shape
    units = wide_low.shape[0]
    main = units // TILE * TILE
    tail = units - main
    steps = 2 * parts

    def body(mix_ref, out_ref, in_ref, wide_ref, one_ref, two_ref, mix_out, out_out, in_out, wide_out, one_out, two_out):
        one_out[...] = one_ref[...]
        two_out[...] = two_ref[...]
        mix_out[...] = mix_ref[...].astype(jnp.float32)
        out_out[...] = out_ref[...].astype(jnp.float32)
        wide_out[...] = wide_ref[...].astype(jnp.float32)
        for c in range(2):
            in_out[c, :, :main] = in_ref[:, c * main : (c + 1) * main].astype(jnp.float32)
            rest = slice(2 * main + c * tail, 2 * main + (c + 1) * tail)
            in_out[c, :, main:] = in_ref[:, rest].astype(jnp.float32)

    def rows_spec(array):
        return pl.BlockSpec((array.shape[0] // steps, array.shape[1]), lambda i: (i, 0))

    mix_spec = pl.BlockSpec((1, width // 2, columns), lambda i: (i // 2, i % 2, 0))
    shapes = (mix_low.shape, out_low.shape, (2, width, units), wide_low.shape)
    return pl.pallas_call(
        body,
        grid=(steps,),
        in_specs=[mix_spec] + [rows_spec(array) for array in (out_low, in_low, wide_low, *rows)],
        out_specs=[
            mix_spec,
            rows_spec(out_low),
            pl.BlockSpec((2, width // steps, units), lambda i: (0, i, 0)),
            rows_spec(wide_low),
            *(rows_spec(array) for array in rows),
        ],
        out_shape=[jax.ShapeDtypeStruct(shape, jnp.float32) for shape in shapes]
        + [jax.ShapeDtypeStruct(array.shape, array.dtype) for array in rows],
        compiler_params=pltpu.CompilerParams(vmem_limit_bytes=VMEM),
        cost_estimate=cost(1e8, 84e6),
        name="widen",
    )(mix_low, out_low, in_low, wide_low, *rows)


def block_decays(rate):
    row = lax.broadcasted_iota(jnp.int32, (BLK, BLK), 0)
    column = lax.broadcasted_iota(jnp.int32, (BLK, BLK), 1)
    distance = (row - column).astype(jnp.float32)
    within = jnp.where(row >= column, jnp.exp(-rate * jnp.maximum(distance, 0.0)), 0.0)
    place = lax.broadcasted_iota(jnp.int32, (BLK, 1), 0).astype(jnp.float32)
    entry = jnp.exp(-rate * (place + 1.0))
    leave = jnp.exp(-rate * (BLK - 1.0 - place))
    whole = jnp.exp(-BLK * rate * jnp.ones((1, HS), jnp.float32))
    return within, entry, leave, whole


def norm_back(values, grad):
    scale = lax.rsqrt(jnp.mean(values * values, axis=-1, keepdims=True) + epsilon)
    unit = values * scale
    return scale * (grad - unit * jnp.mean(grad * unit, axis=-1, keepdims=True))


def square_device(
    hidden, mix_weight, out_weight, ffn_in_weight, ffn_out_weight, seq_lengths, block_seq, cotangent
):
    width = hidden.shape[1]
    units = ffn_out_weight.shape[0]
    normed_all, parts, gated, mixing, states, grads_own, grads_first, whole_weight, live, keep = mix_rows(
        hidden, cotangent, mix_weight, out_weight, seq_lengths, block_seq
    )
    middle, normed_two_all, grad_two_all, act, grad_parts, back_sums, two_sums = gated_unit(
        gated,
        whole_weight,
        hidden,
        live,
        grads_own,
        grads_first,
        ffn_in_weight,
        ffn_out_weight,
    )
    in_low, wide_low, out_low, mix_low, _, _, layer_out, input_grad, *_ = weight_grads(
        act,
        grad_two_all,
        normed_two_all,
        grad_parts,
        back_sums,
        two_sums,
        middle,
        cotangent,
        out_weight,
        mix_weight,
        parts,
        mixing,
        states,
        gated,
        normed_all,
        hidden,
        live,
        keep,
    )
    grad_mix, grad_out, grad_ffn_in, grad_ffn_out, layer_out, input_grad = widen(
        mix_low.reshape(mix_weight.shape),
        out_low.reshape(out_weight.shape),
        in_low.reshape(width, 2 * units),
        wide_low.reshape(units, width),
        (layer_out, input_grad),
    )
    return (layer_out, input_grad, grad_mix, grad_out, grad_ffn_in, grad_ffn_out)


def solution(mesh):
    square = mesh.shape["wide"] == 8 and mesh.shape["narrow"] == 4
    per_device = square_device if square else general_device
    in_specs = (
        P(("wide", "narrow"), None),
        P(None, None, "narrow"),
        P("narrow", None),
        P(None, None, "narrow"),
        P("narrow", None),
        P("wide"),
        P("wide"),
        P(("wide", "narrow"), None),
    )
    out_specs = (
        P(("wide", "narrow"), None),
        P(("wide", "narrow"), None),
        P(None, None, "narrow"),
        P("narrow", None),
        P(None, None, "narrow"),
        P("narrow", None),
    )
    return jax.shard_map(
        per_device, mesh=mesh, in_specs=in_specs, out_specs=out_specs, check_vma=False
    )
```

```python
import functools
import math

import jax
import jax.numpy as jnp
from jax import lax
from jax.experimental import pallas as pl
from jax.experimental.pallas import tpu as pltpu
from jax.sharding import PartitionSpec as P

HEADS = 16
HS = 128
BLK = 256
NBLK = 8


epsilon = 1e-06
head_floor = 1.0
highest = lax.Precision.HIGHEST


def row_norm(values):
    return values * lax.rsqrt(jnp.mean(values * values, axis=-1, keepdims=True) + epsilon)


def head_norm(values):
    return values * lax.rsqrt(jnp.mean(values * values, axis=-1, keepdims=True) + head_floor)


def silu_slope(values):
    sigmoid_part = jax.nn.sigmoid(values)
    return sigmoid_part * (1.0 + values * (1.0 - sigmoid_part))


def decay_tables(decay_rates):
    positions = jnp.arange(BLK, dtype=jnp.float32)
    distance = positions[:, None] - positions[None, :]
    causal = distance >= 0
    clipped = jnp.where(causal, distance, 0.0)
    within = jnp.where(causal[None], jnp.exp(-decay_rates[:, None, None] * clipped[None]), 0.0)
    entry_decay = jnp.exp(-(positions[:, None] + 1.0) * decay_rates[None, :])
    exit_decay = jnp.exp(-(BLK - 1.0 - positions[:, None]) * decay_rates[None, :])
    block_decay = jnp.exp(-BLK * decay_rates)
    return (within, entry_decay, exit_decay, block_decay)


def group_masks(lengths, owners):
    seq_slot = owners - owners[0]
    first_count = jnp.sum((seq_slot == 0).astype(jnp.int32))
    block_ids = jnp.arange(NBLK, dtype=jnp.int32)
    start_block = jnp.where(seq_slot == 0, jnp.int32(0), first_count)
    seq_limit = jnp.where(seq_slot == 0, lengths[0], lengths[1])
    offsets = (block_ids - start_block)[:, None] * BLK + jnp.arange(BLK, dtype=jnp.int32)[None, :]
    valid_rows = (offsets < seq_limit[:, None]).reshape(-1)
    fresh_block = block_ids == start_block
    return (valid_rows, fresh_block)


def forward_block(tables, kv_state, block_in):
    within, entry_decay, exit_decay, block_decay = tables
    queries, keys_in, values, fresh_block = block_in
    kv_state = jnp.where(fresh_block, 0.0, kv_state)
    scores = jnp.einsum("ihs,jhs->hij", queries, keys_in, preferred_element_type=jnp.float32)
    weights = (scores * within).astype(jnp.bfloat16)
    inner_part = jnp.einsum("hij,jhs->ihs", weights, values, preferred_element_type=jnp.float32)
    carried = jnp.einsum(
        "ihs,hst->iht",
        queries.astype(jnp.float32) * entry_decay[:, :, None],
        kv_state,
        precision=highest,
    )
    update = jnp.einsum(
        "ihs,iht->hst",
        keys_in.astype(jnp.float32) * exit_decay[:, :, None],
        values.astype(jnp.float32),
        precision=highest,
    )
    return (block_decay[:, None, None] * kv_state + update, (inner_part + carried, kv_state))


def backward_block(tables, later_grad, block_in):
    within, entry_decay, exit_decay, block_decay = tables
    queries, keys_in, values, grad_mix, kv_state, fresh_block = block_in
    scores = jnp.einsum("ihs,jhs->hij", queries, keys_in, preferred_element_type=jnp.float32)
    weights = (scores * within).astype(jnp.bfloat16)
    grad_values = jnp.einsum("hij,ihs->jhs", weights, grad_mix, preferred_element_type=jnp.float32)
    grad_weights = jnp.einsum("ihs,jhs->hij", grad_mix, values, preferred_element_type=jnp.float32)
    grad_scores = (grad_weights * within).astype(jnp.bfloat16)
    grad_queries = jnp.einsum(
        "hij,jhs->ihs", grad_scores, keys_in, preferred_element_type=jnp.float32
    )
    grad_keys = jnp.einsum("hij,ihs->jhs", grad_scores, queries, preferred_element_type=jnp.float32)
    grad_float = grad_mix.astype(jnp.float32)
    values_float = values.astype(jnp.float32)
    queries_float = queries.astype(jnp.float32)
    keys_float = keys_in.astype(jnp.float32)
    grad_queries = grad_queries + entry_decay[:, :, None] * jnp.einsum(
        "iht,hst->ihs", grad_float, kv_state, precision=highest
    )
    grad_keys = grad_keys + exit_decay[:, :, None] * jnp.einsum(
        "iht,hst->ihs", values_float, later_grad, precision=highest
    )
    grad_values = grad_values + jnp.einsum(
        "ihs,hst->iht", keys_float * exit_decay[:, :, None], later_grad, precision=highest
    )
    grad_state = jnp.einsum(
        "ihs,iht->hst", queries_float * entry_decay[:, :, None], grad_float, precision=highest
    )
    grad_state = grad_state + block_decay[:, None, None] * later_grad
    grad_state = jnp.where(fresh_block, 0.0, grad_state)
    return (grad_state, (grad_queries, grad_keys, grad_values))


def general_device(
    hidden, mix_weight, out_weight, ffn_in_weight, ffn_out_weight, seq_lengths, block_seq, cotangent
):
    local_rows = hidden.shape[0]
    group_rows = NBLK * BLK
    head_width = mix_weight.shape[2]
    head_count = head_width // HS
    narrow_index = lax.axis_index("narrow")
    valid_all, fresh_block = group_masks(seq_lengths, block_seq)
    valid_rows = lax.dynamic_slice_in_dim(
        valid_all.astype(jnp.float32), narrow_index * local_rows, local_rows
    )[:, None]
    head_ids = narrow_index * head_count + jnp.arange(head_count, dtype=jnp.int32)
    decay_rates = 2.0 ** (-8.0 * (head_ids.astype(jnp.float32) + 1.0) / HEADS)
    tables = decay_tables(decay_rates)

    def split_blocks(flat_rows):
        return flat_rows.reshape(NBLK, BLK, head_count, HS)

    inputs = hidden.astype(jnp.float32)
    normed_low = row_norm(inputs).astype(jnp.bfloat16)
    gathered = lax.all_gather(normed_low, "narrow", axis=0, tiled=True)
    projected = jnp.einsum("rd,cde->cre", gathered, mix_weight, preferred_element_type=jnp.float32)
    queries = jax.nn.silu(projected[0]).astype(jnp.bfloat16)
    keys_in = jax.nn.silu(projected[1]).astype(jnp.bfloat16)
    values = projected[2].astype(jnp.bfloat16)
    gate_part = projected[3]
    zero_state = jnp.zeros((head_count, HS, HS), jnp.float32)
    final_state, (mixing, kept_states) = lax.scan(
        lambda state_in, block_in: forward_block(tables, state_in, block_in),
        zero_state,
        (split_blocks(queries), split_blocks(keys_in), split_blocks(values), fresh_block),
    )
    mixing = mixing.reshape(group_rows, head_count, HS)
    headed = head_norm(mixing).reshape(group_rows, head_width)
    gated_low = (headed * gate_part).astype(jnp.bfloat16)
    branch = lax.psum_scatter(
        jnp.dot(gated_low, out_weight, preferred_element_type=jnp.float32).astype(jnp.bfloat16),
        "narrow",
        scatter_dimension=0,
        tiled=True,
    ).astype(jnp.float32)
    middle = inputs + valid_rows * branch
    normed_two_low = row_norm(middle).astype(jnp.bfloat16)
    gathered_two = lax.all_gather(normed_two_low, "narrow", axis=0, tiled=True)
    both_parts = jnp.einsum(
        "rd,cdf->crf", gathered_two, ffn_in_weight, preferred_element_type=jnp.float32
    )
    hidden_low = (both_parts[0] * both_parts[1]).astype(jnp.bfloat16)
    branch_two = lax.psum_scatter(
        jnp.dot(hidden_low, ffn_out_weight, preferred_element_type=jnp.float32).astype(
            jnp.bfloat16
        ),
        "narrow",
        scatter_dimension=0,
        tiled=True,
    ).astype(jnp.float32)
    layer_out = (middle + valid_rows * branch_two).astype(jnp.bfloat16)
    grad_rows = cotangent.astype(jnp.float32)
    ffn_grad_all = lax.all_gather(
        (valid_rows * grad_rows).astype(jnp.bfloat16), "narrow", axis=0, tiled=True
    )
    grad_ffn_out = jnp.einsum(
        "rf,rd->fd", hidden_low, ffn_grad_all, preferred_element_type=jnp.float32
    )
    grad_hidden = jnp.einsum(
        "rd,fd->rf", ffn_grad_all, ffn_out_weight, preferred_element_type=jnp.float32
    )
    grad_parts = jnp.stack([grad_hidden * both_parts[1], grad_hidden * both_parts[0]]).astype(
        jnp.bfloat16
    )
    grad_ffn_in = jnp.einsum(
        "rd,crf->cdf", gathered_two, grad_parts, preferred_element_type=jnp.float32
    )
    grad_slice = grad_parts
    grad_normed_two = lax.psum_scatter(
        jnp.einsum(
            "crf,cdf->rd", grad_slice, ffn_in_weight, preferred_element_type=jnp.float32
        ).astype(jnp.bfloat16),
        "narrow",
        scatter_dimension=0,
        tiled=True,
    ).astype(jnp.float32)
    norm_value, norm_pull = jax.vjp(row_norm, middle)
    grad_middle = grad_rows + norm_pull(grad_normed_two)[0]
    attn_grad_all = lax.all_gather(
        (valid_rows * grad_middle).astype(jnp.bfloat16), "narrow", axis=0, tiled=True
    )
    grad_out_weight = jnp.einsum(
        "re,rd->ed", gated_low, attn_grad_all, preferred_element_type=jnp.float32
    )
    grad_gated = jnp.einsum(
        "rd,ed->re", attn_grad_all, out_weight, preferred_element_type=jnp.float32
    )
    grad_gated = lax.optimization_barrier(grad_gated.astype(jnp.bfloat16)).astype(jnp.float32)
    grad_gate = grad_gated * headed
    grad_headed = (grad_gated * gate_part).reshape(group_rows, head_count, HS)
    head_value, head_pull = jax.vjp(head_norm, mixing)
    grad_mixing = head_pull(grad_headed)[0].astype(jnp.bfloat16)
    first_grad, (grad_queries, grad_keys, grad_values) = lax.scan(
        lambda later_grad, block_in: backward_block(tables, later_grad, block_in),
        zero_state,
        (
            split_blocks(queries),
            split_blocks(keys_in),
            split_blocks(values),
            split_blocks(grad_mixing),
            kept_states,
            fresh_block,
        ),
        reverse=True,
    )
    grad_projected = jnp.stack(
        [
            grad_queries.reshape(group_rows, head_width) * silu_slope(projected[0]),
            grad_keys.reshape(group_rows, head_width) * silu_slope(projected[1]),
            grad_values.reshape(group_rows, head_width),
            grad_gate,
        ]
    ).astype(jnp.bfloat16)
    grad_mix = jnp.einsum(
        "rd,cre->cde", gathered, grad_projected, preferred_element_type=jnp.float32
    )
    grad_slice = grad_projected
    grad_normed = lax.psum_scatter(
        jnp.einsum(
            "cre,cde->rd", grad_slice, mix_weight, preferred_element_type=jnp.float32
        ).astype(jnp.bfloat16),
        "narrow",
        scatter_dimension=0,
        tiled=True,
    ).astype(jnp.float32)
    first_value, first_pull = jax.vjp(row_norm, inputs)
    input_grad = (grad_middle + first_pull(grad_normed)[0]).astype(jnp.bfloat16)
    grad_mix, grad_out_weight, grad_ffn_in, grad_ffn_out = (
        lax.psum(grad_mix.astype(jnp.bfloat16), "wide").astype(jnp.float32),
        lax.psum(grad_out_weight.astype(jnp.bfloat16), "wide").astype(jnp.float32),
        lax.psum(grad_ffn_in.astype(jnp.bfloat16), "wide").astype(jnp.float32),
        lax.psum(grad_ffn_out.astype(jnp.bfloat16), "wide").astype(jnp.float32),
    )
    return (layer_out, input_grad, grad_mix, grad_out_weight, grad_ffn_in, grad_ffn_out)


HALF = BLK
PIECE = 2 * BLK
VMEM = 60 * 1024 * 1024


def add_low(*terms):
    return sum(term.astype(jnp.float32) for term in terms).astype(jnp.bfloat16)


def add_rows(*terms):
    return sum(term.astype(jnp.float32) for term in terms)


def across(left, right):
    return lax.dot_general(left, right, (((1,), (1,)), ((), ())), preferred_element_type=jnp.float32)


def down(left, right):
    return lax.dot_general(left, right, (((0,), (0,)), ((), ())), preferred_element_type=jnp.float32)


def straight(left, right):
    return jnp.dot(left, right, preferred_element_type=jnp.float32)


def any_specs(count):
    return [pl.BlockSpec(memory_space=pl.ANY)] * count


def cost(flops, bytes_accessed):
    return pl.CostEstimate(flops=int(flops), bytes_accessed=int(bytes_accessed), transcendentals=0)


MESH = pl.DeviceIdType.MESH
SLOTS = 12
STAGES = 11
SUB = 128
TILE = 256


def begin(copies):
    for copy in copies:
        copy.start()


def finish(copies):
    for copy in copies:
        copy.wait()


def neighbours():
    wide, narrow = lax.axis_index("wide"), lax.axis_index("narrow")
    z, core = wide // 2, wide % 2
    mate = (wide + 1 - 2 * core, narrow)
    near_x = (wide, narrow + 1 - 2 * (narrow % 2))
    near_y = (wide, (narrow + 2) % 4)
    return wide, narrow, z, core, mate, near_x, near_y


def slot_of(block, narrow):
    off_x = (block // 2 % 2 + narrow % 2) % 2
    off_y = (block // 4 + narrow // 2) % 2
    if block % 2:
        return 1 + 3 * off_x + 2 * off_y + off_x * off_y
    return 2 * off_x + 5 * off_y - off_x * off_y


def head_rate(head):
    return jnp.exp(jnp.full((1, 1), -8.0 / HEADS * math.log(2.0), jnp.float32) * (head.astype(jnp.float32) + 1.0))


def line_scratch():
    low = jnp.bfloat16
    pair = pltpu.VMEM((SLOTS, 2, SUB, TILE), low)
    return [
        pltpu.VMEM((SLOTS, 4, SUB, TILE), low),
        pair,
        pair,
        pair,
        pltpu.VMEM((SLOTS, SUB, TILE), low),
        pair,
        pair,
        pltpu.SemaphoreType.DMA((14, SLOTS)),
        pltpu.SemaphoreType.DMA((4, SLOTS)),
    ]


def enter(neighbour_places):
    wide, narrow, z, core, mate, near_x, near_y = neighbour_places
    barrier = pltpu.get_barrier_semaphore()

    def greet(place):
        pl.semaphore_signal(barrier, inc=1, device_id=place, device_id_type=MESH)

    for place in (mate, near_x, near_y):
        greet(place)
    middle = (z == 1) | (z == 2)

    @pl.when(middle)
    def _():
        greet((2 * (3 - z) + core, narrow))
        greet((6 * (z - 1) + core, narrow))
        pl.semaphore_wait(barrier, 5)

    @pl.when(jnp.logical_not(middle))
    def _():
        greet((2 * (1 + z // 3) + core, narrow))
        pl.semaphore_wait(barrier, 4)


def line_sum(scratch, places, count, product, targets):
    own, met, both, ended, crossed, full, other, sems, out_sems = scratch
    wide, narrow, z, core, mate, _, _ = places
    region = z // 2
    middle = (z == 1) | (z == 2)
    end = jnp.logical_not(middle)
    inward = (2 * (1 + z // 3) + core, narrow)
    across_line = (2 * (3 - z) + core, narrow)
    outward = (6 * (z - 1) + core, narrow)

    def remote(src, dst, kind, slot, place):
        return pltpu.make_async_remote_copy(
            src_ref=src,
            dst_ref=dst,
            send_sem=sems.at[2 * kind, slot],
            recv_sem=sems.at[2 * kind + 1, slot],
            device_id=place,
            device_id_type=MESH,
        )

    def core_one(s):
        return remote(own.at[s, pl.ds(2 * (1 - core), 2)], met.at[s], 0, s, mate)

    def line_one(s):
        return remote(both.at[s], ended.at[s], 1, s, inward)

    def cross_one(s):
        return remote(both.at[s, 1 - region], crossed.at[s], 2, s, across_line)

    def cross_two(s):
        return remote(full.at[s, region], full.at[s, region], 3, s, across_line)

    def out_one(s):
        return remote(full.at[s, region], full.at[s, region], 4, s, outward)

    def out_two(s):
        return remote(full.at[s, 1 - region], full.at[s, 1 - region], 5, s, outward)

    def core_two(s):
        return remote(full.at[s], other.at[s], 6, s, mate)

    def landing(ref, kind, slot):
        return remote(ref, ref, kind, slot, mate)

    def add(left, right):
        return (left.astype(jnp.float32) + right.astype(jnp.float32)).astype(jnp.bfloat16)

    def deliveries(k, s):
        for t in range(2):
            for which, (src, part) in enumerate(
                ((full.at[s, t], 2 * core + t), (other.at[s, t], 2 * (1 - core) + t))
            ):
                for condition, ref in targets(k, part):
                    yield condition, pltpu.make_async_copy(src, ref, out_sems.at[2 * t + which, s])

    def start(k, s):
        product(k, own.at[s])
        core_one(s).start()

    def cores(k, s):
        core_one(s).wait_recv()
        both[s] = add(own[s, pl.ds(2 * core, 2)], met[s])
        pl.when(end)(lambda: line_one(s).start())

    def ends(k, s):
        @pl.when(middle)
        def _():
            landing(ended.at[s], 1, s).wait_recv()
            both[s] = add(both[s], ended[s])
            cross_one(s).start()

    def centre(k, s):
        @pl.when(middle)
        def _():
            cross_one(s).wait_recv()
            full[s, region] = add(both[s, region], crossed[s])
            cross_two(s).start()
            out_one(s).start()

    def pass_on(k, s):
        @pl.when(middle)
        def _():
            cross_two(s).wait_recv()
            out_two(s).start()

    def back(k, s):
        @pl.when(end)
        def _():
            landing(full.at[s, region], 4, s).wait_recv()
            landing(full.at[s, 1 - region], 5, s).wait_recv()

        core_two(s).start()

    def deliver(k, s):
        core_two(s).wait_recv()
        for condition, copy in deliveries(k, s):
            pl.when(condition)(copy.start)

    def clear(k, s):
        core_one(s).wait_send()
        core_two(s).wait_send()

        @pl.when(end)
        def _():
            line_one(s).wait_send()

        @pl.when(middle)
        def _():
            for copy in (cross_one(s), cross_two(s), out_one(s), out_two(s)):
                copy.wait_send()

        for t in range(2):
            for which, src in enumerate((full, other)):
                ref = targets(k, 0)[0][1]
                pltpu.make_async_copy(src.at[s, t], ref, out_sems.at[2 * t + which, s]).wait()

    stages = (
        (11, clear),
        (10, deliver),
        (9, back),
        (7, pass_on),
        (5, centre),
        (3, ends),
        (1, cores),
        (0, start),
    )

    def step(i, carry):
        for delay, work in stages:
            k = i - delay

            @pl.when((k >= 0) & (k < count))
            def _(work=work, k=k):
                work(k, lax.rem(k + SLOTS, SLOTS))

        return carry

    return step


def square_scratch(uses):
    block = pltpu.VMEM((2, BLK, HEADS * HS), jnp.bfloat16)
    return [block, block, pltpu.SemaphoreType.DMA((uses, 6, 2)), pltpu.SemaphoreType.DMA((uses, 2))]


def square_sum(scratch, places, parts, landed, use, side=None):
    met, mid, sems, load_sems = scratch
    top_x, low_y, low_x, top_y, top_d, low_d = parts
    near_x, near_y = places[5:]

    def remote(src, dst, kind, place):
        return pltpu.make_async_remote_copy(
            src_ref=src,
            dst_ref=dst,
            send_sem=sems.at[use, kind, 0],
            recv_sem=sems.at[use, kind, 1],
            device_id=place,
            device_id_type=MESH,
        )

    first = [remote(top_d, met.at[0], 0, near_x), remote(low_d, met.at[1], 1, near_y)]
    direct = [remote(top_x, landed[0], 2, near_x), remote(low_y, landed[1], 3, near_y)]
    second = [remote(mid.at[0], landed[2], 4, near_y), remote(mid.at[1], landed[3], 5, near_x)]
    loads = []
    if top_y is not None:
        loads = [
            pltpu.make_async_copy(top_y, mid.at[0], load_sems.at[use, 0]),
            pltpu.make_async_copy(low_x, mid.at[1], load_sems.at[use, 1]),
        ]

    def open_sum():
        begin(first)
        begin(direct)
        begin(loads)

    def join_sum():
        finish(loads)
        for at in range(2):
            first[at].wait()

            def tile(i, carry, at=at):
                rows = pl.ds(pl.multiple_of(i * 64, 64), 64)
                mine = mid[at, rows, :] if side is None else side[at][rows, :]
                mid[at, rows, :] = add_low(mine, met[at, rows, :])
                return carry

            lax.fori_loop(0, BLK // 64, tile, 0)
        begin(second)

    def close_sum():
        finish(direct)
        finish(second)

    return open_sum, join_sum, close_sum


def weight_grads(
    act,
    grad_two_all,
    normed_two_all,
    grad_parts,
    back_sums,
    two_sums,
    middle,
    cotangent,
    out_weight,
    mix_weight,
    parts_all,
    mixing_all,
    states_all,
    gated,
    normed_all,
    hidden,
    live,
    keep,
):
    rows, units = act.shape
    width = grad_two_all.shape[1]
    local_rows = middle.shape[0]
    parts, _, columns = parts_all.shape
    heads = columns // HS
    low = jnp.bfloat16
    in_columns = grad_parts.shape[1] // TILE
    in_rows = width // PIECE
    out_blocks = units // SUB
    halves = width // 1024
    first_out = in_rows * in_columns
    first_branch = first_out + halves * out_blocks
    first_mix = first_branch + width // TILE
    per_row = columns // TILE
    per_part = in_rows * per_row
    count = first_mix + parts * per_part

    def body(*refs):
        act_in, two_in, normed_two_in, parts_in, back_in, two_sums_in = refs[:6]
        middle_in, cot_in, weight_in, mix_in = refs[6:10]
        all_in, mixing_in, states_in, gated_in, normed_in, hidden_in, live_ref, keep_ref = refs[10:18]
        in_grad, out_grad, branch_grad, mix_grad, branch_out, middle_out, layer_out, input_out = refs[18:26]
        last_landed, two_landed = refs[26:30], refs[30:34]
        shared, wide_ref, act_ref, landed, stage_ref, mid_ref, grad_ref, branch = refs[34:42]
        near, gated_grad, states_ref = refs[42:45]
        normed_sems, parts_sems, load_sems, stage_sems, gather_sems, back_sems, head_sems, mix_sems = refs[45:53]
        tile_sems, last_sems = refs[53:55]
        line, square = refs[55:64], refs[64:68]
        places = neighbours()
        narrow, near_x, near_y = places[1], places[5], places[6]

        def block(at):
            return pl.ds(at * BLK, BLK)

        def cols(at, size):
            return pl.ds(pl.multiple_of(at, 128), size)

        def load_normed_two(at):
            here = cols(at * PIECE, PIECE)
            return pltpu.make_async_copy(normed_two_in.at[:, here], shared.at[:, here], normed_sems.at[at])

        def load_parts(at):
            here = cols(at * TILE, TILE)
            return pltpu.make_async_copy(parts_in.at[:, here], wide_ref.at[:, here], parts_sems.at[at])

        def load_half(src, half, sem):
            here = pl.ds(half * 1024, 1024)
            return pltpu.make_async_copy(src.at[:, here], shared.at[:, here], load_sems.at[sem])

        load_act = pltpu.make_async_copy(act_in, act_ref, load_sems.at[0])
        load_two = [load_half(two_in, half, 1 + half) for half in range(halves)]
        load_normed = [load_half(normed_in, half, 3 + half) for half in range(halves)]
        load_gated = pltpu.make_async_copy(gated_in.at[0], act_ref.at[:, pl.ds(0, columns)], load_sems.at[5])

        def load_branch(at):
            slot = at % 2
            return pltpu.make_async_copy(
                branch_out.at[:, cols(at * TILE, TILE)],
                act_ref.at[:, cols(columns + slot * TILE, TILE)],
                tile_sems.at[slot],
            )

        def product(k, own):
            def split_rows(result):
                for part in range(4):
                    own[part] = result[part * SUB : (part + 1) * SUB]

            @pl.when(k < first_out)
            def _():
                row, column = k // in_columns, k % in_columns

                @pl.when(column == 0)
                def _():
                    load_normed_two(row).wait()

                @pl.when(row == 0)
                def _():
                    load_parts(column).wait()

                here, there = cols(row * PIECE, PIECE), cols(column * TILE, TILE)
                split_rows(down(shared[:, here], wide_ref[:, there]).astype(low))

                @pl.when(k == first_out - in_columns)
                def _():
                    load_two[0].start()

            @pl.when(k == first_out)
            def _():
                begin(load_two[1:])
                load_act.wait()
                load_two[0].wait()

            @pl.when(k == first_out + out_blocks)
            def _():
                finish(load_two[1:])
                load_normed[0].start()

            @pl.when((k >= first_out) & (k < first_branch))
            def _():
                at = k - first_out
                here = cols((at % out_blocks) * SUB, SUB)
                there = cols((at // out_blocks) * 1024, 1024)
                result = down(act_ref[:, here], shared[:, there]).astype(low)
                for part in range(4):
                    own[part] = result[:, part * TILE : (part + 1) * TILE]

            pl.when(k == first_branch - out_blocks + columns // SUB)(lambda: load_gated.start())
            pl.when(k == first_branch - out_blocks + (columns + TILE) // SUB)(lambda: load_branch(0).start())

            @pl.when(k == first_branch)
            def _():
                begin(load_normed[1:])
                load_gated.wait()

            @pl.when((k >= first_branch) & (k < first_mix))
            def _():
                at = k - first_branch
                load_branch(at).wait()
                pl.when(k + 1 < first_mix)(lambda: load_branch(at + 1).start())
                there = cols(columns + (at % 2) * TILE, TILE)
                split_rows(down(act_ref[:, :columns], act_ref[:, there]).astype(low))

            @pl.when(k == first_mix)
            def _():
                finish(load_normed)

            @pl.when(k >= first_mix)
            def _():
                at = k - first_mix
                here = cols(((at // per_row) % in_rows) * PIECE, PIECE)
                there = cols((at // per_part) * columns + (at % per_row) * TILE, TILE)
                split_rows(down(shared[:, here], wide_ref[:, there]).astype(low))

        def targets(k, part):
            one = jnp.minimum(k, first_out - 1)
            two = jnp.clip(k - first_out, 0, first_branch - first_out - 1)
            three = jnp.clip(k - first_branch, 0, first_mix - first_branch - 1)
            four = jnp.maximum(k - first_mix, 0)
            return [
                (
                    k < first_out,
                    in_grad.at[(one // in_columns) * 4 + part, :, cols((one % in_columns) * TILE, TILE)],
                ),
                (
                    (k >= first_out) & (k < first_branch),
                    out_grad.at[two % out_blocks, :, cols((two // out_blocks) * 1024 + part * TILE, TILE)],
                ),
                (
                    (k >= first_branch) & (k < first_mix),
                    branch_grad.at[part, :, cols(three * TILE, TILE)],
                ),
                (
                    k >= first_mix,
                    mix_grad.at[(four // per_row) * 4 + part, :, cols((four % per_row) * TILE, TILE)],
                ),
            ]

        step = line_sum(line, places, count, product, targets)
        now = [0]

        def run(steps):
            lax.fori_loop(now[0], now[0] + steps, step, 0)
            now[0] += steps

        open_sum, join_sum, close_sum = square_sum(
            square,
            places,
            [back_in.at[block(at)] for at in range(2, 8)],
            [landed.at[at] for at in range(4)],
            0,
        )
        load_normed_two(0).start()
        load_parts(0).start()
        enter(places)
        open_sum()
        for at in range(1, in_columns):
            load_parts(at).start()
        for at in range(1, in_rows):
            load_normed_two(at).start()
        load_act.start()

        def spread(src, slot, kind, place):
            return pltpu.make_async_remote_copy(
                src_ref=src,
                dst_ref=branch_out.at[block(slot)],
                send_sem=gather_sems.at[kind, 0],
                recv_sem=gather_sems.at[kind, 1],
                device_id=place,
                device_id_type=MESH,
            )

        def stage(half):
            return [
                pltpu.make_async_copy(back_in.at[block(half)], stage_ref.at[0], stage_sems.at[0]),
                pltpu.make_async_copy(cot_in.at[block(half)], stage_ref.at[1], stage_sems.at[1]),
                pltpu.make_async_copy(middle_in.at[block(half)], mid_ref, stage_sems.at[2]),
            ]

        keep_branch = [
            pltpu.make_async_copy(branch.at[at], branch_out.at[block(at)], stage_sems.at[3 + at])
            for at in range(2)
        ]

        def rows_back(half):
            def tile(i, carry):
                at = pl.ds(pl.multiple_of(i * 32, 32), 32)
                grad = add_rows(stage_ref[0, at, :], landed[half, at, :], landed[2 + half, at, :])
                result = stage_ref[1, at, :].astype(jnp.float32) + norm_back(mid_ref[at, :], grad)
                grad_ref[at, :] = result
                live_at = pl.ds(pl.multiple_of(half * BLK + i * 32, 32), 32)
                branch[half, at, :] = (live_ref[live_at, :1] * result).astype(low)
                return carry

            lax.fori_loop(0, BLK // 32, tile, 0)
            copy = pltpu.make_async_copy(grad_ref, middle_out.at[block(half)], stage_sems.at[5])
            copy.start()
            return copy

        sends = [
            spread(branch.at[0], 2, 0, near_x),
            spread(branch.at[1], 3, 1, near_y),
            spread(branch.at[1], 4, 2, near_x),
            spread(branch.at[0], 5, 3, near_y),
        ]
        later = [
            spread(branch_out.at[block(3)], 7, 4, near_x),
            spread(branch_out.at[block(2)], 6, 5, near_y),
        ]
        weight_loads = [
            pltpu.make_async_copy(weight_in.at[block(at)], landed.at[at], back_sems.at[at])
            for at in range(columns // BLK)
        ]

        def row_loads(slot):
            return [
                pltpu.make_async_copy(branch_out.at[block(slot + at)], stage_ref.at[at], back_sems.at[2 + at])
                for at in range(2)
            ]

        def back_rows(slot, rows_ref):
            for at in range(2):
                for part in range(len(weight_loads)):
                    result = across(rows_ref[at], landed[part]).astype(low)
                    gated_grad[(slot + at) * BLK : (slot + at + 1) * BLK, part * BLK : (part + 1) * BLK] = result

        def head_loads(head):
            here = cols(head * HS, HS)
            loads = [
                pltpu.make_async_copy(
                    all_in.at[c, :, here],
                    wide_ref.at[:, pl.ds(parts * columns + c * HS, HS)],
                    head_sems.at[c],
                )
                for c in range(parts)
            ]
            loads.append(
                pltpu.make_async_copy(
                    mixing_in.at[:, here],
                    wide_ref.at[:, pl.ds(parts * columns + parts * HS, HS)],
                    head_sems.at[parts],
                )
            )
            loads.append(pltpu.make_async_copy(states_in.at[head], states_ref, head_sems.at[parts + 1]))
            return loads

        open_two, join_two, close_two = square_sum(
            square, places, [two_sums_in.at[block(at)] for at in range(2, 8)], two_landed, 1
        )
        run(9)
        join_sum()
        begin(stage(0))
        run(16)
        close_sum()
        finish(stage(0))
        written = rows_back(0)
        sends[0].start()
        begin(stage(1))
        run(1)
        finish(stage(1))
        written.wait()
        written = rows_back(1)
        begin(sends[1:])
        begin(keep_branch)
        begin(weight_loads)
        run(2)
        finish(weight_loads)
        back_rows(0, branch)
        run(6)
        for copy in sends[:2]:
            copy.wait_recv()
        begin(later)
        begin(row_loads(2))
        run(1)
        finish(row_loads(2))
        back_rows(2, stage_ref)
        run(7)
        for copy in sends[2:]:
            copy.wait_recv()
        begin(row_loads(4))
        run(1)
        finish(row_loads(4))
        back_rows(4, stage_ref)
        run(8)
        begin(head_loads(0))
        for copy in later:
            copy.wait_recv()
        begin(row_loads(6))
        run(1)
        finish(row_loads(6))
        back_rows(6, stage_ref)
        written.wait()
        finish(keep_branch)
        for copy in sends + later:
            copy.wait_send()
        open_two()

        def load_mix(at):
            here = pl.ds(pl.multiple_of(at * BLK, BLK), BLK)
            slot = at % 4
            return [
                pltpu.make_async_copy(
                    mix_in.at[c, here, :], landed.at[slot, :, pl.ds(c * columns, columns)], mix_sems.at[slot, c]
                )
                for c in range(parts)
            ]

        for at in range(4):
            begin(load_mix(at))
        attend_from = now[0]
        breaks = (2, 5, NBLK - 1)

        def attend(head, carry):
            rate = head_rate(heads * narrow + head)
            within, entry, leave, whole = block_decays(rate)
            finish(head_loads(head))
            pl.when(head == heads - 1)(join_two)
            later_grad = jnp.zeros((HS, HS), jnp.float32)
            base = parts * columns
            for at in range(NBLK):
                block_at = NBLK - 1 - at
                here = pl.ds(pl.multiple_of(slot_of(block_at, narrow) * BLK, BLK), BLK)

                def load(c, here=here):
                    return wide_ref[here, base + c * HS : base + (c + 1) * HS]

                def store(c, value, here=here):
                    wide_ref[here, cols(c * columns + head * HS, HS)] = value.astype(low)

                raw_queries = load(0).astype(jnp.float32)
                raw_keys = load(1).astype(jnp.float32)
                queries, keys = jax.nn.silu(raw_queries).astype(low), jax.nn.silu(raw_keys).astype(low)
                values = load(2)
                gate = load(3).astype(jnp.float32)
                mixing = load(4).astype(jnp.float32)
                grad_rows = gated_grad[here, cols(head * HS, HS)].astype(jnp.float32)
                scale = lax.rsqrt(jnp.mean(mixing * mixing, axis=-1, keepdims=True) + head_floor)
                headed = mixing * scale
                store(3, grad_rows * headed)
                grad_headed = grad_rows * gate
                inner = jnp.mean(grad_headed * headed, axis=-1, keepdims=True)
                grad = (scale * (grad_headed - headed * inner)).astype(low)
                scores = (across(queries, keys) * within).astype(low)
                grad_scores = (across(grad, values) * within).astype(low)
                later_low = later_grad.astype(low)
                grad_queries = straight(grad_scores, keys) + entry * across(grad, states_ref[block_at])
                grad_keys = down(grad_scores, queries) + leave * across(values, later_low)
                grad_values = down(scores, grad) + leave * straight(keys, later_low)
                early_queries = (queries.astype(jnp.float32) * entry).astype(low)
                later_grad = keep_ref[block_at : block_at + 1, :1] * (
                    whole * later_grad + down(early_queries, grad)
                )
                store(0, grad_queries * silu_slope(raw_queries))
                store(1, grad_keys * silu_slope(raw_keys))
                store(2, grad_values)
                if at == NBLK - 1:
                    pl.when(head + 1 < heads)(lambda: begin(head_loads(head + 1)))
                if at in breaks:
                    step(attend_from + head * len(breaks) + breaks.index(at), 0)
            return carry

        lax.fori_loop(0, heads, attend, 0)
        now[0] += heads * len(breaks)

        sum_from = now[0]
        side = (mid_ref, grad_ref)

        def put(pair):
            def store(at, here, value):
                pair[at, :, here] = value

            return store

        def put_side(at, here, value):
            side[1 - at][:, here] = value.astype(jnp.float32)

        outs = ((3, put(branch)), (1, put(near)), (2, put_side), (0, put(stage_ref)))

        def sum_tile(at, carry):
            finish(load_mix(at))
            here = cols(at * BLK, BLK)
            for which, (piece, store) in enumerate(outs):
                acts = wide_ref[piece * PIECE : (piece + 1) * PIECE, : parts * columns]
                total = across(acts, landed[at % 4]).astype(low)
                store(0, here, total[:HALF])
                store(1, here, total[HALF:])
                if which == 3:
                    pl.when(at + 4 < width // BLK)(lambda: begin(load_mix(at + 4)))
                if which % 2:
                    step(sum_from + 2 * at + which // 2, 0)
            return carry

        lax.fori_loop(0, width // BLK, sum_tile, 0)
        now[0] += 2 * (width // BLK)
        open_last, join_last, close_last = square_sum(
            square,
            places,
            (near.at[0], near.at[1], None, None, branch.at[0], branch.at[1]),
            last_landed,
            2,
            side,
        )
        close_two()
        open_last()
        run(9)
        join_last()

        def block_loads(half, terms, floats):
            loads = [
                pltpu.make_async_copy(src, landed.at[at], last_sems.at[at]) for at, src in enumerate(terms)
            ]
            loads.append(pltpu.make_async_copy(floats.at[block(half)], mid_ref, last_sems.at[3]))
            return loads

        def block_store(half, out):
            return pltpu.make_async_copy(landed.at[3], out.at[block(half)], last_sems.at[4])

        def layer_loads(half):
            terms = (two_sums_in.at[block(half)], two_landed[half], two_landed[2 + half])
            return block_loads(half, terms, middle_in)

        def input_loads(half):
            terms = (last_landed[half], last_landed[2 + half], hidden_in.at[block(half)])
            return block_loads(half, terms, middle_out)

        def layer_tile(i, carry, half):
            at = pl.ds(pl.multiple_of(i * 32, 32), 32)
            live_at = pl.ds(pl.multiple_of(half * BLK + i * 32, 32), 32)
            branch_two = add_rows(landed[0, at, :], landed[1, at, :], landed[2, at, :])
            landed[3, at, :] = (mid_ref[at, :] + live_ref[live_at, :1] * branch_two).astype(low)
            return carry

        def input_tile(i, carry, half):
            at = pl.ds(pl.multiple_of(i * 32, 32), 32)
            grad_normed = add_rows(stage_ref[half, at, :], landed[0, at, :], landed[1, at, :])
            back = norm_back(landed[2, at, :].astype(jnp.float32), grad_normed)
            landed[3, at, :] = (mid_ref[at, :] + back).astype(low)
            return carry

        def rows_out(loads, tile, out):
            tiles = BLK // 32 // 4
            for half in range(2):
                begin(loads(half))
                run(1)
                finish(loads(half))
                if half:
                    block_store(0, out).wait()
                base = now[0]

                def part(at, carry, half=half, base=base):
                    for one in range(tiles):
                        tile(tiles * at + one, 0, half)
                    step(base + at, 0)
                    return carry

                lax.fori_loop(0, 4, part, 0)
                now[0] += 4
                block_store(half, out).start()

        rows_out(layer_loads, layer_tile, layer_out)
        run(first_mix + 31 - now[0])
        block_store(1, layer_out).wait()
        close_last()
        rows_out(input_loads, input_tile, input_out)
        run(count + STAGES - now[0])
        block_store(1, input_out).wait()

    def low_shape(*shape):
        return jax.ShapeDtypeStruct(shape, low)

    sem = pltpu.SemaphoreType.DMA
    return pl.pallas_call(
        body,
        in_specs=any_specs(16) + [pl.BlockSpec(memory_space=pltpu.VMEM)] * 2,
        out_specs=any_specs(16),
        out_shape=[
            low_shape(width // SUB, SUB, grad_parts.shape[1]),
            low_shape(out_blocks, SUB, width),
            low_shape(columns // SUB, SUB, width),
            low_shape(parts * width // SUB, SUB, columns),
            low_shape(rows, width),
            jax.ShapeDtypeStruct((local_rows, width), jnp.float32),
            low_shape(local_rows, width),
            low_shape(local_rows, width),
        ]
        + [low_shape(BLK, width)] * 8,
        scratch_shapes=[
            pltpu.VMEM((rows, width), low),
            pltpu.VMEM(grad_parts.shape, low),
            pltpu.VMEM(act.shape, low),
            pltpu.VMEM((4, BLK, width), low),
            pltpu.VMEM((2, BLK, width), low),
            pltpu.VMEM((BLK, width), jnp.float32),
            pltpu.VMEM((BLK, width), jnp.float32),
            pltpu.VMEM((2, BLK, width), low),
            pltpu.VMEM((2, BLK, width), low),
            pltpu.VMEM((rows, columns), low),
            pltpu.VMEM((NBLK, HS, HS), low),
            sem((in_rows,)),
            sem((in_columns,)),
            sem((6,)),
            sem((6,)),
            sem((6, 2)),
            sem((4,)),
            sem((parts + 2,)),
            sem((4, parts)),
            sem((2,)),
            sem((5,)),
        ]
        + line_scratch()
        + square_scratch(3),
        compiler_params=pltpu.CompilerParams(
            vmem_limit_bytes=VMEM, collective_id=1, has_side_effects=True
        ),
        cost_estimate=cost(2 * rows * width * (3 * units + 9 * columns), 120e6),
        name="weight_grads",
    )(
        act,
        grad_two_all,
        normed_two_all,
        grad_parts,
        back_sums,
        two_sums,
        middle,
        cotangent,
        out_weight,
        mix_weight,
        parts_all,
        mixing_all,
        states_all,
        gated,
        normed_all,
        hidden,
        live,
        keep,
    )


def gated_unit(gated, whole_weight, hidden, live, grads_own, grads_first, ffn_in, ffn_out):
    _, width, units = ffn_in.shape
    local_rows = hidden.shape[0]
    group_rows = NBLK * BLK
    pieces = group_rows // PIECE
    deep = gated.shape[2]
    slices, quarters, slice_rows, _ = whole_weight.shape
    main = units // TILE * TILE
    tail = units - main
    low = jnp.bfloat16
    cuts = ((0, 2 * TILE), (2 * TILE, main - 2 * TILE))
    wide_tile = 1024
    first_half, second_half = pl.ds(0, HALF), pl.ds(HALF, HALF)

    def body(*refs):
        gated_in, weight_in, hidden_in = refs[:3]
        grad_in = refs[3:5]
        in_ref, out_ref, live_ref = refs[5:8]
        middle_out, rows_out, grads_out, act_out, parts_out, back_out, two_out = refs[8:15]
        gated_ref, hidden_ref, middle_ref = refs[15:18]
        rows, grads, sums, w_in, w_out, act, parts, held = refs[18:26]
        load_sems, slice_sems, weight_sems, done_sems, sum_sems, last_sems, gated_sems, gather_sems = refs[26:]
        wide, narrow, _, _, _, near_x, near_y = neighbours()
        far = (wide, 3 - narrow)
        here = pl.ds(pl.multiple_of(narrow * deep, deep), deep)

        def send_gated(slot, to, kind, place):
            return pltpu.make_async_remote_copy(
                src_ref=gated_in.at[0, pl.ds(slot * BLK, BLK)],
                dst_ref=gated_ref.at[(first_half, second_half)[to], here],
                send_sem=gated_sems.at[kind, 0],
                recv_sem=gated_sems.at[kind, 1],
                device_id=place,
                device_id_type=MESH,
            )

        gated_sends = [
            send_gated(6, 0, 0, far),
            send_gated(7, 1, 1, far),
            send_gated(2, 0, 2, near_x),
            send_gated(3, 1, 3, near_y),
            send_gated(4, 1, 4, near_x),
            send_gated(5, 0, 5, near_y),
        ]
        keep_gated = pltpu.make_async_copy(
            gated_in.at[0, pl.ds(0, PIECE)], gated_ref.at[:, here], load_sems.at[0]
        )

        def load_slice(at):
            part, quarter = at // quarters, at % quarters
            to = pl.ds(pl.multiple_of(quarter * deep + part * slice_rows, slice_rows), slice_rows)
            return pltpu.make_async_copy(
                weight_in.at[part, quarter], w_in.at[to, pl.ds(0, width)], slice_sems.at[at]
            )

        def start_slice(at, carry):
            load_slice(at).start()
            return carry

        def wait_slice(at, carry):
            load_slice(at).wait()
            return carry

        load_hidden = pltpu.make_async_copy(hidden_in, hidden_ref, load_sems.at[1])
        load_grads = [
            pltpu.make_async_copy(src, grads.at[at], load_sems.at[2 + at])
            for at, src in enumerate(grad_in)
        ]
        weights = []
        for start, size, first, second in tuple((a, b, a, main + a) for a, b in cuts) + (
            (main, tail, 2 * main, 2 * main + tail),
        ):
            at = pl.ds(start, size)
            weights += [
                pltpu.make_async_copy(in_ref.at[0, :, at], w_in.at[:, pl.ds(first, size)], weight_sems.at[len(weights)]),
                pltpu.make_async_copy(in_ref.at[1, :, at], w_in.at[:, pl.ds(second, size)], weight_sems.at[len(weights) + 1]),
                pltpu.make_async_copy(out_ref.at[at, :], w_out.at[at, :], weight_sems.at[len(weights) + 2]),
            ]

        def remote(src, dst, sems, kind, place):
            return pltpu.make_async_remote_copy(
                src_ref=src,
                dst_ref=dst,
                send_sem=sems.at[kind, 0],
                recv_sem=sems.at[kind, 1],
                device_id=place,
                device_id_type=MESH,
            )

        def half(ref, piece, at):
            return ref.at[piece, (first_half, second_half)[at]]

        def quarter(ref, piece, at):
            return ref.at[piece, pl.ds(at * SUB, SUB)]

        def gather(ref, kind):
            return (
                [
                    remote(half(ref, 0, 0), half(ref, 1, 0), gather_sems, kind, near_x),
                    remote(half(ref, 0, 1), half(ref, 1, 1), gather_sems, kind + 1, near_y),
                ],
                [
                    remote(half(ref, 0, 1), half(ref, 2, 0), gather_sems, kind + 2, near_x),
                    remote(half(ref, 0, 0), half(ref, 2, 1), gather_sems, kind + 3, near_y),
                ],
                [
                    remote(quarter(ref, 1, 2), quarter(ref, 3, 1), gather_sems, kind + 4, near_x),
                    remote(quarter(ref, 1, 0), quarter(ref, 3, 0), gather_sems, kind + 5, near_y),
                ],
                [
                    remote(quarter(ref, 1, 3), quarter(ref, 3, 3), gather_sems, kind + 6, near_x),
                    remote(quarter(ref, 1, 1), quarter(ref, 3, 2), gather_sems, kind + 7, near_y),
                ],
            )

        row_sends = gather(rows, 0)
        grad_sends = gather(grads, 8)

        begin(load_grads)
        begin([keep_gated, load_hidden])
        barrier = pltpu.get_barrier_semaphore()
        for place in (near_x, near_y, far):
            pl.semaphore_signal(barrier, inc=1, device_id=place, device_id_type=MESH)
        pl.semaphore_wait(barrier, 3)
        begin(gated_sends)
        lax.fori_loop(0, slices * quarters, start_slice, 0)
        finish(load_grads)
        begin(grad_sends[1])
        finish([keep_gated, load_hidden])
        lax.fori_loop(0, slices * quarters, wait_slice, 0)
        finish(gated_sends)
        for j in range(width // wide_tile):
            at = slice(j * wide_tile, (j + 1) * wide_tile)
            middle_ref[:, at] = straight(gated_ref[...], w_in[:, at])
        begin(weights)

        def second_norm(i, carry, at):
            here = pl.ds(pl.multiple_of(at * HALF + i * 32, 32), 32)
            middle = hidden_ref[here, :].astype(jnp.float32) + live_ref[here, :1] * middle_ref[here, :]
            middle_ref[here, :] = middle
            rows[0, here, :] = row_norm(middle).astype(low)
            return carry

        for at in range(2):
            lax.fori_loop(0, HALF // 32, functools.partial(second_norm, at=at), 0)
            row_sends[0][at].start()
        begin(row_sends[1])
        store_middle = pltpu.make_async_copy(middle_ref, middle_out, done_sems.at[0])
        store_middle.start()

        def products(size, at, first, second, part_a, part_b, grad_act):
            act[:size, at] = (part_a * part_b).astype(low)
            parts[:size, first] = (grad_act * part_b).astype(low)
            parts[:size, second] = (grad_act * part_a).astype(low)

        def unit(arrived, arrived_grads, size, weights_wait):
            for which, (start, count) in enumerate(cuts):
                at, second = slice(start, start + count), slice(main + start, main + start + count)
                weights_wait(3 * which, 3 * which + 3)
                part_a = straight(arrived[...], w_in[:, at])
                part_b = straight(arrived[...], w_in[:, second])
                grad_act = across(arrived_grads[...], w_out[at, :])
                products(size, at, at, second, part_a, part_b, grad_act)
            weights_wait(6, 9)
            if tail:
                both = straight(arrived[...], w_in[:, 2 * main :])
                grad_act = across(arrived_grads[...], w_out[main:, :])
                products(
                    size,
                    slice(main, units),
                    slice(2 * main, 2 * main + tail),
                    slice(2 * main + tail, 2 * units),
                    both[:, :tail],
                    both[:, tail:],
                    grad_act,
                )

        def row_stores(arrived, arrived_grads, at):
            return [
                pltpu.make_async_copy(arrived, rows_out.at[at, :], done_sems.at[1]),
                pltpu.make_async_copy(arrived_grads, grads_out.at[at, :], done_sems.at[2]),
            ]

        def unit_stores(size, at):
            here = pl.ds(0, size)
            return [
                pltpu.make_async_copy(act.at[here], act_out.at[at, :], done_sems.at[3]),
                pltpu.make_async_copy(parts.at[here], parts_out.at[at, :], done_sems.at[4]),
            ]

        def sum_stores(piece, j):
            tile = pl.ds(j * wide_tile, wide_tile)
            return [
                pltpu.make_async_copy(
                    sums.at[at, :, tile],
                    (back_out, two_out)[at // 2].at[
                        pl.ds(pl.multiple_of(piece * PIECE + (at % 2) * HALF, HALF), HALF), tile
                    ],
                    sum_sems.at[j, at],
                )
                for at in range(4)
            ]

        def work(piece, carry):
            at = pl.ds(pl.multiple_of(piece * PIECE, PIECE), PIECE)
            arrived, arrived_grads = rows.at[piece], grads.at[piece]

            @pl.when(piece == 1)
            def _():
                finish(row_sends[0])
                for step in (2, 3):
                    begin(row_sends[step])
                    begin(grad_sends[step])

            @pl.when(piece == 2)
            def _():
                finish(row_sends[1])
                finish(grad_sends[1])

            stores = row_stores(arrived, arrived_grads, at)
            begin(stores)

            def weights_wait(start, stop):
                pl.when(piece == 0)(lambda: finish(weights[start:stop]))

            unit(arrived, arrived_grads, PIECE, weights_wait)
            more = unit_stores(PIECE, at)
            begin(more)
            for j in range(width // wide_tile):
                tile = slice(j * wide_tile, (j + 1) * wide_tile)

                @pl.when(piece > 0)
                def _(j=j):
                    finish(sum_stores(piece - 1, j))

                back = across(parts[...], w_in[tile, :])
                sums[0, :, tile] = back[:HALF].astype(low)
                sums[1, :, tile] = back[HALF:].astype(low)
                two = straight(act[...], w_out[:, tile])
                sums[2, :, tile] = two[:HALF].astype(low)
                sums[3, :, tile] = two[HALF:].astype(low)
                begin(sum_stores(piece, j))
            finish(stores)
            finish(more)
            return carry

        lax.fori_loop(0, pieces - 1, work, 0)
        for j in range(width // wide_tile):
            finish(sum_stores(pieces - 2, j))

        def last_stores(which):
            return [
                pltpu.make_async_copy(
                    sums.at[2 * total + which, pl.ds(part * SUB, SUB)],
                    (back_out, two_out)[total].at[
                        pl.ds(pl.multiple_of((pieces - 1) * PIECE + part * HALF + which * SUB, SUB), SUB)
                    ],
                    last_sems.at[which, 2 * total + part],
                )
                for total in range(2)
                for part in range(2)
            ]

        def last_work(which, carry):
            here = pl.ds(pl.multiple_of(which * HALF, HALF), HALF)
            at = pl.ds(pl.multiple_of((pieces - 1) * PIECE + which * HALF, HALF), HALF)
            arrived, arrived_grads = rows.at[pieces - 1, here], grads.at[pieces - 1, here]
            pl.when(which == 0)(lambda: finish(row_sends[2]))
            pl.when(which == 1)(lambda: finish(row_sends[3]))
            held[...] = straight(arrived[...], w_in[...])

            def columns_of(start, stop):
                first, second = slice(start, stop), slice(main + start, main + stop)
                if start == main:
                    first, second = slice(2 * main, 2 * main + tail), slice(2 * main + tail, 2 * units)
                return first, second

            ranges = ((0, main), (main, units)) if tail else ((0, main),)
            for start, stop in ranges:
                first, second = columns_of(start, stop)
                act[:HALF, start:stop] = (held[:, first] * held[:, second]).astype(low)
            for j in range(width // wide_tile):
                tile = slice(j * wide_tile, (j + 1) * wide_tile)
                sums[2 + which, :, tile] = straight(act[:HALF], w_out[:, tile]).astype(low)
            pl.when(which == 0)(lambda: finish(grad_sends[2]))
            pl.when(which == 1)(lambda: finish(grad_sends[3]))
            stores = row_stores(arrived, arrived_grads, at)
            begin(stores)
            for start, stop in ranges:
                first, second = columns_of(start, stop)
                grad_act = across(arrived_grads[...], w_out[start:stop, :])
                parts[:HALF, first] = (grad_act * held[:, second]).astype(low)
                parts[:HALF, second] = (grad_act * held[:, first]).astype(low)
            more = unit_stores(HALF, at)
            begin(more)
            for j in range(width // wide_tile):
                tile = slice(j * wide_tile, (j + 1) * wide_tile)
                sums[which, :, tile] = across(parts[:HALF], w_in[tile, :]).astype(low)
            begin(last_stores(which))
            finish(stores)
            finish(more)
            return carry

        lax.fori_loop(0, 2, last_work, 0)
        for which in range(2):
            finish(last_stores(which))
        store_middle.wait()

    return pl.pallas_call(
        body,
        in_specs=any_specs(7) + [pl.BlockSpec(memory_space=pltpu.VMEM)],
        out_specs=any_specs(7),
        out_shape=[
            jax.ShapeDtypeStruct((local_rows, width), jnp.float32),
            jax.ShapeDtypeStruct((group_rows, width), low),
            jax.ShapeDtypeStruct((group_rows, width), low),
            jax.ShapeDtypeStruct((group_rows, units), low),
            jax.ShapeDtypeStruct((group_rows, 2 * units), low),
            jax.ShapeDtypeStruct((group_rows, width), low),
            jax.ShapeDtypeStruct((group_rows, width), low),
        ],
        scratch_shapes=[
            pltpu.VMEM((local_rows, quarters * deep), low),
            pltpu.VMEM((local_rows, width), low),
            pltpu.VMEM((local_rows, width), jnp.float32),
            pltpu.VMEM((pieces, PIECE, width), low),
            pltpu.VMEM((pieces, PIECE, width), low),
            pltpu.VMEM((4, HALF, width), low),
            pltpu.VMEM((width, 2 * units), low),
            pltpu.VMEM((units, width), low),
            pltpu.VMEM((PIECE, units), low),
            pltpu.VMEM((PIECE, 2 * units), low),
            pltpu.VMEM((HALF, 2 * units), jnp.float32),
            pltpu.SemaphoreType.DMA((4,)),
            pltpu.SemaphoreType.DMA((slices * quarters,)),
            pltpu.SemaphoreType.DMA((9,)),
            pltpu.SemaphoreType.DMA((5,)),
            pltpu.SemaphoreType.DMA((width // wide_tile, 4)),
            pltpu.SemaphoreType.DMA((2, 4)),
            pltpu.SemaphoreType.DMA((6, 2)),
            pltpu.SemaphoreType.DMA((16, 2)),
        ],
        compiler_params=pltpu.CompilerParams(
            vmem_limit_bytes=VMEM, collective_id=3, has_side_effects=True
        ),
        cost_estimate=cost(12 * group_rows * width * units, 90e6),
        name="gated_unit",
    )(gated, whole_weight, hidden, grads_own, grads_first, ffn_in, ffn_out, live)


def mix_rows(hidden, cotangent, mix_weight, out_weight, seq_lengths, block_seq):
    local_rows, width = hidden.shape
    parts, _, columns = mix_weight.shape
    heads = columns // HS
    group_rows = NBLK * BLK
    pieces = group_rows // PIECE
    wide_size = lax.axis_size("wide")
    slice_rows = columns // wide_size
    low = jnp.bfloat16
    joined = 2
    halves_at = (pl.ds(0, HALF), pl.ds(HALF, HALF))

    def body(*refs):
        hidden_in, cot_in, mix_in, out_in, length_ref, owner_ref = refs[:6]
        rows_out, parts_out, gated_out, mixing_out, states_out, grads_out, first_out, whole_out = refs[6:14]
        live_ref, keep_ref = refs[14:16]
        hidden_ref, cot_ref, rows, weights, parts_ref, gated_ref, mixing_ref, states_ref = refs[16:24]
        load_sems, mix_sems, store_sems, parts_sems, gather_sems, slice_sems, line_sems, core_sems = refs[24:]
        wide, narrow, z, core, mate, near_x, near_y = neighbours()
        far = (wide, 3 - narrow)
        above, below = (wide + 2, narrow), (wide - 2, narrow)
        barrier = pltpu.get_barrier_semaphore()

        def greet(place):
            pl.semaphore_signal(barrier, inc=1, device_id=place, device_id_type=MESH)

        load_hidden = pltpu.make_async_copy(hidden_in, hidden_ref, load_sems.at[0])
        load_cot = pltpu.make_async_copy(cot_in, cot_ref, load_sems.at[1])
        mix_loads = [
            pltpu.make_async_copy(
                mix_in.at[c], weights.at[:, pl.ds(c * columns, columns)], mix_sems.at[c]
            )
            for c in range(parts)
        ]
        load_hidden.start()
        for place in (near_x, near_y, far, mate):
            greet(place)
        pl.when(z < 3)(lambda: greet(above))
        pl.when(z > 0)(lambda: greet(below))
        middle = (z == 1) | (z == 2)
        pl.when(middle)(lambda: pl.semaphore_wait(barrier, 6))
        pl.when(jnp.logical_not(middle))(lambda: pl.semaphore_wait(barrier, 5))

        def remote(src, dst, sems, kind, place):
            return pltpu.make_async_remote_copy(
                src_ref=src,
                dst_ref=dst,
                send_sem=sems.at[kind, 0],
                recv_sem=sems.at[kind, 1],
                device_id=place,
                device_id_type=MESH,
            )

        slice_at = out_in.at[pl.ds(pl.multiple_of(wide * slice_rows, slice_rows), slice_rows)]
        keep_slice = pltpu.make_async_copy(slice_at, whole_out.at[wide, narrow], load_sems.at[2])
        slice_sends = [
            remote(slice_at, whole_out.at[wide, narrow], slice_sems, at, place)
            for at, place in enumerate((far, near_x, near_y))
        ]

        def up(hop):
            return remote(
                whole_out.at[wide - 2 * (hop - 1)], whole_out.at[wide - 2 * (hop - 1)], line_sems, hop - 1, above
            )

        def down_line(hop):
            return remote(
                whole_out.at[wide + 2 * (hop - 1)], whole_out.at[wide + 2 * (hop - 1)], line_sems, 2 + hop, below
            )

        def to_mate(hop, sign):
            at = wide + sign * 2 * hop
            return remote(whole_out.at[at], whole_out.at[at], core_sems, 3 + sign * hop, mate)

        def send_hop(hop):
            pl.when((z < 3) & (z >= hop - 1))(lambda: up(hop).start())
            pl.when((z > 0) & (z + hop - 1 <= 3))(lambda: down_line(hop).start())

        def take_hop(hop):
            @pl.when(z >= hop)
            def _():
                arrived = whole_out.at[wide - 2 * hop]
                remote(arrived, arrived, line_sems, hop - 1, mate).wait_recv()
                to_mate(hop, -1).start()

            @pl.when(z + hop <= 3)
            def _():
                arrived = whole_out.at[wide + 2 * hop]
                remote(arrived, arrived, line_sems, 2 + hop, mate).wait_recv()
                to_mate(hop, 1).start()

        def end_hop(hop):
            pl.when((z < 3) & (z >= hop - 1))(lambda: up(hop).wait_send())
            pl.when((z > 0) & (z + hop - 1 <= 3))(lambda: down_line(hop).wait_send())
            pl.when(z >= hop)(lambda: to_mate(hop, -1).wait())
            pl.when(z + hop <= 3)(lambda: to_mate(hop, 1).wait())

        begin(slice_sends)
        keep_slice.start()

        def half(piece, at):
            return rows.at[piece, halves_at[at]]

        row_sends = (
            [remote(half(0, 0), half(1, 0), gather_sems, 0, near_x), remote(half(0, 1), half(1, 1), gather_sems, 1, near_y)],
            [remote(half(0, 1), half(2, 0), gather_sems, 2, near_x), remote(half(0, 0), half(2, 1), gather_sems, 3, near_y)],
            [remote(half(1, 1), half(3, 1), gather_sems, 4, near_x), remote(half(1, 0), half(3, 0), gather_sems, 5, near_y)],
        )
        grad_sends = [
            remote(cot_ref.at[halves_at[0]], first_out.at[halves_at[0]], gather_sems, 6, near_x),
            remote(cot_ref.at[halves_at[1]], first_out.at[halves_at[1]], gather_sems, 7, near_y),
        ]
        load_hidden.wait()
        begin(mix_loads)
        load_cot.start()

        def first_norm(i, carry):
            at = pl.ds(pl.multiple_of(i * 32, 32), 32)
            rows[0, at, :] = row_norm(hidden_ref[at, :].astype(jnp.float32)).astype(low)
            return carry

        for at in range(2):
            lax.fori_loop(at * HALF // 32, (at + 1) * HALF // 32, first_norm, 0)
            row_sends[0][at].start()
        begin(row_sends[1])

        def row_store(piece):
            at = pl.ds(piece * PIECE, PIECE)
            return pltpu.make_async_copy(rows.at[piece], rows_out.at[at, :], store_sems.at[piece])

        def part_stores(piece):
            at = pl.ds(piece * PIECE, PIECE)
            return [
                pltpu.make_async_copy(
                    parts_ref.at[at, pl.ds(c * columns, columns)], parts_out.at[c, at, :], parts_sems.at[piece, c]
                )
                for c in range(parts)
            ]

        def project(piece):
            row_store(piece).start()
            for c in range(0, parts, joined):
                if piece == 0:
                    finish(mix_loads[c : c + joined])
                at = slice(c * columns, (c + joined) * columns)
                result = straight(rows[piece], weights[:, at]).astype(low)
                parts_ref[piece * PIECE : (piece + 1) * PIECE, at] = result
            begin(part_stores(piece))

        def same_slot(block):
            return owner_ref[block] == owner_ref[0]

        first_count = sum(jnp.where(same_slot(block), 1, 0) for block in range(NBLK))

        def start_of(block):
            return jnp.where(same_slot(block), 0, first_count)

        for block in range(NBLK):
            entering = jnp.where(start_of(block) == block, 0.0, 1.0)
            keep_ref[block : block + 1, :] = jnp.full((1, HS), entering, jnp.float32)
        for at in range(local_rows // BLK):
            block = narrow * (local_rows // BLK) + at
            limit = jnp.where(same_slot(block), length_ref[0], length_ref[1])
            place = lax.broadcasted_iota(jnp.int32, (BLK, HS), 0) + (block - start_of(block)) * BLK
            live_ref[at * BLK : (at + 1) * BLK, :] = jnp.where(place < limit, 1.0, 0.0)
        project(0)
        load_cot.wait()

        def live_cot(i, carry):
            at = pl.ds(pl.multiple_of(i * 32, 32), 32)
            cot_ref[at, :] = (live_ref[at, :1] * cot_ref[at, :].astype(jnp.float32)).astype(low)
            return carry

        keep_slice.wait()
        finish(slice_sends)
        to_mate(0, 1).start()
        send_hop(1)
        lax.fori_loop(0, local_rows // 32, live_cot, 0)
        store_grads = pltpu.make_async_copy(cot_ref, grads_out, load_sems.at[3])
        store_grads.start()
        finish(row_sends[0])
        begin(row_sends[2])
        begin(grad_sends)
        project(1)
        take_hop(1)
        send_hop(2)
        finish(row_sends[1])
        project(2)
        take_hop(2)
        send_hop(3)
        finish(row_sends[2])
        project(3)

        def attend(head, carry):
            within, entry, leave, whole = block_decays(head_rate(heads * narrow + head))
            state = jnp.zeros((HS, HS), jnp.float32)

            def part(c, rows_at):
                at = pl.ds(pl.multiple_of(c * columns + head * HS, HS), HS)
                return parts_ref[rows_at, at]

            for block in range(NBLK):
                rows_at = pl.ds(pl.multiple_of(slot_of(block, narrow) * BLK, BLK), BLK)
                queries = jax.nn.silu(part(0, rows_at).astype(jnp.float32)).astype(low)
                keys = jax.nn.silu(part(1, rows_at).astype(jnp.float32)).astype(low)
                values = part(2, rows_at)
                gate = part(3, rows_at).astype(jnp.float32)
                state = keep_ref[block : block + 1, :] * state
                state_low = state.astype(low)
                states_ref[head, block] = state_low
                scores = (across(queries, keys) * within).astype(low)
                mixing = straight(scores, values) + entry * straight(queries, state_low)
                late_keys = (keys.astype(jnp.float32) * leave).astype(low)
                state = whole * state + down(late_keys, values)
                scale = lax.rsqrt(jnp.mean(mixing * mixing, axis=-1, keepdims=True) + head_floor)
                at = pl.ds(pl.multiple_of(head * HS, HS), HS)
                gated_ref[rows_at, at] = (mixing * scale * gate).astype(low)
                mixing_ref[rows_at, at] = mixing.astype(low)
            return carry

        lax.fori_loop(0, heads // 2, attend, 0)
        take_hop(3)
        lax.fori_loop(heads // 2, heads, attend, 0)
        stores = [
            pltpu.make_async_copy(gated_ref, gated_out.at[0], load_sems.at[4]),
            pltpu.make_async_copy(mixing_ref, mixing_out, load_sems.at[5]),
            pltpu.make_async_copy(states_ref, states_out, load_sems.at[6]),
        ]
        begin(stores)
        to_mate(0, 1).wait()
        for hop in range(1, 4):
            end_hop(hop)
        finish(grad_sends)
        store_grads.wait()
        for piece in range(pieces):
            row_store(piece).wait()
            finish(part_stores(piece))
        finish(stores)

    low_shape = functools.partial(jax.ShapeDtypeStruct, dtype=low)
    return pl.pallas_call(
        body,
        in_specs=any_specs(4) + [pl.BlockSpec(memory_space=pltpu.SMEM)] * 2,
        out_specs=any_specs(8) + [pl.BlockSpec(memory_space=pltpu.VMEM)] * 2,
        out_shape=[
            low_shape((group_rows, width)),
            low_shape((parts, group_rows, columns)),
            low_shape((1, group_rows, columns)),
            low_shape((group_rows, columns)),
            low_shape((heads, NBLK, HS, HS)),
            low_shape((local_rows, width)),
            low_shape((local_rows, width)),
            low_shape((wide_size, pieces, slice_rows, width)),
            jax.ShapeDtypeStruct((local_rows, HS), jnp.float32),
            jax.ShapeDtypeStruct((NBLK, HS), jnp.float32),
        ],
        scratch_shapes=[
            pltpu.VMEM((local_rows, width), low),
            pltpu.VMEM((local_rows, width), low),
            pltpu.VMEM((pieces, PIECE, width), low),
            pltpu.VMEM((width, parts * columns), low),
            pltpu.VMEM((group_rows, parts * columns), low),
            pltpu.VMEM((group_rows, columns), low),
            pltpu.VMEM((group_rows, columns), low),
            pltpu.VMEM((heads, NBLK, HS, HS), low),
            pltpu.SemaphoreType.DMA((7,)),
            pltpu.SemaphoreType.DMA((parts,)),
            pltpu.SemaphoreType.DMA((pieces,)),
            pltpu.SemaphoreType.DMA((pieces, parts)),
            pltpu.SemaphoreType.DMA((8, 2)),
            pltpu.SemaphoreType.DMA((3, 2)),
            pltpu.SemaphoreType.DMA((6, 2)),
            pltpu.SemaphoreType.DMA((7, 2)),
        ],
        compiler_params=pltpu.CompilerParams(
            vmem_limit_bytes=VMEM, collective_id=4, has_side_effects=True
        ),
        cost_estimate=cost(2 * group_rows * parts * width * columns, 50e6),
        name="mix_rows",
    )(hidden, cotangent, mix_weight, out_weight, seq_lengths, block_seq)


def widen(mix_low, out_low, in_low, wide_low, rows):
    parts, width, columns = mix_low.shape
    units = wide_low.shape[0]
    main = units // TILE * TILE
    tail = units - main
    steps = 2 * parts

    def body(mix_ref, out_ref, in_ref, wide_ref, one_ref, two_ref, mix_out, out_out, in_out, wide_out, one_out, two_out):
        one_out[...] = one_ref[...]
        two_out[...] = two_ref[...]
        mix_out[...] = mix_ref[...].astype(jnp.float32)
        out_out[...] = out_ref[...].astype(jnp.float32)
        wide_out[...] = wide_ref[...].astype(jnp.float32)
        for c in range(2):
            in_out[c, :, :main] = in_ref[:, c * main : (c + 1) * main].astype(jnp.float32)
            rest = slice(2 * main + c * tail, 2 * main + (c + 1) * tail)
            in_out[c, :, main:] = in_ref[:, rest].astype(jnp.float32)

    def rows_spec(array):
        return pl.BlockSpec((array.shape[0] // steps, array.shape[1]), lambda i: (i, 0))

    mix_spec = pl.BlockSpec((1, width // 2, columns), lambda i: (i // 2, i % 2, 0))
    shapes = (mix_low.shape, out_low.shape, (2, width, units), wide_low.shape)
    return pl.pallas_call(
        body,
        grid=(steps,),
        in_specs=[mix_spec] + [rows_spec(array) for array in (out_low, in_low, wide_low, *rows)],
        out_specs=[
            mix_spec,
            rows_spec(out_low),
            pl.BlockSpec((2, width // steps, units), lambda i: (0, i, 0)),
            rows_spec(wide_low),
            *(rows_spec(array) for array in rows),
        ],
        out_shape=[jax.ShapeDtypeStruct(shape, jnp.float32) for shape in shapes]
        + [jax.ShapeDtypeStruct(array.shape, array.dtype) for array in rows],
        compiler_params=pltpu.CompilerParams(vmem_limit_bytes=VMEM),
        cost_estimate=cost(1e8, 84e6),
        name="widen",
    )(mix_low, out_low, in_low, wide_low, *rows)


def block_decays(rate):
    row = lax.broadcasted_iota(jnp.int32, (BLK, BLK), 0)
    column = lax.broadcasted_iota(jnp.int32, (BLK, BLK), 1)
    distance = (row - column).astype(jnp.float32)
    within = jnp.where(row >= column, jnp.exp(-rate * jnp.maximum(distance, 0.0)), 0.0)
    place = lax.broadcasted_iota(jnp.int32, (BLK, 1), 0).astype(jnp.float32)
    entry = jnp.exp(-rate * (place + 1.0))
    leave = jnp.exp(-rate * (BLK - 1.0 - place))
    whole = jnp.exp(-BLK * rate * jnp.ones((1, HS), jnp.float32))
    return within, entry, leave, whole


def norm_back(values, grad):
    scale = lax.rsqrt(jnp.mean(values * values, axis=-1, keepdims=True) + epsilon)
    unit = values * scale
    return scale * (grad - unit * jnp.mean(grad * unit, axis=-1, keepdims=True))


def square_device(
    hidden, mix_weight, out_weight, ffn_in_weight, ffn_out_weight, seq_lengths, block_seq, cotangent
):
    width = hidden.shape[1]
    units = ffn_out_weight.shape[0]
    normed_all, parts, gated, mixing, states, grads_own, grads_first, whole_weight, live, keep = mix_rows(
        hidden, cotangent, mix_weight, out_weight, seq_lengths, block_seq
    )
    middle, normed_two_all, grad_two_all, act, grad_parts, back_sums, two_sums = gated_unit(
        gated,
        whole_weight,
        hidden,
        live,
        grads_own,
        grads_first,
        ffn_in_weight,
        ffn_out_weight,
    )
    in_low, wide_low, out_low, mix_low, _, _, layer_out, input_grad, *_ = weight_grads(
        act,
        grad_two_all,
        normed_two_all,
        grad_parts,
        back_sums,
        two_sums,
        middle,
        cotangent,
        out_weight,
        mix_weight,
        parts,
        mixing,
        states,
        gated,
        normed_all,
        hidden,
        live,
        keep,
    )
    grad_mix, grad_out, grad_ffn_in, grad_ffn_out, layer_out, input_grad = widen(
        mix_low.reshape(mix_weight.shape),
        out_low.reshape(out_weight.shape),
        in_low.reshape(width, 2 * units),
        wide_low.reshape(units, width),
        (layer_out, input_grad),
    )
    return (layer_out, input_grad, grad_mix, grad_out, grad_ffn_in, grad_ffn_out)


def solution(mesh):
    square = mesh.shape["wide"] == 8 and mesh.shape["narrow"] == 4
    per_device = square_device if square else general_device
    in_specs = (
        P(("wide", "narrow"), None),
        P(None, None, "narrow"),
        P("narrow", None),
        P(None, None, "narrow"),
        P("narrow", None),
        P("wide"),
        P("wide"),
        P(("wide", "narrow"), None),
    )
    out_specs = (
        P(("wide", "narrow"), None),
        P(("wide", "narrow"), None),
        P(None, None, "narrow"),
        P("narrow", None),
        P(None, None, "narrow"),
        P("narrow", None),
    )
    return jax.shard_map(
        per_device, mesh=mesh, in_specs=in_specs, out_specs=out_specs, check_vma=False
    )
```

```python
import functools
import math

import jax
import jax.numpy as jnp
from jax import lax
from jax.experimental import pallas as pl
from jax.experimental.pallas import tpu as pltpu
from jax.sharding import PartitionSpec as P

HEADS = 16
HS = 128
BLK = 256
NBLK = 8


epsilon = 1e-06
head_floor = 1.0
highest = lax.Precision.HIGHEST


def row_norm(values):
    return values * lax.rsqrt(jnp.mean(values * values, axis=-1, keepdims=True) + epsilon)


def head_norm(values):
    return values * lax.rsqrt(jnp.mean(values * values, axis=-1, keepdims=True) + head_floor)


def silu_slope(values):
    sigmoid_part = jax.nn.sigmoid(values)
    return sigmoid_part * (1.0 + values * (1.0 - sigmoid_part))


def decay_tables(decay_rates):
    positions = jnp.arange(BLK, dtype=jnp.float32)
    distance = positions[:, None] - positions[None, :]
    causal = distance >= 0
    clipped = jnp.where(causal, distance, 0.0)
    within = jnp.where(causal[None], jnp.exp(-decay_rates[:, None, None] * clipped[None]), 0.0)
    entry_decay = jnp.exp(-(positions[:, None] + 1.0) * decay_rates[None, :])
    exit_decay = jnp.exp(-(BLK - 1.0 - positions[:, None]) * decay_rates[None, :])
    block_decay = jnp.exp(-BLK * decay_rates)
    return (within, entry_decay, exit_decay, block_decay)


def group_masks(lengths, owners):
    seq_slot = owners - owners[0]
    first_count = jnp.sum((seq_slot == 0).astype(jnp.int32))
    block_ids = jnp.arange(NBLK, dtype=jnp.int32)
    start_block = jnp.where(seq_slot == 0, jnp.int32(0), first_count)
    seq_limit = jnp.where(seq_slot == 0, lengths[0], lengths[1])
    offsets = (block_ids - start_block)[:, None] * BLK + jnp.arange(BLK, dtype=jnp.int32)[None, :]
    valid_rows = (offsets < seq_limit[:, None]).reshape(-1)
    fresh_block = block_ids == start_block
    return (valid_rows, fresh_block)


def forward_block(tables, kv_state, block_in):
    within, entry_decay, exit_decay, block_decay = tables
    queries, keys_in, values, fresh_block = block_in
    kv_state = jnp.where(fresh_block, 0.0, kv_state)
    scores = jnp.einsum("ihs,jhs->hij", queries, keys_in, preferred_element_type=jnp.float32)
    weights = (scores * within).astype(jnp.bfloat16)
    inner_part = jnp.einsum("hij,jhs->ihs", weights, values, preferred_element_type=jnp.float32)
    carried = jnp.einsum(
        "ihs,hst->iht",
        queries.astype(jnp.float32) * entry_decay[:, :, None],
        kv_state,
        precision=highest,
    )
    update = jnp.einsum(
        "ihs,iht->hst",
        keys_in.astype(jnp.float32) * exit_decay[:, :, None],
        values.astype(jnp.float32),
        precision=highest,
    )
    return (block_decay[:, None, None] * kv_state + update, (inner_part + carried, kv_state))


def backward_block(tables, later_grad, block_in):
    within, entry_decay, exit_decay, block_decay = tables
    queries, keys_in, values, grad_mix, kv_state, fresh_block = block_in
    scores = jnp.einsum("ihs,jhs->hij", queries, keys_in, preferred_element_type=jnp.float32)
    weights = (scores * within).astype(jnp.bfloat16)
    grad_values = jnp.einsum("hij,ihs->jhs", weights, grad_mix, preferred_element_type=jnp.float32)
    grad_weights = jnp.einsum("ihs,jhs->hij", grad_mix, values, preferred_element_type=jnp.float32)
    grad_scores = (grad_weights * within).astype(jnp.bfloat16)
    grad_queries = jnp.einsum(
        "hij,jhs->ihs", grad_scores, keys_in, preferred_element_type=jnp.float32
    )
    grad_keys = jnp.einsum("hij,ihs->jhs", grad_scores, queries, preferred_element_type=jnp.float32)
    grad_float = grad_mix.astype(jnp.float32)
    values_float = values.astype(jnp.float32)
    queries_float = queries.astype(jnp.float32)
    keys_float = keys_in.astype(jnp.float32)
    grad_queries = grad_queries + entry_decay[:, :, None] * jnp.einsum(
        "iht,hst->ihs", grad_float, kv_state, precision=highest
    )
    grad_keys = grad_keys + exit_decay[:, :, None] * jnp.einsum(
        "iht,hst->ihs", values_float, later_grad, precision=highest
    )
    grad_values = grad_values + jnp.einsum(
        "ihs,hst->iht", keys_float * exit_decay[:, :, None], later_grad, precision=highest
    )
    grad_state = jnp.einsum(
        "ihs,iht->hst", queries_float * entry_decay[:, :, None], grad_float, precision=highest
    )
    grad_state = grad_state + block_decay[:, None, None] * later_grad
    grad_state = jnp.where(fresh_block, 0.0, grad_state)
    return (grad_state, (grad_queries, grad_keys, grad_values))


def general_device(
    hidden, mix_weight, out_weight, ffn_in_weight, ffn_out_weight, seq_lengths, block_seq, cotangent
):
    local_rows = hidden.shape[0]
    group_rows = NBLK * BLK
    head_width = mix_weight.shape[2]
    head_count = head_width // HS
    narrow_index = lax.axis_index("narrow")
    valid_all, fresh_block = group_masks(seq_lengths, block_seq)
    valid_rows = lax.dynamic_slice_in_dim(
        valid_all.astype(jnp.float32), narrow_index * local_rows, local_rows
    )[:, None]
    head_ids = narrow_index * head_count + jnp.arange(head_count, dtype=jnp.int32)
    decay_rates = 2.0 ** (-8.0 * (head_ids.astype(jnp.float32) + 1.0) / HEADS)
    tables = decay_tables(decay_rates)

    def split_blocks(flat_rows):
        return flat_rows.reshape(NBLK, BLK, head_count, HS)

    inputs = hidden.astype(jnp.float32)
    normed_low = row_norm(inputs).astype(jnp.bfloat16)
    gathered = lax.all_gather(normed_low, "narrow", axis=0, tiled=True)
    projected = jnp.einsum("rd,cde->cre", gathered, mix_weight, preferred_element_type=jnp.float32)
    queries = jax.nn.silu(projected[0]).astype(jnp.bfloat16)
    keys_in = jax.nn.silu(projected[1]).astype(jnp.bfloat16)
    values = projected[2].astype(jnp.bfloat16)
    gate_part = projected[3]
    zero_state = jnp.zeros((head_count, HS, HS), jnp.float32)
    final_state, (mixing, kept_states) = lax.scan(
        lambda state_in, block_in: forward_block(tables, state_in, block_in),
        zero_state,
        (split_blocks(queries), split_blocks(keys_in), split_blocks(values), fresh_block),
    )
    mixing = mixing.reshape(group_rows, head_count, HS)
    headed = head_norm(mixing).reshape(group_rows, head_width)
    gated_low = (headed * gate_part).astype(jnp.bfloat16)
    branch = lax.psum_scatter(
        jnp.dot(gated_low, out_weight, preferred_element_type=jnp.float32).astype(jnp.bfloat16),
        "narrow",
        scatter_dimension=0,
        tiled=True,
    ).astype(jnp.float32)
    middle = inputs + valid_rows * branch
    normed_two_low = row_norm(middle).astype(jnp.bfloat16)
    gathered_two = lax.all_gather(normed_two_low, "narrow", axis=0, tiled=True)
    both_parts = jnp.einsum(
        "rd,cdf->crf", gathered_two, ffn_in_weight, preferred_element_type=jnp.float32
    )
    hidden_low = (both_parts[0] * both_parts[1]).astype(jnp.bfloat16)
    branch_two = lax.psum_scatter(
        jnp.dot(hidden_low, ffn_out_weight, preferred_element_type=jnp.float32).astype(
            jnp.bfloat16
        ),
        "narrow",
        scatter_dimension=0,
        tiled=True,
    ).astype(jnp.float32)
    layer_out = (middle + valid_rows * branch_two).astype(jnp.bfloat16)
    grad_rows = cotangent.astype(jnp.float32)
    ffn_grad_all = lax.all_gather(
        (valid_rows * grad_rows).astype(jnp.bfloat16), "narrow", axis=0, tiled=True
    )
    grad_ffn_out = jnp.einsum(
        "rf,rd->fd", hidden_low, ffn_grad_all, preferred_element_type=jnp.float32
    )
    grad_hidden = jnp.einsum(
        "rd,fd->rf", ffn_grad_all, ffn_out_weight, preferred_element_type=jnp.float32
    )
    grad_parts = jnp.stack([grad_hidden * both_parts[1], grad_hidden * both_parts[0]]).astype(
        jnp.bfloat16
    )
    grad_ffn_in = jnp.einsum(
        "rd,crf->cdf", gathered_two, grad_parts, preferred_element_type=jnp.float32
    )
    grad_slice = grad_parts
    grad_normed_two = lax.psum_scatter(
        jnp.einsum(
            "crf,cdf->rd", grad_slice, ffn_in_weight, preferred_element_type=jnp.float32
        ).astype(jnp.bfloat16),
        "narrow",
        scatter_dimension=0,
        tiled=True,
    ).astype(jnp.float32)
    norm_value, norm_pull = jax.vjp(row_norm, middle)
    grad_middle = grad_rows + norm_pull(grad_normed_two)[0]
    attn_grad_all = lax.all_gather(
        (valid_rows * grad_middle).astype(jnp.bfloat16), "narrow", axis=0, tiled=True
    )
    grad_out_weight = jnp.einsum(
        "re,rd->ed", gated_low, attn_grad_all, preferred_element_type=jnp.float32
    )
    grad_gated = jnp.einsum(
        "rd,ed->re", attn_grad_all, out_weight, preferred_element_type=jnp.float32
    )
    grad_gated = lax.optimization_barrier(grad_gated.astype(jnp.bfloat16)).astype(jnp.float32)
    grad_gate = grad_gated * headed
    grad_headed = (grad_gated * gate_part).reshape(group_rows, head_count, HS)
    head_value, head_pull = jax.vjp(head_norm, mixing)
    grad_mixing = head_pull(grad_headed)[0].astype(jnp.bfloat16)
    first_grad, (grad_queries, grad_keys, grad_values) = lax.scan(
        lambda later_grad, block_in: backward_block(tables, later_grad, block_in),
        zero_state,
        (
            split_blocks(queries),
            split_blocks(keys_in),
            split_blocks(values),
            split_blocks(grad_mixing),
            kept_states,
            fresh_block,
        ),
        reverse=True,
    )
    grad_projected = jnp.stack(
        [
            grad_queries.reshape(group_rows, head_width) * silu_slope(projected[0]),
            grad_keys.reshape(group_rows, head_width) * silu_slope(projected[1]),
            grad_values.reshape(group_rows, head_width),
            grad_gate,
        ]
    ).astype(jnp.bfloat16)
    grad_mix = jnp.einsum(
        "rd,cre->cde", gathered, grad_projected, preferred_element_type=jnp.float32
    )
    grad_slice = grad_projected
    grad_normed = lax.psum_scatter(
        jnp.einsum(
            "cre,cde->rd", grad_slice, mix_weight, preferred_element_type=jnp.float32
        ).astype(jnp.bfloat16),
        "narrow",
        scatter_dimension=0,
        tiled=True,
    ).astype(jnp.float32)
    first_value, first_pull = jax.vjp(row_norm, inputs)
    input_grad = (grad_middle + first_pull(grad_normed)[0]).astype(jnp.bfloat16)
    grad_mix, grad_out_weight, grad_ffn_in, grad_ffn_out = (
        lax.psum(grad_mix.astype(jnp.bfloat16), "wide").astype(jnp.float32),
        lax.psum(grad_out_weight.astype(jnp.bfloat16), "wide").astype(jnp.float32),
        lax.psum(grad_ffn_in.astype(jnp.bfloat16), "wide").astype(jnp.float32),
        lax.psum(grad_ffn_out.astype(jnp.bfloat16), "wide").astype(jnp.float32),
    )
    return (layer_out, input_grad, grad_mix, grad_out_weight, grad_ffn_in, grad_ffn_out)


HALF = BLK
PIECE = 2 * BLK
VMEM = 60 * 1024 * 1024


def add_low(*terms):
    return sum(term.astype(jnp.float32) for term in terms).astype(jnp.bfloat16)


def add_rows(*terms):
    return sum(term.astype(jnp.float32) for term in terms)


def across(left, right):
    return lax.dot_general(left, right, (((1,), (1,)), ((), ())), preferred_element_type=jnp.float32)


def down(left, right):
    return lax.dot_general(left, right, (((0,), (0,)), ((), ())), preferred_element_type=jnp.float32)


def straight(left, right):
    return jnp.dot(left, right, preferred_element_type=jnp.float32)


def any_specs(count):
    return [pl.BlockSpec(memory_space=pl.ANY)] * count


def cost(flops, bytes_accessed):
    return pl.CostEstimate(flops=int(flops), bytes_accessed=int(bytes_accessed), transcendentals=0)


MESH = pl.DeviceIdType.MESH
SLOTS = 12
STAGES = 11
SUB = 128
TILE = 256


def begin(copies):
    for copy in copies:
        copy.start()


def finish(copies):
    for copy in copies:
        copy.wait()


def neighbours():
    wide, narrow = lax.axis_index("wide"), lax.axis_index("narrow")
    z, core = wide // 2, wide % 2
    mate = (wide + 1 - 2 * core, narrow)
    near_x = (wide, narrow + 1 - 2 * (narrow % 2))
    near_y = (wide, (narrow + 2) % 4)
    return wide, narrow, z, core, mate, near_x, near_y


def slot_of(block, narrow):
    off_x = (block // 2 % 2 + narrow % 2) % 2
    off_y = (block // 4 + narrow // 2) % 2
    if block % 2:
        return 1 + 3 * off_x + 2 * off_y + off_x * off_y
    return 2 * off_x + 5 * off_y - off_x * off_y


def head_rate(head):
    return jnp.exp(jnp.full((1, 1), -8.0 / HEADS * math.log(2.0), jnp.float32) * (head.astype(jnp.float32) + 1.0))


def line_scratch():
    low = jnp.bfloat16
    pair = pltpu.VMEM((SLOTS, 2, SUB, TILE), low)
    return [
        pltpu.VMEM((SLOTS, 4, SUB, TILE), low),
        pair,
        pair,
        pair,
        pltpu.VMEM((SLOTS, SUB, TILE), low),
        pair,
        pair,
        pltpu.SemaphoreType.DMA((14, SLOTS)),
        pltpu.SemaphoreType.DMA((4, SLOTS)),
    ]


def enter(neighbour_places):
    wide, narrow, z, core, mate, near_x, near_y = neighbour_places
    barrier = pltpu.get_barrier_semaphore()

    def greet(place):
        pl.semaphore_signal(barrier, inc=1, device_id=place, device_id_type=MESH)

    for place in (mate, near_x, near_y):
        greet(place)
    middle = (z == 1) | (z == 2)

    @pl.when(middle)
    def _():
        greet((2 * (3 - z) + core, narrow))
        greet((6 * (z - 1) + core, narrow))
        pl.semaphore_wait(barrier, 5)

    @pl.when(jnp.logical_not(middle))
    def _():
        greet((2 * (1 + z // 3) + core, narrow))
        pl.semaphore_wait(barrier, 4)


def line_sum(scratch, places, count, product, targets):
    own, met, both, ended, crossed, full, other, sems, out_sems = scratch
    wide, narrow, z, core, mate, _, _ = places
    region = z // 2
    middle = (z == 1) | (z == 2)
    end = jnp.logical_not(middle)
    inward = (2 * (1 + z // 3) + core, narrow)
    across_line = (2 * (3 - z) + core, narrow)
    outward = (6 * (z - 1) + core, narrow)

    def remote(src, dst, kind, slot, place):
        return pltpu.make_async_remote_copy(
            src_ref=src,
            dst_ref=dst,
            send_sem=sems.at[2 * kind, slot],
            recv_sem=sems.at[2 * kind + 1, slot],
            device_id=place,
            device_id_type=MESH,
        )

    def core_one(s):
        return remote(own.at[s, pl.ds(2 * (1 - core), 2)], met.at[s], 0, s, mate)

    def line_one(s):
        return remote(both.at[s], ended.at[s], 1, s, inward)

    def cross_one(s):
        return remote(both.at[s, 1 - region], crossed.at[s], 2, s, across_line)

    def cross_two(s):
        return remote(full.at[s, region], full.at[s, region], 3, s, across_line)

    def out_one(s):
        return remote(full.at[s, region], full.at[s, region], 4, s, outward)

    def out_two(s):
        return remote(full.at[s, 1 - region], full.at[s, 1 - region], 5, s, outward)

    def core_two(s):
        return remote(full.at[s], other.at[s], 6, s, mate)

    def landing(ref, kind, slot):
        return remote(ref, ref, kind, slot, mate)

    def add(left, right):
        return (left.astype(jnp.float32) + right.astype(jnp.float32)).astype(jnp.bfloat16)

    def deliveries(k, s):
        for t in range(2):
            for which, (src, part) in enumerate(
                ((full.at[s, t], 2 * core + t), (other.at[s, t], 2 * (1 - core) + t))
            ):
                for condition, ref in targets(k, part):
                    yield condition, pltpu.make_async_copy(src, ref, out_sems.at[2 * t + which, s])

    def start(k, s):
        product(k, own.at[s])
        core_one(s).start()

    def cores(k, s):
        core_one(s).wait_recv()
        both[s] = add(own[s, pl.ds(2 * core, 2)], met[s])
        pl.when(end)(lambda: line_one(s).start())

    def ends(k, s):
        @pl.when(middle)
        def _():
            landing(ended.at[s], 1, s).wait_recv()
            both[s] = add(both[s], ended[s])
            cross_one(s).start()

    def centre(k, s):
        @pl.when(middle)
        def _():
            cross_one(s).wait_recv()
            full[s, region] = add(both[s, region], crossed[s])
            cross_two(s).start()
            out_one(s).start()

    def pass_on(k, s):
        @pl.when(middle)
        def _():
            cross_two(s).wait_recv()
            out_two(s).start()

    def back(k, s):
        @pl.when(end)
        def _():
            landing(full.at[s, region], 4, s).wait_recv()
            landing(full.at[s, 1 - region], 5, s).wait_recv()

        core_two(s).start()

    def deliver(k, s):
        core_two(s).wait_recv()
        for condition, copy in deliveries(k, s):
            pl.when(condition)(copy.start)

    def clear(k, s):
        core_one(s).wait_send()
        core_two(s).wait_send()

        @pl.when(end)
        def _():
            line_one(s).wait_send()

        @pl.when(middle)
        def _():
            for copy in (cross_one(s), cross_two(s), out_one(s), out_two(s)):
                copy.wait_send()

        for t in range(2):
            for which, src in enumerate((full, other)):
                ref = targets(k, 0)[0][1]
                pltpu.make_async_copy(src.at[s, t], ref, out_sems.at[2 * t + which, s]).wait()

    stages = (
        (11, clear),
        (10, deliver),
        (9, back),
        (7, pass_on),
        (5, centre),
        (3, ends),
        (1, cores),
        (0, start),
    )

    def step(i, carry):
        for delay, work in stages:
            k = i - delay

            @pl.when((k >= 0) & (k < count))
            def _(work=work, k=k):
                work(k, lax.rem(k + SLOTS, SLOTS))

        return carry

    return step


def square_scratch(uses):
    block = pltpu.VMEM((2, BLK, HEADS * HS), jnp.bfloat16)
    return [block, block, pltpu.SemaphoreType.DMA((uses, 6, 2)), pltpu.SemaphoreType.DMA((uses, 2))]


def square_sum(scratch, places, parts, landed, use, side=None):
    met, mid, sems, load_sems = scratch
    top_x, low_y, low_x, top_y, top_d, low_d = parts
    near_x, near_y = places[5:]

    def remote(src, dst, kind, place):
        return pltpu.make_async_remote_copy(
            src_ref=src,
            dst_ref=dst,
            send_sem=sems.at[use, kind, 0],
            recv_sem=sems.at[use, kind, 1],
            device_id=place,
            device_id_type=MESH,
        )

    first = [remote(top_d, met.at[0], 0, near_x), remote(low_d, met.at[1], 1, near_y)]
    direct = [remote(top_x, landed[0], 2, near_x), remote(low_y, landed[1], 3, near_y)]
    second = [remote(mid.at[0], landed[2], 4, near_y), remote(mid.at[1], landed[3], 5, near_x)]
    loads = []
    if top_y is not None:
        loads = [
            pltpu.make_async_copy(top_y, mid.at[0], load_sems.at[use, 0]),
            pltpu.make_async_copy(low_x, mid.at[1], load_sems.at[use, 1]),
        ]

    def open_sum():
        begin(first)
        begin(direct)
        begin(loads)

    def join_sum():
        finish(loads)
        for at in range(2):
            first[at].wait()

            def tile(i, carry, at=at):
                rows = pl.ds(pl.multiple_of(i * 64, 64), 64)
                mine = mid[at, rows, :] if side is None else side[at][rows, :]
                mid[at, rows, :] = add_low(mine, met[at, rows, :])
                return carry

            lax.fori_loop(0, BLK // 64, tile, 0)
        begin(second)

    def close_sum():
        finish(direct)
        finish(second)

    return open_sum, join_sum, close_sum


def weight_grads(
    act,
    grad_two_all,
    normed_two_all,
    grad_parts,
    back_sums,
    two_sums,
    middle,
    cotangent,
    out_weight,
    mix_weight,
    parts_all,
    mixing_all,
    states_all,
    gated,
    normed_all,
    hidden,
    live,
    keep,
):
    rows, units = act.shape
    width = grad_two_all.shape[1]
    local_rows = middle.shape[0]
    parts, _, columns = parts_all.shape
    heads = columns // HS
    low = jnp.bfloat16
    in_columns = grad_parts.shape[1] // TILE
    in_rows = width // PIECE
    out_blocks = units // SUB
    halves = width // 1024
    first_out = in_rows * in_columns
    first_branch = first_out + halves * out_blocks
    first_mix = first_branch + width // TILE
    per_row = columns // TILE
    per_part = in_rows * per_row
    count = first_mix + parts * per_part

    def body(*refs):
        act_in, two_in, normed_two_in, parts_in, back_in, two_sums_in = refs[:6]
        middle_in, cot_in, weight_in, mix_in = refs[6:10]
        all_in, mixing_in, states_in, gated_in, normed_in, hidden_in, live_ref, keep_ref = refs[10:18]
        in_grad, out_grad, branch_grad, mix_grad, branch_out, middle_out, layer_out, input_out = refs[18:26]
        last_landed, two_landed = refs[26:30], refs[30:34]
        shared, wide_ref, act_ref, landed, stage_ref, mid_ref, grad_ref, branch = refs[34:42]
        near, gated_grad, states_ref = refs[42:45]
        normed_sems, parts_sems, load_sems, stage_sems, gather_sems, back_sems, head_sems, mix_sems = refs[45:53]
        tile_sems, last_sems = refs[53:55]
        line, square = refs[55:64], refs[64:68]
        places = neighbours()
        narrow, near_x, near_y = places[1], places[5], places[6]

        def block(at):
            return pl.ds(at * BLK, BLK)

        def cols(at, size):
            return pl.ds(pl.multiple_of(at, 128), size)

        def load_normed_two(at):
            here = cols(at * PIECE, PIECE)
            return pltpu.make_async_copy(normed_two_in.at[:, here], shared.at[:, here], normed_sems.at[at])

        def load_parts(at):
            here = cols(at * TILE, TILE)
            return pltpu.make_async_copy(parts_in.at[:, here], wide_ref.at[:, here], parts_sems.at[at])

        def load_half(src, half, sem):
            here = pl.ds(half * 1024, 1024)
            return pltpu.make_async_copy(src.at[:, here], shared.at[:, here], load_sems.at[sem])

        load_act = pltpu.make_async_copy(act_in, act_ref, load_sems.at[0])
        load_two = [load_half(two_in, half, 1 + half) for half in range(halves)]
        load_normed = [load_half(normed_in, half, 3 + half) for half in range(halves)]
        load_gated = pltpu.make_async_copy(gated_in.at[0], act_ref.at[:, pl.ds(0, columns)], load_sems.at[5])

        def load_branch(at):
            slot = at % 2
            return pltpu.make_async_copy(
                branch_out.at[:, cols(at * TILE, TILE)],
                act_ref.at[:, cols(columns + slot * TILE, TILE)],
                tile_sems.at[slot],
            )

        def product(k, own):
            def split_rows(result):
                for part in range(4):
                    own[part] = result[part * SUB : (part + 1) * SUB]

            @pl.when(k < first_out)
            def _():
                row, column = k // in_columns, k % in_columns

                @pl.when(column == 0)
                def _():
                    load_normed_two(row).wait()

                @pl.when(row == 0)
                def _():
                    load_parts(column).wait()

                here, there = cols(row * PIECE, PIECE), cols(column * TILE, TILE)
                split_rows(down(shared[:, here], wide_ref[:, there]).astype(low))

                @pl.when(k == first_out - in_columns)
                def _():
                    load_two[0].start()

            @pl.when(k == first_out)
            def _():
                begin(load_two[1:])
                load_act.wait()
                load_two[0].wait()

            @pl.when(k == first_out + out_blocks)
            def _():
                finish(load_two[1:])
                load_normed[0].start()

            @pl.when((k >= first_out) & (k < first_branch))
            def _():
                at = k - first_out
                here = cols((at % out_blocks) * SUB, SUB)
                there = cols((at // out_blocks) * 1024, 1024)
                result = down(act_ref[:, here], shared[:, there]).astype(low)
                for part in range(4):
                    own[part] = result[:, part * TILE : (part + 1) * TILE]

            pl.when(k == first_branch - out_blocks + columns // SUB)(lambda: load_gated.start())
            pl.when(k == first_branch - out_blocks + (columns + TILE) // SUB)(lambda: load_branch(0).start())

            @pl.when(k == first_branch)
            def _():
                begin(load_normed[1:])
                load_gated.wait()

            @pl.when((k >= first_branch) & (k < first_mix))
            def _():
                at = k - first_branch
                load_branch(at).wait()
                pl.when(k + 1 < first_mix)(lambda: load_branch(at + 1).start())
                there = cols(columns + (at % 2) * TILE, TILE)
                split_rows(down(act_ref[:, :columns], act_ref[:, there]).astype(low))

            @pl.when(k == first_mix)
            def _():
                finish(load_normed)

            @pl.when(k >= first_mix)
            def _():
                at = k - first_mix
                here = cols(((at // per_row) % in_rows) * PIECE, PIECE)
                there = cols((at // per_part) * columns + (at % per_row) * TILE, TILE)
                split_rows(down(shared[:, here], wide_ref[:, there]).astype(low))

        def targets(k, part):
            one = jnp.minimum(k, first_out - 1)
            two = jnp.clip(k - first_out, 0, first_branch - first_out - 1)
            three = jnp.clip(k - first_branch, 0, first_mix - first_branch - 1)
            four = jnp.maximum(k - first_mix, 0)
            return [
                (
                    k < first_out,
                    in_grad.at[(one // in_columns) * 4 + part, :, cols((one % in_columns) * TILE, TILE)],
                ),
                (
                    (k >= first_out) & (k < first_branch),
                    out_grad.at[two % out_blocks, :, cols((two // out_blocks) * 1024 + part * TILE, TILE)],
                ),
                (
                    (k >= first_branch) & (k < first_mix),
                    branch_grad.at[part, :, cols(three * TILE, TILE)],
                ),
                (
                    k >= first_mix,
                    mix_grad.at[(four // per_row) * 4 + part, :, cols((four % per_row) * TILE, TILE)],
                ),
            ]

        step = line_sum(line, places, count, product, targets)
        now = [0]

        def run(steps):
            lax.fori_loop(now[0], now[0] + steps, step, 0)
            now[0] += steps

        open_sum, join_sum, close_sum = square_sum(
            square,
            places,
            [back_in.at[block(at)] for at in range(2, 8)],
            [landed.at[at] for at in range(4)],
            0,
        )
        load_normed_two(0).start()
        load_parts(0).start()
        enter(places)
        open_sum()
        for at in range(1, in_columns):
            load_parts(at).start()
        for at in range(1, in_rows):
            load_normed_two(at).start()
        load_act.start()

        def spread(src, slot, kind, place):
            return pltpu.make_async_remote_copy(
                src_ref=src,
                dst_ref=branch_out.at[block(slot)],
                send_sem=gather_sems.at[kind, 0],
                recv_sem=gather_sems.at[kind, 1],
                device_id=place,
                device_id_type=MESH,
            )

        def stage(half):
            return [
                pltpu.make_async_copy(back_in.at[block(half)], stage_ref.at[0], stage_sems.at[0]),
                pltpu.make_async_copy(cot_in.at[block(half)], stage_ref.at[1], stage_sems.at[1]),
                pltpu.make_async_copy(middle_in.at[block(half)], mid_ref, stage_sems.at[2]),
            ]

        keep_branch = [
            pltpu.make_async_copy(branch.at[at], branch_out.at[block(at)], stage_sems.at[3 + at])
            for at in range(2)
        ]

        def rows_back(half):
            def tile(i, carry):
                at = pl.ds(pl.multiple_of(i * 32, 32), 32)
                grad = add_rows(stage_ref[0, at, :], landed[half, at, :], landed[2 + half, at, :])
                result = stage_ref[1, at, :].astype(jnp.float32) + norm_back(mid_ref[at, :], grad)
                grad_ref[at, :] = result
                live_at = pl.ds(pl.multiple_of(half * BLK + i * 32, 32), 32)
                branch[half, at, :] = (live_ref[live_at, :1] * result).astype(low)
                return carry

            lax.fori_loop(0, BLK // 32, tile, 0)
            copy = pltpu.make_async_copy(grad_ref, middle_out.at[block(half)], stage_sems.at[5])
            copy.start()
            return copy

        sends = [
            spread(branch.at[0], 2, 0, near_x),
            spread(branch.at[1], 3, 1, near_y),
            spread(branch.at[1], 4, 2, near_x),
            spread(branch.at[0], 5, 3, near_y),
        ]
        later = [
            spread(branch_out.at[block(3)], 7, 4, near_x),
            spread(branch_out.at[block(2)], 6, 5, near_y),
        ]
        weight_loads = [
            pltpu.make_async_copy(weight_in.at[block(at)], landed.at[at], back_sems.at[at])
            for at in range(columns // BLK)
        ]

        def row_loads(slot):
            return [
                pltpu.make_async_copy(branch_out.at[block(slot + at)], stage_ref.at[at], back_sems.at[2 + at])
                for at in range(2)
            ]

        def back_rows(slot, rows_ref):
            for at in range(2):
                for part in range(len(weight_loads)):
                    result = across(rows_ref[at], landed[part]).astype(low)
                    gated_grad[(slot + at) * BLK : (slot + at + 1) * BLK, part * BLK : (part + 1) * BLK] = result

        def head_loads(head):
            here = cols(head * HS, HS)
            loads = [
                pltpu.make_async_copy(
                    all_in.at[c, :, here],
                    wide_ref.at[:, pl.ds(parts * columns + c * HS, HS)],
                    head_sems.at[c],
                )
                for c in range(parts)
            ]
            loads.append(
                pltpu.make_async_copy(
                    mixing_in.at[:, here],
                    wide_ref.at[:, pl.ds(parts * columns + parts * HS, HS)],
                    head_sems.at[parts],
                )
            )
            loads.append(pltpu.make_async_copy(states_in.at[head], states_ref, head_sems.at[parts + 1]))
            return loads

        open_two, join_two, close_two = square_sum(
            square, places, [two_sums_in.at[block(at)] for at in range(2, 8)], two_landed, 1
        )
        run(9)
        join_sum()
        begin(stage(0))
        run(16)
        close_sum()
        finish(stage(0))
        written = rows_back(0)
        sends[0].start()
        begin(stage(1))
        run(1)
        finish(stage(1))
        written.wait()
        written = rows_back(1)
        begin(sends[1:])
        begin(keep_branch)
        begin(weight_loads)
        run(2)
        finish(weight_loads)
        back_rows(0, branch)
        run(6)
        for copy in sends[:2]:
            copy.wait_recv()
        begin(later)
        begin(row_loads(2))
        run(1)
        finish(row_loads(2))
        back_rows(2, stage_ref)
        run(7)
        for copy in sends[2:]:
            copy.wait_recv()
        begin(row_loads(4))
        run(1)
        finish(row_loads(4))
        back_rows(4, stage_ref)
        run(8)
        begin(head_loads(0))
        for copy in later:
            copy.wait_recv()
        begin(row_loads(6))
        run(1)
        finish(row_loads(6))
        back_rows(6, stage_ref)
        written.wait()
        finish(keep_branch)
        for copy in sends + later:
            copy.wait_send()
        open_two()

        def load_mix(at):
            here = pl.ds(pl.multiple_of(at * BLK, BLK), BLK)
            slot = at % 4
            return [
                pltpu.make_async_copy(
                    mix_in.at[c, here, :], landed.at[slot, :, pl.ds(c * columns, columns)], mix_sems.at[slot, c]
                )
                for c in range(parts)
            ]

        for at in range(4):
            begin(load_mix(at))
        attend_from = now[0]
        breaks = (2, 5, NBLK - 1)

        def attend(head, carry):
            rate = head_rate(heads * narrow + head)
            within, entry, leave, whole = block_decays(rate)
            finish(head_loads(head))
            pl.when(head == heads - 1)(join_two)
            later_grad = jnp.zeros((HS, HS), jnp.float32)
            base = parts * columns
            for at in range(NBLK):
                block_at = NBLK - 1 - at
                here = pl.ds(pl.multiple_of(slot_of(block_at, narrow) * BLK, BLK), BLK)

                def load(c, here=here):
                    return wide_ref[here, base + c * HS : base + (c + 1) * HS]

                def store(c, value, here=here):
                    wide_ref[here, cols(c * columns + head * HS, HS)] = value.astype(low)

                raw_queries = load(0).astype(jnp.float32)
                raw_keys = load(1).astype(jnp.float32)
                queries, keys = jax.nn.silu(raw_queries).astype(low), jax.nn.silu(raw_keys).astype(low)
                values = load(2)
                gate = load(3).astype(jnp.float32)
                mixing = load(4).astype(jnp.float32)
                grad_rows = gated_grad[here, cols(head * HS, HS)].astype(jnp.float32)
                scale = lax.rsqrt(jnp.mean(mixing * mixing, axis=-1, keepdims=True) + head_floor)
                headed = mixing * scale
                store(3, grad_rows * headed)
                grad_headed = grad_rows * gate
                inner = jnp.mean(grad_headed * headed, axis=-1, keepdims=True)
                grad = (scale * (grad_headed - headed * inner)).astype(low)
                scores = (across(queries, keys) * within).astype(low)
                grad_scores = (across(grad, values) * within).astype(low)
                later_low = later_grad.astype(low)
                grad_queries = straight(grad_scores, keys) + entry * across(grad, states_ref[block_at])
                grad_keys = down(grad_scores, queries) + leave * across(values, later_low)
                grad_values = down(scores, grad) + leave * straight(keys, later_low)
                early_queries = (queries.astype(jnp.float32) * entry).astype(low)
                later_grad = keep_ref[block_at : block_at + 1, :1] * (
                    whole * later_grad + down(early_queries, grad)
                )
                store(0, grad_queries * silu_slope(raw_queries))
                store(1, grad_keys * silu_slope(raw_keys))
                store(2, grad_values)
                if at == NBLK - 1:
                    pl.when(head + 1 < heads)(lambda: begin(head_loads(head + 1)))
                if at in breaks:
                    step(attend_from + head * len(breaks) + breaks.index(at), 0)
            return carry

        lax.fori_loop(0, heads, attend, 0)
        now[0] += heads * len(breaks)

        sum_from = now[0]
        side = (mid_ref, grad_ref)

        def put(pair):
            def store(at, here, value):
                pair[at, :, here] = value

            return store

        def put_side(at, here, value):
            side[1 - at][:, here] = value.astype(jnp.float32)

        outs = ((3, put(branch)), (1, put(near)), (2, put_side), (0, put(stage_ref)))

        def sum_tile(at, carry):
            finish(load_mix(at))
            here = cols(at * BLK, BLK)
            for which, (piece, store) in enumerate(outs):
                acts = wide_ref[piece * PIECE : (piece + 1) * PIECE, : parts * columns]
                total = across(acts, landed[at % 4]).astype(low)
                store(0, here, total[:HALF])
                store(1, here, total[HALF:])
                if which == 3:
                    pl.when(at + 4 < width // BLK)(lambda: begin(load_mix(at + 4)))
                if which % 2:
                    step(sum_from + 2 * at + which // 2, 0)
            return carry

        lax.fori_loop(0, width // BLK, sum_tile, 0)
        now[0] += 2 * (width // BLK)
        open_last, join_last, close_last = square_sum(
            square,
            places,
            (near.at[0], near.at[1], None, None, branch.at[0], branch.at[1]),
            last_landed,
            2,
            side,
        )
        close_two()
        open_last()
        run(9)
        join_last()

        def block_loads(half, terms, floats):
            loads = [
                pltpu.make_async_copy(src, landed.at[at], last_sems.at[at]) for at, src in enumerate(terms)
            ]
            loads.append(pltpu.make_async_copy(floats.at[block(half)], mid_ref, last_sems.at[3]))
            return loads

        def block_store(half, out):
            return pltpu.make_async_copy(landed.at[3], out.at[block(half)], last_sems.at[4])

        def layer_loads(half):
            terms = (two_sums_in.at[block(half)], two_landed[half], two_landed[2 + half])
            return block_loads(half, terms, middle_in)

        def input_loads(half):
            terms = (last_landed[half], last_landed[2 + half], hidden_in.at[block(half)])
            return block_loads(half, terms, middle_out)

        def layer_tile(i, carry, half):
            at = pl.ds(pl.multiple_of(i * 32, 32), 32)
            live_at = pl.ds(pl.multiple_of(half * BLK + i * 32, 32), 32)
            branch_two = add_rows(landed[0, at, :], landed[1, at, :], landed[2, at, :])
            landed[3, at, :] = (mid_ref[at, :] + live_ref[live_at, :1] * branch_two).astype(low)
            return carry

        def input_tile(i, carry, half):
            at = pl.ds(pl.multiple_of(i * 32, 32), 32)
            grad_normed = add_rows(stage_ref[half, at, :], landed[0, at, :], landed[1, at, :])
            back = norm_back(landed[2, at, :].astype(jnp.float32), grad_normed)
            landed[3, at, :] = (mid_ref[at, :] + back).astype(low)
            return carry

        def rows_out(loads, tile, out):
            tiles = BLK // 32 // 4
            for half in range(2):
                begin(loads(half))
                run(1)
                finish(loads(half))
                if half:
                    block_store(0, out).wait()
                base = now[0]

                def part(at, carry, half=half, base=base):
                    for one in range(tiles):
                        tile(tiles * at + one, 0, half)
                    step(base + at, 0)
                    return carry

                lax.fori_loop(0, 4, part, 0)
                now[0] += 4
                block_store(half, out).start()

        rows_out(layer_loads, layer_tile, layer_out)
        run(first_mix + 31 - now[0])
        block_store(1, layer_out).wait()
        close_last()
        rows_out(input_loads, input_tile, input_out)
        run(count + STAGES - now[0])
        block_store(1, input_out).wait()

    def low_shape(*shape):
        return jax.ShapeDtypeStruct(shape, low)

    sem = pltpu.SemaphoreType.DMA
    return pl.pallas_call(
        body,
        in_specs=any_specs(16) + [pl.BlockSpec(memory_space=pltpu.VMEM)] * 2,
        out_specs=any_specs(16),
        out_shape=[
            low_shape(width // SUB, SUB, grad_parts.shape[1]),
            low_shape(out_blocks, SUB, width),
            low_shape(columns // SUB, SUB, width),
            low_shape(parts * width // SUB, SUB, columns),
            low_shape(rows, width),
            jax.ShapeDtypeStruct((local_rows, width), jnp.float32),
            low_shape(local_rows, width),
            low_shape(local_rows, width),
        ]
        + [low_shape(BLK, width)] * 8,
        scratch_shapes=[
            pltpu.VMEM((rows, width), low),
            pltpu.VMEM(grad_parts.shape, low),
            pltpu.VMEM(act.shape, low),
            pltpu.VMEM((4, BLK, width), low),
            pltpu.VMEM((2, BLK, width), low),
            pltpu.VMEM((BLK, width), jnp.float32),
            pltpu.VMEM((BLK, width), jnp.float32),
            pltpu.VMEM((2, BLK, width), low),
            pltpu.VMEM((2, BLK, width), low),
            pltpu.VMEM((rows, columns), low),
            pltpu.VMEM((NBLK, HS, HS), low),
            sem((in_rows,)),
            sem((in_columns,)),
            sem((6,)),
            sem((6,)),
            sem((6, 2)),
            sem((4,)),
            sem((parts + 2,)),
            sem((4, parts)),
            sem((2,)),
            sem((5,)),
        ]
        + line_scratch()
        + square_scratch(3),
        compiler_params=pltpu.CompilerParams(
            vmem_limit_bytes=VMEM, collective_id=1, has_side_effects=True
        ),
        cost_estimate=cost(2 * rows * width * (3 * units + 9 * columns), 120e6),
        name="weight_grads",
    )(
        act,
        grad_two_all,
        normed_two_all,
        grad_parts,
        back_sums,
        two_sums,
        middle,
        cotangent,
        out_weight,
        mix_weight,
        parts_all,
        mixing_all,
        states_all,
        gated,
        normed_all,
        hidden,
        live,
        keep,
    )


def gated_unit(gated, whole_weight, hidden, live, grads_own, grads_first, ffn_in, ffn_out):
    _, width, units = ffn_in.shape
    local_rows = hidden.shape[0]
    group_rows = NBLK * BLK
    pieces = group_rows // PIECE
    deep = gated.shape[2]
    slices, quarters, slice_rows, _ = whole_weight.shape
    main = units // TILE * TILE
    tail = units - main
    low = jnp.bfloat16
    cuts = ((0, 2 * TILE), (2 * TILE, main - 2 * TILE))
    wide_tile = 1024
    first_half, second_half = pl.ds(0, HALF), pl.ds(HALF, HALF)

    def body(*refs):
        gated_in, weight_in, hidden_in = refs[:3]
        grad_in = refs[3:5]
        in_ref, out_ref, live_ref = refs[5:8]
        middle_out, rows_out, grads_out, act_out, parts_out, back_out, two_out = refs[8:15]
        gated_ref, hidden_ref, middle_ref = refs[15:18]
        rows, grads, sums, w_in, w_out, act, parts, held = refs[18:26]
        load_sems, slice_sems, weight_sems, done_sems, sum_sems, last_sems, gated_sems, gather_sems = refs[26:]
        wide, narrow, _, _, _, near_x, near_y = neighbours()
        far = (wide, 3 - narrow)
        here = pl.ds(pl.multiple_of(narrow * deep, deep), deep)

        def send_gated(slot, to, kind, place):
            return pltpu.make_async_remote_copy(
                src_ref=gated_in.at[0, pl.ds(slot * BLK, BLK)],
                dst_ref=gated_ref.at[(first_half, second_half)[to], here],
                send_sem=gated_sems.at[kind, 0],
                recv_sem=gated_sems.at[kind, 1],
                device_id=place,
                device_id_type=MESH,
            )

        gated_sends = [
            send_gated(6, 0, 0, far),
            send_gated(7, 1, 1, far),
            send_gated(2, 0, 2, near_x),
            send_gated(3, 1, 3, near_y),
            send_gated(4, 1, 4, near_x),
            send_gated(5, 0, 5, near_y),
        ]
        keep_gated = pltpu.make_async_copy(
            gated_in.at[0, pl.ds(0, PIECE)], gated_ref.at[:, here], load_sems.at[0]
        )

        def load_slice(at):
            part, quarter = at // quarters, at % quarters
            to = pl.ds(pl.multiple_of(quarter * deep + part * slice_rows, slice_rows), slice_rows)
            return pltpu.make_async_copy(
                weight_in.at[part, quarter], w_in.at[to, pl.ds(0, width)], slice_sems.at[at]
            )

        def start_slice(at, carry):
            load_slice(at).start()
            return carry

        def wait_slice(at, carry):
            load_slice(at).wait()
            return carry

        load_hidden = pltpu.make_async_copy(hidden_in, hidden_ref, load_sems.at[1])
        load_grads = [
            pltpu.make_async_copy(src, grads.at[at], load_sems.at[2 + at])
            for at, src in enumerate(grad_in)
        ]
        weights = []
        for start, size, first, second in tuple((a, b, a, main + a) for a, b in cuts) + (
            (main, tail, 2 * main, 2 * main + tail),
        ):
            at = pl.ds(start, size)
            weights += [
                pltpu.make_async_copy(in_ref.at[0, :, at], w_in.at[:, pl.ds(first, size)], weight_sems.at[len(weights)]),
                pltpu.make_async_copy(in_ref.at[1, :, at], w_in.at[:, pl.ds(second, size)], weight_sems.at[len(weights) + 1]),
                pltpu.make_async_copy(out_ref.at[at, :], w_out.at[at, :], weight_sems.at[len(weights) + 2]),
            ]

        def remote(src, dst, sems, kind, place):
            return pltpu.make_async_remote_copy(
                src_ref=src,
                dst_ref=dst,
                send_sem=sems.at[kind, 0],
                recv_sem=sems.at[kind, 1],
                device_id=place,
                device_id_type=MESH,
            )

        def half(ref, piece, at):
            return ref.at[piece, (first_half, second_half)[at]]

        def quarter(ref, piece, at):
            return ref.at[piece, pl.ds(at * SUB, SUB)]

        def gather(ref, kind):
            return (
                [
                    remote(half(ref, 0, 0), half(ref, 1, 0), gather_sems, kind, near_x),
                    remote(half(ref, 0, 1), half(ref, 1, 1), gather_sems, kind + 1, near_y),
                ],
                [
                    remote(half(ref, 0, 1), half(ref, 2, 0), gather_sems, kind + 2, near_x),
                    remote(half(ref, 0, 0), half(ref, 2, 1), gather_sems, kind + 3, near_y),
                ],
                [
                    remote(quarter(ref, 1, 2), quarter(ref, 3, 1), gather_sems, kind + 4, near_x),
                    remote(quarter(ref, 1, 0), quarter(ref, 3, 0), gather_sems, kind + 5, near_y),
                ],
                [
                    remote(quarter(ref, 1, 3), quarter(ref, 3, 3), gather_sems, kind + 6, near_x),
                    remote(quarter(ref, 1, 1), quarter(ref, 3, 2), gather_sems, kind + 7, near_y),
                ],
            )

        row_sends = gather(rows, 0)
        grad_sends = gather(grads, 8)

        begin(load_grads)
        begin([keep_gated, load_hidden])
        barrier = pltpu.get_barrier_semaphore()
        for place in (near_x, near_y, far):
            pl.semaphore_signal(barrier, inc=1, device_id=place, device_id_type=MESH)
        pl.semaphore_wait(barrier, 3)
        begin(gated_sends)
        lax.fori_loop(0, slices * quarters, start_slice, 0)
        finish(load_grads)
        begin(grad_sends[1])
        finish([keep_gated, load_hidden])
        lax.fori_loop(0, slices * quarters, wait_slice, 0)
        finish(gated_sends)
        for j in range(width // wide_tile):
            at = slice(j * wide_tile, (j + 1) * wide_tile)
            middle_ref[:, at] = straight(gated_ref[...], w_in[:, at])
        begin(weights)

        def second_norm(i, carry, at):
            here = pl.ds(pl.multiple_of(at * HALF + i * 32, 32), 32)
            middle = hidden_ref[here, :].astype(jnp.float32) + live_ref[here, :1] * middle_ref[here, :]
            middle_ref[here, :] = middle
            rows[0, here, :] = row_norm(middle).astype(low)
            return carry

        for at in range(2):
            lax.fori_loop(0, HALF // 32, functools.partial(second_norm, at=at), 0)
            row_sends[0][at].start()
        begin(row_sends[1])
        store_middle = pltpu.make_async_copy(middle_ref, middle_out, done_sems.at[0])
        store_middle.start()

        def products(size, at, first, second, part_a, part_b, grad_act):
            act[:size, at] = (part_a * part_b).astype(low)
            parts[:size, first] = (grad_act * part_b).astype(low)
            parts[:size, second] = (grad_act * part_a).astype(low)

        def unit(arrived, arrived_grads, size, weights_wait):
            for which, (start, count) in enumerate(cuts):
                at, second = slice(start, start + count), slice(main + start, main + start + count)
                weights_wait(3 * which, 3 * which + 3)
                part_a = straight(arrived[...], w_in[:, at])
                part_b = straight(arrived[...], w_in[:, second])
                grad_act = across(arrived_grads[...], w_out[at, :])
                products(size, at, at, second, part_a, part_b, grad_act)
            weights_wait(6, 9)
            if tail:
                both = straight(arrived[...], w_in[:, 2 * main :])
                grad_act = across(arrived_grads[...], w_out[main:, :])
                products(
                    size,
                    slice(main, units),
                    slice(2 * main, 2 * main + tail),
                    slice(2 * main + tail, 2 * units),
                    both[:, :tail],
                    both[:, tail:],
                    grad_act,
                )

        def row_stores(arrived, arrived_grads, at):
            return [
                pltpu.make_async_copy(arrived, rows_out.at[at, :], done_sems.at[1]),
                pltpu.make_async_copy(arrived_grads, grads_out.at[at, :], done_sems.at[2]),
            ]

        def unit_stores(size, at):
            here = pl.ds(0, size)
            return [
                pltpu.make_async_copy(act.at[here], act_out.at[at, :], done_sems.at[3]),
                pltpu.make_async_copy(parts.at[here], parts_out.at[at, :], done_sems.at[4]),
            ]

        def sum_stores(piece, j):
            tile = pl.ds(j * wide_tile, wide_tile)
            return [
                pltpu.make_async_copy(
                    sums.at[at, :, tile],
                    (back_out, two_out)[at // 2].at[
                        pl.ds(pl.multiple_of(piece * PIECE + (at % 2) * HALF, HALF), HALF), tile
                    ],
                    sum_sems.at[j, at],
                )
                for at in range(4)
            ]

        def work(piece, carry):
            at = pl.ds(pl.multiple_of(piece * PIECE, PIECE), PIECE)
            arrived, arrived_grads = rows.at[piece], grads.at[piece]

            @pl.when(piece == 1)
            def _():
                finish(row_sends[0])
                for step in (2, 3):
                    begin(row_sends[step])
                    begin(grad_sends[step])

            @pl.when(piece == 2)
            def _():
                finish(row_sends[1])
                finish(grad_sends[1])

            stores = row_stores(arrived, arrived_grads, at)
            begin(stores)

            def weights_wait(start, stop):
                pl.when(piece == 0)(lambda: finish(weights[start:stop]))

            unit(arrived, arrived_grads, PIECE, weights_wait)
            more = unit_stores(PIECE, at)
            begin(more)
            for j in range(width // wide_tile):
                tile = slice(j * wide_tile, (j + 1) * wide_tile)

                @pl.when(piece > 0)
                def _(j=j):
                    finish(sum_stores(piece - 1, j))

                back = across(parts[...], w_in[tile, :])
                sums[0, :, tile] = back[:HALF].astype(low)
                sums[1, :, tile] = back[HALF:].astype(low)
                two = straight(act[...], w_out[:, tile])
                sums[2, :, tile] = two[:HALF].astype(low)
                sums[3, :, tile] = two[HALF:].astype(low)
                begin(sum_stores(piece, j))
            finish(stores)
            finish(more)
            return carry

        lax.fori_loop(0, pieces - 1, work, 0)
        for j in range(width // wide_tile):
            finish(sum_stores(pieces - 2, j))

        def last_stores(which):
            return [
                pltpu.make_async_copy(
                    sums.at[2 * total + which, pl.ds(part * SUB, SUB)],
                    (back_out, two_out)[total].at[
                        pl.ds(pl.multiple_of((pieces - 1) * PIECE + part * HALF + which * SUB, SUB), SUB)
                    ],
                    last_sems.at[which, 2 * total + part],
                )
                for total in range(2)
                for part in range(2)
            ]

        def last_work(which, carry):
            here = pl.ds(pl.multiple_of(which * HALF, HALF), HALF)
            at = pl.ds(pl.multiple_of((pieces - 1) * PIECE + which * HALF, HALF), HALF)
            arrived, arrived_grads = rows.at[pieces - 1, here], grads.at[pieces - 1, here]
            pl.when(which == 0)(lambda: finish(row_sends[2]))
            pl.when(which == 1)(lambda: finish(row_sends[3]))
            held[...] = straight(arrived[...], w_in[...])

            def columns_of(start, stop):
                first, second = slice(start, stop), slice(main + start, main + stop)
                if start == main:
                    first, second = slice(2 * main, 2 * main + tail), slice(2 * main + tail, 2 * units)
                return first, second

            ranges = ((0, main), (main, units)) if tail else ((0, main),)
            for start, stop in ranges:
                first, second = columns_of(start, stop)
                act[:HALF, start:stop] = (held[:, first] * held[:, second]).astype(low)
            for j in range(width // wide_tile):
                tile = slice(j * wide_tile, (j + 1) * wide_tile)
                sums[2 + which, :, tile] = straight(act[:HALF], w_out[:, tile]).astype(low)
            pl.when(which == 0)(lambda: finish(grad_sends[2]))
            pl.when(which == 1)(lambda: finish(grad_sends[3]))
            stores = row_stores(arrived, arrived_grads, at)
            begin(stores)
            for start, stop in ranges:
                first, second = columns_of(start, stop)
                grad_act = across(arrived_grads[...], w_out[start:stop, :])
                parts[:HALF, first] = (grad_act * held[:, second]).astype(low)
                parts[:HALF, second] = (grad_act * held[:, first]).astype(low)
            more = unit_stores(HALF, at)
            begin(more)
            for j in range(width // wide_tile):
                tile = slice(j * wide_tile, (j + 1) * wide_tile)
                sums[which, :, tile] = across(parts[:HALF], w_in[tile, :]).astype(low)
            begin(last_stores(which))
            finish(stores)
            finish(more)
            return carry

        lax.fori_loop(0, 2, last_work, 0)
        for which in range(2):
            finish(last_stores(which))
        store_middle.wait()

    return pl.pallas_call(
        body,
        in_specs=any_specs(7) + [pl.BlockSpec(memory_space=pltpu.VMEM)],
        out_specs=any_specs(7),
        out_shape=[
            jax.ShapeDtypeStruct((local_rows, width), jnp.float32),
            jax.ShapeDtypeStruct((group_rows, width), low),
            jax.ShapeDtypeStruct((group_rows, width), low),
            jax.ShapeDtypeStruct((group_rows, units), low),
            jax.ShapeDtypeStruct((group_rows, 2 * units), low),
            jax.ShapeDtypeStruct((group_rows, width), low),
            jax.ShapeDtypeStruct((group_rows, width), low),
        ],
        scratch_shapes=[
            pltpu.VMEM((local_rows, quarters * deep), low),
            pltpu.VMEM((local_rows, width), low),
            pltpu.VMEM((local_rows, width), jnp.float32),
            pltpu.VMEM((pieces, PIECE, width), low),
            pltpu.VMEM((pieces, PIECE, width), low),
            pltpu.VMEM((4, HALF, width), low),
            pltpu.VMEM((width, 2 * units), low),
            pltpu.VMEM((units, width), low),
            pltpu.VMEM((PIECE, units), low),
            pltpu.VMEM((PIECE, 2 * units), low),
            pltpu.VMEM((HALF, 2 * units), jnp.float32),
            pltpu.SemaphoreType.DMA((4,)),
            pltpu.SemaphoreType.DMA((slices * quarters,)),
            pltpu.SemaphoreType.DMA((9,)),
            pltpu.SemaphoreType.DMA((5,)),
            pltpu.SemaphoreType.DMA((width // wide_tile, 4)),
            pltpu.SemaphoreType.DMA((2, 4)),
            pltpu.SemaphoreType.DMA((6, 2)),
            pltpu.SemaphoreType.DMA((16, 2)),
        ],
        compiler_params=pltpu.CompilerParams(
            vmem_limit_bytes=VMEM, collective_id=3, has_side_effects=True
        ),
        cost_estimate=cost(12 * group_rows * width * units, 90e6),
        name="gated_unit",
    )(gated, whole_weight, hidden, grads_own, grads_first, ffn_in, ffn_out, live)


def mix_rows(hidden, cotangent, mix_weight, out_weight, seq_lengths, block_seq):
    local_rows, width = hidden.shape
    parts, _, columns = mix_weight.shape
    heads = columns // HS
    group_rows = NBLK * BLK
    pieces = group_rows // PIECE
    wide_size = lax.axis_size("wide")
    slice_rows = columns // wide_size
    low = jnp.bfloat16
    joined = 2
    halves_at = (pl.ds(0, HALF), pl.ds(HALF, HALF))

    def body(*refs):
        hidden_in, cot_in, mix_in, out_in, length_ref, owner_ref = refs[:6]
        rows_out, parts_out, gated_out, mixing_out, states_out, grads_out, first_out, whole_out = refs[6:14]
        live_ref, keep_ref = refs[14:16]
        hidden_ref, cot_ref, rows, weights, parts_ref, gated_ref, mixing_ref, states_ref = refs[16:24]
        load_sems, mix_sems, store_sems, parts_sems, gather_sems, slice_sems, line_sems, core_sems = refs[24:]
        wide, narrow, z, core, mate, near_x, near_y = neighbours()
        far = (wide, 3 - narrow)
        above, below = (wide + 2, narrow), (wide - 2, narrow)
        barrier = pltpu.get_barrier_semaphore()

        def greet(place):
            pl.semaphore_signal(barrier, inc=1, device_id=place, device_id_type=MESH)

        load_hidden = pltpu.make_async_copy(hidden_in, hidden_ref, load_sems.at[0])
        load_cot = pltpu.make_async_copy(cot_in, cot_ref, load_sems.at[1])
        mix_loads = [
            pltpu.make_async_copy(
                mix_in.at[c], weights.at[:, pl.ds(c * columns, columns)], mix_sems.at[c]
            )
            for c in range(parts)
        ]
        load_hidden.start()
        for place in (near_x, near_y, far, mate):
            greet(place)
        pl.when(z < 3)(lambda: greet(above))
        pl.when(z > 0)(lambda: greet(below))
        middle = (z == 1) | (z == 2)
        pl.when(middle)(lambda: pl.semaphore_wait(barrier, 6))
        pl.when(jnp.logical_not(middle))(lambda: pl.semaphore_wait(barrier, 5))

        def remote(src, dst, sems, kind, place):
            return pltpu.make_async_remote_copy(
                src_ref=src,
                dst_ref=dst,
                send_sem=sems.at[kind, 0],
                recv_sem=sems.at[kind, 1],
                device_id=place,
                device_id_type=MESH,
            )

        slice_at = out_in.at[pl.ds(pl.multiple_of(wide * slice_rows, slice_rows), slice_rows)]
        keep_slice = pltpu.make_async_copy(slice_at, whole_out.at[wide, narrow], load_sems.at[2])
        slice_sends = [
            remote(slice_at, whole_out.at[wide, narrow], slice_sems, at, place)
            for at, place in enumerate((far, near_x, near_y))
        ]

        def up(hop):
            return remote(
                whole_out.at[wide - 2 * (hop - 1)], whole_out.at[wide - 2 * (hop - 1)], line_sems, hop - 1, above
            )

        def down_line(hop):
            return remote(
                whole_out.at[wide + 2 * (hop - 1)], whole_out.at[wide + 2 * (hop - 1)], line_sems, 2 + hop, below
            )

        def to_mate(hop, sign):
            at = wide + sign * 2 * hop
            return remote(whole_out.at[at], whole_out.at[at], core_sems, 3 + sign * hop, mate)

        def send_hop(hop):
            pl.when((z < 3) & (z >= hop - 1))(lambda: up(hop).start())
            pl.when((z > 0) & (z + hop - 1 <= 3))(lambda: down_line(hop).start())

        def take_hop(hop):
            @pl.when(z >= hop)
            def _():
                arrived = whole_out.at[wide - 2 * hop]
                remote(arrived, arrived, line_sems, hop - 1, mate).wait_recv()
                to_mate(hop, -1).start()

            @pl.when(z + hop <= 3)
            def _():
                arrived = whole_out.at[wide + 2 * hop]
                remote(arrived, arrived, line_sems, 2 + hop, mate).wait_recv()
                to_mate(hop, 1).start()

        def end_hop(hop):
            pl.when((z < 3) & (z >= hop - 1))(lambda: up(hop).wait_send())
            pl.when((z > 0) & (z + hop - 1 <= 3))(lambda: down_line(hop).wait_send())
            pl.when(z >= hop)(lambda: to_mate(hop, -1).wait())
            pl.when(z + hop <= 3)(lambda: to_mate(hop, 1).wait())

        begin(slice_sends)
        keep_slice.start()

        def half(piece, at):
            return rows.at[piece, halves_at[at]]

        row_sends = (
            [remote(half(0, 0), half(1, 0), gather_sems, 0, near_x), remote(half(0, 1), half(1, 1), gather_sems, 1, near_y)],
            [remote(half(0, 1), half(2, 0), gather_sems, 2, near_x), remote(half(0, 0), half(2, 1), gather_sems, 3, near_y)],
            [remote(half(1, 1), half(3, 1), gather_sems, 4, near_x), remote(half(1, 0), half(3, 0), gather_sems, 5, near_y)],
        )
        grad_sends = [
            remote(cot_ref.at[halves_at[0]], first_out.at[halves_at[0]], gather_sems, 6, near_x),
            remote(cot_ref.at[halves_at[1]], first_out.at[halves_at[1]], gather_sems, 7, near_y),
        ]
        load_hidden.wait()
        begin(mix_loads)
        load_cot.start()

        def first_norm(i, carry):
            at = pl.ds(pl.multiple_of(i * 32, 32), 32)
            rows[0, at, :] = row_norm(hidden_ref[at, :].astype(jnp.float32)).astype(low)
            return carry

        for at in range(2):
            lax.fori_loop(at * HALF // 32, (at + 1) * HALF // 32, first_norm, 0)
            row_sends[0][at].start()
        begin(row_sends[1])

        def row_store(piece):
            at = pl.ds(piece * PIECE, PIECE)
            return pltpu.make_async_copy(rows.at[piece], rows_out.at[at, :], store_sems.at[piece])

        def part_stores(piece):
            at = pl.ds(piece * PIECE, PIECE)
            return [
                pltpu.make_async_copy(
                    parts_ref.at[at, pl.ds(c * columns, columns)], parts_out.at[c, at, :], parts_sems.at[piece, c]
                )
                for c in range(parts)
            ]

        def project(piece):
            row_store(piece).start()
            for c in range(0, parts, joined):
                if piece == 0:
                    finish(mix_loads[c : c + joined])
                at = slice(c * columns, (c + joined) * columns)
                result = straight(rows[piece], weights[:, at]).astype(low)
                parts_ref[piece * PIECE : (piece + 1) * PIECE, at] = result
            begin(part_stores(piece))

        def same_slot(block):
            return owner_ref[block] == owner_ref[0]

        first_count = sum(jnp.where(same_slot(block), 1, 0) for block in range(NBLK))

        def start_of(block):
            return jnp.where(same_slot(block), 0, first_count)

        for block in range(NBLK):
            entering = jnp.where(start_of(block) == block, 0.0, 1.0)
            keep_ref[block : block + 1, :] = jnp.full((1, HS), entering, jnp.float32)
        for at in range(local_rows // BLK):
            block = narrow * (local_rows // BLK) + at
            limit = jnp.where(same_slot(block), length_ref[0], length_ref[1])
            place = lax.broadcasted_iota(jnp.int32, (BLK, HS), 0) + (block - start_of(block)) * BLK
            live_ref[at * BLK : (at + 1) * BLK, :] = jnp.where(place < limit, 1.0, 0.0)
        project(0)
        load_cot.wait()

        def live_cot(i, carry):
            at = pl.ds(pl.multiple_of(i * 32, 32), 32)
            cot_ref[at, :] = (live_ref[at, :1] * cot_ref[at, :].astype(jnp.float32)).astype(low)
            return carry

        keep_slice.wait()
        finish(slice_sends)
        to_mate(0, 1).start()
        send_hop(1)
        lax.fori_loop(0, local_rows // 32, live_cot, 0)
        store_grads = pltpu.make_async_copy(cot_ref, grads_out, load_sems.at[3])
        store_grads.start()
        finish(row_sends[0])
        begin(row_sends[2])
        begin(grad_sends)
        project(1)
        take_hop(1)
        send_hop(2)
        finish(row_sends[1])
        project(2)
        take_hop(2)
        send_hop(3)
        finish(row_sends[2])
        project(3)

        def attend(head, carry):
            within, entry, leave, whole = block_decays(head_rate(heads * narrow + head))
            state = jnp.zeros((HS, HS), jnp.float32)

            def part(c, rows_at):
                at = pl.ds(pl.multiple_of(c * columns + head * HS, HS), HS)
                return parts_ref[rows_at, at]

            for block in range(NBLK):
                rows_at = pl.ds(pl.multiple_of(slot_of(block, narrow) * BLK, BLK), BLK)
                queries = jax.nn.silu(part(0, rows_at).astype(jnp.float32)).astype(low)
                keys = jax.nn.silu(part(1, rows_at).astype(jnp.float32)).astype(low)
                values = part(2, rows_at)
                gate = part(3, rows_at).astype(jnp.float32)
                state = keep_ref[block : block + 1, :] * state
                state_low = state.astype(low)
                states_ref[head, block] = state_low
                scores = (across(queries, keys) * within).astype(low)
                mixing = straight(scores, values) + entry * straight(queries, state_low)
                late_keys = (keys.astype(jnp.float32) * leave).astype(low)
                state = whole * state + down(late_keys, values)
                scale = lax.rsqrt(jnp.mean(mixing * mixing, axis=-1, keepdims=True) + head_floor)
                at = pl.ds(pl.multiple_of(head * HS, HS), HS)
                gated_ref[rows_at, at] = (mixing * scale * gate).astype(low)
                mixing_ref[rows_at, at] = mixing.astype(low)
            return carry

        lax.fori_loop(0, heads // 2, attend, 0)
        take_hop(3)
        lax.fori_loop(heads // 2, heads, attend, 0)
        stores = [
            pltpu.make_async_copy(gated_ref, gated_out.at[0], load_sems.at[4]),
            pltpu.make_async_copy(mixing_ref, mixing_out, load_sems.at[5]),
            pltpu.make_async_copy(states_ref, states_out, load_sems.at[6]),
        ]
        begin(stores)
        to_mate(0, 1).wait()
        for hop in range(1, 4):
            end_hop(hop)
        finish(grad_sends)
        store_grads.wait()
        for piece in range(pieces):
            row_store(piece).wait()
            finish(part_stores(piece))
        finish(stores)

    low_shape = functools.partial(jax.ShapeDtypeStruct, dtype=low)
    return pl.pallas_call(
        body,
        in_specs=any_specs(4) + [pl.BlockSpec(memory_space=pltpu.SMEM)] * 2,
        out_specs=any_specs(8) + [pl.BlockSpec(memory_space=pltpu.VMEM)] * 2,
        out_shape=[
            low_shape((group_rows, width)),
            low_shape((parts, group_rows, columns)),
            low_shape((1, group_rows, columns)),
            low_shape((group_rows, columns)),
            low_shape((heads, NBLK, HS, HS)),
            low_shape((local_rows, width)),
            low_shape((local_rows, width)),
            low_shape((wide_size, pieces, slice_rows, width)),
            jax.ShapeDtypeStruct((local_rows, HS), jnp.float32),
            jax.ShapeDtypeStruct((NBLK, HS), jnp.float32),
        ],
        scratch_shapes=[
            pltpu.VMEM((local_rows, width), low),
            pltpu.VMEM((local_rows, width), low),
            pltpu.VMEM((pieces, PIECE, width), low),
            pltpu.VMEM((width, parts * columns), low),
            pltpu.VMEM((group_rows, parts * columns), low),
            pltpu.VMEM((group_rows, columns), low),
            pltpu.VMEM((group_rows, columns), low),
            pltpu.VMEM((heads, NBLK, HS, HS), low),
            pltpu.SemaphoreType.DMA((7,)),
            pltpu.SemaphoreType.DMA((parts,)),
            pltpu.SemaphoreType.DMA((pieces,)),
            pltpu.SemaphoreType.DMA((pieces, parts)),
            pltpu.SemaphoreType.DMA((8, 2)),
            pltpu.SemaphoreType.DMA((3, 2)),
            pltpu.SemaphoreType.DMA((6, 2)),
            pltpu.SemaphoreType.DMA((7, 2)),
        ],
        compiler_params=pltpu.CompilerParams(
            vmem_limit_bytes=VMEM, collective_id=4, has_side_effects=True
        ),
        cost_estimate=cost(2 * group_rows * parts * width * columns, 50e6),
        name="mix_rows",
    )(hidden, cotangent, mix_weight, out_weight, seq_lengths, block_seq)


def widen(mix_low, out_low, in_low, wide_low, rows):
    parts, width, columns = mix_low.shape
    units = wide_low.shape[0]
    main = units // TILE * TILE
    tail = units - main
    steps = parts

    def body(mix_ref, out_ref, in_ref, wide_ref, one_ref, two_ref, mix_out, out_out, in_out, wide_out, one_out, two_out):
        one_out[...] = one_ref[...]
        two_out[...] = two_ref[...]
        mix_out[...] = mix_ref[...].astype(jnp.float32)
        out_out[...] = out_ref[...].astype(jnp.float32)
        wide_out[...] = wide_ref[...].astype(jnp.float32)
        for c in range(2):
            in_out[c, :, :main] = in_ref[:, c * main : (c + 1) * main].astype(jnp.float32)
            rest = slice(2 * main + c * tail, 2 * main + (c + 1) * tail)
            in_out[c, :, main:] = in_ref[:, rest].astype(jnp.float32)

    def rows_spec(array):
        return pl.BlockSpec((array.shape[0] // steps, array.shape[1]), lambda i: (i, 0))

    mix_spec = pl.BlockSpec((1, width, columns), lambda i: (i, 0, 0))
    shapes = (mix_low.shape, out_low.shape, (2, width, units), wide_low.shape)
    return pl.pallas_call(
        body,
        grid=(steps,),
        in_specs=[mix_spec] + [rows_spec(array) for array in (out_low, in_low, wide_low, *rows)],
        out_specs=[
            mix_spec,
            rows_spec(out_low),
            pl.BlockSpec((2, width // steps, units), lambda i: (0, i, 0)),
            rows_spec(wide_low),
            *(rows_spec(array) for array in rows),
        ],
        out_shape=[jax.ShapeDtypeStruct(shape, jnp.float32) for shape in shapes]
        + [jax.ShapeDtypeStruct(array.shape, array.dtype) for array in rows],
        compiler_params=pltpu.CompilerParams(vmem_limit_bytes=VMEM),
        cost_estimate=cost(1e8, 84e6),
        name="widen",
    )(mix_low, out_low, in_low, wide_low, *rows)


def block_decays(rate):
    row = lax.broadcasted_iota(jnp.int32, (BLK, BLK), 0)
    column = lax.broadcasted_iota(jnp.int32, (BLK, BLK), 1)
    distance = (row - column).astype(jnp.float32)
    within = jnp.where(row >= column, jnp.exp(-rate * jnp.maximum(distance, 0.0)), 0.0)
    place = lax.broadcasted_iota(jnp.int32, (BLK, 1), 0).astype(jnp.float32)
    entry = jnp.exp(-rate * (place + 1.0))
    leave = jnp.exp(-rate * (BLK - 1.0 - place))
    whole = jnp.exp(-BLK * rate * jnp.ones((1, HS), jnp.float32))
    return within, entry, leave, whole


def norm_back(values, grad):
    scale = lax.rsqrt(jnp.mean(values * values, axis=-1, keepdims=True) + epsilon)
    unit = values * scale
    return scale * (grad - unit * jnp.mean(grad * unit, axis=-1, keepdims=True))


def square_device(
    hidden, mix_weight, out_weight, ffn_in_weight, ffn_out_weight, seq_lengths, block_seq, cotangent
):
    width = hidden.shape[1]
    units = ffn_out_weight.shape[0]
    normed_all, parts, gated, mixing, states, grads_own, grads_first, whole_weight, live, keep = mix_rows(
        hidden, cotangent, mix_weight, out_weight, seq_lengths, block_seq
    )
    middle, normed_two_all, grad_two_all, act, grad_parts, back_sums, two_sums = gated_unit(
        gated,
        whole_weight,
        hidden,
        live,
        grads_own,
        grads_first,
        ffn_in_weight,
        ffn_out_weight,
    )
    in_low, wide_low, out_low, mix_low, _, _, layer_out, input_grad, *_ = weight_grads(
        act,
        grad_two_all,
        normed_two_all,
        grad_parts,
        back_sums,
        two_sums,
        middle,
        cotangent,
        out_weight,
        mix_weight,
        parts,
        mixing,
        states,
        gated,
        normed_all,
        hidden,
        live,
        keep,
    )
    grad_mix, grad_out, grad_ffn_in, grad_ffn_out, layer_out, input_grad = widen(
        mix_low.reshape(mix_weight.shape),
        out_low.reshape(out_weight.shape),
        in_low.reshape(width, 2 * units),
        wide_low.reshape(units, width),
        (layer_out, input_grad),
    )
    return (layer_out, input_grad, grad_mix, grad_out, grad_ffn_in, grad_ffn_out)


def solution(mesh):
    square = mesh.shape["wide"] == 8 and mesh.shape["narrow"] == 4
    per_device = square_device if square else general_device
    in_specs = (
        P(("wide", "narrow"), None),
        P(None, None, "narrow"),
        P("narrow", None),
        P(None, None, "narrow"),
        P("narrow", None),
        P("wide"),
        P("wide"),
        P(("wide", "narrow"), None),
    )
    out_specs = (
        P(("wide", "narrow"), None),
        P(("wide", "narrow"), None),
        P(None, None, "narrow"),
        P("narrow", None),
        P(None, None, "narrow"),
        P("narrow", None),
    )
    return jax.shard_map(
        per_device, mesh=mesh, in_specs=in_specs, out_specs=out_specs, check_vma=False
    )
```

```python
import functools
import math

import jax
import jax.numpy as jnp
from jax import lax
from jax.experimental import pallas as pl
from jax.experimental.pallas import tpu as pltpu
from jax.sharding import PartitionSpec as P

HEADS = 16
HS = 128
BLK = 256
NBLK = 8


epsilon = 1e-06
head_floor = 1.0
highest = lax.Precision.HIGHEST


def row_norm(values):
    return values * lax.rsqrt(jnp.mean(values * values, axis=-1, keepdims=True) + epsilon)


def head_norm(values):
    return values * lax.rsqrt(jnp.mean(values * values, axis=-1, keepdims=True) + head_floor)


def silu_slope(values):
    sigmoid_part = jax.nn.sigmoid(values)
    return sigmoid_part * (1.0 + values * (1.0 - sigmoid_part))


def decay_tables(decay_rates):
    positions = jnp.arange(BLK, dtype=jnp.float32)
    distance = positions[:, None] - positions[None, :]
    causal = distance >= 0
    clipped = jnp.where(causal, distance, 0.0)
    within = jnp.where(causal[None], jnp.exp(-decay_rates[:, None, None] * clipped[None]), 0.0)
    entry_decay = jnp.exp(-(positions[:, None] + 1.0) * decay_rates[None, :])
    exit_decay = jnp.exp(-(BLK - 1.0 - positions[:, None]) * decay_rates[None, :])
    block_decay = jnp.exp(-BLK * decay_rates)
    return (within, entry_decay, exit_decay, block_decay)


def group_masks(lengths, owners):
    seq_slot = owners - owners[0]
    first_count = jnp.sum((seq_slot == 0).astype(jnp.int32))
    block_ids = jnp.arange(NBLK, dtype=jnp.int32)
    start_block = jnp.where(seq_slot == 0, jnp.int32(0), first_count)
    seq_limit = jnp.where(seq_slot == 0, lengths[0], lengths[1])
    offsets = (block_ids - start_block)[:, None] * BLK + jnp.arange(BLK, dtype=jnp.int32)[None, :]
    valid_rows = (offsets < seq_limit[:, None]).reshape(-1)
    fresh_block = block_ids == start_block
    return (valid_rows, fresh_block)


def forward_block(tables, kv_state, block_in):
    within, entry_decay, exit_decay, block_decay = tables
    queries, keys_in, values, fresh_block = block_in
    kv_state = jnp.where(fresh_block, 0.0, kv_state)
    scores = jnp.einsum("ihs,jhs->hij", queries, keys_in, preferred_element_type=jnp.float32)
    weights = (scores * within).astype(jnp.bfloat16)
    inner_part = jnp.einsum("hij,jhs->ihs", weights, values, preferred_element_type=jnp.float32)
    carried = jnp.einsum(
        "ihs,hst->iht",
        queries.astype(jnp.float32) * entry_decay[:, :, None],
        kv_state,
        precision=highest,
    )
    update = jnp.einsum(
        "ihs,iht->hst",
        keys_in.astype(jnp.float32) * exit_decay[:, :, None],
        values.astype(jnp.float32),
        precision=highest,
    )
    return (block_decay[:, None, None] * kv_state + update, (inner_part + carried, kv_state))


def backward_block(tables, later_grad, block_in):
    within, entry_decay, exit_decay, block_decay = tables
    queries, keys_in, values, grad_mix, kv_state, fresh_block = block_in
    scores = jnp.einsum("ihs,jhs->hij", queries, keys_in, preferred_element_type=jnp.float32)
    weights = (scores * within).astype(jnp.bfloat16)
    grad_values = jnp.einsum("hij,ihs->jhs", weights, grad_mix, preferred_element_type=jnp.float32)
    grad_weights = jnp.einsum("ihs,jhs->hij", grad_mix, values, preferred_element_type=jnp.float32)
    grad_scores = (grad_weights * within).astype(jnp.bfloat16)
    grad_queries = jnp.einsum(
        "hij,jhs->ihs", grad_scores, keys_in, preferred_element_type=jnp.float32
    )
    grad_keys = jnp.einsum("hij,ihs->jhs", grad_scores, queries, preferred_element_type=jnp.float32)
    grad_float = grad_mix.astype(jnp.float32)
    values_float = values.astype(jnp.float32)
    queries_float = queries.astype(jnp.float32)
    keys_float = keys_in.astype(jnp.float32)
    grad_queries = grad_queries + entry_decay[:, :, None] * jnp.einsum(
        "iht,hst->ihs", grad_float, kv_state, precision=highest
    )
    grad_keys = grad_keys + exit_decay[:, :, None] * jnp.einsum(
        "iht,hst->ihs", values_float, later_grad, precision=highest
    )
    grad_values = grad_values + jnp.einsum(
        "ihs,hst->iht", keys_float * exit_decay[:, :, None], later_grad, precision=highest
    )
    grad_state = jnp.einsum(
        "ihs,iht->hst", queries_float * entry_decay[:, :, None], grad_float, precision=highest
    )
    grad_state = grad_state + block_decay[:, None, None] * later_grad
    grad_state = jnp.where(fresh_block, 0.0, grad_state)
    return (grad_state, (grad_queries, grad_keys, grad_values))


def general_device(
    hidden, mix_weight, out_weight, ffn_in_weight, ffn_out_weight, seq_lengths, block_seq, cotangent
):
    local_rows = hidden.shape[0]
    group_rows = NBLK * BLK
    head_width = mix_weight.shape[2]
    head_count = head_width // HS
    narrow_index = lax.axis_index("narrow")
    valid_all, fresh_block = group_masks(seq_lengths, block_seq)
    valid_rows = lax.dynamic_slice_in_dim(
        valid_all.astype(jnp.float32), narrow_index * local_rows, local_rows
    )[:, None]
    head_ids = narrow_index * head_count + jnp.arange(head_count, dtype=jnp.int32)
    decay_rates = 2.0 ** (-8.0 * (head_ids.astype(jnp.float32) + 1.0) / HEADS)
    tables = decay_tables(decay_rates)

    def split_blocks(flat_rows):
        return flat_rows.reshape(NBLK, BLK, head_count, HS)

    inputs = hidden.astype(jnp.float32)
    normed_low = row_norm(inputs).astype(jnp.bfloat16)
    gathered = lax.all_gather(normed_low, "narrow", axis=0, tiled=True)
    projected = jnp.einsum("rd,cde->cre", gathered, mix_weight, preferred_element_type=jnp.float32)
    queries = jax.nn.silu(projected[0]).astype(jnp.bfloat16)
    keys_in = jax.nn.silu(projected[1]).astype(jnp.bfloat16)
    values = projected[2].astype(jnp.bfloat16)
    gate_part = projected[3]
    zero_state = jnp.zeros((head_count, HS, HS), jnp.float32)
    final_state, (mixing, kept_states) = lax.scan(
        lambda state_in, block_in: forward_block(tables, state_in, block_in),
        zero_state,
        (split_blocks(queries), split_blocks(keys_in), split_blocks(values), fresh_block),
    )
    mixing = mixing.reshape(group_rows, head_count, HS)
    headed = head_norm(mixing).reshape(group_rows, head_width)
    gated_low = (headed * gate_part).astype(jnp.bfloat16)
    branch = lax.psum_scatter(
        jnp.dot(gated_low, out_weight, preferred_element_type=jnp.float32).astype(jnp.bfloat16),
        "narrow",
        scatter_dimension=0,
        tiled=True,
    ).astype(jnp.float32)
    middle = inputs + valid_rows * branch
    normed_two_low = row_norm(middle).astype(jnp.bfloat16)
    gathered_two = lax.all_gather(normed_two_low, "narrow", axis=0, tiled=True)
    both_parts = jnp.einsum(
        "rd,cdf->crf", gathered_two, ffn_in_weight, preferred_element_type=jnp.float32
    )
    hidden_low = (both_parts[0] * both_parts[1]).astype(jnp.bfloat16)
    branch_two = lax.psum_scatter(
        jnp.dot(hidden_low, ffn_out_weight, preferred_element_type=jnp.float32).astype(
            jnp.bfloat16
        ),
        "narrow",
        scatter_dimension=0,
        tiled=True,
    ).astype(jnp.float32)
    layer_out = (middle + valid_rows * branch_two).astype(jnp.bfloat16)
    grad_rows = cotangent.astype(jnp.float32)
    ffn_grad_all = lax.all_gather(
        (valid_rows * grad_rows).astype(jnp.bfloat16), "narrow", axis=0, tiled=True
    )
    grad_ffn_out = jnp.einsum(
        "rf,rd->fd", hidden_low, ffn_grad_all, preferred_element_type=jnp.float32
    )
    grad_hidden = jnp.einsum(
        "rd,fd->rf", ffn_grad_all, ffn_out_weight, preferred_element_type=jnp.float32
    )
    grad_parts = jnp.stack([grad_hidden * both_parts[1], grad_hidden * both_parts[0]]).astype(
        jnp.bfloat16
    )
    grad_ffn_in = jnp.einsum(
        "rd,crf->cdf", gathered_two, grad_parts, preferred_element_type=jnp.float32
    )
    grad_slice = grad_parts
    grad_normed_two = lax.psum_scatter(
        jnp.einsum(
            "crf,cdf->rd", grad_slice, ffn_in_weight, preferred_element_type=jnp.float32
        ).astype(jnp.bfloat16),
        "narrow",
        scatter_dimension=0,
        tiled=True,
    ).astype(jnp.float32)
    norm_value, norm_pull = jax.vjp(row_norm, middle)
    grad_middle = grad_rows + norm_pull(grad_normed_two)[0]
    attn_grad_all = lax.all_gather(
        (valid_rows * grad_middle).astype(jnp.bfloat16), "narrow", axis=0, tiled=True
    )
    grad_out_weight = jnp.einsum(
        "re,rd->ed", gated_low, attn_grad_all, preferred_element_type=jnp.float32
    )
    grad_gated = jnp.einsum(
        "rd,ed->re", attn_grad_all, out_weight, preferred_element_type=jnp.float32
    )
    grad_gated = lax.optimization_barrier(grad_gated.astype(jnp.bfloat16)).astype(jnp.float32)
    grad_gate = grad_gated * headed
    grad_headed = (grad_gated * gate_part).reshape(group_rows, head_count, HS)
    head_value, head_pull = jax.vjp(head_norm, mixing)
    grad_mixing = head_pull(grad_headed)[0].astype(jnp.bfloat16)
    first_grad, (grad_queries, grad_keys, grad_values) = lax.scan(
        lambda later_grad, block_in: backward_block(tables, later_grad, block_in),
        zero_state,
        (
            split_blocks(queries),
            split_blocks(keys_in),
            split_blocks(values),
            split_blocks(grad_mixing),
            kept_states,
            fresh_block,
        ),
        reverse=True,
    )
    grad_projected = jnp.stack(
        [
            grad_queries.reshape(group_rows, head_width) * silu_slope(projected[0]),
            grad_keys.reshape(group_rows, head_width) * silu_slope(projected[1]),
            grad_values.reshape(group_rows, head_width),
            grad_gate,
        ]
    ).astype(jnp.bfloat16)
    grad_mix = jnp.einsum(
        "rd,cre->cde", gathered, grad_projected, preferred_element_type=jnp.float32
    )
    grad_slice = grad_projected
    grad_normed = lax.psum_scatter(
        jnp.einsum(
            "cre,cde->rd", grad_slice, mix_weight, preferred_element_type=jnp.float32
        ).astype(jnp.bfloat16),
        "narrow",
        scatter_dimension=0,
        tiled=True,
    ).astype(jnp.float32)
    first_value, first_pull = jax.vjp(row_norm, inputs)
    input_grad = (grad_middle + first_pull(grad_normed)[0]).astype(jnp.bfloat16)
    grad_mix, grad_out_weight, grad_ffn_in, grad_ffn_out = (
        lax.psum(grad_mix.astype(jnp.bfloat16), "wide").astype(jnp.float32),
        lax.psum(grad_out_weight.astype(jnp.bfloat16), "wide").astype(jnp.float32),
        lax.psum(grad_ffn_in.astype(jnp.bfloat16), "wide").astype(jnp.float32),
        lax.psum(grad_ffn_out.astype(jnp.bfloat16), "wide").astype(jnp.float32),
    )
    return (layer_out, input_grad, grad_mix, grad_out_weight, grad_ffn_in, grad_ffn_out)


HALF = BLK
PIECE = 2 * BLK
VMEM = 60 * 1024 * 1024


def add_low(*terms):
    return sum(term.astype(jnp.float32) for term in terms).astype(jnp.bfloat16)


def add_rows(*terms):
    return sum(term.astype(jnp.float32) for term in terms)


def across(left, right):
    return lax.dot_general(left, right, (((1,), (1,)), ((), ())), preferred_element_type=jnp.float32)


def down(left, right):
    return lax.dot_general(left, right, (((0,), (0,)), ((), ())), preferred_element_type=jnp.float32)


def straight(left, right):
    return jnp.dot(left, right, preferred_element_type=jnp.float32)


def any_specs(count):
    return [pl.BlockSpec(memory_space=pl.ANY)] * count


def cost(flops, bytes_accessed):
    return pl.CostEstimate(flops=int(flops), bytes_accessed=int(bytes_accessed), transcendentals=0)


MESH = pl.DeviceIdType.MESH
SLOTS = 12
STAGES = 11
SUB = 128
TILE = 256


def begin(copies):
    for copy in copies:
        copy.start()


def finish(copies):
    for copy in copies:
        copy.wait()


def neighbours():
    wide, narrow = lax.axis_index("wide"), lax.axis_index("narrow")
    z, core = wide // 2, wide % 2
    mate = (wide + 1 - 2 * core, narrow)
    near_x = (wide, narrow + 1 - 2 * (narrow % 2))
    near_y = (wide, (narrow + 2) % 4)
    return wide, narrow, z, core, mate, near_x, near_y


def slot_of(block, narrow):
    off_x = (block // 2 % 2 + narrow % 2) % 2
    off_y = (block // 4 + narrow // 2) % 2
    if block % 2:
        return 1 + 3 * off_x + 2 * off_y + off_x * off_y
    return 2 * off_x + 5 * off_y - off_x * off_y


def head_rate(head):
    return jnp.exp(jnp.full((1, 1), -8.0 / HEADS * math.log(2.0), jnp.float32) * (head.astype(jnp.float32) + 1.0))


def line_scratch():
    low = jnp.bfloat16
    pair = pltpu.VMEM((SLOTS, 2, SUB, TILE), low)
    return [
        pltpu.VMEM((SLOTS, 4, SUB, TILE), low),
        pair,
        pair,
        pair,
        pltpu.VMEM((SLOTS, SUB, TILE), low),
        pair,
        pair,
        pltpu.SemaphoreType.DMA((14, SLOTS)),
        pltpu.SemaphoreType.DMA((4, SLOTS)),
    ]


def enter(neighbour_places):
    wide, narrow, z, core, mate, near_x, near_y = neighbour_places
    barrier = pltpu.get_barrier_semaphore()

    def greet(place):
        pl.semaphore_signal(barrier, inc=1, device_id=place, device_id_type=MESH)

    for place in (mate, near_x, near_y):
        greet(place)
    middle = (z == 1) | (z == 2)

    @pl.when(middle)
    def _():
        greet((2 * (3 - z) + core, narrow))
        greet((6 * (z - 1) + core, narrow))
        pl.semaphore_wait(barrier, 5)

    @pl.when(jnp.logical_not(middle))
    def _():
        greet((2 * (1 + z // 3) + core, narrow))
        pl.semaphore_wait(barrier, 4)


def line_sum(scratch, places, count, product, targets):
    own, met, both, ended, crossed, full, other, sems, out_sems = scratch
    wide, narrow, z, core, mate, _, _ = places
    region = z // 2
    middle = (z == 1) | (z == 2)
    end = jnp.logical_not(middle)
    inward = (2 * (1 + z // 3) + core, narrow)
    across_line = (2 * (3 - z) + core, narrow)
    outward = (6 * (z - 1) + core, narrow)

    def remote(src, dst, kind, slot, place):
        return pltpu.make_async_remote_copy(
            src_ref=src,
            dst_ref=dst,
            send_sem=sems.at[2 * kind, slot],
            recv_sem=sems.at[2 * kind + 1, slot],
            device_id=place,
            device_id_type=MESH,
        )

    def core_one(s):
        return remote(own.at[s, pl.ds(2 * (1 - core), 2)], met.at[s], 0, s, mate)

    def line_one(s):
        return remote(both.at[s], ended.at[s], 1, s, inward)

    def cross_one(s):
        return remote(both.at[s, 1 - region], crossed.at[s], 2, s, across_line)

    def cross_two(s):
        return remote(full.at[s, region], full.at[s, region], 3, s, across_line)

    def out_one(s):
        return remote(full.at[s, region], full.at[s, region], 4, s, outward)

    def out_two(s):
        return remote(full.at[s, 1 - region], full.at[s, 1 - region], 5, s, outward)

    def core_two(s):
        return remote(full.at[s], other.at[s], 6, s, mate)

    def landing(ref, kind, slot):
        return remote(ref, ref, kind, slot, mate)

    def add(left, right):
        return (left.astype(jnp.float32) + right.astype(jnp.float32)).astype(jnp.bfloat16)

    def deliveries(k, s):
        for t in range(2):
            for which, (src, part) in enumerate(
                ((full.at[s, t], 2 * core + t), (other.at[s, t], 2 * (1 - core) + t))
            ):
                for condition, ref in targets(k, part):
                    yield condition, pltpu.make_async_copy(src, ref, out_sems.at[2 * t + which, s])

    def start(k, s):
        product(k, own.at[s])
        core_one(s).start()

    def cores(k, s):
        core_one(s).wait_recv()
        both[s] = add(own[s, pl.ds(2 * core, 2)], met[s])
        pl.when(end)(lambda: line_one(s).start())

    def ends(k, s):
        @pl.when(middle)
        def _():
            landing(ended.at[s], 1, s).wait_recv()
            both[s] = add(both[s], ended[s])
            cross_one(s).start()

    def centre(k, s):
        @pl.when(middle)
        def _():
            cross_one(s).wait_recv()
            full[s, region] = add(both[s, region], crossed[s])
            cross_two(s).start()
            out_one(s).start()

    def pass_on(k, s):
        @pl.when(middle)
        def _():
            cross_two(s).wait_recv()
            out_two(s).start()

    def back(k, s):
        @pl.when(end)
        def _():
            landing(full.at[s, region], 4, s).wait_recv()
            landing(full.at[s, 1 - region], 5, s).wait_recv()

        core_two(s).start()

    def deliver(k, s):
        core_two(s).wait_recv()
        for condition, copy in deliveries(k, s):
            pl.when(condition)(copy.start)

    def clear(k, s):
        core_one(s).wait_send()
        core_two(s).wait_send()

        @pl.when(end)
        def _():
            line_one(s).wait_send()

        @pl.when(middle)
        def _():
            for copy in (cross_one(s), cross_two(s), out_one(s), out_two(s)):
                copy.wait_send()

        for t in range(2):
            for which, src in enumerate((full, other)):
                ref = targets(k, 0)[0][1]
                pltpu.make_async_copy(src.at[s, t], ref, out_sems.at[2 * t + which, s]).wait()

    stages = (
        (11, clear),
        (10, deliver),
        (9, back),
        (7, pass_on),
        (5, centre),
        (3, ends),
        (1, cores),
        (0, start),
    )

    def step(i, carry):
        for delay, work in stages:
            k = i - delay

            @pl.when((k >= 0) & (k < count))
            def _(work=work, k=k):
                work(k, lax.rem(k + SLOTS, SLOTS))

        return carry

    return step


def square_scratch(uses):
    block = pltpu.VMEM((2, BLK, HEADS * HS), jnp.bfloat16)
    return [block, block, pltpu.SemaphoreType.DMA((uses, 6, 2)), pltpu.SemaphoreType.DMA((uses, 2))]


def square_sum(scratch, places, parts, landed, use, side=None):
    met, mid, sems, load_sems = scratch
    top_x, low_y, low_x, top_y, top_d, low_d = parts
    near_x, near_y = places[5:]

    def remote(src, dst, kind, place):
        return pltpu.make_async_remote_copy(
            src_ref=src,
            dst_ref=dst,
            send_sem=sems.at[use, kind, 0],
            recv_sem=sems.at[use, kind, 1],
            device_id=place,
            device_id_type=MESH,
        )

    first = [remote(top_d, met.at[0], 0, near_x), remote(low_d, met.at[1], 1, near_y)]
    direct = [remote(top_x, landed[0], 2, near_x), remote(low_y, landed[1], 3, near_y)]
    second = [remote(mid.at[0], landed[2], 4, near_y), remote(mid.at[1], landed[3], 5, near_x)]
    loads = []
    if top_y is not None:
        loads = [
            pltpu.make_async_copy(top_y, mid.at[0], load_sems.at[use, 0]),
            pltpu.make_async_copy(low_x, mid.at[1], load_sems.at[use, 1]),
        ]

    def open_sum():
        begin(first)
        begin(direct)
        begin(loads)

    def join_sum():
        finish(loads)
        for at in range(2):
            first[at].wait()

            def tile(i, carry, at=at):
                rows = pl.ds(pl.multiple_of(i * 64, 64), 64)
                mine = mid[at, rows, :] if side is None else side[at][rows, :]
                mid[at, rows, :] = add_low(mine, met[at, rows, :])
                return carry

            lax.fori_loop(0, BLK // 64, tile, 0)
        begin(second)

    def close_sum():
        finish(direct)
        finish(second)

    return open_sum, join_sum, close_sum


def weight_grads(
    act,
    grad_two_all,
    normed_two_all,
    grad_parts,
    back_sums,
    two_sums,
    middle,
    cotangent,
    out_weight,
    mix_weight,
    parts_all,
    mixing_all,
    states_all,
    gated,
    normed_all,
    hidden,
    live,
    keep,
):
    rows, units = act.shape
    width = grad_two_all.shape[1]
    local_rows = middle.shape[0]
    parts, _, columns = parts_all.shape
    heads = columns // HS
    low = jnp.bfloat16
    in_columns = grad_parts.shape[1] // TILE
    in_rows = width // PIECE
    out_blocks = units // SUB
    halves = width // 1024
    first_out = in_rows * in_columns
    first_branch = first_out + halves * out_blocks
    first_mix = first_branch + width // TILE
    per_row = columns // TILE
    per_part = in_rows * per_row
    count = first_mix + parts * per_part

    def body(*refs):
        act_in, two_in, normed_two_in, parts_in, back_in, two_sums_in = refs[:6]
        middle_in, cot_in, weight_in, mix_in = refs[6:10]
        all_in, mixing_in, states_in, gated_in, normed_in, hidden_in, live_ref, keep_ref = refs[10:18]
        in_grad, out_grad, branch_grad, mix_grad, branch_out, middle_out, layer_out, input_out = refs[18:26]
        last_landed, two_landed = refs[26:30], refs[30:34]
        shared, wide_ref, act_ref, landed, stage_ref, mid_ref, grad_ref, branch = refs[34:42]
        near, gated_grad, states_ref = refs[42:45]
        normed_sems, parts_sems, load_sems, stage_sems, gather_sems, back_sems, head_sems, mix_sems = refs[45:53]
        tile_sems, last_sems = refs[53:55]
        line, square = refs[55:64], refs[64:68]
        places = neighbours()
        narrow, near_x, near_y = places[1], places[5], places[6]

        def block(at):
            return pl.ds(at * BLK, BLK)

        def cols(at, size):
            return pl.ds(pl.multiple_of(at, 128), size)

        def load_normed_two(at):
            here = cols(at * PIECE, PIECE)
            return pltpu.make_async_copy(normed_two_in.at[:, here], shared.at[:, here], normed_sems.at[at])

        def load_parts(at):
            here = cols(at * TILE, TILE)
            return pltpu.make_async_copy(parts_in.at[:, here], wide_ref.at[:, here], parts_sems.at[at])

        def load_half(src, half, sem):
            here = pl.ds(half * 1024, 1024)
            return pltpu.make_async_copy(src.at[:, here], shared.at[:, here], load_sems.at[sem])

        load_act = pltpu.make_async_copy(act_in, act_ref, load_sems.at[0])
        load_two = [load_half(two_in, half, 1 + half) for half in range(halves)]
        load_normed = [load_half(normed_in, half, 3 + half) for half in range(halves)]
        load_gated = pltpu.make_async_copy(gated_in.at[0], act_ref.at[:, pl.ds(0, columns)], load_sems.at[5])

        def load_branch(at):
            slot = at % 2
            return pltpu.make_async_copy(
                branch_out.at[:, cols(at * TILE, TILE)],
                act_ref.at[:, cols(columns + slot * TILE, TILE)],
                tile_sems.at[slot],
            )

        def product(k, own):
            def split_rows(result):
                for part in range(4):
                    own[part] = result[part * SUB : (part + 1) * SUB]

            @pl.when(k < first_out)
            def _():
                row, column = k // in_columns, k % in_columns

                @pl.when(column == 0)
                def _():
                    load_normed_two(row).wait()

                @pl.when(row == 0)
                def _():
                    load_parts(column).wait()

                here, there = cols(row * PIECE, PIECE), cols(column * TILE, TILE)
                split_rows(down(shared[:, here], wide_ref[:, there]).astype(low))

                @pl.when(k == first_out - in_columns)
                def _():
                    load_two[0].start()

            @pl.when(k == first_out)
            def _():
                begin(load_two[1:])
                load_act.wait()
                load_two[0].wait()

            @pl.when(k == first_out + out_blocks)
            def _():
                finish(load_two[1:])
                load_normed[0].start()

            @pl.when((k >= first_out) & (k < first_branch))
            def _():
                at = k - first_out
                here = cols((at % out_blocks) * SUB, SUB)
                there = cols((at // out_blocks) * 1024, 1024)
                result = down(act_ref[:, here], shared[:, there]).astype(low)
                for part in range(4):
                    own[part] = result[:, part * TILE : (part + 1) * TILE]

            pl.when(k == first_branch - out_blocks + columns // SUB)(lambda: load_gated.start())
            pl.when(k == first_branch - out_blocks + (columns + TILE) // SUB)(lambda: load_branch(0).start())

            @pl.when(k == first_branch)
            def _():
                begin(load_normed[1:])
                load_gated.wait()

            @pl.when((k >= first_branch) & (k < first_mix))
            def _():
                at = k - first_branch
                load_branch(at).wait()
                pl.when(k + 1 < first_mix)(lambda: load_branch(at + 1).start())
                there = cols(columns + (at % 2) * TILE, TILE)
                split_rows(down(act_ref[:, :columns], act_ref[:, there]).astype(low))

            @pl.when(k == first_mix)
            def _():
                finish(load_normed)

            @pl.when(k >= first_mix)
            def _():
                at = k - first_mix
                here = cols(((at // per_row) % in_rows) * PIECE, PIECE)
                there = cols((at // per_part) * columns + (at % per_row) * TILE, TILE)
                split_rows(down(shared[:, here], wide_ref[:, there]).astype(low))

        def targets(k, part):
            one = jnp.minimum(k, first_out - 1)
            two = jnp.clip(k - first_out, 0, first_branch - first_out - 1)
            three = jnp.clip(k - first_branch, 0, first_mix - first_branch - 1)
            four = jnp.maximum(k - first_mix, 0)
            return [
                (
                    k < first_out,
                    in_grad.at[(one // in_columns) * 4 + part, :, cols((one % in_columns) * TILE, TILE)],
                ),
                (
                    (k >= first_out) & (k < first_branch),
                    out_grad.at[two % out_blocks, :, cols((two // out_blocks) * 1024 + part * TILE, TILE)],
                ),
                (
                    (k >= first_branch) & (k < first_mix),
                    branch_grad.at[part, :, cols(three * TILE, TILE)],
                ),
                (
                    k >= first_mix,
                    mix_grad.at[(four // per_row) * 4 + part, :, cols((four % per_row) * TILE, TILE)],
                ),
            ]

        step = line_sum(line, places, count, product, targets)
        now = [0]

        def run(steps):
            lax.fori_loop(now[0], now[0] + steps, step, 0)
            now[0] += steps

        open_sum, join_sum, close_sum = square_sum(
            square,
            places,
            [back_in.at[block(at)] for at in range(2, 8)],
            [landed.at[at] for at in range(4)],
            0,
        )
        ahead = min(3, in_columns)
        load_normed_two(0).start()
        for at in range(ahead):
            load_parts(at).start()
        enter(places)
        run(1)
        open_sum()
        for at in range(ahead, in_columns):
            load_parts(at).start()
        for at in range(1, in_rows):
            load_normed_two(at).start()
        load_act.start()

        def spread(src, slot, kind, place):
            return pltpu.make_async_remote_copy(
                src_ref=src,
                dst_ref=branch_out.at[block(slot)],
                send_sem=gather_sems.at[kind, 0],
                recv_sem=gather_sems.at[kind, 1],
                device_id=place,
                device_id_type=MESH,
            )

        def stage(half):
            return [
                pltpu.make_async_copy(back_in.at[block(half)], stage_ref.at[0], stage_sems.at[0]),
                pltpu.make_async_copy(cot_in.at[block(half)], stage_ref.at[1], stage_sems.at[1]),
                pltpu.make_async_copy(middle_in.at[block(half)], mid_ref, stage_sems.at[2]),
            ]

        keep_branch = [
            pltpu.make_async_copy(branch.at[at], branch_out.at[block(at)], stage_sems.at[3 + at])
            for at in range(2)
        ]

        def rows_back(half):
            def tile(i, carry):
                at = pl.ds(pl.multiple_of(i * 32, 32), 32)
                grad = add_rows(stage_ref[0, at, :], landed[half, at, :], landed[2 + half, at, :])
                result = stage_ref[1, at, :].astype(jnp.float32) + norm_back(mid_ref[at, :], grad)
                grad_ref[at, :] = result
                live_at = pl.ds(pl.multiple_of(half * BLK + i * 32, 32), 32)
                branch[half, at, :] = (live_ref[live_at, :1] * result).astype(low)
                return carry

            lax.fori_loop(0, BLK // 32, tile, 0)
            copy = pltpu.make_async_copy(grad_ref, middle_out.at[block(half)], stage_sems.at[5])
            copy.start()
            return copy

        sends = [
            spread(branch.at[0], 2, 0, near_x),
            spread(branch.at[1], 3, 1, near_y),
            spread(branch.at[1], 4, 2, near_x),
            spread(branch.at[0], 5, 3, near_y),
        ]
        later = [
            spread(branch_out.at[block(3)], 7, 4, near_x),
            spread(branch_out.at[block(2)], 6, 5, near_y),
        ]
        weight_loads = [
            pltpu.make_async_copy(weight_in.at[block(at)], landed.at[at], back_sems.at[at])
            for at in range(columns // BLK)
        ]

        def row_loads(slot):
            return [
                pltpu.make_async_copy(branch_out.at[block(slot + at)], stage_ref.at[at], back_sems.at[2 + at])
                for at in range(2)
            ]

        def back_rows(slot, rows_ref):
            for at in range(2):
                for part in range(len(weight_loads)):
                    result = across(rows_ref[at], landed[part]).astype(low)
                    gated_grad[(slot + at) * BLK : (slot + at + 1) * BLK, part * BLK : (part + 1) * BLK] = result

        def head_loads(head):
            here = cols(head * HS, HS)
            loads = [
                pltpu.make_async_copy(
                    all_in.at[c, :, here],
                    wide_ref.at[:, pl.ds(parts * columns + c * HS, HS)],
                    head_sems.at[c],
                )
                for c in range(parts)
            ]
            loads.append(
                pltpu.make_async_copy(
                    mixing_in.at[:, here],
                    wide_ref.at[:, pl.ds(parts * columns + parts * HS, HS)],
                    head_sems.at[parts],
                )
            )
            loads.append(pltpu.make_async_copy(states_in.at[head], states_ref, head_sems.at[parts + 1]))
            return loads

        open_two, join_two, close_two = square_sum(
            square, places, [two_sums_in.at[block(at)] for at in range(2, 8)], two_landed, 1
        )
        run(9)
        join_sum()
        begin(stage(0))
        run(16)
        close_sum()
        finish(stage(0))
        written = rows_back(0)
        sends[0].start()
        begin(stage(1))
        run(1)
        finish(stage(1))
        written.wait()
        written = rows_back(1)
        begin(sends[1:])
        begin(keep_branch)
        begin(weight_loads)
        run(2)
        finish(weight_loads)
        back_rows(0, branch)
        run(6)
        for copy in sends[:2]:
            copy.wait_recv()
        begin(later)
        begin(row_loads(2))
        run(1)
        finish(row_loads(2))
        back_rows(2, stage_ref)
        run(7)
        for copy in sends[2:]:
            copy.wait_recv()
        begin(row_loads(4))
        run(1)
        finish(row_loads(4))
        back_rows(4, stage_ref)
        run(8)
        begin(head_loads(0))
        for copy in later:
            copy.wait_recv()
        begin(row_loads(6))
        run(1)
        finish(row_loads(6))
        back_rows(6, stage_ref)
        written.wait()
        finish(keep_branch)
        for copy in sends + later:
            copy.wait_send()
        open_two()

        def load_mix(at):
            here = pl.ds(pl.multiple_of(at * BLK, BLK), BLK)
            slot = at % 4
            return [
                pltpu.make_async_copy(
                    mix_in.at[c, here, :], landed.at[slot, :, pl.ds(c * columns, columns)], mix_sems.at[slot, c]
                )
                for c in range(parts)
            ]

        for at in range(4):
            begin(load_mix(at))
        attend_from = now[0]
        breaks = (2, 5, NBLK - 1)

        def attend(head, carry):
            rate = head_rate(heads * narrow + head)
            within, entry, leave, whole = block_decays(rate)
            finish(head_loads(head))
            pl.when(head == heads - 1)(join_two)
            later_grad = jnp.zeros((HS, HS), jnp.float32)
            base = parts * columns
            for at in range(NBLK):
                block_at = NBLK - 1 - at
                here = pl.ds(pl.multiple_of(slot_of(block_at, narrow) * BLK, BLK), BLK)

                def load(c, here=here):
                    return wide_ref[here, base + c * HS : base + (c + 1) * HS]

                def store(c, value, here=here):
                    wide_ref[here, cols(c * columns + head * HS, HS)] = value.astype(low)

                raw_queries = load(0).astype(jnp.float32)
                raw_keys = load(1).astype(jnp.float32)
                queries, keys = jax.nn.silu(raw_queries).astype(low), jax.nn.silu(raw_keys).astype(low)
                values = load(2)
                gate = load(3).astype(jnp.float32)
                mixing = load(4).astype(jnp.float32)
                grad_rows = gated_grad[here, cols(head * HS, HS)].astype(jnp.float32)
                scale = lax.rsqrt(jnp.mean(mixing * mixing, axis=-1, keepdims=True) + head_floor)
                headed = mixing * scale
                store(3, grad_rows * headed)
                grad_headed = grad_rows * gate
                inner = jnp.mean(grad_headed * headed, axis=-1, keepdims=True)
                grad = (scale * (grad_headed - headed * inner)).astype(low)
                scores = (across(queries, keys) * within).astype(low)
                grad_scores = (across(grad, values) * within).astype(low)
                later_low = later_grad.astype(low)
                grad_queries = straight(grad_scores, keys) + entry * across(grad, states_ref[block_at])
                grad_keys = down(grad_scores, queries) + leave * across(values, later_low)
                grad_values = down(scores, grad) + leave * straight(keys, later_low)
                early_queries = (queries.astype(jnp.float32) * entry).astype(low)
                later_grad = keep_ref[block_at : block_at + 1, :1] * (
                    whole * later_grad + down(early_queries, grad)
                )
                store(0, grad_queries * silu_slope(raw_queries))
                store(1, grad_keys * silu_slope(raw_keys))
                store(2, grad_values)
                if at == NBLK - 1:
                    pl.when(head + 1 < heads)(lambda: begin(head_loads(head + 1)))
                if at in breaks:
                    step(attend_from + head * len(breaks) + breaks.index(at), 0)
            return carry

        lax.fori_loop(0, heads, attend, 0)
        now[0] += heads * len(breaks)

        sum_from = now[0]
        side = (mid_ref, grad_ref)

        def put(pair):
            def store(at, here, value):
                pair[at, :, here] = value

            return store

        def put_side(at, here, value):
            side[1 - at][:, here] = value.astype(jnp.float32)

        outs = ((3, put(branch)), (1, put(near)), (2, put_side), (0, put(stage_ref)))

        def sum_tile(at, carry):
            finish(load_mix(at))
            here = cols(at * BLK, BLK)
            for which, (piece, store) in enumerate(outs):
                acts = wide_ref[piece * PIECE : (piece + 1) * PIECE, : parts * columns]
                total = across(acts, landed[at % 4]).astype(low)
                store(0, here, total[:HALF])
                store(1, here, total[HALF:])
                if which == 3:
                    pl.when(at + 4 < width // BLK)(lambda: begin(load_mix(at + 4)))
                if which % 2:
                    step(sum_from + 2 * at + which // 2, 0)
            return carry

        lax.fori_loop(0, width // BLK, sum_tile, 0)
        now[0] += 2 * (width // BLK)
        open_last, join_last, close_last = square_sum(
            square,
            places,
            (near.at[0], near.at[1], None, None, branch.at[0], branch.at[1]),
            last_landed,
            2,
            side,
        )
        close_two()
        open_last()
        run(9)
        join_last()

        def block_loads(half, terms, floats):
            loads = [
                pltpu.make_async_copy(src, landed.at[at], last_sems.at[at]) for at, src in enumerate(terms)
            ]
            loads.append(pltpu.make_async_copy(floats.at[block(half)], mid_ref, last_sems.at[3]))
            return loads

        def block_store(half, out):
            return pltpu.make_async_copy(landed.at[3], out.at[block(half)], last_sems.at[4])

        def layer_loads(half):
            terms = (two_sums_in.at[block(half)], two_landed[half], two_landed[2 + half])
            return block_loads(half, terms, middle_in)

        def input_loads(half):
            terms = (last_landed[half], last_landed[2 + half], hidden_in.at[block(half)])
            return block_loads(half, terms, middle_out)

        def layer_tile(i, carry, half):
            at = pl.ds(pl.multiple_of(i * 32, 32), 32)
            live_at = pl.ds(pl.multiple_of(half * BLK + i * 32, 32), 32)
            branch_two = add_rows(landed[0, at, :], landed[1, at, :], landed[2, at, :])
            landed[3, at, :] = (mid_ref[at, :] + live_ref[live_at, :1] * branch_two).astype(low)
            return carry

        def input_tile(i, carry, half):
            at = pl.ds(pl.multiple_of(i * 32, 32), 32)
            grad_normed = add_rows(stage_ref[half, at, :], landed[0, at, :], landed[1, at, :])
            back = norm_back(landed[2, at, :].astype(jnp.float32), grad_normed)
            landed[3, at, :] = (mid_ref[at, :] + back).astype(low)
            return carry

        def rows_out(loads, tile, out):
            tiles = BLK // 32 // 4
            for half in range(2):
                begin(loads(half))
                run(1)
                finish(loads(half))
                if half:
                    block_store(0, out).wait()
                base = now[0]

                def part(at, carry, half=half, base=base):
                    for one in range(tiles):
                        tile(tiles * at + one, 0, half)
                    step(base + at, 0)
                    return carry

                lax.fori_loop(0, 4, part, 0)
                now[0] += 4
                block_store(half, out).start()

        rows_out(layer_loads, layer_tile, layer_out)
        run(first_mix + 32 - now[0])
        block_store(1, layer_out).wait()
        close_last()
        rows_out(input_loads, input_tile, input_out)
        run(count + STAGES - now[0])
        block_store(1, input_out).wait()

    def low_shape(*shape):
        return jax.ShapeDtypeStruct(shape, low)

    sem = pltpu.SemaphoreType.DMA
    return pl.pallas_call(
        body,
        in_specs=any_specs(16) + [pl.BlockSpec(memory_space=pltpu.VMEM)] * 2,
        out_specs=any_specs(16),
        out_shape=[
            low_shape(width // SUB, SUB, grad_parts.shape[1]),
            low_shape(out_blocks, SUB, width),
            low_shape(columns // SUB, SUB, width),
            low_shape(parts * width // SUB, SUB, columns),
            low_shape(rows, width),
            jax.ShapeDtypeStruct((local_rows, width), jnp.float32),
            low_shape(local_rows, width),
            low_shape(local_rows, width),
        ]
        + [low_shape(BLK, width)] * 8,
        scratch_shapes=[
            pltpu.VMEM((rows, width), low),
            pltpu.VMEM(grad_parts.shape, low),
            pltpu.VMEM(act.shape, low),
            pltpu.VMEM((4, BLK, width), low),
            pltpu.VMEM((2, BLK, width), low),
            pltpu.VMEM((BLK, width), jnp.float32),
            pltpu.VMEM((BLK, width), jnp.float32),
            pltpu.VMEM((2, BLK, width), low),
            pltpu.VMEM((2, BLK, width), low),
            pltpu.VMEM((rows, columns), low),
            pltpu.VMEM((NBLK, HS, HS), low),
            sem((in_rows,)),
            sem((in_columns,)),
            sem((6,)),
            sem((6,)),
            sem((6, 2)),
            sem((4,)),
            sem((parts + 2,)),
            sem((4, parts)),
            sem((2,)),
            sem((5,)),
        ]
        + line_scratch()
        + square_scratch(3),
        compiler_params=pltpu.CompilerParams(
            vmem_limit_bytes=VMEM, collective_id=1, has_side_effects=True
        ),
        cost_estimate=cost(2 * rows * width * (3 * units + 9 * columns), 120e6),
        name="weight_grads",
    )(
        act,
        grad_two_all,
        normed_two_all,
        grad_parts,
        back_sums,
        two_sums,
        middle,
        cotangent,
        out_weight,
        mix_weight,
        parts_all,
        mixing_all,
        states_all,
        gated,
        normed_all,
        hidden,
        live,
        keep,
    )


def gated_unit(gated, whole_weight, hidden, live, grads_own, grads_first, ffn_in, ffn_out):
    _, width, units = ffn_in.shape
    local_rows = hidden.shape[0]
    group_rows = NBLK * BLK
    pieces = group_rows // PIECE
    deep = gated.shape[2]
    slices, quarters, slice_rows, _ = whole_weight.shape
    main = units // TILE * TILE
    tail = units - main
    low = jnp.bfloat16
    cuts = ((0, 2 * TILE), (2 * TILE, main - 2 * TILE))
    wide_tile = 1024
    first_half, second_half = pl.ds(0, HALF), pl.ds(HALF, HALF)

    def body(*refs):
        gated_in, weight_in, hidden_in = refs[:3]
        grad_in = refs[3:5]
        in_ref, out_ref, live_ref = refs[5:8]
        middle_out, rows_out, grads_out, act_out, parts_out, back_out, two_out = refs[8:15]
        gated_ref, hidden_ref, middle_ref = refs[15:18]
        rows, grads, sums, w_in, w_out, act, parts, held = refs[18:26]
        load_sems, slice_sems, weight_sems, done_sems, sum_sems, last_sems, gated_sems, gather_sems = refs[26:]
        wide, narrow, _, _, _, near_x, near_y = neighbours()
        far = (wide, 3 - narrow)
        here = pl.ds(pl.multiple_of(narrow * deep, deep), deep)

        def send_gated(slot, to, kind, place):
            return pltpu.make_async_remote_copy(
                src_ref=gated_in.at[0, pl.ds(slot * BLK, BLK)],
                dst_ref=gated_ref.at[(first_half, second_half)[to], here],
                send_sem=gated_sems.at[kind, 0],
                recv_sem=gated_sems.at[kind, 1],
                device_id=place,
                device_id_type=MESH,
            )

        gated_sends = [
            send_gated(6, 0, 0, far),
            send_gated(7, 1, 1, far),
            send_gated(2, 0, 2, near_x),
            send_gated(3, 1, 3, near_y),
            send_gated(4, 1, 4, near_x),
            send_gated(5, 0, 5, near_y),
        ]
        keep_gated = pltpu.make_async_copy(
            gated_in.at[0, pl.ds(0, PIECE)], gated_ref.at[:, here], load_sems.at[0]
        )

        def load_slice(at):
            part, quarter = at // quarters, at % quarters
            to = pl.ds(pl.multiple_of(quarter * deep + part * slice_rows, slice_rows), slice_rows)
            return pltpu.make_async_copy(
                weight_in.at[part, quarter], w_in.at[to, pl.ds(0, width)], slice_sems.at[at]
            )

        def start_slice(at, carry):
            load_slice(at).start()
            return carry

        def wait_slice(at, carry):
            load_slice(at).wait()
            return carry

        load_hidden = pltpu.make_async_copy(hidden_in, hidden_ref, load_sems.at[1])
        load_grads = [
            pltpu.make_async_copy(src, grads.at[at], load_sems.at[2 + at])
            for at, src in enumerate(grad_in)
        ]
        weights = []
        for start, size, first, second in tuple((a, b, a, main + a) for a, b in cuts) + (
            (main, tail, 2 * main, 2 * main + tail),
        ):
            at = pl.ds(start, size)
            weights += [
                pltpu.make_async_copy(in_ref.at[0, :, at], w_in.at[:, pl.ds(first, size)], weight_sems.at[len(weights)]),
                pltpu.make_async_copy(in_ref.at[1, :, at], w_in.at[:, pl.ds(second, size)], weight_sems.at[len(weights) + 1]),
                pltpu.make_async_copy(out_ref.at[at, :], w_out.at[at, :], weight_sems.at[len(weights) + 2]),
            ]

        def remote(src, dst, sems, kind, place):
            return pltpu.make_async_remote_copy(
                src_ref=src,
                dst_ref=dst,
                send_sem=sems.at[kind, 0],
                recv_sem=sems.at[kind, 1],
                device_id=place,
                device_id_type=MESH,
            )

        def half(ref, piece, at):
            return ref.at[piece, (first_half, second_half)[at]]

        def quarter(ref, piece, at):
            return ref.at[piece, pl.ds(at * SUB, SUB)]

        def gather(ref, kind):
            return (
                [
                    remote(half(ref, 0, 0), half(ref, 1, 0), gather_sems, kind, near_x),
                    remote(half(ref, 0, 1), half(ref, 1, 1), gather_sems, kind + 1, near_y),
                ],
                [
                    remote(half(ref, 0, 1), half(ref, 2, 0), gather_sems, kind + 2, near_x),
                    remote(half(ref, 0, 0), half(ref, 2, 1), gather_sems, kind + 3, near_y),
                ],
                [
                    remote(quarter(ref, 1, 2), quarter(ref, 3, 1), gather_sems, kind + 4, near_x),
                    remote(quarter(ref, 1, 0), quarter(ref, 3, 0), gather_sems, kind + 5, near_y),
                ],
                [
                    remote(quarter(ref, 1, 3), quarter(ref, 3, 3), gather_sems, kind + 6, near_x),
                    remote(quarter(ref, 1, 1), quarter(ref, 3, 2), gather_sems, kind + 7, near_y),
                ],
            )

        row_sends = gather(rows, 0)
        grad_sends = gather(grads, 8)

        begin(load_grads)
        begin([keep_gated, load_hidden])
        barrier = pltpu.get_barrier_semaphore()
        for place in (near_x, near_y, far):
            pl.semaphore_signal(barrier, inc=1, device_id=place, device_id_type=MESH)
        pl.semaphore_wait(barrier, 3)
        begin(gated_sends)
        lax.fori_loop(0, slices * quarters, start_slice, 0)
        finish(load_grads)
        begin(grad_sends[1])
        finish([keep_gated, load_hidden])
        lax.fori_loop(0, slices * quarters, wait_slice, 0)
        finish(gated_sends)
        for j in range(width // wide_tile):
            at = slice(j * wide_tile, (j + 1) * wide_tile)
            middle_ref[:, at] = straight(gated_ref[...], w_in[:, at])
        begin(weights)

        def second_norm(i, carry, at):
            here = pl.ds(pl.multiple_of(at * HALF + i * 32, 32), 32)
            middle = hidden_ref[here, :].astype(jnp.float32) + live_ref[here, :1] * middle_ref[here, :]
            middle_ref[here, :] = middle
            rows[0, here, :] = row_norm(middle).astype(low)
            return carry

        for at in range(2):
            lax.fori_loop(0, HALF // 32, functools.partial(second_norm, at=at), 0)
            row_sends[0][at].start()
        begin(row_sends[1])
        store_middle = pltpu.make_async_copy(middle_ref, middle_out, done_sems.at[0])
        store_middle.start()

        def products(size, at, first, second, part_a, part_b, grad_act):
            act[:size, at] = (part_a * part_b).astype(low)
            parts[:size, first] = (grad_act * part_b).astype(low)
            parts[:size, second] = (grad_act * part_a).astype(low)

        def unit(arrived, arrived_grads, size, weights_wait):
            for which, (start, count) in enumerate(cuts):
                at, second = slice(start, start + count), slice(main + start, main + start + count)
                weights_wait(3 * which, 3 * which + 3)
                part_a = straight(arrived[...], w_in[:, at])
                part_b = straight(arrived[...], w_in[:, second])
                grad_act = across(arrived_grads[...], w_out[at, :])
                products(size, at, at, second, part_a, part_b, grad_act)
            weights_wait(6, 9)
            if tail:
                both = straight(arrived[...], w_in[:, 2 * main :])
                grad_act = across(arrived_grads[...], w_out[main:, :])
                products(
                    size,
                    slice(main, units),
                    slice(2 * main, 2 * main + tail),
                    slice(2 * main + tail, 2 * units),
                    both[:, :tail],
                    both[:, tail:],
                    grad_act,
                )

        def row_stores(arrived, arrived_grads, at):
            return [
                pltpu.make_async_copy(arrived, rows_out.at[at, :], done_sems.at[1]),
                pltpu.make_async_copy(arrived_grads, grads_out.at[at, :], done_sems.at[2]),
            ]

        def unit_stores(size, at):
            here = pl.ds(0, size)
            return [
                pltpu.make_async_copy(act.at[here], act_out.at[at, :], done_sems.at[3]),
                pltpu.make_async_copy(parts.at[here], parts_out.at[at, :], done_sems.at[4]),
            ]

        def sum_stores(piece, j):
            tile = pl.ds(j * wide_tile, wide_tile)
            return [
                pltpu.make_async_copy(
                    sums.at[at, :, tile],
                    (back_out, two_out)[at // 2].at[
                        pl.ds(pl.multiple_of(piece * PIECE + (at % 2) * HALF, HALF), HALF), tile
                    ],
                    sum_sems.at[j, at],
                )
                for at in range(4)
            ]

        def work(piece, carry):
            at = pl.ds(pl.multiple_of(piece * PIECE, PIECE), PIECE)
            arrived, arrived_grads = rows.at[piece], grads.at[piece]

            @pl.when(piece == 1)
            def _():
                finish(row_sends[0])
                for step in (2, 3):
                    begin(row_sends[step])
                    begin(grad_sends[step])

            @pl.when(piece == 2)
            def _():
                finish(row_sends[1])
                finish(grad_sends[1])

            stores = row_stores(arrived, arrived_grads, at)
            begin(stores)

            def weights_wait(start, stop):
                pl.when(piece == 0)(lambda: finish(weights[start:stop]))

            unit(arrived, arrived_grads, PIECE, weights_wait)
            more = unit_stores(PIECE, at)
            begin(more)
            for j in range(width // wide_tile):
                tile = slice(j * wide_tile, (j + 1) * wide_tile)

                @pl.when(piece > 0)
                def _(j=j):
                    finish(sum_stores(piece - 1, j))

                back = across(parts[...], w_in[tile, :])
                sums[0, :, tile] = back[:HALF].astype(low)
                sums[1, :, tile] = back[HALF:].astype(low)
                two = straight(act[...], w_out[:, tile])
                sums[2, :, tile] = two[:HALF].astype(low)
                sums[3, :, tile] = two[HALF:].astype(low)
                begin(sum_stores(piece, j))
            finish(stores)
            finish(more)
            return carry

        lax.fori_loop(0, pieces - 1, work, 0)
        for j in range(width // wide_tile):
            finish(sum_stores(pieces - 2, j))

        def last_stores(which, total, j):
            tile = pl.ds(j * wide_tile, wide_tile)
            return [
                pltpu.make_async_copy(
                    sums.at[2 * total + which, pl.ds(part * SUB, SUB), tile],
                    (back_out, two_out)[total].at[
                        pl.ds(pl.multiple_of((pieces - 1) * PIECE + part * HALF + which * SUB, SUB), SUB), tile
                    ],
                    last_sems.at[which, 2 * total + part, j],
                )
                for part in range(2)
            ]

        def last_work(which, carry):
            here = pl.ds(pl.multiple_of(which * HALF, HALF), HALF)
            at = pl.ds(pl.multiple_of((pieces - 1) * PIECE + which * HALF, HALF), HALF)
            arrived, arrived_grads = rows.at[pieces - 1, here], grads.at[pieces - 1, here]
            pl.when(which == 0)(lambda: finish(row_sends[2]))
            pl.when(which == 1)(lambda: finish(row_sends[3]))
            held[...] = straight(arrived[...], w_in[...])

            def columns_of(start, stop):
                first, second = slice(start, stop), slice(main + start, main + stop)
                if start == main:
                    first, second = slice(2 * main, 2 * main + tail), slice(2 * main + tail, 2 * units)
                return first, second

            ranges = ((0, main), (main, units)) if tail else ((0, main),)
            for start, stop in ranges:
                first, second = columns_of(start, stop)
                act[:HALF, start:stop] = (held[:, first] * held[:, second]).astype(low)
            for j in range(width // wide_tile):
                tile = slice(j * wide_tile, (j + 1) * wide_tile)
                sums[2 + which, :, tile] = straight(act[:HALF], w_out[:, tile]).astype(low)
                begin(last_stores(which, 1, j))
            pl.when(which == 0)(lambda: finish(grad_sends[2]))
            pl.when(which == 1)(lambda: finish(grad_sends[3]))
            stores = row_stores(arrived, arrived_grads, at)
            begin(stores)
            for start, stop in ranges:
                first, second = columns_of(start, stop)
                grad_act = across(arrived_grads[...], w_out[start:stop, :])
                parts[:HALF, first] = (grad_act * held[:, second]).astype(low)
                parts[:HALF, second] = (grad_act * held[:, first]).astype(low)
            more = unit_stores(HALF, at)
            begin(more)
            for j in range(width // wide_tile):
                tile = slice(j * wide_tile, (j + 1) * wide_tile)
                sums[which, :, tile] = across(parts[:HALF], w_in[tile, :]).astype(low)
                begin(last_stores(which, 0, j))
            finish(stores)
            finish(more)
            return carry

        lax.fori_loop(0, 2, last_work, 0)
        for which in range(2):
            for total in range(2):
                for j in range(width // wide_tile):
                    finish(last_stores(which, total, j))
        store_middle.wait()

    return pl.pallas_call(
        body,
        in_specs=any_specs(7) + [pl.BlockSpec(memory_space=pltpu.VMEM)],
        out_specs=any_specs(7),
        out_shape=[
            jax.ShapeDtypeStruct((local_rows, width), jnp.float32),
            jax.ShapeDtypeStruct((group_rows, width), low),
            jax.ShapeDtypeStruct((group_rows, width), low),
            jax.ShapeDtypeStruct((group_rows, units), low),
            jax.ShapeDtypeStruct((group_rows, 2 * units), low),
            jax.ShapeDtypeStruct((group_rows, width), low),
            jax.ShapeDtypeStruct((group_rows, width), low),
        ],
        scratch_shapes=[
            pltpu.VMEM((local_rows, quarters * deep), low),
            pltpu.VMEM((local_rows, width), low),
            pltpu.VMEM((local_rows, width), jnp.float32),
            pltpu.VMEM((pieces, PIECE, width), low),
            pltpu.VMEM((pieces, PIECE, width), low),
            pltpu.VMEM((4, HALF, width), low),
            pltpu.VMEM((width, 2 * units), low),
            pltpu.VMEM((units, width), low),
            pltpu.VMEM((PIECE, units), low),
            pltpu.VMEM((PIECE, 2 * units), low),
            pltpu.VMEM((HALF, 2 * units), jnp.float32),
            pltpu.SemaphoreType.DMA((4,)),
            pltpu.SemaphoreType.DMA((slices * quarters,)),
            pltpu.SemaphoreType.DMA((9,)),
            pltpu.SemaphoreType.DMA((5,)),
            pltpu.SemaphoreType.DMA((width // wide_tile, 4)),
            pltpu.SemaphoreType.DMA((2, 4, width // wide_tile)),
            pltpu.SemaphoreType.DMA((6, 2)),
            pltpu.SemaphoreType.DMA((16, 2)),
        ],
        compiler_params=pltpu.CompilerParams(
            vmem_limit_bytes=VMEM, collective_id=3, has_side_effects=True
        ),
        cost_estimate=cost(12 * group_rows * width * units, 90e6),
        name="gated_unit",
    )(gated, whole_weight, hidden, grads_own, grads_first, ffn_in, ffn_out, live)


def mix_rows(hidden, cotangent, mix_weight, out_weight, seq_lengths, block_seq):
    local_rows, width = hidden.shape
    parts, _, columns = mix_weight.shape
    heads = columns // HS
    group_rows = NBLK * BLK
    pieces = group_rows // PIECE
    wide_size = lax.axis_size("wide")
    slice_rows = columns // wide_size
    low = jnp.bfloat16
    joined = 2
    halves_at = (pl.ds(0, HALF), pl.ds(HALF, HALF))

    def body(*refs):
        hidden_in, cot_in, mix_in, out_in, length_ref, owner_ref = refs[:6]
        rows_out, parts_out, gated_out, mixing_out, states_out, grads_out, first_out, whole_out = refs[6:14]
        live_ref, keep_ref = refs[14:16]
        hidden_ref, cot_ref, rows, weights, parts_ref, gated_ref, mixing_ref, states_ref = refs[16:24]
        load_sems, mix_sems, store_sems, parts_sems, gather_sems, slice_sems, line_sems, core_sems = refs[24:]
        wide, narrow, z, core, mate, near_x, near_y = neighbours()
        far = (wide, 3 - narrow)
        above, below = (wide + 2, narrow), (wide - 2, narrow)
        barrier = pltpu.get_barrier_semaphore()

        def greet(place):
            pl.semaphore_signal(barrier, inc=1, device_id=place, device_id_type=MESH)

        load_hidden = pltpu.make_async_copy(hidden_in, hidden_ref, load_sems.at[0])
        load_cot = pltpu.make_async_copy(cot_in, cot_ref, load_sems.at[1])
        mix_loads = [
            pltpu.make_async_copy(
                mix_in.at[c], weights.at[:, pl.ds(c * columns, columns)], mix_sems.at[c]
            )
            for c in range(parts)
        ]
        load_hidden.start()
        for place in (near_x, near_y, far, mate):
            greet(place)
        pl.when(z < 3)(lambda: greet(above))
        pl.when(z > 0)(lambda: greet(below))
        middle = (z == 1) | (z == 2)
        pl.when(middle)(lambda: pl.semaphore_wait(barrier, 6))
        pl.when(jnp.logical_not(middle))(lambda: pl.semaphore_wait(barrier, 5))

        def remote(src, dst, sems, kind, place):
            return pltpu.make_async_remote_copy(
                src_ref=src,
                dst_ref=dst,
                send_sem=sems.at[kind, 0],
                recv_sem=sems.at[kind, 1],
                device_id=place,
                device_id_type=MESH,
            )

        slice_at = out_in.at[pl.ds(pl.multiple_of(wide * slice_rows, slice_rows), slice_rows)]
        keep_slice = pltpu.make_async_copy(slice_at, whole_out.at[wide, narrow], load_sems.at[2])
        slice_sends = [
            remote(slice_at, whole_out.at[wide, narrow], slice_sems, at, place)
            for at, place in enumerate((far, near_x, near_y))
        ]

        def up(hop):
            return remote(
                whole_out.at[wide - 2 * (hop - 1)], whole_out.at[wide - 2 * (hop - 1)], line_sems, hop - 1, above
            )

        def down_line(hop):
            return remote(
                whole_out.at[wide + 2 * (hop - 1)], whole_out.at[wide + 2 * (hop - 1)], line_sems, 2 + hop, below
            )

        def to_mate(hop, sign):
            at = wide + sign * 2 * hop
            return remote(whole_out.at[at], whole_out.at[at], core_sems, 3 + sign * hop, mate)

        def send_hop(hop):
            pl.when((z < 3) & (z >= hop - 1))(lambda: up(hop).start())
            pl.when((z > 0) & (z + hop - 1 <= 3))(lambda: down_line(hop).start())

        def take_hop(hop):
            @pl.when(z >= hop)
            def _():
                arrived = whole_out.at[wide - 2 * hop]
                remote(arrived, arrived, line_sems, hop - 1, mate).wait_recv()
                to_mate(hop, -1).start()

            @pl.when(z + hop <= 3)
            def _():
                arrived = whole_out.at[wide + 2 * hop]
                remote(arrived, arrived, line_sems, 2 + hop, mate).wait_recv()
                to_mate(hop, 1).start()

        def end_hop(hop):
            pl.when((z < 3) & (z >= hop - 1))(lambda: up(hop).wait_send())
            pl.when((z > 0) & (z + hop - 1 <= 3))(lambda: down_line(hop).wait_send())
            pl.when(z >= hop)(lambda: to_mate(hop, -1).wait())
            pl.when(z + hop <= 3)(lambda: to_mate(hop, 1).wait())

        begin(slice_sends)
        keep_slice.start()

        def half(piece, at):
            return rows.at[piece, halves_at[at]]

        row_sends = (
            [remote(half(0, 0), half(1, 0), gather_sems, 0, near_x), remote(half(0, 1), half(1, 1), gather_sems, 1, near_y)],
            [remote(half(0, 1), half(2, 0), gather_sems, 2, near_x), remote(half(0, 0), half(2, 1), gather_sems, 3, near_y)],
            [remote(half(1, 1), half(3, 1), gather_sems, 4, near_x), remote(half(1, 0), half(3, 0), gather_sems, 5, near_y)],
        )
        grad_sends = [
            remote(cot_ref.at[halves_at[0]], first_out.at[halves_at[0]], gather_sems, 6, near_x),
            remote(cot_ref.at[halves_at[1]], first_out.at[halves_at[1]], gather_sems, 7, near_y),
        ]
        load_hidden.wait()
        begin(mix_loads)
        load_cot.start()

        def first_norm(i, carry):
            at = pl.ds(pl.multiple_of(i * 32, 32), 32)
            rows[0, at, :] = row_norm(hidden_ref[at, :].astype(jnp.float32)).astype(low)
            return carry

        for at in range(2):
            lax.fori_loop(at * HALF // 32, (at + 1) * HALF // 32, first_norm, 0)
            row_sends[0][at].start()
        begin(row_sends[1])

        def row_store(piece):
            at = pl.ds(piece * PIECE, PIECE)
            return pltpu.make_async_copy(rows.at[piece], rows_out.at[at, :], store_sems.at[piece])

        def part_stores(piece):
            at = pl.ds(piece * PIECE, PIECE)
            return [
                pltpu.make_async_copy(
                    parts_ref.at[at, pl.ds(c * columns, columns)], parts_out.at[c, at, :], parts_sems.at[piece, c]
                )
                for c in range(parts)
            ]

        def project(piece):
            row_store(piece).start()
            for c in range(0, parts, joined):
                if piece == 0:
                    finish(mix_loads[c : c + joined])
                at = slice(c * columns, (c + joined) * columns)
                result = straight(rows[piece], weights[:, at]).astype(low)
                parts_ref[piece * PIECE : (piece + 1) * PIECE, at] = result
            begin(part_stores(piece))

        def same_slot(block):
            return owner_ref[block] == owner_ref[0]

        first_count = sum(jnp.where(same_slot(block), 1, 0) for block in range(NBLK))

        def start_of(block):
            return jnp.where(same_slot(block), 0, first_count)

        for block in range(NBLK):
            entering = jnp.where(start_of(block) == block, 0.0, 1.0)
            keep_ref[block : block + 1, :] = jnp.full((1, HS), entering, jnp.float32)
        for at in range(local_rows // BLK):
            block = narrow * (local_rows // BLK) + at
            limit = jnp.where(same_slot(block), length_ref[0], length_ref[1])
            place = lax.broadcasted_iota(jnp.int32, (BLK, HS), 0) + (block - start_of(block)) * BLK
            live_ref[at * BLK : (at + 1) * BLK, :] = jnp.where(place < limit, 1.0, 0.0)
        project(0)
        load_cot.wait()

        def live_cot(i, carry):
            at = pl.ds(pl.multiple_of(i * 32, 32), 32)
            cot_ref[at, :] = (live_ref[at, :1] * cot_ref[at, :].astype(jnp.float32)).astype(low)
            return carry

        keep_slice.wait()
        finish(slice_sends)
        to_mate(0, 1).start()
        send_hop(1)
        lax.fori_loop(0, local_rows // 32, live_cot, 0)
        store_grads = pltpu.make_async_copy(cot_ref, grads_out, load_sems.at[3])
        store_grads.start()
        finish(row_sends[0])
        begin(row_sends[2])
        begin(grad_sends)
        project(1)
        take_hop(1)
        send_hop(2)
        finish(row_sends[1])
        project(2)
        take_hop(2)
        send_hop(3)
        finish(row_sends[2])
        project(3)

        def attend(head, carry):
            within, entry, leave, whole = block_decays(head_rate(heads * narrow + head))
            state = jnp.zeros((HS, HS), jnp.float32)

            def part(c, rows_at):
                at = pl.ds(pl.multiple_of(c * columns + head * HS, HS), HS)
                return parts_ref[rows_at, at]

            for block in range(NBLK):
                rows_at = pl.ds(pl.multiple_of(slot_of(block, narrow) * BLK, BLK), BLK)
                queries = jax.nn.silu(part(0, rows_at).astype(jnp.float32)).astype(low)
                keys = jax.nn.silu(part(1, rows_at).astype(jnp.float32)).astype(low)
                values = part(2, rows_at)
                gate = part(3, rows_at).astype(jnp.float32)
                state = keep_ref[block : block + 1, :] * state
                state_low = state.astype(low)
                states_ref[head, block] = state_low
                scores = (across(queries, keys) * within).astype(low)
                mixing = straight(scores, values) + entry * straight(queries, state_low)
                late_keys = (keys.astype(jnp.float32) * leave).astype(low)
                state = whole * state + down(late_keys, values)
                scale = lax.rsqrt(jnp.mean(mixing * mixing, axis=-1, keepdims=True) + head_floor)
                at = pl.ds(pl.multiple_of(head * HS, HS), HS)
                gated_ref[rows_at, at] = (mixing * scale * gate).astype(low)
                mixing_ref[rows_at, at] = mixing.astype(low)
            return carry

        lax.fori_loop(0, heads // 2, attend, 0)
        take_hop(3)
        lax.fori_loop(heads // 2, heads, attend, 0)
        stores = [
            pltpu.make_async_copy(gated_ref, gated_out.at[0], load_sems.at[4]),
            pltpu.make_async_copy(mixing_ref, mixing_out, load_sems.at[5]),
            pltpu.make_async_copy(states_ref, states_out, load_sems.at[6]),
        ]
        begin(stores)
        to_mate(0, 1).wait()
        for hop in range(1, 4):
            end_hop(hop)
        finish(grad_sends)
        store_grads.wait()
        for piece in range(pieces):
            row_store(piece).wait()
            finish(part_stores(piece))
        finish(stores)

    low_shape = functools.partial(jax.ShapeDtypeStruct, dtype=low)
    return pl.pallas_call(
        body,
        in_specs=any_specs(4) + [pl.BlockSpec(memory_space=pltpu.SMEM)] * 2,
        out_specs=any_specs(8) + [pl.BlockSpec(memory_space=pltpu.VMEM)] * 2,
        out_shape=[
            low_shape((group_rows, width)),
            low_shape((parts, group_rows, columns)),
            low_shape((1, group_rows, columns)),
            low_shape((group_rows, columns)),
            low_shape((heads, NBLK, HS, HS)),
            low_shape((local_rows, width)),
            low_shape((local_rows, width)),
            low_shape((wide_size, pieces, slice_rows, width)),
            jax.ShapeDtypeStruct((local_rows, HS), jnp.float32),
            jax.ShapeDtypeStruct((NBLK, HS), jnp.float32),
        ],
        scratch_shapes=[
            pltpu.VMEM((local_rows, width), low),
            pltpu.VMEM((local_rows, width), low),
            pltpu.VMEM((pieces, PIECE, width), low),
            pltpu.VMEM((width, parts * columns), low),
            pltpu.VMEM((group_rows, parts * columns), low),
            pltpu.VMEM((group_rows, columns), low),
            pltpu.VMEM((group_rows, columns), low),
            pltpu.VMEM((heads, NBLK, HS, HS), low),
            pltpu.SemaphoreType.DMA((7,)),
            pltpu.SemaphoreType.DMA((parts,)),
            pltpu.SemaphoreType.DMA((pieces,)),
            pltpu.SemaphoreType.DMA((pieces, parts)),
            pltpu.SemaphoreType.DMA((8, 2)),
            pltpu.SemaphoreType.DMA((3, 2)),
            pltpu.SemaphoreType.DMA((6, 2)),
            pltpu.SemaphoreType.DMA((7, 2)),
        ],
        compiler_params=pltpu.CompilerParams(
            vmem_limit_bytes=VMEM, collective_id=4, has_side_effects=True
        ),
        cost_estimate=cost(2 * group_rows * parts * width * columns, 50e6),
        name="mix_rows",
    )(hidden, cotangent, mix_weight, out_weight, seq_lengths, block_seq)


def widen(mix_low, out_low, in_low, wide_low, rows):
    parts, width, columns = mix_low.shape
    units = wide_low.shape[0]
    main = units // TILE * TILE
    tail = units - main
    steps = parts

    def body(mix_ref, out_ref, in_ref, wide_ref, one_ref, two_ref, mix_out, out_out, in_out, wide_out, one_out, two_out):
        one_out[...] = one_ref[...]
        two_out[...] = two_ref[...]
        mix_out[...] = mix_ref[...].astype(jnp.float32)
        out_out[...] = out_ref[...].astype(jnp.float32)
        wide_out[...] = wide_ref[...].astype(jnp.float32)
        for c in range(2):
            in_out[c, :, :main] = in_ref[:, c * main : (c + 1) * main].astype(jnp.float32)
            rest = slice(2 * main + c * tail, 2 * main + (c + 1) * tail)
            in_out[c, :, main:] = in_ref[:, rest].astype(jnp.float32)

    def rows_spec(array):
        return pl.BlockSpec((array.shape[0] // steps, array.shape[1]), lambda i: (i, 0))

    mix_spec = pl.BlockSpec((1, width, columns), lambda i: (i, 0, 0))
    shapes = (mix_low.shape, out_low.shape, (2, width, units), wide_low.shape)
    return pl.pallas_call(
        body,
        grid=(steps,),
        in_specs=[mix_spec] + [rows_spec(array) for array in (out_low, in_low, wide_low, *rows)],
        out_specs=[
            mix_spec,
            rows_spec(out_low),
            pl.BlockSpec((2, width // steps, units), lambda i: (0, i, 0)),
            rows_spec(wide_low),
            *(rows_spec(array) for array in rows),
        ],
        out_shape=[jax.ShapeDtypeStruct(shape, jnp.float32) for shape in shapes]
        + [jax.ShapeDtypeStruct(array.shape, array.dtype) for array in rows],
        compiler_params=pltpu.CompilerParams(vmem_limit_bytes=VMEM),
        cost_estimate=cost(1e8, 84e6),
        name="widen",
    )(mix_low, out_low, in_low, wide_low, *rows)


def block_decays(rate):
    row = lax.broadcasted_iota(jnp.int32, (BLK, BLK), 0)
    column = lax.broadcasted_iota(jnp.int32, (BLK, BLK), 1)
    distance = (row - column).astype(jnp.float32)
    within = jnp.where(row >= column, jnp.exp(-rate * jnp.maximum(distance, 0.0)), 0.0)
    place = lax.broadcasted_iota(jnp.int32, (BLK, 1), 0).astype(jnp.float32)
    entry = jnp.exp(-rate * (place + 1.0))
    leave = jnp.exp(-rate * (BLK - 1.0 - place))
    whole = jnp.exp(-BLK * rate * jnp.ones((1, HS), jnp.float32))
    return within, entry, leave, whole


def norm_back(values, grad):
    scale = lax.rsqrt(jnp.mean(values * values, axis=-1, keepdims=True) + epsilon)
    unit = values * scale
    return scale * (grad - unit * jnp.mean(grad * unit, axis=-1, keepdims=True))


def square_device(
    hidden, mix_weight, out_weight, ffn_in_weight, ffn_out_weight, seq_lengths, block_seq, cotangent
):
    width = hidden.shape[1]
    units = ffn_out_weight.shape[0]
    normed_all, parts, gated, mixing, states, grads_own, grads_first, whole_weight, live, keep = mix_rows(
        hidden, cotangent, mix_weight, out_weight, seq_lengths, block_seq
    )
    middle, normed_two_all, grad_two_all, act, grad_parts, back_sums, two_sums = gated_unit(
        gated,
        whole_weight,
        hidden,
        live,
        grads_own,
        grads_first,
        ffn_in_weight,
        ffn_out_weight,
    )
    in_low, wide_low, out_low, mix_low, _, _, layer_out, input_grad, *_ = weight_grads(
        act,
        grad_two_all,
        normed_two_all,
        grad_parts,
        back_sums,
        two_sums,
        middle,
        cotangent,
        out_weight,
        mix_weight,
        parts,
        mixing,
        states,
        gated,
        normed_all,
        hidden,
        live,
        keep,
    )
    grad_mix, grad_out, grad_ffn_in, grad_ffn_out, layer_out, input_grad = widen(
        mix_low.reshape(mix_weight.shape),
        out_low.reshape(out_weight.shape),
        in_low.reshape(width, 2 * units),
        wide_low.reshape(units, width),
        (layer_out, input_grad),
    )
    return (layer_out, input_grad, grad_mix, grad_out, grad_ffn_in, grad_ffn_out)


def solution(mesh):
    square = mesh.shape["wide"] == 8 and mesh.shape["narrow"] == 4
    per_device = square_device if square else general_device
    in_specs = (
        P(("wide", "narrow"), None),
        P(None, None, "narrow"),
        P("narrow", None),
        P(None, None, "narrow"),
        P("narrow", None),
        P("wide"),
        P("wide"),
        P(("wide", "narrow"), None),
    )
    out_specs = (
        P(("wide", "narrow"), None),
        P(("wide", "narrow"), None),
        P(None, None, "narrow"),
        P("narrow", None),
        P(None, None, "narrow"),
        P("narrow", None),
    )
    return jax.shard_map(
        per_device, mesh=mesh, in_specs=in_specs, out_specs=out_specs, check_vma=False
    )
```
